32 devices in a mesh: grp: 2 (over x), seq: 16 (over z, y, core).
Axes of the slice: x: 2, y: 2, z: 4, core: 2. Of those that a mesh axis runs over, the one named last changes fastest.
Arguments:
- frames: bfloat16 [4096, 2048], P(('grp', 'seq')), parts along dimension 0
- conv_weight: bfloat16 [4, 2048], replicated, may hold values from -2.390625 to 2.390625
- qkv_weight: bfloat16 [2048, 3072], P(None, 'seq'), may hold values from -0.125 to 0.125
- track_ids: int32 [4096], P(('grp', 'seq')), parts along dimension 0, may hold values from 0 to 63, as said below
- track_owner: int32 [128], P('grp'), parts along dimension 0, may hold values from 0 to 15, as said below
Outputs:
- context: bfloat16 [4096, 1024], P(('grp', 'seq')), parts along dimension 0
The draws below stay inside these ranges and needn't reach their ends.
There are 2 independent parts, one for each index of `grp`. The reference program is written for one: setup_inputs(seed, part) draws one part's arguments, and reference() takes and returns one part's arrays. A program takes and returns all parts, laid end to end along the dimension named above; an argument that names none is the same for every part. Nothing has to cross between parts.
Inputs may be any that keep to these rules, and one draw needn't show every extreme that they name: `track_ids`: counting each token by track_owner of its track, the tokens of one device fall on each owning device at most 16 times, and one owning device receives exactly 16 tokens from every device. `track_owner`: every device owns exactly 4 tracks.
All inputs are finite; a program needn't handle non-finite values.
Results may differ from the reference program's by a relative error of at most 0.005.
The reference program's roundings to bfloat16 on the way (of `hidden`, `projected` and `weights`) count: a program that leaves them out, or rounds other values in their place, can miss the bound.
Values may be sent and summed in bfloat16 or wider, within the bound.
No kernel may reach another device: no remote copies, remote signals or barrier semaphores. Data moves between devices by JAX's collectives and lax.ppermute only.
A program may use at most 64 MiB of HBM per device.

```python
import jax
import jax.numpy as jnp
from jax import lax

D = 2048
HD = 128
HEADS = 8
KW = 4
TRK_DEV = 4
TOK_DEV = 128
TOKENS = 2048
NTRACKS = 64
CAP = 16
N_SEQ = 16


def route_draw(key):
    table_key, hot_key, rows_key = jax.random.split(key, 3)
    track_total = TRK_DEV * N_SEQ
    shuffled = jax.random.permutation(table_key, track_total).astype(jnp.int32)
    owner_table = (shuffled // TRK_DEV).astype(jnp.int32)
    inverse = jnp.zeros((track_total,), jnp.int32).at[shuffled].set(jnp.arange(track_total, dtype=jnp.int32))
    hot_owner = jax.random.randint(hot_key, (), 0, N_SEQ).astype(jnp.int32)
    others = (hot_owner + 1 + jnp.arange(N_SEQ - 1, dtype=jnp.int32)) % N_SEQ
    pool = jnp.repeat(others, CAP)

    def one_device(device_key):
        pick_key, order_key, track_key = jax.random.split(device_key, 3)
        chosen = jax.random.permutation(pick_key, pool)[:TOK_DEV - CAP]
        targets = jnp.concatenate([jnp.full((CAP,), hot_owner, jnp.int32), chosen.astype(jnp.int32)])
        targets = jax.random.permutation(order_key, targets)
        within = jax.random.randint(track_key, (TOK_DEV,), 0, TRK_DEV).astype(jnp.int32)
        return inverse[targets * TRK_DEV + within]
    device_keys = jax.random.split(rows_key, N_SEQ)
    tracks = jax.vmap(one_device)(device_keys).reshape(-1).astype(jnp.int32)
    return (owner_table, tracks)


def draw_track_owner(key, part):
    routes = route_draw(key)
    return routes[0]


def draw_track_ids(key, part):
    routes = route_draw(key)
    return routes[1]


def draw_frames(key, part):
    key = jax.random.fold_in(key, 7)
    value_key = jax.random.fold_in(key, 0)
    values = jnp.clip(jax.random.normal(value_key, (TOKENS, D), jnp.float32), -6.0, 6.0)
    return values.astype(jnp.bfloat16)


def block_levels(stream_key, extent, shards, least, largest):
    level = 1.0
    for position, blocks in shards:
        heights = jax.random.uniform(jax.random.fold_in(jax.random.fold_in(stream_key, 6), position), (blocks,), jnp.float32, least / len(shards), largest / len(shards))
        level = level * jnp.repeat(jnp.exp(heights), extent[position] // blocks).reshape((-1,) + (1,) * (len(extent) - 1 - position))
    return level


def scatter_about(stream_key, dims, width, most, cuts=(), held_as=jnp.bfloat16):
    entries = jax.random.normal(stream_key, dims, jnp.float32) * width
    if len(cuts) > 0:
        entries = block_levels(stream_key, dims, cuts, -0.22, 0.18) * entries
    return jnp.clip(entries, min=-most, max=most).astype(held_as)


def setup_inputs(seed: int = 0, part: int = 0) -> dict:
    splits = jax.random.split(jax.random.key(seed), 6)
    part_splits = jax.random.split(jax.random.fold_in(splits[5], part), 6)
    frames = draw_frames(jax.random.fold_in(jax.random.fold_in(splits[5], part), 71), part)
    conv_weight = scatter_about(splits[1], (KW, D), 0.4, 2.390625)
    qkv_weight = scatter_about(splits[2], (D, 3 * HEADS * HD), D ** -0.5, 0.125, ((1, 16),))
    track_ids = draw_track_ids(jax.random.fold_in(jax.random.fold_in(splits[5], part), 71), part)
    track_owner = draw_track_owner(jax.random.fold_in(jax.random.fold_in(splits[5], part), 71), part)
    return dict(frames=frames, conv_weight=conv_weight, qkv_weight=qkv_weight, track_ids=track_ids, track_owner=track_owner)


def attend_slots(packed, positions):
    slot_count = packed.shape[0]
    inner = packed.shape[1] // 3
    head_count = inner // HD
    query = packed[:, :inner].reshape(slot_count, head_count, HD).astype(jnp.float32)
    keys_all = packed[:, inner:2 * inner].reshape(slot_count, head_count, HD).astype(jnp.float32)
    values_all = packed[:, 2 * inner:].reshape(slot_count, head_count, HD).astype(jnp.float32)
    slot_ids = jnp.arange(slot_count, dtype=jnp.int32)
    block_rows = slot_count if slot_count <= 1024 else 512
    score_scale = 1.0 / (HD ** 0.5)

    def one_block(block_id):
        offset = (block_id * block_rows).astype(jnp.int32)
        query_block = lax.dynamic_slice_in_dim(query, offset, block_rows, 0)
        pos_block = lax.dynamic_slice_in_dim(positions, offset, block_rows, 0)
        ids_block = offset + jnp.arange(block_rows, dtype=jnp.int32)
        scores = jnp.einsum("qhd,khd->hqk", query_block, keys_all) * score_scale
        allowed = ((positions[None, :] >= 0) & (positions[None, :] <= pos_block[:, None])) | (ids_block[:, None] == slot_ids[None, :])
        scores = jnp.where(allowed[None], scores, jnp.float32(-1e30))
        top_score = jnp.max(scores, axis=-1, keepdims=True)
        expd = jnp.exp(scores - top_score)
        weights = (expd / jnp.sum(expd, axis=-1, keepdims=True)).astype(jnp.bfloat16)
        mixed = jnp.einsum("hqk,khd->qhd", weights.astype(jnp.float32), values_all)
        return mixed.astype(jnp.bfloat16).reshape(block_rows, inner)

    blocks = lax.map(one_block, jnp.arange(slot_count // block_rows, dtype=jnp.int32))
    return blocks.reshape(slot_count, inner)


def reference(frames, conv_weight, qkv_weight, track_ids, track_owner):
    frames_f = frames.astype(jnp.float32)
    padded = jnp.concatenate([jnp.zeros((KW - 1, D), jnp.float32), frames_f], axis=0)
    conv_sum = frames_f
    for tap in range(KW):
        conv_sum = conv_sum + conv_weight[tap].astype(jnp.float32)[None, :] * padded[KW - 1 - tap:KW - 1 - tap + TOKENS]
    hidden = conv_sum.astype(jnp.bfloat16)
    projected = jnp.dot(hidden, qkv_weight, preferred_element_type=jnp.float32).astype(jnp.bfloat16)
    group = jnp.sum(jnp.where(track_ids[:, None] == jnp.arange(NTRACKS, dtype=jnp.int32)[None, :], track_owner[None, :], 0), axis=1).astype(jnp.int32)
    slot_total = CAP * N_SEQ
    inner = HEADS * HD

    def per_owner(owner_id):
        order = jnp.argsort((group != owner_id).astype(jnp.int32), stable=True)[:slot_total].astype(jnp.int32)
        valid = group[order] == owner_id
        slot_rows = jnp.where(valid[:, None], projected[order], jnp.zeros((), jnp.bfloat16))
        positions = jnp.where(valid, order, -1).astype(jnp.int32)
        mixed = attend_slots(slot_rows, positions)
        return mixed, jnp.where(valid, order, TOKENS).astype(jnp.int32)

    mixed_all, where_all = lax.map(per_owner, jnp.arange(N_SEQ, dtype=jnp.int32))
    context = jnp.zeros((TOKENS, inner), jnp.bfloat16)
    context = context.at[where_all.reshape(-1)].set(mixed_all.reshape(-1, inner), mode="drop")
    return context
```

```python
import jax
import jax.numpy as jnp
from jax import lax
from jax.sharding import Mesh
from jax.sharding import PartitionSpec as P

HD = 128
KW = 4


def from_behind(value, axis, by):
    size = lax.axis_size(axis)
    pairs = [(i, i + by) for i in range(size) if 0 <= i + by < size]
    return lax.ppermute(value, axis, pairs)


def track_groups(track_ids, track_owner):
    track_total = track_owner.shape[0]
    return jnp.sum(
        jnp.where(
            track_ids[:, None] == jnp.arange(track_total, dtype=jnp.int32)[None, :],
            track_owner[None, :],
            0,
        ),
        axis=1,
    )


def convolve(frames, conv_weight, rim_rows):
    tok_rows = frames.shape[0]
    extended = jnp.concatenate([rim_rows, frames], axis=0).astype(jnp.float32)
    conv_sum = frames.astype(jnp.float32)
    for tap in range(KW):
        conv_sum = (
            conv_sum
            + conv_weight[tap].astype(jnp.float32)[None, :]
            * extended[KW - 1 - tap : KW - 1 - tap + tok_rows]
        )
    return conv_sum.astype(jnp.bfloat16)


def attend_slots(packed, positions):
    slot_count = packed.shape[0]
    inner = packed.shape[1] // 3
    head_count = inner // HD
    query = packed[:, :inner].reshape(slot_count, head_count, HD)
    keys_all = packed[:, inner : 2 * inner].reshape(slot_count, head_count, HD)
    values_all = packed[:, 2 * inner :].reshape(slot_count, head_count, HD)
    slot_ids = jnp.arange(slot_count, dtype=jnp.int32)
    score_scale = 1.0 / HD**0.5
    scores = (
        jnp.einsum("qhd,khd->hqk", query, keys_all, preferred_element_type=jnp.float32)
        * score_scale
    )
    allowed = (positions[None, :] >= 0) & (positions[None, :] <= positions[:, None]) | (
        slot_ids[:, None] == slot_ids[None, :]
    )
    scores = jnp.where(allowed[None], scores, jnp.float32(-1e30))
    top_score = jnp.max(scores, axis=-1, keepdims=True)
    expd = jnp.exp(scores - top_score)
    weights = (expd / jnp.sum(expd, axis=-1, keepdims=True)).astype(jnp.bfloat16)
    mixed = jnp.einsum("hqk,khd->qhd", weights, values_all, preferred_element_type=jnp.float32)
    return mixed.astype(jnp.bfloat16).reshape(slot_count, inner)


def body_by_owner(frames, conv_weight, qkv_weight, track_ids, track_owner):
    tok_rows = frames.shape[0]
    peer_count = lax.axis_size("seq")
    capacity = 2 * tok_rows // peer_count
    slot_total = capacity * peer_count
    my_index = lax.axis_index("seq")
    rim_rows = from_behind(frames[tok_rows - (KW - 1) :], "seq", 1)
    hidden = convolve(frames, conv_weight, rim_rows)
    group = track_groups(track_ids, track_owner)
    owner_hits = (group[:, None] == jnp.arange(peer_count, dtype=jnp.int32)[None, :]).astype(
        jnp.int32
    )
    running = jnp.cumsum(owner_hits, axis=0) - 1
    rank_rows = jnp.sum(jnp.where(owner_hits > 0, running, 0), axis=1)
    slot_of_row = group * capacity + rank_rows
    row_ids = jnp.arange(tok_rows, dtype=jnp.int32)
    source_row = jnp.full((slot_total,), tok_rows, jnp.int32).at[slot_of_row].set(row_ids)
    positions = my_index * tok_rows + row_ids
    send_times = jnp.full((slot_total,), -1, jnp.int32).at[slot_of_row].set(positions)
    projected = jnp.dot(
        hidden,
        lax.all_gather(qkv_weight, "seq", axis=1, tiled=True),
        preferred_element_type=jnp.float32,
    ).astype(jnp.bfloat16)
    padded_rows = jnp.concatenate(
        [projected, jnp.zeros((1, projected.shape[1]), jnp.bfloat16)], axis=0
    )
    outgoing = padded_rows[source_row]
    received, got_times = (
        lax.all_to_all(outgoing, "seq", split_axis=0, concat_axis=0, tiled=True),
        lax.all_to_all(send_times, "seq", split_axis=0, concat_axis=0, tiled=True),
    )
    mixed = attend_slots(received, got_times)
    returned = lax.all_to_all(mixed, "seq", split_axis=0, concat_axis=0, tiled=True)
    return returned[slot_of_row]


def body_by_head(frames, conv_weight, qkv_weight, track_ids, track_owner):
    tok_rows = frames.shape[0]
    chips = lax.axis_size("chip")
    devices = 2 * chips
    core = lax.axis_index("core")
    chip = lax.axis_index("chip")
    me = 2 * chip + core
    both = ("chip", "core")
    half = HD // 2

    group = track_groups(track_ids, track_owner)
    all_groups = lax.all_gather(group, both, axis=0, tiled=True)

    held = qkv_weight.T.reshape(3, half, qkv_weight.shape[0])
    moved = [
        lax.ppermute(held[j], both, [(d, (3 * d + j) % devices) for d in range(devices)])
        for j in range(3)
    ]
    turn = lax.rem(me, 3)
    mine = lax.dynamic_slice_in_dim(jnp.stack(moved + moved[:2]), turn, 3, 0)
    swap = [(0, 1), (1, 0)]
    theirs = lax.ppermute(mine, "core", swap)
    first = jnp.where(core == 0, mine, theirs)
    second = jnp.where(core == 0, theirs, mine)
    head_weight = jnp.stack([first, second], axis=1).reshape(3 * HD, -1)

    rim_rows = lax.ppermute(
        frames[tok_rows - (KW - 1) :], both, [(i, i + 1) for i in range(devices - 1)]
    )
    hidden = convolve(frames, conv_weight, rim_rows)
    stream = lax.all_gather(hidden, "chip", axis=0, tiled=True)
    projected = lax.dot_general(
        stream, head_weight, (((1,), (1,)), ((), ())), preferred_element_type=jnp.float32
    ).astype(jnp.bfloat16)
    query = projected[:, :HD]
    own = projected[:, HD:]
    other = lax.ppermute(own, "core", swap)
    keyed = jnp.concatenate([own, other], axis=0)

    times = jnp.arange(devices * tok_rows, dtype=jnp.int32).reshape(chips, 2, tok_rows)
    groups = all_groups.reshape(chips, 2, tok_rows)
    rows = chips * tok_rows

    def of_core(values, which):
        return lax.dynamic_index_in_dim(values, which, 1, False).reshape(rows)

    own_times, own_groups = of_core(times, core), of_core(groups, core)
    key_times = jnp.concatenate([own_times, of_core(times, 1 - core)])
    key_groups = jnp.concatenate([own_groups, of_core(groups, 1 - core)])
    scores = lax.dot_general(
        query, keyed[:, :HD], (((1,), (1,)), ((), ())), preferred_element_type=jnp.float32
    ) * (1.0 / HD**0.5)
    allowed = (key_times[None, :] <= own_times[:, None]) & (
        key_groups[None, :] == own_groups[:, None]
    )
    scores = jnp.where(allowed, scores, jnp.float32(-1e30))
    expd = jnp.exp(scores - jnp.max(scores, axis=-1, keepdims=True))
    weights = (expd / jnp.sum(expd, axis=-1, keepdims=True)).astype(jnp.bfloat16)
    mixed = jnp.dot(weights, keyed[:, HD:], preferred_element_type=jnp.float32)
    mixed = mixed.astype(jnp.bfloat16).reshape(chips, tok_rows, HD)
    returned = lax.all_to_all(mixed, "chip", split_axis=0, concat_axis=0, tiled=True)
    return returned.transpose(1, 0, 2).reshape(tok_rows, chips * HD)


def solution(mesh):
    grp, seq = mesh.devices.shape
    out_by_owner = P(("grp", "seq"), None)
    by_owner = jax.shard_map(
        body_by_owner,
        mesh=mesh,
        in_specs=(P(("grp", "seq"), None), P(), P(None, "seq"), P(("grp", "seq")), P("grp")),
        out_specs=out_by_owner,
        check_vma=False,
    )
    split = Mesh(mesh.devices.reshape(grp, seq // 2, 2), ("grp", "chip", "core"))
    rows = P(("grp", "chip", "core"))
    by_head = jax.shard_map(
        body_by_head,
        mesh=split,
        in_specs=(rows, P(), P(None, ("chip", "core")), rows, P("grp")),
        out_specs=rows,
        check_vma=False,
    )

    def run(frames, conv_weight, qkv_weight, track_ids, track_owner):
        heads = qkv_weight.shape[1] // (3 * HD)
        plan = by_head if seq == 2 * heads else by_owner
        return plan(frames, conv_weight, qkv_weight, track_ids, track_owner)

    return run
```

```python
import jax
import jax.numpy as jnp
from jax import lax
from jax.sharding import Mesh
from jax.sharding import PartitionSpec as P

HD = 128
KW = 4


def from_behind(value, axis, by):
    size = lax.axis_size(axis)
    pairs = [(i, i + by) for i in range(size) if 0 <= i + by < size]
    return lax.ppermute(value, axis, pairs)


def track_groups(track_ids, track_owner):
    track_total = track_owner.shape[0]
    return jnp.sum(
        jnp.where(
            track_ids[:, None] == jnp.arange(track_total, dtype=jnp.int32)[None, :],
            track_owner[None, :],
            0,
        ),
        axis=1,
    )


def convolve(frames, conv_weight, rim_rows):
    tok_rows = frames.shape[0]
    extended = jnp.concatenate([rim_rows, frames], axis=0).astype(jnp.float32)
    conv_sum = frames.astype(jnp.float32)
    for tap in range(KW):
        conv_sum = (
            conv_sum
            + conv_weight[tap].astype(jnp.float32)[None, :]
            * extended[KW - 1 - tap : KW - 1 - tap + tok_rows]
        )
    return conv_sum.astype(jnp.bfloat16)


def attend_slots(packed, positions):
    slot_count = packed.shape[0]
    inner = packed.shape[1] // 3
    head_count = inner // HD
    query = packed[:, :inner].reshape(slot_count, head_count, HD)
    keys_all = packed[:, inner : 2 * inner].reshape(slot_count, head_count, HD)
    values_all = packed[:, 2 * inner :].reshape(slot_count, head_count, HD)
    slot_ids = jnp.arange(slot_count, dtype=jnp.int32)
    score_scale = 1.0 / HD**0.5
    scores = (
        jnp.einsum("qhd,khd->hqk", query, keys_all, preferred_element_type=jnp.float32)
        * score_scale
    )
    allowed = (positions[None, :] >= 0) & (positions[None, :] <= positions[:, None]) | (
        slot_ids[:, None] == slot_ids[None, :]
    )
    scores = jnp.where(allowed[None], scores, jnp.float32(-1e30))
    top_score = jnp.max(scores, axis=-1, keepdims=True)
    expd = jnp.exp(scores - top_score)
    weights = (expd / jnp.sum(expd, axis=-1, keepdims=True)).astype(jnp.bfloat16)
    mixed = jnp.einsum("hqk,khd->qhd", weights, values_all, preferred_element_type=jnp.float32)
    return mixed.astype(jnp.bfloat16).reshape(slot_count, inner)


def body_by_owner(frames, conv_weight, qkv_weight, track_ids, track_owner):
    tok_rows = frames.shape[0]
    peer_count = lax.axis_size("seq")
    capacity = 2 * tok_rows // peer_count
    slot_total = capacity * peer_count
    my_index = lax.axis_index("seq")
    rim_rows = from_behind(frames[tok_rows - (KW - 1) :], "seq", 1)
    hidden = convolve(frames, conv_weight, rim_rows)
    group = track_groups(track_ids, track_owner)
    owner_hits = (group[:, None] == jnp.arange(peer_count, dtype=jnp.int32)[None, :]).astype(
        jnp.int32
    )
    running = jnp.cumsum(owner_hits, axis=0) - 1
    rank_rows = jnp.sum(jnp.where(owner_hits > 0, running, 0), axis=1)
    slot_of_row = group * capacity + rank_rows
    row_ids = jnp.arange(tok_rows, dtype=jnp.int32)
    source_row = jnp.full((slot_total,), tok_rows, jnp.int32).at[slot_of_row].set(row_ids)
    positions = my_index * tok_rows + row_ids
    send_times = jnp.full((slot_total,), -1, jnp.int32).at[slot_of_row].set(positions)
    projected = jnp.dot(
        hidden,
        lax.all_gather(qkv_weight, "seq", axis=1, tiled=True),
        preferred_element_type=jnp.float32,
    ).astype(jnp.bfloat16)
    padded_rows = jnp.concatenate(
        [projected, jnp.zeros((1, projected.shape[1]), jnp.bfloat16)], axis=0
    )
    outgoing = padded_rows[source_row]
    received, got_times = (
        lax.all_to_all(outgoing, "seq", split_axis=0, concat_axis=0, tiled=True),
        lax.all_to_all(send_times, "seq", split_axis=0, concat_axis=0, tiled=True),
    )
    mixed = attend_slots(received, got_times)
    returned = lax.all_to_all(mixed, "seq", split_axis=0, concat_axis=0, tiled=True)
    return returned[slot_of_row]


def all_by_doubling(values, axes, devices, me):
    step = 1
    while step < devices:
        theirs = lax.ppermute(values, axes, [(d, d ^ step) for d in range(devices)])
        low = me & step == 0
        values = jnp.concatenate(
            [jnp.where(low, values, theirs), jnp.where(low, theirs, values)], axis=0
        )
        step *= 2
    return values


def body_by_head(frames, conv_weight, qkv_weight, track_ids, track_owner):
    tok_rows = frames.shape[0]
    chips = lax.axis_size("chip")
    devices = 2 * chips
    core = lax.axis_index("core")
    chip = lax.axis_index("chip")
    me = 2 * chip + core
    both = ("chip", "core")
    half = HD // 2
    part = tok_rows // 2

    ring = list(range(0, chips, 2)) + list(range(chips - 1, 0, -2))
    place = jnp.where(chip & 1 == 0, chip >> 1, chips - 1 - (chip >> 1))

    def chip_at(position):
        position = jnp.where(position >= chips, position - chips, position)
        return jnp.where(position < chips // 2, 2 * position, 2 * (chips - 1 - position) + 1)

    onward = [(ring[i], ring[(i + 1) % chips]) for i in range(chips)]
    backward = [(t, f) for f, t in onward]

    rim_rows = lax.ppermute(
        frames[tok_rows - (KW - 1) :], both, [(i, i + 1) for i in range(devices - 1)]
    )
    late = convolve(frames[part:], conv_weight, frames[part - (KW - 1) : part])
    early = convolve(frames[:part], conv_weight, rim_rows)

    group = track_groups(track_ids, track_owner)
    all_groups = all_by_doubling(group[None, :], both, devices, me)

    held = qkv_weight.T.reshape(3, half, qkv_weight.shape[0])
    moved = [
        lax.ppermute(held[j], both, [(d, (3 * d + j) % devices) for d in range(devices)])
        for j in range(3)
    ]
    turn = lax.rem(me, 3)
    mine = lax.dynamic_slice_in_dim(jnp.stack(moved + moved[:2]), turn, 3, 0)
    swap = [(0, 1), (1, 0)]
    theirs = lax.ppermute(mine, "core", swap)
    first = jnp.where(core == 0, mine, theirs)
    second = jnp.where(core == 0, theirs, mine)
    head_weight = jnp.stack([first, second], axis=1).reshape(3 * HD, -1)

    projected = jnp.zeros((chips, tok_rows, 3 * HD), jnp.bfloat16)

    def project(rows, where, offset, projected):
        done = lax.dot_general(
            rows, head_weight, (((1,), (1,)), ((), ())), preferred_element_type=jnp.float32
        ).astype(jnp.bfloat16)
        return lax.dynamic_update_slice(projected, done[None], (where, offset, 0))

    for step in range(chips):
        projected = project(late, chip_at(place + step), part, projected)
        projected = project(early, chip_at(place + chips - step), 0, projected)
        if step < chips - 1:
            late = lax.ppermute(late, "chip", backward)
            early = lax.ppermute(early, "chip", onward)

    rows = chips * tok_rows
    projected = projected.reshape(rows, 3 * HD)
    query = projected[:, :HD]
    own = projected[:, HD:]
    other = lax.ppermute(own, "core", swap)
    keyed = jnp.concatenate([own, other], axis=0)

    times = jnp.arange(devices * tok_rows, dtype=jnp.int32).reshape(chips, 2, tok_rows)
    groups = all_groups.reshape(chips, 2, tok_rows)

    def of_core(values, which):
        return lax.dynamic_index_in_dim(values, which, 1, False).reshape(rows)

    own_times, own_groups = of_core(times, core), of_core(groups, core)
    key_times = jnp.concatenate([own_times, of_core(times, 1 - core)])
    key_groups = jnp.concatenate([own_groups, of_core(groups, 1 - core)])
    scores = lax.dot_general(
        query, keyed[:, :HD], (((1,), (1,)), ((), ())), preferred_element_type=jnp.float32
    ) * (1.0 / HD**0.5)
    allowed = (key_times[None, :] <= own_times[:, None]) & (
        key_groups[None, :] == own_groups[:, None]
    )
    scores = jnp.where(allowed, scores, jnp.float32(-1e30))
    expd = jnp.exp(scores - jnp.max(scores, axis=-1, keepdims=True))
    weights = (expd / jnp.sum(expd, axis=-1, keepdims=True)).astype(jnp.bfloat16)
    mixed = jnp.dot(weights, keyed[:, HD:], preferred_element_type=jnp.float32)
    mixed = mixed.astype(jnp.bfloat16).reshape(chips, tok_rows, HD)
    returned = lax.all_to_all(mixed, "chip", split_axis=0, concat_axis=0, tiled=True)
    return returned.transpose(1, 0, 2).reshape(tok_rows, chips * HD)


def solution(mesh):
    grp, seq = mesh.devices.shape
    out_by_owner = P(("grp", "seq"), None)
    by_owner = jax.shard_map(
        body_by_owner,
        mesh=mesh,
        in_specs=(P(("grp", "seq"), None), P(), P(None, "seq"), P(("grp", "seq")), P("grp")),
        out_specs=out_by_owner,
        check_vma=False,
    )
    split = Mesh(mesh.devices.reshape(grp, seq // 2, 2), ("grp", "chip", "core"))
    rows = P(("grp", "chip", "core"))
    by_head = jax.shard_map(
        body_by_head,
        mesh=split,
        in_specs=(rows, P(), P(None, ("chip", "core")), rows, P("grp")),
        out_specs=rows,
        check_vma=False,
    )

    def run(frames, conv_weight, qkv_weight, track_ids, track_owner):
        heads = qkv_weight.shape[1] // (3 * HD)
        plan = by_head if seq == 2 * heads else by_owner
        return plan(frames, conv_weight, qkv_weight, track_ids, track_owner)

    return run
```

```python
import jax
import jax.numpy as jnp
from jax import lax
from jax.sharding import Mesh
from jax.sharding import PartitionSpec as P

HD = 128
KW = 4


def from_behind(value, axis, by):
    size = lax.axis_size(axis)
    pairs = [(i, i + by) for i in range(size) if 0 <= i + by < size]
    return lax.ppermute(value, axis, pairs)


def track_groups(track_ids, track_owner):
    track_total = track_owner.shape[0]
    return jnp.sum(
        jnp.where(
            track_ids[:, None] == jnp.arange(track_total, dtype=jnp.int32)[None, :],
            track_owner[None, :],
            0,
        ),
        axis=1,
    )


def convolve(frames, conv_weight, rim_rows):
    tok_rows = frames.shape[0]
    extended = jnp.concatenate([rim_rows, frames], axis=0).astype(jnp.float32)
    conv_sum = frames.astype(jnp.float32)
    for tap in range(KW):
        conv_sum = (
            conv_sum
            + conv_weight[tap].astype(jnp.float32)[None, :]
            * extended[KW - 1 - tap : KW - 1 - tap + tok_rows]
        )
    return conv_sum.astype(jnp.bfloat16)


def attend_slots(packed, positions):
    slot_count = packed.shape[0]
    inner = packed.shape[1] // 3
    head_count = inner // HD
    query = packed[:, :inner].reshape(slot_count, head_count, HD)
    keys_all = packed[:, inner : 2 * inner].reshape(slot_count, head_count, HD)
    values_all = packed[:, 2 * inner :].reshape(slot_count, head_count, HD)
    slot_ids = jnp.arange(slot_count, dtype=jnp.int32)
    score_scale = 1.0 / HD**0.5
    scores = (
        jnp.einsum("qhd,khd->hqk", query, keys_all, preferred_element_type=jnp.float32)
        * score_scale
    )
    allowed = (positions[None, :] >= 0) & (positions[None, :] <= positions[:, None]) | (
        slot_ids[:, None] == slot_ids[None, :]
    )
    scores = jnp.where(allowed[None], scores, jnp.float32(-1e30))
    top_score = jnp.max(scores, axis=-1, keepdims=True)
    expd = jnp.exp(scores - top_score)
    weights = (expd / jnp.sum(expd, axis=-1, keepdims=True)).astype(jnp.bfloat16)
    mixed = jnp.einsum("hqk,khd->qhd", weights, values_all, preferred_element_type=jnp.float32)
    return mixed.astype(jnp.bfloat16).reshape(slot_count, inner)


def body_by_owner(frames, conv_weight, qkv_weight, track_ids, track_owner):
    tok_rows = frames.shape[0]
    peer_count = lax.axis_size("seq")
    capacity = 2 * tok_rows // peer_count
    slot_total = capacity * peer_count
    my_index = lax.axis_index("seq")
    rim_rows = from_behind(frames[tok_rows - (KW - 1) :], "seq", 1)
    hidden = convolve(frames, conv_weight, rim_rows)
    group = track_groups(track_ids, track_owner)
    owner_hits = (group[:, None] == jnp.arange(peer_count, dtype=jnp.int32)[None, :]).astype(
        jnp.int32
    )
    running = jnp.cumsum(owner_hits, axis=0) - 1
    rank_rows = jnp.sum(jnp.where(owner_hits > 0, running, 0), axis=1)
    slot_of_row = group * capacity + rank_rows
    row_ids = jnp.arange(tok_rows, dtype=jnp.int32)
    source_row = jnp.full((slot_total,), tok_rows, jnp.int32).at[slot_of_row].set(row_ids)
    positions = my_index * tok_rows + row_ids
    send_times = jnp.full((slot_total,), -1, jnp.int32).at[slot_of_row].set(positions)
    projected = jnp.dot(
        hidden,
        lax.all_gather(qkv_weight, "seq", axis=1, tiled=True),
        preferred_element_type=jnp.float32,
    ).astype(jnp.bfloat16)
    padded_rows = jnp.concatenate(
        [projected, jnp.zeros((1, projected.shape[1]), jnp.bfloat16)], axis=0
    )
    outgoing = padded_rows[source_row]
    received, got_times = (
        lax.all_to_all(outgoing, "seq", split_axis=0, concat_axis=0, tiled=True),
        lax.all_to_all(send_times, "seq", split_axis=0, concat_axis=0, tiled=True),
    )
    mixed = attend_slots(received, got_times)
    returned = lax.all_to_all(mixed, "seq", split_axis=0, concat_axis=0, tiled=True)
    return returned[slot_of_row]


def xor_swap(value, bit, axes=("chip", "core")):
    count = lax.axis_size(axes)
    return lax.ppermute(value, axes, [(d, d ^ bit) for d in range(count)])


def by_bit(bit, mine, theirs, axis):
    return jnp.stack(
        [jnp.where(bit == 0, mine, theirs), jnp.where(bit == 0, theirs, mine)], axis=axis
    )


def body_by_head(frames, conv_weight, qkv_weight, track_ids, track_owner):
    tok_rows = frames.shape[0]
    chips = lax.axis_size("chip")
    devices = 2 * chips
    core = lax.axis_index("core")
    chip = lax.axis_index("chip")
    grp = lax.axis_index("grp")
    me = 2 * chip + core
    both = ("chip", "core")
    every = ("grp", "chip", "core")
    part = tok_rows // 2
    features = frames.shape[1]
    CORE, Y, Z0, Z1 = 1, 2, 4, 8

    rim_rows = lax.ppermute(
        frames[tok_rows - (KW - 1) :], both, [(i, i + 1) for i in range(devices - 1)]
    )
    late = convolve(frames[part:], conv_weight, frames[part - (KW - 1) : part])
    early = convolve(frames[:part], conv_weight, rim_rows)

    far_late = xor_swap(late, Z1)
    far_early = xor_swap(early, Z1)
    own = jnp.concatenate([early, late], axis=0)
    beside = xor_swap(own, Y)
    far_beside_late = xor_swap(far_late, Y)
    far_beside_early = xor_swap(far_early, Y)

    half = features // 2
    held = lax.dynamic_slice_in_dim(qkv_weight.T, grp * half, half, 1).reshape(3, HD // 2, half)
    moved = [
        lax.ppermute(held[j], both, [(d, (3 * d + j) % devices) for d in range(devices)])
        for j in range(3)
    ]
    mine = lax.dynamic_slice_in_dim(jnp.stack(moved + moved[:2]), lax.rem(me, 3), 3, 0)
    paired = xor_swap(mine, Z0)

    def whole_head(quarter):
        wide = by_bit(grp, quarter, xor_swap(quarter, devices, every), 2)
        wide = wide.reshape(3, HD // 2, features)
        return by_bit(core, wide, xor_swap(wide, CORE), 1).reshape(3 * HD, features)

    two_heads = jnp.concatenate([whole_head(mine), whole_head(paired)], axis=0)

    def project(rows):
        done = lax.dot_general(
            rows, two_heads, (((1,), (1,)), ((), ())), preferred_element_type=jnp.float32
        ).astype(jnp.bfloat16)
        return jnp.concatenate([done[:, : 3 * HD], xor_swap(done[:, 3 * HD :], Z0)], axis=0)

    first = project(jnp.concatenate([own, beside, far_late, far_beside_late], axis=0))
    second = project(jnp.concatenate([far_early, far_beside_early], axis=0))

    first_rows = [(0, 0, tok_rows), (Y, 0, tok_rows), (Z1, part, part), (Z1 | Y, part, part)]
    second_rows = [(Z1, 0, part), (Z1 | Y, 0, part)]
    order = []
    for pieces in (first_rows, second_rows):
        order += pieces + [(far ^ Z0, start, count) for far, start, count in pieces]

    groups = track_groups(track_ids, track_owner)[None, :]
    for bit in (CORE, Y, Z0, Z1):
        groups = jnp.concatenate([groups, xor_swap(groups, bit)], axis=0)

    def of_rows(bit):
        times = [
            (me ^ far ^ bit) * tok_rows + start + jnp.arange(count, dtype=jnp.int32)
            for far, start, count in order
        ]
        marks = [groups[far ^ bit, start : start + count] for far, start, count in order]
        return jnp.concatenate(times), jnp.concatenate(marks)

    projected = jnp.concatenate([first, second], axis=0)
    query = projected[:, :HD]
    keyed = jnp.concatenate(
        [projected[:, HD:], xor_swap(first[:, HD:], CORE), xor_swap(second[:, HD:], CORE)], axis=0
    )
    own_times, own_groups = of_rows(0)
    other_times, other_groups = of_rows(CORE)
    key_times = jnp.concatenate([own_times, other_times])
    key_groups = jnp.concatenate([own_groups, other_groups])
    scores = lax.dot_general(
        query, keyed[:, :HD], (((1,), (1,)), ((), ())), preferred_element_type=jnp.float32
    ) * (1.0 / HD**0.5)
    allowed = (key_times[None, :] <= own_times[:, None]) & (
        key_groups[None, :] == own_groups[:, None]
    )
    scores = jnp.where(allowed, scores, jnp.float32(-1e30))
    expd = jnp.exp(scores - jnp.max(scores, axis=-1, keepdims=True))
    weights = (expd / jnp.sum(expd, axis=-1, keepdims=True)).astype(jnp.bfloat16)
    mixed = jnp.dot(weights, keyed[:, HD:], preferred_element_type=jnp.float32)
    mixed = mixed.astype(jnp.bfloat16)

    sent = jnp.zeros((chips, tok_rows, HD), jnp.bfloat16)
    at = 0
    for far, start, count in order:
        rows = mixed[at : at + count]
        sent = lax.dynamic_update_slice(sent, rows[None], ((me ^ far) >> 1, start, 0))
        at += count
    returned = lax.all_to_all(sent, "chip", split_axis=0, concat_axis=0, tiled=True)
    return returned.transpose(1, 0, 2).reshape(tok_rows, chips * HD)


def solution(mesh):
    grp, seq = mesh.devices.shape
    out_by_owner = P(("grp", "seq"), None)
    by_owner = jax.shard_map(
        body_by_owner,
        mesh=mesh,
        in_specs=(P(("grp", "seq"), None), P(), P(None, "seq"), P(("grp", "seq")), P("grp")),
        out_specs=out_by_owner,
        check_vma=False,
    )
    split = Mesh(mesh.devices.reshape(grp, seq // 2, 2), ("grp", "chip", "core"))
    rows = P(("grp", "chip", "core"))
    by_head = jax.shard_map(
        body_by_head,
        mesh=split,
        in_specs=(rows, P(), P(None, ("chip", "core")), rows, P("grp")),
        out_specs=rows,
        check_vma=False,
    )

    def run(frames, conv_weight, qkv_weight, track_ids, track_owner):
        heads = qkv_weight.shape[1] // (3 * HD)
        plan = by_head if (grp, seq, heads) == (2, 16, 8) else by_owner
        return plan(frames, conv_weight, qkv_weight, track_ids, track_owner)

    return run
```

```python
import jax
import jax.numpy as jnp
from jax import lax
from jax.sharding import Mesh
from jax.sharding import PartitionSpec as P

HD = 128
KW = 4


def from_behind(value, axis, by):
    size = lax.axis_size(axis)
    pairs = [(i, i + by) for i in range(size) if 0 <= i + by < size]
    return lax.ppermute(value, axis, pairs)


def track_groups(track_ids, track_owner):
    track_total = track_owner.shape[0]
    return jnp.sum(
        jnp.where(
            track_ids[:, None] == jnp.arange(track_total, dtype=jnp.int32)[None, :],
            track_owner[None, :],
            0,
        ),
        axis=1,
    )


def convolve(frames, conv_weight, rim_rows):
    tok_rows = frames.shape[0]
    extended = jnp.concatenate([rim_rows, frames], axis=0).astype(jnp.float32)
    conv_sum = frames.astype(jnp.float32)
    for tap in range(KW):
        conv_sum = (
            conv_sum
            + conv_weight[tap].astype(jnp.float32)[None, :]
            * extended[KW - 1 - tap : KW - 1 - tap + tok_rows]
        )
    return conv_sum.astype(jnp.bfloat16)


def attend_slots(packed, positions):
    slot_count = packed.shape[0]
    inner = packed.shape[1] // 3
    head_count = inner // HD
    query = packed[:, :inner].reshape(slot_count, head_count, HD)
    keys_all = packed[:, inner : 2 * inner].reshape(slot_count, head_count, HD)
    values_all = packed[:, 2 * inner :].reshape(slot_count, head_count, HD)
    slot_ids = jnp.arange(slot_count, dtype=jnp.int32)
    score_scale = 1.0 / HD**0.5
    scores = (
        jnp.einsum("qhd,khd->hqk", query, keys_all, preferred_element_type=jnp.float32)
        * score_scale
    )
    allowed = (positions[None, :] >= 0) & (positions[None, :] <= positions[:, None]) | (
        slot_ids[:, None] == slot_ids[None, :]
    )
    scores = jnp.where(allowed[None], scores, jnp.float32(-1e30))
    top_score = jnp.max(scores, axis=-1, keepdims=True)
    expd = jnp.exp(scores - top_score)
    weights = (expd / jnp.sum(expd, axis=-1, keepdims=True)).astype(jnp.bfloat16)
    mixed = jnp.einsum("hqk,khd->qhd", weights, values_all, preferred_element_type=jnp.float32)
    return mixed.astype(jnp.bfloat16).reshape(slot_count, inner)


def body_by_owner(frames, conv_weight, qkv_weight, track_ids, track_owner):
    tok_rows = frames.shape[0]
    peer_count = lax.axis_size("seq")
    capacity = 2 * tok_rows // peer_count
    slot_total = capacity * peer_count
    my_index = lax.axis_index("seq")
    rim_rows = from_behind(frames[tok_rows - (KW - 1) :], "seq", 1)
    hidden = convolve(frames, conv_weight, rim_rows)
    group = track_groups(track_ids, track_owner)
    owner_hits = (group[:, None] == jnp.arange(peer_count, dtype=jnp.int32)[None, :]).astype(
        jnp.int32
    )
    running = jnp.cumsum(owner_hits, axis=0) - 1
    rank_rows = jnp.sum(jnp.where(owner_hits > 0, running, 0), axis=1)
    slot_of_row = group * capacity + rank_rows
    row_ids = jnp.arange(tok_rows, dtype=jnp.int32)
    source_row = jnp.full((slot_total,), tok_rows, jnp.int32).at[slot_of_row].set(row_ids)
    positions = my_index * tok_rows + row_ids
    send_times = jnp.full((slot_total,), -1, jnp.int32).at[slot_of_row].set(positions)
    projected = jnp.dot(
        hidden,
        lax.all_gather(qkv_weight, "seq", axis=1, tiled=True),
        preferred_element_type=jnp.float32,
    ).astype(jnp.bfloat16)
    padded_rows = jnp.concatenate(
        [projected, jnp.zeros((1, projected.shape[1]), jnp.bfloat16)], axis=0
    )
    outgoing = padded_rows[source_row]
    received, got_times = (
        lax.all_to_all(outgoing, "seq", split_axis=0, concat_axis=0, tiled=True),
        lax.all_to_all(send_times, "seq", split_axis=0, concat_axis=0, tiled=True),
    )
    mixed = attend_slots(received, got_times)
    returned = lax.all_to_all(mixed, "seq", split_axis=0, concat_axis=0, tiled=True)
    return returned[slot_of_row]


def by_bit(bit, mine, theirs, axis):
    return jnp.stack(
        [jnp.where(bit == 0, mine, theirs), jnp.where(bit == 0, theirs, mine)], axis=axis
    )


FOUR = ("far", "near", "quad")
CORE, Y, NEAR, FAR = 1, 2, 4, 8


def swap_seq(value, bit):
    count = lax.axis_size(FOUR)
    return lax.ppermute(value, FOUR, [(d, d ^ bit) for d in range(count)])


def swap_grp(value):
    return lax.ppermute(value, "grp", [(0, 1), (1, 0)])


def body_by_head(frames, conv_weight, qkv_weight, track_ids, track_owner):
    tok_rows = frames.shape[0]
    grp = lax.axis_index("grp")
    far, near, quad = (lax.axis_index(name) for name in FOUR)
    me = far * FAR + near * NEAR + quad
    devices = lax.axis_size(FOUR)
    head = far * 4 + quad
    part = tok_rows // 2
    features = frames.shape[1]

    rim_rows = lax.ppermute(
        frames[tok_rows - (KW - 1) :], FOUR, [(i, i + 1) for i in range(devices - 1)]
    )
    late = convolve(frames[part:], conv_weight, frames[part - (KW - 1) : part])
    early = convolve(frames[:part], conv_weight, rim_rows)

    far_late = swap_seq(late, FAR)
    far_early = swap_seq(early, FAR)
    own = jnp.concatenate([early, late], axis=0)
    beside = swap_seq(own, Y)
    far_beside_late = swap_seq(far_late, Y)
    far_beside_early = swap_seq(far_early, Y)
    first_rows = [(0, 0, tok_rows), (Y, 0, tok_rows), (FAR, part, part), (FAR | Y, part, part)]
    second_rows = [(FAR, 0, part), (FAR | Y, 0, part)]
    rest = jnp.concatenate([beside, far_late, far_beside_late], axis=0)
    last = jnp.concatenate([far_early, far_beside_early], axis=0)
    first = jnp.concatenate([own, rest, swap_seq(own, CORE), swap_seq(rest, CORE)], axis=0)
    second = jnp.concatenate([last, swap_seq(last, CORE)], axis=0)

    def home(block):
        of_head, side = block % devices // 2, block % 2
        return of_head // 4 * FAR + side * NEAR + of_head % 4

    half = features // 2
    held = lax.dynamic_slice_in_dim(qkv_weight.T, grp * half, half, 1).reshape(3, HD // 2, half)
    moved = [
        lax.ppermute(held[j], FOUR, [(d, home(3 * d + j)) for d in range(devices)])
        for j in range(3)
    ]
    turn = lax.rem(2 * head + near, 3)
    mine = lax.dynamic_slice_in_dim(jnp.stack(moved + moved[:2]), turn, 3, 0)
    paired = swap_seq(mine, NEAR)
    mine = by_bit(grp, mine, swap_grp(mine), 2)
    paired = by_bit(grp, paired, swap_grp(paired), 2)
    head_weight = by_bit(near, mine, paired, 1).reshape(3 * HD, features)

    def project(rows):
        done = lax.dot_general(
            rows, head_weight, (((1,), (1,)), ((), ())), preferred_element_type=jnp.float32
        ).astype(jnp.bfloat16)
        return done[:, :HD], done[:, HD:], swap_seq(done[:, HD:], NEAR)

    parts = [project(first), project(second)]
    query = jnp.concatenate([p[0] for p in parts], axis=0)
    keyed = jnp.concatenate([p[1] for p in parts] + [p[2] for p in parts], axis=0)

    order = []
    for pieces in (first_rows, second_rows):
        order += pieces + [(hop ^ CORE, start, count) for hop, start, count in pieces]

    groups, _ = lax.optimization_barrier((track_groups(track_ids, track_owner)[None, :], paired))
    for bit in (CORE, Y, NEAR, FAR):
        groups = jnp.concatenate([groups, swap_seq(groups, bit)], axis=0)

    def of_rows(bit):
        times = [
            (me ^ hop ^ bit) * tok_rows + start + jnp.arange(count, dtype=jnp.int32)
            for hop, start, count in order
        ]
        marks = [groups[hop ^ bit, start : start + count] for hop, start, count in order]
        return jnp.concatenate(times), jnp.concatenate(marks)

    own_times, own_groups = of_rows(0)
    other_times, other_groups = of_rows(NEAR)
    key_times = jnp.concatenate([own_times, other_times])
    key_groups = jnp.concatenate([own_groups, other_groups])
    scores = lax.dot_general(
        query, keyed[:, :HD], (((1,), (1,)), ((), ())), preferred_element_type=jnp.float32
    ) * (1.0 / HD**0.5)
    allowed = (key_times[None, :] <= own_times[:, None]) & (
        key_groups[None, :] == own_groups[:, None]
    )
    scores = jnp.where(allowed, scores, jnp.float32(-1e30))
    expd = jnp.exp(scores - jnp.max(scores, axis=-1, keepdims=True))
    weights = (expd / jnp.sum(expd, axis=-1, keepdims=True)).astype(jnp.bfloat16)
    mixed = jnp.dot(weights, keyed[:, HD:], preferred_element_type=jnp.float32)
    mixed = mixed.astype(jnp.bfloat16)

    sent = jnp.zeros((devices // 2, tok_rows, HD), jnp.bfloat16)
    at = 0
    for hop, start, count in order:
        rows = mixed[at : at + count]
        there = head ^ (hop // FAR * 4 + hop % 4)
        sent = lax.dynamic_update_slice(sent, rows[None], (there, start, 0))
        at += count
    returned = lax.all_to_all(sent, ("far", "quad"), split_axis=0, concat_axis=0, tiled=True)
    return returned.transpose(1, 0, 2).reshape(tok_rows, devices // 2 * HD)


def solution(mesh):
    grp, seq = mesh.devices.shape
    out_by_owner = P(("grp", "seq"), None)
    by_owner = jax.shard_map(
        body_by_owner,
        mesh=mesh,
        in_specs=(P(("grp", "seq"), None), P(), P(None, "seq"), P(("grp", "seq")), P("grp")),
        out_specs=out_by_owner,
        check_vma=False,
    )
    fits = (grp, seq) == (2, 16)
    if fits:
        split = Mesh(mesh.devices.reshape(grp, 2, 2, 4), ("grp",) + FOUR)
        rows = P(("grp",) + FOUR)
        by_head = jax.shard_map(
            body_by_head,
            mesh=split,
            in_specs=(rows, P(), P(None, FOUR), rows, P("grp")),
            out_specs=rows,
            check_vma=False,
        )

    def run(frames, conv_weight, qkv_weight, track_ids, track_owner):
        heads = qkv_weight.shape[1] // (3 * HD)
        plan = by_head if fits and heads == 8 else by_owner
        return plan(frames, conv_weight, qkv_weight, track_ids, track_owner)

    return run
```

```python
import jax
import jax.numpy as jnp
from jax import lax
from jax.experimental import pallas as pl
from jax.experimental.pallas import tpu as pltpu
from jax.sharding import Mesh
from jax.sharding import PartitionSpec as P

HD = 128
KW = 4


def from_behind(value, axis, by):
    size = lax.axis_size(axis)
    pairs = [(i, i + by) for i in range(size) if 0 <= i + by < size]
    return lax.ppermute(value, axis, pairs)


def track_groups(track_ids, track_owner):
    track_total = track_owner.shape[0]
    return jnp.sum(
        jnp.where(
            track_ids[:, None] == jnp.arange(track_total, dtype=jnp.int32)[None, :],
            track_owner[None, :],
            0,
        ),
        axis=1,
    )


def convolve(frames, conv_weight, rim_rows):
    tok_rows = frames.shape[0]
    extended = jnp.concatenate([rim_rows, frames], axis=0).astype(jnp.float32)
    conv_sum = frames.astype(jnp.float32)
    for tap in range(KW):
        conv_sum = (
            conv_sum
            + conv_weight[tap].astype(jnp.float32)[None, :]
            * extended[KW - 1 - tap : KW - 1 - tap + tok_rows]
        )
    return conv_sum.astype(jnp.bfloat16)


def attend_slots(packed, positions):
    slot_count = packed.shape[0]
    inner = packed.shape[1] // 3
    head_count = inner // HD
    query = packed[:, :inner].reshape(slot_count, head_count, HD)
    keys_all = packed[:, inner : 2 * inner].reshape(slot_count, head_count, HD)
    values_all = packed[:, 2 * inner :].reshape(slot_count, head_count, HD)
    slot_ids = jnp.arange(slot_count, dtype=jnp.int32)
    score_scale = 1.0 / HD**0.5
    scores = (
        jnp.einsum("qhd,khd->hqk", query, keys_all, preferred_element_type=jnp.float32)
        * score_scale
    )
    allowed = (positions[None, :] >= 0) & (positions[None, :] <= positions[:, None]) | (
        slot_ids[:, None] == slot_ids[None, :]
    )
    scores = jnp.where(allowed[None], scores, jnp.float32(-1e30))
    top_score = jnp.max(scores, axis=-1, keepdims=True)
    expd = jnp.exp(scores - top_score)
    weights = (expd / jnp.sum(expd, axis=-1, keepdims=True)).astype(jnp.bfloat16)
    mixed = jnp.einsum("hqk,khd->qhd", weights, values_all, preferred_element_type=jnp.float32)
    return mixed.astype(jnp.bfloat16).reshape(slot_count, inner)


def body_by_owner(frames, conv_weight, qkv_weight, track_ids, track_owner):
    tok_rows = frames.shape[0]
    peer_count = lax.axis_size("seq")
    capacity = 2 * tok_rows // peer_count
    slot_total = capacity * peer_count
    my_index = lax.axis_index("seq")
    rim_rows = from_behind(frames[tok_rows - (KW - 1) :], "seq", 1)
    hidden = convolve(frames, conv_weight, rim_rows)
    group = track_groups(track_ids, track_owner)
    owner_hits = (group[:, None] == jnp.arange(peer_count, dtype=jnp.int32)[None, :]).astype(
        jnp.int32
    )
    running = jnp.cumsum(owner_hits, axis=0) - 1
    rank_rows = jnp.sum(jnp.where(owner_hits > 0, running, 0), axis=1)
    slot_of_row = group * capacity + rank_rows
    row_ids = jnp.arange(tok_rows, dtype=jnp.int32)
    source_row = jnp.full((slot_total,), tok_rows, jnp.int32).at[slot_of_row].set(row_ids)
    positions = my_index * tok_rows + row_ids
    send_times = jnp.full((slot_total,), -1, jnp.int32).at[slot_of_row].set(positions)
    projected = jnp.dot(
        hidden,
        lax.all_gather(qkv_weight, "seq", axis=1, tiled=True),
        preferred_element_type=jnp.float32,
    ).astype(jnp.bfloat16)
    padded_rows = jnp.concatenate(
        [projected, jnp.zeros((1, projected.shape[1]), jnp.bfloat16)], axis=0
    )
    outgoing = padded_rows[source_row]
    received, got_times = (
        lax.all_to_all(outgoing, "seq", split_axis=0, concat_axis=0, tiled=True),
        lax.all_to_all(send_times, "seq", split_axis=0, concat_axis=0, tiled=True),
    )
    mixed = attend_slots(received, got_times)
    returned = lax.all_to_all(mixed, "seq", split_axis=0, concat_axis=0, tiled=True)
    return returned[slot_of_row]


FOUR = ("far", "near", "quad")
CORE, Y, NEAR, FAR = 1, 2, 4, 8
QUADS = (0, Y, CORE, Y | CORE)
RIM = 16
VMEM_LIMIT = 40 * 2**20


def swap_seq(value, bit):
    count = lax.axis_size(FOUR)
    return lax.ppermute(value, FOUR, [(d, d ^ bit) for d in range(count)])


def swap_grp(value):
    return lax.ppermute(value, "grp", [(0, 1), (1, 0)])


def call(kernel, out_shape, operands, name, scalars=None, scratch=(), flops=0, anywhere=0):
    in_specs = [pl.BlockSpec(memory_space=pltpu.VMEM)] * (len(operands) - anywhere)
    in_specs += [pl.BlockSpec(memory_space=pl.ANY)] * anywhere
    if scalars is not None:
        operands = [scalars] + list(operands)
        in_specs = [pl.BlockSpec(memory_space=pltpu.SMEM)] + in_specs
    many = isinstance(out_shape, (list, tuple))
    shapes = list(out_shape) if many else [out_shape]
    size = sum(2 * o.size for o in list(operands) + shapes)
    whole = pl.BlockSpec(memory_space=pltpu.VMEM)
    return pl.pallas_call(
        kernel,
        out_shape=out_shape,
        in_specs=in_specs,
        out_specs=[whole] * len(shapes) if many else whole,
        scratch_shapes=list(scratch),
        cost_estimate=pl.CostEstimate(flops=flops, bytes_accessed=size, transcendentals=0),
        compiler_params=pltpu.CompilerParams(vmem_limit_bytes=VMEM_LIMIT),
        name=name,
    )(*operands)


def bf16(*shape):
    return jax.ShapeDtypeStruct(shape, jnp.bfloat16)


def after_kernel(*refs):
    del refs


def after(value, *others):
    anywhere = pl.BlockSpec(memory_space=pl.ANY)
    return pl.pallas_call(
        after_kernel,
        out_shape=jax.ShapeDtypeStruct(value.shape, value.dtype),
        in_specs=[anywhere] * (1 + len(others)),
        out_specs=anywhere,
        input_output_aliases={0: 0},
        name="after",
    )(value, *others)


def convolved(before, rows, taps):
    count = rows.shape[0]
    rows = rows.astype(jnp.float32)
    extended = jnp.concatenate([before.astype(jnp.float32), rows], axis=0)
    taps = taps.astype(jnp.float32)
    total = rows
    for tap in range(KW):
        total = total + taps[tap : tap + 1] * extended[RIM - tap : RIM - tap + count]
    return total.astype(jnp.bfloat16)


def conv_late_kernel(frames_ref, taps_ref, late_ref, middle_ref):
    cut = frames_ref.shape[0] // 4
    rows = convolved(frames_ref[cut - RIM : cut], frames_ref[cut:], taps_ref[...])
    middle_ref[...] = rows[: 2 * cut]
    late_ref[...] = rows[2 * cut :]


def conv_early_kernel(rim_ref, frames_ref, taps_ref, late_ref, middle_ref, early_ref, own_ref):
    cut = frames_ref.shape[0] // 4
    early = convolved(rim_ref[...], frames_ref[:cut], taps_ref[...])
    early_ref[...] = early
    own_ref[:cut] = early
    own_ref[cut : 3 * cut] = middle_ref[...]
    own_ref[3 * cut :] = late_ref[...]


ME, SIDE, GRP, TURN, TURN_PAIRED, HEAD = range(6)


def project_kernel(row_refs, scalars, *refs):
    rows, pieces = refs[:row_refs], refs[row_refs : row_refs + 4]
    query_ref, keyed_ref, weight = refs[-3:]
    side, grp = scalars[SIDE], scalars[GRP]
    half = pieces[0].shape[2]
    for n, piece in enumerate(pieces):
        column = n // 2 + side - 2 * (n // 2) * side
        feature = n % 2 + grp - 2 * (n % 2) * grp
        turn = scalars[TURN if n < 2 else TURN_PAIRED]
        for j in range(3):
            part = lax.rem(j + 3 - turn, 3)
            start = pl.multiple_of(part * HD + column * (HD // 2), HD // 2)
            lanes = pl.ds(pl.multiple_of(feature * half, half), half)
            weight[pl.ds(start, HD // 2), lanes] = piece[j]
    at = 0
    for ref in rows:
        count = ref.shape[0]
        done = lax.dot_general(
            ref[...], weight[...], (((1,), (1,)), ((), ())), preferred_element_type=jnp.float32
        ).astype(jnp.bfloat16)
        query_ref[at : at + count] = done[:, :HD]
        keyed_ref[at : at + count] = done[:, HD:]
        at += count


def project(scalars, rows, pieces, following=()):
    total = sum(r.shape[0] for r in rows)
    features = rows[0].shape[1]

    def kernel(scalars_ref, *refs):
        front = len(rows) + 4
        project_kernel(len(rows), scalars_ref, *refs[:front], *refs[front + len(following) :])

    return call(
        kernel,
        [bf16(total, HD), bf16(total, 2 * HD)],
        list(rows) + list(pieces) + list(following),
        "project",
        scalars=scalars,
        scratch=[pltpu.VMEM((3 * HD, features), jnp.bfloat16)],
        flops=2 * total * 3 * HD * features,
        anywhere=len(following),
    )


def attend_kernel(scalars, groups_ref, *refs):
    queries, mine, theirs, outs = refs[:3], refs[3:6], refs[6:9], refs[9:17]
    keys, values, key_marks, query_marks, asked, mixed = refs[17:]
    devices, tok_rows = groups_ref.shape
    cut = tok_rows // 4
    rest = tok_rows - cut
    span = devices * tok_rows
    me = scalars[ME]
    groups = groups_ref[...] * span
    columns = groups.astype(jnp.float32).T.astype(jnp.int32)

    for j in range(devices):
        at = pl.multiple_of((me ^ j) * tok_rows, tok_rows)
        time = at + lax.broadcasted_iota(jnp.int32, (1, tok_rows), 1)
        marks = jnp.broadcast_to(groups[j : j + 1] + time, (8, tok_rows))
        key_marks[:, pl.ds(at, tok_rows)] = marks
    for hop, sources in ((0, mine), (NEAR, theirs)):
        for n, quad in enumerate(QUADS):
            whole = pl.multiple_of((me ^ hop ^ quad) * tok_rows, tok_rows)
            other = pl.multiple_of((me ^ hop ^ quad ^ FAR) * tok_rows, tok_rows)
            for target, lanes in ((keys, slice(0, HD)), (values, slice(HD, 2 * HD))):
                target[pl.ds(whole, tok_rows)] = sources[0][n * tok_rows : (n + 1) * tok_rows, lanes]
                target[pl.ds(other + cut, rest)] = sources[1][n * rest : (n + 1) * rest, lanes]
                target[pl.ds(other, cut)] = sources[2][n * cut : (n + 1) * cut, lanes]
    for n, quad in enumerate(QUADS):
        asked[n] = queries[0][n * tok_rows : (n + 1) * tok_rows]
        asked[n + 4, cut:] = queries[1][n * rest : (n + 1) * rest]
        asked[n + 4, :cut] = queries[2][n * cut : (n + 1) * cut]
        query_marks[n] = columns[:, quad : quad + 1]
        query_marks[n + 4] = columns[:, (quad | FAR) : (quad | FAR) + 1]

    def block(i, _):
        device = me ^ ((i & 1) * Y + ((i >> 1) & 1) * CORE + (i >> 2) * FAR)
        query = asked[i]
        least = query_marks[i]
        most = least + device * tok_rows + lax.broadcasted_iota(jnp.int32, (tok_rows, 1), 0)
        for reach in range(4, devices + 1, 4):

            @pl.when((device >= reach - 4) & (device < reach))
            def _(count=reach * tok_rows):
                scores = lax.dot_general(
                    query,
                    keys[:count],
                    (((1,), (1,)), ((), ())),
                    preferred_element_type=jnp.float32,
                ) * (1.0 / HD**0.5)
                marks = key_marks[0:1, :count]
                allowed = (marks >= least) & (marks <= most)
                scores = jnp.where(allowed, scores, jnp.float32(-1e30))
                expd = jnp.exp(scores - jnp.max(scores, axis=1, keepdims=True))
                scaled = expd * (1.0 / jnp.sum(expd, axis=1, keepdims=True))
                out = jnp.dot(
                    scaled.astype(jnp.bfloat16), values[:count], preferred_element_type=jnp.float32
                )
                mixed[i] = out.astype(jnp.bfloat16)

        return 0

    lax.fori_loop(0, 8, block, 0)
    for n in range(8):
        outs[n][...] = mixed[n]


def attend(scalars, groups, queries, mine, theirs):
    devices, tok_rows = groups.shape
    span = devices * tok_rows
    return call(
        attend_kernel,
        [bf16(tok_rows, HD)] * 8,
        [groups] + queries + mine + theirs,
        "attend",
        scalars=scalars,
        scratch=[
            pltpu.VMEM((span, HD), jnp.bfloat16),
            pltpu.VMEM((span, HD), jnp.bfloat16),
            pltpu.VMEM((8, span), jnp.int32),
            pltpu.VMEM((8, tok_rows, 1), jnp.int32),
            pltpu.VMEM((8, tok_rows, HD), jnp.bfloat16),
            pltpu.VMEM((8, tok_rows, HD), jnp.bfloat16),
        ],
        flops=2 * span * span * HD,
    )


def place_kernel(scalars, *refs):
    out_ref = refs[-1]
    for n, ref in enumerate(refs[:-1]):
        hop = QUADS[n % 4] + n // 4 * FAR
        head = scalars[HEAD] ^ (hop // FAR * 4 + hop % 4)
        out_ref[:, pl.ds(pl.multiple_of(head * HD, HD), HD)] = ref[...]


def body_by_head(frames, conv_weight, qkv_weight, track_ids, track_owner):
    tok_rows, features = frames.shape
    grp = lax.axis_index("grp")
    far, near, quad = (lax.axis_index(name) for name in FOUR)
    me = far * FAR + near * NEAR + quad
    devices = lax.axis_size(FOUR)
    head = far * 4 + quad
    cut = tok_rows // 4
    turn = lax.rem(2 * head + near, 3)
    turn_paired = lax.rem(2 * head + 1 - near, 3)
    scalars = jnp.stack([me, near, grp, turn, turn_paired, head]).astype(jnp.int32)

    rim_rows = lax.ppermute(
        frames[tok_rows - RIM :], FOUR, [(i, i + 1) for i in range(devices - 1)]
    )
    late, middle = call(
        conv_late_kernel,
        [bf16(cut, features), bf16(2 * cut, features)],
        [frames, conv_weight],
        "conv_late",
    )
    early, own = call(
        conv_early_kernel,
        [bf16(cut, features), bf16(tok_rows, features)],
        [rim_rows, frames, conv_weight, late, middle],
        "conv_early",
    )

    far_late = swap_seq(late, FAR)
    far_middle = swap_seq(middle, FAR)
    far_early = swap_seq(early, FAR)
    beside = swap_seq(own, Y)

    groups = track_groups(track_ids, track_owner)[None, :]
    for bit in (CORE, Y, NEAR, FAR):
        groups = jnp.concatenate([groups, swap_seq(groups, bit)], axis=0)

    def home(block):
        of_head, side = block % devices // 2, block % 2
        return of_head // 4 * FAR + side * NEAR + of_head % 4

    half = features // 2
    held = lax.dynamic_slice_in_dim(qkv_weight.T, grp * half, half, 1)
    held = held.reshape(3, HD // 2, half)
    mine = jnp.stack(
        [
            lax.ppermute(held[j], FOUR, [(d, home(3 * d + j)) for d in range(devices)])
            for j in range(3)
        ]
    )
    mine = after(mine, far_late)
    mine_too = swap_grp(mine)
    paired = swap_seq(mine, NEAR)
    paired_too = swap_grp(paired)
    pieces = [mine, mine_too, paired, paired_too]
    far_rest = jnp.concatenate([far_middle, far_late], axis=0)
    far_rest = after(far_rest, mine_too, paired, groups)

    def with_core(first, second, *others):
        both = jnp.concatenate([first, second], axis=0)
        return [first, second, swap_seq(after(both, *others) if others else both, CORE)]

    query, keyed = [], []

    def onward(rows):
        done = project(scalars, rows, pieces, query[-1:])
        query.append(done[0])
        keyed.append(done[1])

    far_rest_beside, far_early_beside = swap_seq(far_rest, Y), swap_seq(far_early, Y)
    onward(with_core(own, beside))
    onward(with_core(far_rest, far_rest_beside, paired_too, far_early))
    onward(with_core(far_early, far_early_beside, query[0]))
    swapped = [swap_seq(k, NEAR) for k in keyed]

    blocks = attend(scalars, groups, query, keyed, swapped)
    hops = [hop | far_hop for far_hop in (0, FAR) for hop in QUADS]
    home_blocks = {hop: swap_seq(blocks[n], hop) for n, hop in list(enumerate(hops))[:0:-1]}
    home_blocks[0] = blocks[0]
    return call(
        place_kernel,
        bf16(tok_rows, 8 * HD),
        [home_blocks[hop] for hop in hops],
        "place",
        scalars=scalars,
    )


def solution(mesh):
    grp, seq = mesh.devices.shape
    out_by_owner = P(("grp", "seq"), None)
    by_owner = jax.shard_map(
        body_by_owner,
        mesh=mesh,
        in_specs=(P(("grp", "seq"), None), P(), P(None, "seq"), P(("grp", "seq")), P("grp")),
        out_specs=out_by_owner,
        check_vma=False,
    )
    fits = (grp, seq) == (2, 16)
    if fits:
        split = Mesh(mesh.devices.reshape(grp, 2, 2, 4), ("grp",) + FOUR)
        rows = P(("grp",) + FOUR)
        by_head = jax.shard_map(
            body_by_head,
            mesh=split,
            in_specs=(rows, P(), P(None, FOUR), rows, P("grp")),
            out_specs=rows,
            check_vma=False,
        )

    def run(frames, conv_weight, qkv_weight, track_ids, track_owner):
        heads = qkv_weight.shape[1] // (3 * HD)
        plan = by_head if fits and heads == 8 else by_owner
        return plan(frames, conv_weight, qkv_weight, track_ids, track_owner)

    return run
```

```python
import jax
import jax.numpy as jnp
from jax import lax
from jax.experimental import pallas as pl
from jax.experimental.pallas import tpu as pltpu
from jax.sharding import Mesh
from jax.sharding import PartitionSpec as P

HD = 128
KW = 4


def from_behind(value, axis, by):
    size = lax.axis_size(axis)
    pairs = [(i, i + by) for i in range(size) if 0 <= i + by < size]
    return lax.ppermute(value, axis, pairs)


def track_groups(track_ids, track_owner):
    track_total = track_owner.shape[0]
    return jnp.sum(
        jnp.where(
            track_ids[:, None] == jnp.arange(track_total, dtype=jnp.int32)[None, :],
            track_owner[None, :],
            0,
        ),
        axis=1,
    )


def convolve(frames, conv_weight, rim_rows):
    tok_rows = frames.shape[0]
    extended = jnp.concatenate([rim_rows, frames], axis=0).astype(jnp.float32)
    conv_sum = frames.astype(jnp.float32)
    for tap in range(KW):
        conv_sum = (
            conv_sum
            + conv_weight[tap].astype(jnp.float32)[None, :]
            * extended[KW - 1 - tap : KW - 1 - tap + tok_rows]
        )
    return conv_sum.astype(jnp.bfloat16)


def attend_slots(packed, positions):
    slot_count = packed.shape[0]
    inner = packed.shape[1] // 3
    head_count = inner // HD
    query = packed[:, :inner].reshape(slot_count, head_count, HD)
    keys_all = packed[:, inner : 2 * inner].reshape(slot_count, head_count, HD)
    values_all = packed[:, 2 * inner :].reshape(slot_count, head_count, HD)
    slot_ids = jnp.arange(slot_count, dtype=jnp.int32)
    score_scale = 1.0 / HD**0.5
    scores = (
        jnp.einsum("qhd,khd->hqk", query, keys_all, preferred_element_type=jnp.float32)
        * score_scale
    )
    allowed = (positions[None, :] >= 0) & (positions[None, :] <= positions[:, None]) | (
        slot_ids[:, None] == slot_ids[None, :]
    )
    scores = jnp.where(allowed[None], scores, jnp.float32(-1e30))
    top_score = jnp.max(scores, axis=-1, keepdims=True)
    expd = jnp.exp(scores - top_score)
    weights = (expd / jnp.sum(expd, axis=-1, keepdims=True)).astype(jnp.bfloat16)
    mixed = jnp.einsum("hqk,khd->qhd", weights, values_all, preferred_element_type=jnp.float32)
    return mixed.astype(jnp.bfloat16).reshape(slot_count, inner)


def body_by_owner(frames, conv_weight, qkv_weight, track_ids, track_owner):
    tok_rows = frames.shape[0]
    peer_count = lax.axis_size("seq")
    capacity = 2 * tok_rows // peer_count
    slot_total = capacity * peer_count
    my_index = lax.axis_index("seq")
    rim_rows = from_behind(frames[tok_rows - (KW - 1) :], "seq", 1)
    hidden = convolve(frames, conv_weight, rim_rows)
    group = track_groups(track_ids, track_owner)
    owner_hits = (group[:, None] == jnp.arange(peer_count, dtype=jnp.int32)[None, :]).astype(
        jnp.int32
    )
    running = jnp.cumsum(owner_hits, axis=0) - 1
    rank_rows = jnp.sum(jnp.where(owner_hits > 0, running, 0), axis=1)
    slot_of_row = group * capacity + rank_rows
    row_ids = jnp.arange(tok_rows, dtype=jnp.int32)
    source_row = jnp.full((slot_total,), tok_rows, jnp.int32).at[slot_of_row].set(row_ids)
    positions = my_index * tok_rows + row_ids
    send_times = jnp.full((slot_total,), -1, jnp.int32).at[slot_of_row].set(positions)
    projected = jnp.dot(
        hidden,
        lax.all_gather(qkv_weight, "seq", axis=1, tiled=True),
        preferred_element_type=jnp.float32,
    ).astype(jnp.bfloat16)
    padded_rows = jnp.concatenate(
        [projected, jnp.zeros((1, projected.shape[1]), jnp.bfloat16)], axis=0
    )
    outgoing = padded_rows[source_row]
    received, got_times = (
        lax.all_to_all(outgoing, "seq", split_axis=0, concat_axis=0, tiled=True),
        lax.all_to_all(send_times, "seq", split_axis=0, concat_axis=0, tiled=True),
    )
    mixed = attend_slots(received, got_times)
    returned = lax.all_to_all(mixed, "seq", split_axis=0, concat_axis=0, tiled=True)
    return returned[slot_of_row]


FOUR = ("far", "near", "quad")
CORE, Y, NEAR, FAR = 1, 2, 4, 8
QUADS = (0, Y, CORE, Y | CORE)
RIM = 16
VMEM_LIMIT = 40 * 2**20


def swap_seq(value, bit):
    count = lax.axis_size(FOUR)
    return lax.ppermute(value, FOUR, [(d, d ^ bit) for d in range(count)])


def swap_grp(value):
    return lax.ppermute(value, "grp", [(0, 1), (1, 0)])


def call(kernel, out_shape, operands, name, scalars=None, scratch=(), flops=0, anywhere=0):
    in_specs = [pl.BlockSpec(memory_space=pltpu.VMEM)] * (len(operands) - anywhere)
    in_specs += [pl.BlockSpec(memory_space=pl.ANY)] * anywhere
    if scalars is not None:
        operands = [scalars] + list(operands)
        in_specs = [pl.BlockSpec(memory_space=pltpu.SMEM)] + in_specs
    many = isinstance(out_shape, (list, tuple))
    shapes = list(out_shape) if many else [out_shape]
    size = sum(2 * o.size for o in list(operands) + shapes)
    whole = pl.BlockSpec(memory_space=pltpu.VMEM)
    return pl.pallas_call(
        kernel,
        out_shape=out_shape,
        in_specs=in_specs,
        out_specs=[whole] * len(shapes) if many else whole,
        scratch_shapes=list(scratch),
        cost_estimate=pl.CostEstimate(flops=flops, bytes_accessed=size, transcendentals=0),
        compiler_params=pltpu.CompilerParams(vmem_limit_bytes=VMEM_LIMIT),
        name=name,
    )(*operands)


def bf16(*shape):
    return jax.ShapeDtypeStruct(shape, jnp.bfloat16)


def after_kernel(*refs):
    del refs


def after(value, *others):
    anywhere = pl.BlockSpec(memory_space=pl.ANY)
    return pl.pallas_call(
        after_kernel,
        out_shape=jax.ShapeDtypeStruct(value.shape, value.dtype),
        in_specs=[anywhere] * (1 + len(others)),
        out_specs=anywhere,
        input_output_aliases={0: 0},
        name="after",
    )(value, *others)


def convolved(before, rows, taps):
    count = rows.shape[0]
    rows = rows.astype(jnp.float32)
    extended = jnp.concatenate([before.astype(jnp.float32), rows], axis=0)
    taps = taps.astype(jnp.float32)
    total = rows
    for tap in range(KW):
        total = total + taps[tap : tap + 1] * extended[RIM - tap : RIM - tap + count]
    return total.astype(jnp.bfloat16)


def conv_late_kernel(frames_ref, taps_ref, late_ref):
    part = late_ref.shape[0]
    late_ref[...] = convolved(frames_ref[part - RIM : part], frames_ref[part:], taps_ref[...])


def conv_early_kernel(rim_ref, frames_ref, taps_ref, late_ref, early_ref, own_ref):
    part = late_ref.shape[0]
    early = convolved(rim_ref[...], frames_ref[:part], taps_ref[...])
    early_ref[...] = early
    own_ref[:part] = early
    own_ref[part:] = late_ref[...]


def by_bit(bit, mine, theirs, axis):
    return jnp.stack(
        [jnp.where(bit == 0, mine, theirs), jnp.where(bit == 0, theirs, mine)], axis=axis
    )


def body_by_head(frames, conv_weight, qkv_weight, track_ids, track_owner):
    tok_rows, features = frames.shape
    grp = lax.axis_index("grp")
    far, near, quad = (lax.axis_index(name) for name in FOUR)
    me = far * FAR + near * NEAR + quad
    devices = lax.axis_size(FOUR)
    head = far * 4 + quad
    part = tok_rows // 2

    def home(block):
        of_head, side = block % devices // 2, block % 2
        return of_head // 4 * FAR + side * NEAR + of_head % 4

    half = features // 2
    held = lax.dynamic_slice_in_dim(qkv_weight.T, grp * half, half, 1)
    held = held.reshape(3, HD // 2, half)
    moved = [
        lax.ppermute(held[j], FOUR, [(d, home(3 * d + j)) for d in range(devices)])
        for j in range(3)
    ]
    turn = lax.rem(2 * head + near, 3)
    mine = lax.dynamic_slice_in_dim(jnp.stack(moved + moved[:2]), turn, 3, 0)
    mine_too = swap_grp(mine)
    paired = swap_seq(mine, NEAR)
    paired_too = swap_grp(paired)
    head_weight = by_bit(
        near, by_bit(grp, mine, mine_too, 2), by_bit(grp, paired, paired_too, 2), 1
    ).reshape(3 * HD, features)

    rim_rows = lax.ppermute(
        frames[tok_rows - RIM :], FOUR, [(i, i + 1) for i in range(devices - 1)]
    )
    late = call(conv_late_kernel, bf16(part, features), [frames, conv_weight], "conv_late")
    early, own = call(
        conv_early_kernel,
        [bf16(part, features), bf16(tok_rows, features)],
        [rim_rows, frames, conv_weight, late],
        "conv_early",
    )
    beside = swap_seq(own, Y)
    far_late = after(swap_seq(late, FAR), mine_too)
    far_late_beside = swap_seq(far_late, Y)
    far_early = swap_seq(after(early, far_late), FAR)
    far_early_beside = swap_seq(after(far_early, paired_too), Y)

    groups = track_groups(track_ids, track_owner)[None, :]
    groups = jnp.concatenate([groups, swap_seq(groups, NEAR)], axis=0)

    parts = []

    def project(rows, *others):
        rows = jnp.concatenate(rows, axis=0)
        rows = jnp.concatenate([rows, swap_seq(rows, CORE)], axis=0)
        done = lax.dot_general(
            after(rows, *others) if others else rows,
            head_weight,
            (((1,), (1,)), ((), ())),
            preferred_element_type=jnp.float32,
        ).astype(jnp.bfloat16)
        parts.append((done[:, :HD], done[:, HD:], swap_seq(done[:, HD:], NEAR)))
        return done

    done = project([own, beside])
    groups = after(groups, done)
    for bit in (FAR, CORE, Y):
        groups = jnp.concatenate([groups, swap_seq(groups, bit)], axis=0)
    project([far_late, far_late_beside], done)
    project([far_early, after(far_early_beside, done)], groups)
    query = jnp.concatenate([p[0] for p in parts], axis=0)
    keyed = jnp.concatenate([p[1] for p in parts] + [p[2] for p in parts], axis=0)

    row_of = {}
    for bit in (0, NEAR, FAR, CORE, Y):
        row_of.update({seen ^ bit: len(row_of) + n for n, seen in enumerate(list(row_of) or [0])})

    order = [(hop, 0, tok_rows) for hop in QUADS]
    order += [(hop | FAR, part, part) for hop in QUADS]
    order += [(hop | FAR, 0, part) for hop in QUADS]

    def of_rows(bit):
        times = [
            (me ^ hop ^ bit) * tok_rows + start + jnp.arange(count, dtype=jnp.int32)
            for hop, start, count in order
        ]
        marks = [groups[row_of[hop ^ bit], start : start + count] for hop, start, count in order]
        return jnp.concatenate(times), jnp.concatenate(marks)

    own_times, own_groups = of_rows(0)
    other_times, other_groups = of_rows(NEAR)
    key_times = jnp.concatenate([own_times, other_times])
    key_groups = jnp.concatenate([own_groups, other_groups])
    scores = lax.dot_general(
        query, keyed[:, :HD], (((1,), (1,)), ((), ())), preferred_element_type=jnp.float32
    ) * (1.0 / HD**0.5)
    allowed = (key_times[None, :] <= own_times[:, None]) & (
        key_groups[None, :] == own_groups[:, None]
    )
    scores = jnp.where(allowed, scores, jnp.float32(-1e30))
    expd = jnp.exp(scores - jnp.max(scores, axis=-1, keepdims=True))
    weights = (expd / jnp.sum(expd, axis=-1, keepdims=True)).astype(jnp.bfloat16)
    mixed = jnp.dot(weights, keyed[:, HD:], preferred_element_type=jnp.float32)
    mixed = mixed.astype(jnp.bfloat16)

    sent = jnp.zeros((devices // 2, tok_rows, HD), jnp.bfloat16)
    at = 0
    for hop, start, count in order:
        rows = mixed[at : at + count]
        there = head ^ (hop // FAR * 4 + hop % 4)
        sent = lax.dynamic_update_slice(sent, rows[None], (there, start, 0))
        at += count
    returned = lax.all_to_all(sent, ("far", "quad"), split_axis=0, concat_axis=0, tiled=True)
    return returned.transpose(1, 0, 2).reshape(tok_rows, devices // 2 * HD)


def solution(mesh):
    grp, seq = mesh.devices.shape
    out_by_owner = P(("grp", "seq"), None)
    by_owner = jax.shard_map(
        body_by_owner,
        mesh=mesh,
        in_specs=(P(("grp", "seq"), None), P(), P(None, "seq"), P(("grp", "seq")), P("grp")),
        out_specs=out_by_owner,
        check_vma=False,
    )
    fits = (grp, seq) == (2, 16)
    if fits:
        split = Mesh(mesh.devices.reshape(grp, 2, 2, 4), ("grp",) + FOUR)
        rows = P(("grp",) + FOUR)
        by_head = jax.shard_map(
            body_by_head,
            mesh=split,
            in_specs=(rows, P(), P(None, FOUR), rows, P("grp")),
            out_specs=rows,
            check_vma=False,
        )

    def run(frames, conv_weight, qkv_weight, track_ids, track_owner):
        heads = qkv_weight.shape[1] // (3 * HD)
        plan = by_head if fits and heads == 8 else by_owner
        return plan(frames, conv_weight, qkv_weight, track_ids, track_owner)

    return run
```

```python
import jax
import jax.numpy as jnp
from jax import lax
from jax.experimental import pallas as pl
from jax.experimental.pallas import tpu as pltpu
from jax.sharding import Mesh
from jax.sharding import PartitionSpec as P

HD = 128
KW = 4


def from_behind(value, axis, by):
    size = lax.axis_size(axis)
    pairs = [(i, i + by) for i in range(size) if 0 <= i + by < size]
    return lax.ppermute(value, axis, pairs)


def track_groups(track_ids, track_owner):
    track_total = track_owner.shape[0]
    return jnp.sum(
        jnp.where(
            track_ids[:, None] == jnp.arange(track_total, dtype=jnp.int32)[None, :],
            track_owner[None, :],
            0,
        ),
        axis=1,
    )


def convolve(frames, conv_weight, rim_rows):
    tok_rows = frames.shape[0]
    extended = jnp.concatenate([rim_rows, frames], axis=0).astype(jnp.float32)
    conv_sum = frames.astype(jnp.float32)
    for tap in range(KW):
        conv_sum = (
            conv_sum
            + conv_weight[tap].astype(jnp.float32)[None, :]
            * extended[KW - 1 - tap : KW - 1 - tap + tok_rows]
        )
    return conv_sum.astype(jnp.bfloat16)


def attend_slots(packed, positions):
    slot_count = packed.shape[0]
    inner = packed.shape[1] // 3
    head_count = inner // HD
    query = packed[:, :inner].reshape(slot_count, head_count, HD)
    keys_all = packed[:, inner : 2 * inner].reshape(slot_count, head_count, HD)
    values_all = packed[:, 2 * inner :].reshape(slot_count, head_count, HD)
    slot_ids = jnp.arange(slot_count, dtype=jnp.int32)
    score_scale = 1.0 / HD**0.5
    scores = (
        jnp.einsum("qhd,khd->hqk", query, keys_all, preferred_element_type=jnp.float32)
        * score_scale
    )
    allowed = (positions[None, :] >= 0) & (positions[None, :] <= positions[:, None]) | (
        slot_ids[:, None] == slot_ids[None, :]
    )
    scores = jnp.where(allowed[None], scores, jnp.float32(-1e30))
    top_score = jnp.max(scores, axis=-1, keepdims=True)
    expd = jnp.exp(scores - top_score)
    weights = (expd / jnp.sum(expd, axis=-1, keepdims=True)).astype(jnp.bfloat16)
    mixed = jnp.einsum("hqk,khd->qhd", weights, values_all, preferred_element_type=jnp.float32)
    return mixed.astype(jnp.bfloat16).reshape(slot_count, inner)


def body_by_owner(frames, conv_weight, qkv_weight, track_ids, track_owner):
    tok_rows = frames.shape[0]
    peer_count = lax.axis_size("seq")
    capacity = 2 * tok_rows // peer_count
    slot_total = capacity * peer_count
    my_index = lax.axis_index("seq")
    rim_rows = from_behind(frames[tok_rows - (KW - 1) :], "seq", 1)
    hidden = convolve(frames, conv_weight, rim_rows)
    group = track_groups(track_ids, track_owner)
    owner_hits = (group[:, None] == jnp.arange(peer_count, dtype=jnp.int32)[None, :]).astype(
        jnp.int32
    )
    running = jnp.cumsum(owner_hits, axis=0) - 1
    rank_rows = jnp.sum(jnp.where(owner_hits > 0, running, 0), axis=1)
    slot_of_row = group * capacity + rank_rows
    row_ids = jnp.arange(tok_rows, dtype=jnp.int32)
    source_row = jnp.full((slot_total,), tok_rows, jnp.int32).at[slot_of_row].set(row_ids)
    positions = my_index * tok_rows + row_ids
    send_times = jnp.full((slot_total,), -1, jnp.int32).at[slot_of_row].set(positions)
    projected = jnp.dot(
        hidden,
        lax.all_gather(qkv_weight, "seq", axis=1, tiled=True),
        preferred_element_type=jnp.float32,
    ).astype(jnp.bfloat16)
    padded_rows = jnp.concatenate(
        [projected, jnp.zeros((1, projected.shape[1]), jnp.bfloat16)], axis=0
    )
    outgoing = padded_rows[source_row]
    received, got_times = (
        lax.all_to_all(outgoing, "seq", split_axis=0, concat_axis=0, tiled=True),
        lax.all_to_all(send_times, "seq", split_axis=0, concat_axis=0, tiled=True),
    )
    mixed = attend_slots(received, got_times)
    returned = lax.all_to_all(mixed, "seq", split_axis=0, concat_axis=0, tiled=True)
    return returned[slot_of_row]


FOUR = ("far", "near", "quad")
CORE, Y, NEAR, FAR = 1, 2, 4, 8
QUADS = (0, Y, CORE, Y | CORE)
RIM = 16
VMEM_LIMIT = 6 * 2**20


def swap_seq(value, bit):
    count = lax.axis_size(FOUR)
    return lax.ppermute(value, FOUR, [(d, d ^ bit) for d in range(count)])


def swap_grp(value):
    return lax.ppermute(value, "grp", [(0, 1), (1, 0)])


def call(kernel, out_shape, operands, name, scalars=None, scratch=(), flops=0, anywhere=0):
    in_specs = [pl.BlockSpec(memory_space=pltpu.VMEM)] * (len(operands) - anywhere)
    in_specs += [pl.BlockSpec(memory_space=pl.ANY)] * anywhere
    if scalars is not None:
        operands = [scalars] + list(operands)
        in_specs = [pl.BlockSpec(memory_space=pltpu.SMEM)] + in_specs
    many = isinstance(out_shape, (list, tuple))
    shapes = list(out_shape) if many else [out_shape]
    size = sum(2 * o.size for o in list(operands) + shapes)
    whole = pl.BlockSpec(memory_space=pltpu.VMEM)
    return pl.pallas_call(
        kernel,
        out_shape=out_shape,
        in_specs=in_specs,
        out_specs=[whole] * len(shapes) if many else whole,
        scratch_shapes=list(scratch),
        cost_estimate=pl.CostEstimate(flops=flops, bytes_accessed=size, transcendentals=0),
        compiler_params=pltpu.CompilerParams(vmem_limit_bytes=VMEM_LIMIT),
        name=name,
    )(*operands)


def bf16(*shape):
    return jax.ShapeDtypeStruct(shape, jnp.bfloat16)


def after_kernel(*refs):
    del refs


def after(value, *others):
    anywhere = pl.BlockSpec(memory_space=pl.ANY)
    return pl.pallas_call(
        after_kernel,
        out_shape=jax.ShapeDtypeStruct(value.shape, value.dtype),
        in_specs=[anywhere] * (1 + len(others)),
        out_specs=anywhere,
        input_output_aliases={0: 0},
        compiler_params=pltpu.CompilerParams(vmem_limit_bytes=2**20),
        name="after",
    )(value, *others)


def convolved(before, rows, taps):
    count = rows.shape[0]
    rows = rows.astype(jnp.float32)
    extended = jnp.concatenate([before.astype(jnp.float32), rows], axis=0)
    taps = taps.astype(jnp.float32)
    total = rows
    for tap in range(KW):
        total = total + taps[tap : tap + 1] * extended[RIM - tap : RIM - tap + count]
    return total.astype(jnp.bfloat16)


def conv_late_kernel(frames_ref, taps_ref, late_ref):
    part = late_ref.shape[0]
    late_ref[...] = convolved(frames_ref[part - RIM : part], frames_ref[part:], taps_ref[...])


def conv_early_kernel(rim_ref, frames_ref, taps_ref, late_ref, early_ref, own_ref):
    part = late_ref.shape[0]
    early = convolved(rim_ref[...], frames_ref[:part], taps_ref[...])
    early_ref[...] = early
    own_ref[:part] = early
    own_ref[part:] = late_ref[...]


def by_bit(bit, mine, theirs, axis):
    return jnp.stack(
        [jnp.where(bit == 0, mine, theirs), jnp.where(bit == 0, theirs, mine)], axis=axis
    )


def body_by_head(frames, conv_weight, qkv_weight, track_ids, track_owner):
    tok_rows, features = frames.shape
    grp = lax.axis_index("grp")
    far, near, quad = (lax.axis_index(name) for name in FOUR)
    me = far * FAR + near * NEAR + quad
    devices = lax.axis_size(FOUR)
    head = far * 4 + quad
    part = tok_rows // 2

    def home(block):
        of_head, side = block % devices // 2, block % 2
        return of_head // 4 * FAR + side * NEAR + of_head % 4

    half = features // 2
    held = lax.dynamic_slice_in_dim(qkv_weight.T, grp * half, half, 1)
    held = held.reshape(3, HD // 2, half)
    moved = [
        lax.ppermute(held[j], FOUR, [(d, home(3 * d + j)) for d in range(devices)])
        for j in range(3)
    ]
    turn = lax.rem(2 * head + near, 3)
    mine = lax.dynamic_slice_in_dim(jnp.stack(moved + moved[:2]), turn, 3, 0)
    mine_too = swap_grp(mine)
    paired = swap_seq(mine, NEAR)
    paired_too = swap_grp(paired)
    head_weight = by_bit(
        near, by_bit(grp, mine, mine_too, 2), by_bit(grp, paired, paired_too, 2), 1
    ).reshape(3 * HD, features)

    rim_rows = lax.ppermute(
        frames[tok_rows - RIM :], FOUR, [(i, i + 1) for i in range(devices - 1)]
    )
    late = call(conv_late_kernel, bf16(part, features), [frames, conv_weight], "conv_late")
    early, own = call(
        conv_early_kernel,
        [bf16(part, features), bf16(tok_rows, features)],
        [rim_rows, frames, conv_weight, late],
        "conv_early",
    )
    beside = swap_seq(own, Y)
    far_late = after(swap_seq(late, FAR), mine_too)
    far_late_beside = swap_seq(far_late, Y)
    far_early = swap_seq(after(early, far_late), FAR)
    far_early_beside = swap_seq(after(far_early, paired_too), Y)

    groups = track_groups(track_ids, track_owner)[None, :]
    groups = jnp.concatenate([groups, swap_seq(groups, NEAR)], axis=0)

    parts = []

    def project(rows, *others):
        rows = jnp.concatenate(rows, axis=0)
        rows = jnp.concatenate([rows, swap_seq(rows, CORE)], axis=0)
        done = lax.dot_general(
            after(rows, *others) if others else rows,
            head_weight,
            (((1,), (1,)), ((), ())),
            preferred_element_type=jnp.float32,
        ).astype(jnp.bfloat16)
        parts.append((done[:, :HD], done[:, HD:], swap_seq(done[:, HD:], NEAR)))
        return done

    done = project([own, beside])
    groups = after(groups, done)
    for bit in (FAR, CORE, Y):
        groups = jnp.concatenate([groups, swap_seq(groups, bit)], axis=0)
    project([far_late, far_late_beside], done)
    project([far_early, after(far_early_beside, done)], groups)
    query = jnp.concatenate([p[0] for p in parts], axis=0)
    keyed = jnp.concatenate([p[1] for p in parts] + [p[2] for p in parts], axis=0)

    row_of = {}
    for bit in (0, NEAR, FAR, CORE, Y):
        row_of.update({seen ^ bit: len(row_of) + n for n, seen in enumerate(list(row_of) or [0])})

    order = [(hop, 0, tok_rows) for hop in QUADS]
    order += [(hop | FAR, part, part) for hop in QUADS]
    order += [(hop | FAR, 0, part) for hop in QUADS]

    def of_rows(bit):
        times = [
            (me ^ hop ^ bit) * tok_rows + start + jnp.arange(count, dtype=jnp.int32)
            for hop, start, count in order
        ]
        marks = [groups[row_of[hop ^ bit], start : start + count] for hop, start, count in order]
        return jnp.concatenate(times), jnp.concatenate(marks)

    own_times, own_groups = of_rows(0)
    other_times, other_groups = of_rows(NEAR)
    key_times = jnp.concatenate([own_times, other_times])
    key_groups = jnp.concatenate([own_groups, other_groups])
    scores = lax.dot_general(
        query, keyed[:, :HD], (((1,), (1,)), ((), ())), preferred_element_type=jnp.float32
    ) * (1.0 / HD**0.5)
    allowed = (key_times[None, :] <= own_times[:, None]) & (
        key_groups[None, :] == own_groups[:, None]
    )
    scores = jnp.where(allowed, scores, jnp.float32(-1e30))
    expd = jnp.exp(scores - jnp.max(scores, axis=-1, keepdims=True))
    weights = (expd / jnp.sum(expd, axis=-1, keepdims=True)).astype(jnp.bfloat16)
    mixed = jnp.dot(weights, keyed[:, HD:], preferred_element_type=jnp.float32)
    mixed = mixed.astype(jnp.bfloat16)

    sent = jnp.zeros((devices // 2, tok_rows, HD), jnp.bfloat16)
    at = 0
    for hop, start, count in order:
        rows = mixed[at : at + count]
        there = head ^ (hop // FAR * 4 + hop % 4)
        sent = lax.dynamic_update_slice(sent, rows[None], (there, start, 0))
        at += count
    returned = lax.all_to_all(sent, ("far", "quad"), split_axis=0, concat_axis=0, tiled=True)
    return returned.transpose(1, 0, 2).reshape(tok_rows, devices // 2 * HD)


def solution(mesh):
    grp, seq = mesh.devices.shape
    out_by_owner = P(("grp", "seq"), None)
    by_owner = jax.shard_map(
        body_by_owner,
        mesh=mesh,
        in_specs=(P(("grp", "seq"), None), P(), P(None, "seq"), P(("grp", "seq")), P("grp")),
        out_specs=out_by_owner,
        check_vma=False,
    )
    fits = (grp, seq) == (2, 16)
    if fits:
        split = Mesh(mesh.devices.reshape(grp, 2, 2, 4), ("grp",) + FOUR)
        rows = P(("grp",) + FOUR)
        by_head = jax.shard_map(
            body_by_head,
            mesh=split,
            in_specs=(rows, P(), P(None, FOUR), rows, P("grp")),
            out_specs=rows,
            check_vma=False,
        )

    def run(frames, conv_weight, qkv_weight, track_ids, track_owner):
        heads = qkv_weight.shape[1] // (3 * HD)
        plan = by_head if fits and heads == 8 else by_owner
        return plan(frames, conv_weight, qkv_weight, track_ids, track_owner)

    return run
```

```python
import jax
import jax.numpy as jnp
from jax import lax
from jax.experimental import pallas as pl
from jax.experimental.pallas import tpu as pltpu
from jax.sharding import Mesh
from jax.sharding import PartitionSpec as P

HD = 128
KW = 4


def from_behind(value, axis, by):
    size = lax.axis_size(axis)
    pairs = [(i, i + by) for i in range(size) if 0 <= i + by < size]
    return lax.ppermute(value, axis, pairs)


def track_groups(track_ids, track_owner):
    track_total = track_owner.shape[0]
    return jnp.sum(
        jnp.where(
            track_ids[:, None] == jnp.arange(track_total, dtype=jnp.int32)[None, :],
            track_owner[None, :],
            0,
        ),
        axis=1,
    )


def convolve(frames, conv_weight, rim_rows):
    tok_rows = frames.shape[0]
    extended = jnp.concatenate([rim_rows, frames], axis=0).astype(jnp.float32)
    conv_sum = frames.astype(jnp.float32)
    for tap in range(KW):
        conv_sum = (
            conv_sum
            + conv_weight[tap].astype(jnp.float32)[None, :]
            * extended[KW - 1 - tap : KW - 1 - tap + tok_rows]
        )
    return conv_sum.astype(jnp.bfloat16)


def attend_slots(packed, positions):
    slot_count = packed.shape[0]
    inner = packed.shape[1] // 3
    head_count = inner // HD
    query = packed[:, :inner].reshape(slot_count, head_count, HD)
    keys_all = packed[:, inner : 2 * inner].reshape(slot_count, head_count, HD)
    values_all = packed[:, 2 * inner :].reshape(slot_count, head_count, HD)
    slot_ids = jnp.arange(slot_count, dtype=jnp.int32)
    score_scale = 1.0 / HD**0.5
    scores = (
        jnp.einsum("qhd,khd->hqk", query, keys_all, preferred_element_type=jnp.float32)
        * score_scale
    )
    allowed = (positions[None, :] >= 0) & (positions[None, :] <= positions[:, None]) | (
        slot_ids[:, None] == slot_ids[None, :]
    )
    scores = jnp.where(allowed[None], scores, jnp.float32(-1e30))
    top_score = jnp.max(scores, axis=-1, keepdims=True)
    expd = jnp.exp(scores - top_score)
    weights = (expd / jnp.sum(expd, axis=-1, keepdims=True)).astype(jnp.bfloat16)
    mixed = jnp.einsum("hqk,khd->qhd", weights, values_all, preferred_element_type=jnp.float32)
    return mixed.astype(jnp.bfloat16).reshape(slot_count, inner)


def body_by_owner(frames, conv_weight, qkv_weight, track_ids, track_owner):
    tok_rows = frames.shape[0]
    peer_count = lax.axis_size("seq")
    capacity = 2 * tok_rows // peer_count
    slot_total = capacity * peer_count
    my_index = lax.axis_index("seq")
    rim_rows = from_behind(frames[tok_rows - (KW - 1) :], "seq", 1)
    hidden = convolve(frames, conv_weight, rim_rows)
    group = track_groups(track_ids, track_owner)
    owner_hits = (group[:, None] == jnp.arange(peer_count, dtype=jnp.int32)[None, :]).astype(
        jnp.int32
    )
    running = jnp.cumsum(owner_hits, axis=0) - 1
    rank_rows = jnp.sum(jnp.where(owner_hits > 0, running, 0), axis=1)
    slot_of_row = group * capacity + rank_rows
    row_ids = jnp.arange(tok_rows, dtype=jnp.int32)
    source_row = jnp.full((slot_total,), tok_rows, jnp.int32).at[slot_of_row].set(row_ids)
    positions = my_index * tok_rows + row_ids
    send_times = jnp.full((slot_total,), -1, jnp.int32).at[slot_of_row].set(positions)
    projected = jnp.dot(
        hidden,
        lax.all_gather(qkv_weight, "seq", axis=1, tiled=True),
        preferred_element_type=jnp.float32,
    ).astype(jnp.bfloat16)
    padded_rows = jnp.concatenate(
        [projected, jnp.zeros((1, projected.shape[1]), jnp.bfloat16)], axis=0
    )
    outgoing = padded_rows[source_row]
    received, got_times = (
        lax.all_to_all(outgoing, "seq", split_axis=0, concat_axis=0, tiled=True),
        lax.all_to_all(send_times, "seq", split_axis=0, concat_axis=0, tiled=True),
    )
    mixed = attend_slots(received, got_times)
    returned = lax.all_to_all(mixed, "seq", split_axis=0, concat_axis=0, tiled=True)
    return returned[slot_of_row]


FOUR = ("far", "near", "quad")
CORE, Y, NEAR, FAR = 1, 2, 4, 8
QUADS = (0, Y, CORE, Y | CORE)
RIM = 16


def swap_seq(value, bit):
    count = lax.axis_size(FOUR)
    return lax.ppermute(value, FOUR, [(d, d ^ bit) for d in range(count)])


def swap_grp(value):
    return lax.ppermute(value, "grp", [(0, 1), (1, 0)])


def call(kernel, out_shape, operands, name, smem=0, flops=0, limit=6):
    whole = pl.BlockSpec(memory_space=pltpu.VMEM)
    scalars = pl.BlockSpec(memory_space=pltpu.SMEM)
    many = isinstance(out_shape, (list, tuple))
    shapes = list(out_shape) if many else [out_shape]
    return pl.pallas_call(
        kernel,
        out_shape=out_shape,
        in_specs=[scalars] * smem + [whole] * (len(operands) - smem),
        out_specs=[whole] * len(shapes) if many else whole,
        cost_estimate=pl.CostEstimate(
            flops=flops,
            bytes_accessed=sum(2 * o.size for o in list(operands) + shapes),
            transcendentals=0,
        ),
        compiler_params=pltpu.CompilerParams(vmem_limit_bytes=limit * 2**20),
        name=name,
    )(*operands)


def bf16(*shape):
    return jax.ShapeDtypeStruct(shape, jnp.bfloat16)


def after_kernel(*refs):
    del refs


def after(value, *others):
    anywhere = pl.BlockSpec(memory_space=pl.ANY)
    return pl.pallas_call(
        after_kernel,
        out_shape=jax.ShapeDtypeStruct(value.shape, value.dtype),
        in_specs=[anywhere] * (1 + len(others)),
        out_specs=anywhere,
        input_output_aliases={0: 0},
        compiler_params=pltpu.CompilerParams(vmem_limit_bytes=2**20),
        name="after",
    )(value, *others)


def convolved(before, rows, taps):
    count = rows.shape[0]
    rows = rows.astype(jnp.float32)
    extended = jnp.concatenate([before.astype(jnp.float32), rows], axis=0)
    taps = taps.astype(jnp.float32)
    total = rows
    for tap in range(KW):
        total = total + taps[tap : tap + 1] * extended[RIM - tap : RIM - tap + count]
    return total.astype(jnp.bfloat16)


ME, SIDE, GRP, TURN, TURN_PAIRED = range(5)


def first_kernel(scalars, owner, ids, frames, weight, taps, late, rim, block0, block1, block2, code):
    tok_rows = frames.shape[0]
    part = late.shape[0]
    half = block0.shape[1]
    tracks = owner.shape[0]
    span = 16 * tok_rows
    late[...] = convolved(frames[part - RIM : part], frames[part:], taps[...])
    rim[...] = frames[tok_rows - RIM :]
    lanes = pl.ds(pl.multiple_of(scalars[GRP] * half, half), half)
    for j, block in enumerate((block0, block1, block2)):
        block[...] = weight[j * (HD // 2) : (j + 1) * (HD // 2), lanes]
    group = jnp.zeros(ids.shape, jnp.int32)
    for track in range(tracks):
        group = jnp.where(ids[...] == track, owner[track], group)
    time = scalars[ME] * tok_rows + lax.broadcasted_iota(jnp.int32, ids.shape, 1)
    code[...] = group * span + time


def early_kernel(rim, frames, taps, late, early, own):
    part = late.shape[0]
    rows = convolved(rim[...], frames[:part], taps[...])
    early[...] = rows
    own[:part] = rows
    own[part:] = late[...]


def assemble_kernel(scalars, *refs):
    pieces, weight = refs[:4], refs[4]
    side, grp = scalars[SIDE], scalars[GRP]
    half = pieces[0].shape[2]
    for n, piece in enumerate(pieces):
        column = side if n < 2 else 1 - side
        feature = grp if n % 2 == 0 else 1 - grp
        turn = scalars[TURN if n < 2 else TURN_PAIRED]
        for j in range(3):
            start = lax.rem(j + 3 - turn, 3) * HD + column * (HD // 2)
            rows = pl.ds(pl.multiple_of(start, HD // 2), HD // 2)
            weight[rows, pl.ds(pl.multiple_of(feature * half, half), half)] = piece[j]


def body_by_head(frames, conv_weight, qkv_weight, track_ids, track_owner):
    tok_rows, features = frames.shape
    grp = lax.axis_index("grp")
    far, near, quad = (lax.axis_index(name) for name in FOUR)
    me = far * FAR + near * NEAR + quad
    devices = lax.axis_size(FOUR)
    head = far * 4 + quad
    part = tok_rows // 2

    half = features // 2
    turn = lax.rem(2 * head + near, 3)
    turn_paired = lax.rem(2 * head + 1 - near, 3)
    scalars = jnp.stack([me, near, grp, turn, turn_paired]).astype(jnp.int32)

    late, rim_rows, *blocks, code = call(
        first_kernel,
        [bf16(part, features), bf16(RIM, features)]
        + [bf16(HD // 2, half)] * 3
        + [jax.ShapeDtypeStruct((1, tok_rows), jnp.int32)],
        [scalars, track_owner, track_ids[None, :], frames, qkv_weight.T, conv_weight],
        "first",
        smem=2,
        limit=10,
    )

    def home(block):
        of_head, side = block % devices // 2, block % 2
        return of_head // 4 * FAR + side * NEAR + of_head % 4

    mine = jnp.stack(
        [
            lax.ppermute(block, FOUR, [(d, home(3 * d + j)) for d in range(devices)])
            for j, block in enumerate(blocks)
        ]
    )
    mine_too = swap_grp(mine)
    paired = swap_seq(mine, NEAR)
    paired_too = swap_grp(paired)
    head_weight = call(
        assemble_kernel,
        bf16(3 * HD, features),
        [scalars, mine, mine_too, paired, paired_too],
        "assemble",
        smem=1,
    )

    rim_rows = lax.ppermute(rim_rows, FOUR, [(i, i + 1) for i in range(devices - 1)])
    early, own = call(
        early_kernel,
        [bf16(part, features), bf16(tok_rows, features)],
        [rim_rows, frames, conv_weight, late],
        "early",
    )
    beside = swap_seq(own, Y)
    far_late = after(swap_seq(late, FAR), mine_too)
    far_late_beside = swap_seq(far_late, Y)
    far_early = swap_seq(after(early, far_late), FAR)

    seen = [0]
    codes = after(code, far_late)
    for bit in (Y, CORE, NEAR, FAR):
        seen += [hop ^ bit for hop in seen]
        codes = jnp.concatenate([codes, swap_seq(codes, bit)], axis=0)
    far_early_beside = swap_seq(after(far_early, paired_too, codes), Y)

    parts = []

    def project(rows, *others):
        rows = jnp.concatenate(rows, axis=0)
        rows = jnp.concatenate([rows, swap_seq(rows, CORE)], axis=0)
        done = lax.dot_general(
            after(rows, *others) if others else rows,
            head_weight,
            (((1,), (1,)), ((), ())),
            preferred_element_type=jnp.float32,
        ).astype(jnp.bfloat16)
        parts.append((done[:, :HD], done[:, HD:], swap_seq(done[:, HD:], NEAR)))
        return done

    done = project([own, beside])
    project([far_late, far_late_beside], done)
    project([far_early, after(far_early_beside, done)])
    query = jnp.concatenate([p[0] for p in parts], axis=0)
    keyed = jnp.concatenate([p[1] for p in parts] + [p[2] for p in parts], axis=0)

    order = [(hop, 0, tok_rows) for hop in QUADS]
    order += [(hop | FAR, part, part) for hop in QUADS]
    order += [(hop | FAR, 0, part) for hop in QUADS]

    def codes_at(bit):
        return jnp.concatenate(
            [codes[seen.index(hop ^ bit), start : start + count] for hop, start, count in order]
        )

    asking = codes_at(0)
    keys = jnp.concatenate([asking, codes_at(NEAR)])
    span = devices * tok_rows
    least = asking // span * span
    scores = lax.dot_general(
        query, keyed[:, :HD], (((1,), (1,)), ((), ())), preferred_element_type=jnp.float32
    ) * (1.0 / HD**0.5)
    allowed = (keys[None, :] <= asking[:, None]) & (keys[None, :] >= least[:, None])
    scores = jnp.where(allowed, scores, jnp.float32(-1e30))
    expd = jnp.exp(scores - jnp.max(scores, axis=-1, keepdims=True))
    weights = (expd / jnp.sum(expd, axis=-1, keepdims=True)).astype(jnp.bfloat16)
    mixed = jnp.dot(weights, keyed[:, HD:], preferred_element_type=jnp.float32)
    mixed = mixed.astype(jnp.bfloat16)

    sent = jnp.zeros((devices // 2, tok_rows, HD), jnp.bfloat16)
    at = 0
    for hop, start, count in order:
        rows = mixed[at : at + count]
        there = head ^ (hop // FAR * 4 + hop % 4)
        sent = lax.dynamic_update_slice(sent, rows[None], (there, start, 0))
        at += count
    returned = lax.all_to_all(sent, ("far", "quad"), split_axis=0, concat_axis=0, tiled=True)
    return returned.transpose(1, 0, 2).reshape(tok_rows, devices // 2 * HD)


def solution(mesh):
    grp, seq = mesh.devices.shape
    out_by_owner = P(("grp", "seq"), None)
    by_owner = jax.shard_map(
        body_by_owner,
        mesh=mesh,
        in_specs=(P(("grp", "seq"), None), P(), P(None, "seq"), P(("grp", "seq")), P("grp")),
        out_specs=out_by_owner,
        check_vma=False,
    )
    fits = (grp, seq) == (2, 16)
    if fits:
        split = Mesh(mesh.devices.reshape(grp, 2, 2, 4), ("grp",) + FOUR)
        rows = P(("grp",) + FOUR)
        by_head = jax.shard_map(
            body_by_head,
            mesh=split,
            in_specs=(rows, P(), P(None, FOUR), rows, P("grp")),
            out_specs=rows,
            check_vma=False,
        )

    def run(frames, conv_weight, qkv_weight, track_ids, track_owner):
        heads = qkv_weight.shape[1] // (3 * HD)
        plan = by_head if fits and heads == 8 else by_owner
        return plan(frames, conv_weight, qkv_weight, track_ids, track_owner)

    return run
```

```python
import jax
import jax.numpy as jnp
from jax import lax
from jax.experimental import pallas as pl
from jax.experimental.pallas import tpu as pltpu
from jax.sharding import Mesh
from jax.sharding import PartitionSpec as P

HD = 128
KW = 4


def from_behind(value, axis, by):
    size = lax.axis_size(axis)
    pairs = [(i, i + by) for i in range(size) if 0 <= i + by < size]
    return lax.ppermute(value, axis, pairs)


def track_groups(track_ids, track_owner):
    track_total = track_owner.shape[0]
    return jnp.sum(
        jnp.where(
            track_ids[:, None] == jnp.arange(track_total, dtype=jnp.int32)[None, :],
            track_owner[None, :],
            0,
        ),
        axis=1,
    )


def convolve(frames, conv_weight, rim_rows):
    tok_rows = frames.shape[0]
    extended = jnp.concatenate([rim_rows, frames], axis=0).astype(jnp.float32)
    conv_sum = frames.astype(jnp.float32)
    for tap in range(KW):
        conv_sum = (
            conv_sum
            + conv_weight[tap].astype(jnp.float32)[None, :]
            * extended[KW - 1 - tap : KW - 1 - tap + tok_rows]
        )
    return conv_sum.astype(jnp.bfloat16)


def attend_slots(packed, positions):
    slot_count = packed.shape[0]
    inner = packed.shape[1] // 3
    head_count = inner // HD
    query = packed[:, :inner].reshape(slot_count, head_count, HD)
    keys_all = packed[:, inner : 2 * inner].reshape(slot_count, head_count, HD)
    values_all = packed[:, 2 * inner :].reshape(slot_count, head_count, HD)
    slot_ids = jnp.arange(slot_count, dtype=jnp.int32)
    score_scale = 1.0 / HD**0.5
    scores = (
        jnp.einsum("qhd,khd->hqk", query, keys_all, preferred_element_type=jnp.float32)
        * score_scale
    )
    allowed = (positions[None, :] >= 0) & (positions[None, :] <= positions[:, None]) | (
        slot_ids[:, None] == slot_ids[None, :]
    )
    scores = jnp.where(allowed[None], scores, jnp.float32(-1e30))
    top_score = jnp.max(scores, axis=-1, keepdims=True)
    expd = jnp.exp(scores - top_score)
    weights = (expd / jnp.sum(expd, axis=-1, keepdims=True)).astype(jnp.bfloat16)
    mixed = jnp.einsum("hqk,khd->qhd", weights, values_all, preferred_element_type=jnp.float32)
    return mixed.astype(jnp.bfloat16).reshape(slot_count, inner)


def body_by_owner(frames, conv_weight, qkv_weight, track_ids, track_owner):
    tok_rows = frames.shape[0]
    peer_count = lax.axis_size("seq")
    capacity = 2 * tok_rows // peer_count
    slot_total = capacity * peer_count
    my_index = lax.axis_index("seq")
    rim_rows = from_behind(frames[tok_rows - (KW - 1) :], "seq", 1)
    hidden = convolve(frames, conv_weight, rim_rows)
    group = track_groups(track_ids, track_owner)
    owner_hits = (group[:, None] == jnp.arange(peer_count, dtype=jnp.int32)[None, :]).astype(
        jnp.int32
    )
    running = jnp.cumsum(owner_hits, axis=0) - 1
    rank_rows = jnp.sum(jnp.where(owner_hits > 0, running, 0), axis=1)
    slot_of_row = group * capacity + rank_rows
    row_ids = jnp.arange(tok_rows, dtype=jnp.int32)
    source_row = jnp.full((slot_total,), tok_rows, jnp.int32).at[slot_of_row].set(row_ids)
    positions = my_index * tok_rows + row_ids
    send_times = jnp.full((slot_total,), -1, jnp.int32).at[slot_of_row].set(positions)
    projected = jnp.dot(
        hidden,
        lax.all_gather(qkv_weight, "seq", axis=1, tiled=True),
        preferred_element_type=jnp.float32,
    ).astype(jnp.bfloat16)
    padded_rows = jnp.concatenate(
        [projected, jnp.zeros((1, projected.shape[1]), jnp.bfloat16)], axis=0
    )
    outgoing = padded_rows[source_row]
    received, got_times = (
        lax.all_to_all(outgoing, "seq", split_axis=0, concat_axis=0, tiled=True),
        lax.all_to_all(send_times, "seq", split_axis=0, concat_axis=0, tiled=True),
    )
    mixed = attend_slots(received, got_times)
    returned = lax.all_to_all(mixed, "seq", split_axis=0, concat_axis=0, tiled=True)
    return returned[slot_of_row]


FOUR = ("far", "near", "quad")
CORE, Y, NEAR, FAR = 1, 2, 4, 8
RIM = 16


def swap_seq(value, bit):
    count = lax.axis_size(FOUR)
    return lax.ppermute(value, FOUR, [(d, d ^ bit) for d in range(count)])


def swap_grp(value):
    return lax.ppermute(value, "grp", [(0, 1), (1, 0)])


def call(kernel, out_shape, operands, name, smem=0, flops=0, limit=6):
    whole = pl.BlockSpec()
    scalars = pl.BlockSpec(memory_space=pltpu.SMEM)
    many = isinstance(out_shape, (list, tuple))
    shapes = list(out_shape) if many else [out_shape]
    return pl.pallas_call(
        kernel,
        out_shape=out_shape,
        in_specs=[scalars] * smem + [whole] * (len(operands) - smem),
        out_specs=[whole] * len(shapes) if many else whole,
        cost_estimate=pl.CostEstimate(
            flops=flops,
            bytes_accessed=sum(2 * o.size for o in list(operands) + shapes),
            transcendentals=0,
        ),
        compiler_params=pltpu.CompilerParams(vmem_limit_bytes=limit * 2**20),
        name=name,
    )(*operands)


def bf16(*shape):
    return jax.ShapeDtypeStruct(shape, jnp.bfloat16)


def after_kernel(*refs):
    del refs


def after(value, *others):
    anywhere = pl.BlockSpec(memory_space=pl.ANY)
    return pl.pallas_call(
        after_kernel,
        out_shape=jax.ShapeDtypeStruct(value.shape, value.dtype),
        in_specs=[anywhere] * (1 + len(others)),
        out_specs=anywhere,
        input_output_aliases={0: 0},
        compiler_params=pltpu.CompilerParams(vmem_limit_bytes=2**20),
        name="after",
    )(value, *others)


def convolved(before, rows, taps):
    count = rows.shape[0]
    rows = rows.astype(jnp.float32)
    extended = jnp.concatenate([before.astype(jnp.float32), rows], axis=0)
    taps = taps.astype(jnp.float32)
    total = rows
    for tap in range(KW):
        total = total + taps[tap : tap + 1] * extended[RIM - tap : RIM - tap + count]
    return total.astype(jnp.bfloat16)


ME, SIDE, GRP, TURN, TURN_PAIRED = range(5)


def first_kernel(scalars, owner, ids, frames, weight, taps, late, rim, block0, block1, block2, code):
    tok_rows = frames.shape[0]
    part = late.shape[0]
    half = block0.shape[1]
    tracks = owner.shape[0]
    span = 16 * tok_rows
    late[...] = convolved(frames[part - RIM : part], frames[part:], taps[...])
    rim[...] = frames[tok_rows - RIM :]
    lanes = pl.ds(pl.multiple_of(scalars[GRP] * half, half), half)
    for j, block in enumerate((block0, block1, block2)):
        block[...] = weight[j * (HD // 2) : (j + 1) * (HD // 2), lanes]
    group = jnp.zeros(ids.shape, jnp.int32)
    for track in range(tracks):
        group = jnp.where(ids[...] == track, owner[track], group)
    time = scalars[ME] * tok_rows + lax.broadcasted_iota(jnp.int32, ids.shape, 1)
    code[...] = group * span + time


def early_kernel(rim, frames, taps, late, early, own):
    part = late.shape[0]
    rows = convolved(rim[...], frames[:part], taps[...])
    early[...] = rows
    own[:part] = rows
    own[part:] = late[...]


def assemble_kernel(scalars, mine, mine_too, paired, diagonal0, diagonal1, weight):
    side, grp = scalars[SIDE], scalars[GRP]
    half, cut = mine.shape[2], diagonal0.shape[2]
    for piece, column, start, turn in (
        (mine, side, grp * half, TURN),
        (mine_too, side, (1 - grp) * half, TURN),
        (paired, 1 - side, grp * half, TURN_PAIRED),
        (diagonal0, 1 - side, (1 - grp) * half, TURN_PAIRED),
        (diagonal1, 1 - side, (1 - grp) * half + cut, TURN_PAIRED),
    ):
        lanes = pl.ds(pl.multiple_of(start, cut), piece.shape[2])
        for j in range(3):
            at = lax.rem(j + 3 - scalars[turn], 3) * HD + column * (HD // 2)
            weight[pl.ds(pl.multiple_of(at, HD // 2), HD // 2), lanes] = piece[j]


def body_by_head(frames, conv_weight, qkv_weight, track_ids, track_owner):
    tok_rows, features = frames.shape
    grp = lax.axis_index("grp")
    far, near, quad = (lax.axis_index(name) for name in FOUR)
    me = far * FAR + near * NEAR + quad
    devices = lax.axis_size(FOUR)
    head = far * 4 + quad
    part = tok_rows // 2

    half = features // 2
    turn = lax.rem(2 * head + near, 3)
    turn_paired = lax.rem(2 * head + 1 - near, 3)
    scalars = jnp.stack([me, near, grp, turn, turn_paired]).astype(jnp.int32)

    late, rim_rows, *blocks, code = call(
        first_kernel,
        [bf16(part, features), bf16(RIM, features)]
        + [bf16(HD // 2, half)] * 3
        + [jax.ShapeDtypeStruct((1, tok_rows), jnp.int32)],
        [scalars, track_owner, track_ids[None, :], frames, qkv_weight.T, conv_weight],
        "first",
        smem=2,
        limit=10,
    )

    def home(block):
        of_head, side = block % devices // 2, block % 2
        return of_head // 4 * FAR + side * NEAR + of_head % 4

    mine = jnp.stack(
        [
            lax.ppermute(block, FOUR, [(d, home(3 * d + j)) for d in range(devices)])
            for j, block in enumerate(blocks)
        ]
    )
    far_late = swap_seq(late, FAR)
    codes = jnp.concatenate([code, swap_seq(code, NEAR)], axis=0)
    mine = after(mine, far_late, codes)
    mine_too = swap_grp(mine)
    paired = swap_seq(mine, NEAR)
    cut = half // 2
    diagonal = [swap_grp(paired[:, :, :cut]), swap_seq(mine_too[:, :, cut:], NEAR)]
    head_weight = call(
        assemble_kernel,
        bf16(3 * HD, features),
        [scalars, mine, mine_too, paired] + diagonal,
        "assemble",
        smem=1,
    )

    rim_rows = lax.ppermute(rim_rows, FOUR, [(i, i + 1) for i in range(devices - 1)])
    early, own = call(
        early_kernel,
        [bf16(part, features), bf16(tok_rows, features)],
        [rim_rows, frames, conv_weight, late],
        "early",
    )
    own = after(own, mine)
    beside = swap_seq(own, Y)
    far_late_beside = after(swap_seq(far_late, Y), *diagonal)
    far_early = swap_seq(after(early, far_late), FAR)
    far_early = after(far_early, *diagonal)
    far_early_beside = swap_seq(far_early, Y)

    parts = []

    def project(*rows):
        rows = jnp.concatenate(rows + tuple(swap_seq(r, CORE) for r in rows), axis=0)
        done = lax.dot_general(
            rows, head_weight, (((1,), (1,)), ((), ())), preferred_element_type=jnp.float32
        ).astype(jnp.bfloat16)
        parts.append((done[:, :HD], done[:, HD:], swap_seq(done[:, HD:], NEAR)))
        return done

    done = project(own, beside, far_late, far_late_beside)
    done = project(far_early, after(far_early_beside, done))

    seen = [0, NEAR]
    codes = after(codes, done)
    for bit in (FAR, CORE, Y):
        seen += [hop ^ bit for hop in seen]
        codes = jnp.concatenate([codes, swap_seq(codes, bit)], axis=0)

    query = jnp.concatenate([p[0] for p in parts], axis=0)
    keyed = jnp.concatenate([p[1] for p in parts] + [p[2] for p in parts], axis=0)

    order = []
    for core in (0, CORE):
        order += [(core, 0, tok_rows), (core | Y, 0, tok_rows)]
        order += [(core | FAR, part, part), (core | FAR | Y, part, part)]
    for core in (0, CORE):
        order += [(core | FAR, 0, part), (core | FAR | Y, 0, part)]

    def codes_at(bit):
        return jnp.concatenate(
            [codes[seen.index(hop ^ bit), start : start + count] for hop, start, count in order]
        )

    asking = codes_at(0)
    keys = jnp.concatenate([asking, codes_at(NEAR)])
    span = devices * tok_rows
    least = asking // span * span
    scores = lax.dot_general(
        query, keyed[:, :HD], (((1,), (1,)), ((), ())), preferred_element_type=jnp.float32
    ) * (1.0 / HD**0.5)
    allowed = (keys[None, :] <= asking[:, None]) & (keys[None, :] >= least[:, None])
    scores = jnp.where(allowed, scores, jnp.float32(-1e30))
    expd = jnp.exp(scores - jnp.max(scores, axis=-1, keepdims=True))
    weights = (expd / jnp.sum(expd, axis=-1, keepdims=True)).astype(jnp.bfloat16)
    mixed = jnp.dot(weights, keyed[:, HD:], preferred_element_type=jnp.float32)
    mixed = mixed.astype(jnp.bfloat16)

    sent = jnp.zeros((devices // 2, tok_rows, HD), jnp.bfloat16)
    at = 0
    for hop, start, count in order:
        rows = mixed[at : at + count]
        there = head ^ (hop // FAR * 4 + hop % 4)
        sent = lax.dynamic_update_slice(sent, rows[None], (there, start, 0))
        at += count
    returned = lax.all_to_all(sent, ("far", "quad"), split_axis=0, concat_axis=0, tiled=True)
    return returned.transpose(1, 0, 2).reshape(tok_rows, devices // 2 * HD)


def solution(mesh):
    grp, seq = mesh.devices.shape
    out_by_owner = P(("grp", "seq"), None)
    by_owner = jax.shard_map(
        body_by_owner,
        mesh=mesh,
        in_specs=(P(("grp", "seq"), None), P(), P(None, "seq"), P(("grp", "seq")), P("grp")),
        out_specs=out_by_owner,
        check_vma=False,
    )
    fits = (grp, seq) == (2, 16)
    if fits:
        split = Mesh(mesh.devices.reshape(grp, 2, 2, 4), ("grp",) + FOUR)
        rows = P(("grp",) + FOUR)
        by_head = jax.shard_map(
            body_by_head,
            mesh=split,
            in_specs=(rows, P(), P(None, FOUR), rows, P("grp")),
            out_specs=rows,
            check_vma=False,
        )

    def run(frames, conv_weight, qkv_weight, track_ids, track_owner):
        heads = qkv_weight.shape[1] // (3 * HD)
        plan = by_head if fits and heads == 8 else by_owner
        return plan(frames, conv_weight, qkv_weight, track_ids, track_owner)

    return run
```

```python
import jax
import jax.numpy as jnp
from jax import lax
from jax.experimental import pallas as pl
from jax.experimental.pallas import tpu as pltpu
from jax.sharding import Mesh
from jax.sharding import PartitionSpec as P

HD = 128
KW = 4


def from_behind(value, axis, by):
    size = lax.axis_size(axis)
    pairs = [(i, i + by) for i in range(size) if 0 <= i + by < size]
    return lax.ppermute(value, axis, pairs)


def track_groups(track_ids, track_owner):
    track_total = track_owner.shape[0]
    return jnp.sum(
        jnp.where(
            track_ids[:, None] == jnp.arange(track_total, dtype=jnp.int32)[None, :],
            track_owner[None, :],
            0,
        ),
        axis=1,
    )


def convolve(frames, conv_weight, rim_rows):
    tok_rows = frames.shape[0]
    extended = jnp.concatenate([rim_rows, frames], axis=0).astype(jnp.float32)
    conv_sum = frames.astype(jnp.float32)
    for tap in range(KW):
        conv_sum = (
            conv_sum
            + conv_weight[tap].astype(jnp.float32)[None, :]
            * extended[KW - 1 - tap : KW - 1 - tap + tok_rows]
        )
    return conv_sum.astype(jnp.bfloat16)


def attend_slots(packed, positions):
    slot_count = packed.shape[0]
    inner = packed.shape[1] // 3
    head_count = inner // HD
    query = packed[:, :inner].reshape(slot_count, head_count, HD)
    keys_all = packed[:, inner : 2 * inner].reshape(slot_count, head_count, HD)
    values_all = packed[:, 2 * inner :].reshape(slot_count, head_count, HD)
    slot_ids = jnp.arange(slot_count, dtype=jnp.int32)
    score_scale = 1.0 / HD**0.5
    scores = (
        jnp.einsum("qhd,khd->hqk", query, keys_all, preferred_element_type=jnp.float32)
        * score_scale
    )
    allowed = (positions[None, :] >= 0) & (positions[None, :] <= positions[:, None]) | (
        slot_ids[:, None] == slot_ids[None, :]
    )
    scores = jnp.where(allowed[None], scores, jnp.float32(-1e30))
    top_score = jnp.max(scores, axis=-1, keepdims=True)
    expd = jnp.exp(scores - top_score)
    weights = (expd / jnp.sum(expd, axis=-1, keepdims=True)).astype(jnp.bfloat16)
    mixed = jnp.einsum("hqk,khd->qhd", weights, values_all, preferred_element_type=jnp.float32)
    return mixed.astype(jnp.bfloat16).reshape(slot_count, inner)


def body_by_owner(frames, conv_weight, qkv_weight, track_ids, track_owner):
    tok_rows = frames.shape[0]
    peer_count = lax.axis_size("seq")
    capacity = 2 * tok_rows // peer_count
    slot_total = capacity * peer_count
    my_index = lax.axis_index("seq")
    rim_rows = from_behind(frames[tok_rows - (KW - 1) :], "seq", 1)
    hidden = convolve(frames, conv_weight, rim_rows)
    group = track_groups(track_ids, track_owner)
    owner_hits = (group[:, None] == jnp.arange(peer_count, dtype=jnp.int32)[None, :]).astype(
        jnp.int32
    )
    running = jnp.cumsum(owner_hits, axis=0) - 1
    rank_rows = jnp.sum(jnp.where(owner_hits > 0, running, 0), axis=1)
    slot_of_row = group * capacity + rank_rows
    row_ids = jnp.arange(tok_rows, dtype=jnp.int32)
    source_row = jnp.full((slot_total,), tok_rows, jnp.int32).at[slot_of_row].set(row_ids)
    positions = my_index * tok_rows + row_ids
    send_times = jnp.full((slot_total,), -1, jnp.int32).at[slot_of_row].set(positions)
    projected = jnp.dot(
        hidden,
        lax.all_gather(qkv_weight, "seq", axis=1, tiled=True),
        preferred_element_type=jnp.float32,
    ).astype(jnp.bfloat16)
    padded_rows = jnp.concatenate(
        [projected, jnp.zeros((1, projected.shape[1]), jnp.bfloat16)], axis=0
    )
    outgoing = padded_rows[source_row]
    received, got_times = (
        lax.all_to_all(outgoing, "seq", split_axis=0, concat_axis=0, tiled=True),
        lax.all_to_all(send_times, "seq", split_axis=0, concat_axis=0, tiled=True),
    )
    mixed = attend_slots(received, got_times)
    returned = lax.all_to_all(mixed, "seq", split_axis=0, concat_axis=0, tiled=True)
    return returned[slot_of_row]


FOUR = ("far", "near", "quad")
CORE, Y, NEAR, FAR = 1, 2, 4, 8
RIM = 16


def swap_seq(value, bit):
    count = lax.axis_size(FOUR)
    return lax.ppermute(value, FOUR, [(d, d ^ bit) for d in range(count)])


def swap_grp(value):
    return lax.ppermute(value, "grp", [(0, 1), (1, 0)])


def call(kernel, out_shape, operands, name, smem=0, flops=0, limit=6):
    whole = pl.BlockSpec()
    scalars = pl.BlockSpec(memory_space=pltpu.SMEM)
    many = isinstance(out_shape, (list, tuple))
    shapes = list(out_shape) if many else [out_shape]
    return pl.pallas_call(
        kernel,
        out_shape=out_shape,
        in_specs=[scalars] * smem + [whole] * (len(operands) - smem),
        out_specs=[whole] * len(shapes) if many else whole,
        cost_estimate=pl.CostEstimate(
            flops=flops,
            bytes_accessed=sum(2 * o.size for o in list(operands) + shapes),
            transcendentals=0,
        ),
        compiler_params=pltpu.CompilerParams(vmem_limit_bytes=limit * 2**20),
        name=name,
    )(*operands)


def bf16(*shape):
    return jax.ShapeDtypeStruct(shape, jnp.bfloat16)


def after_kernel(*refs):
    del refs


def after(value, *others):
    anywhere = pl.BlockSpec(memory_space=pl.ANY)
    return pl.pallas_call(
        after_kernel,
        out_shape=jax.ShapeDtypeStruct(value.shape, value.dtype),
        in_specs=[anywhere] * (1 + len(others)),
        out_specs=anywhere,
        input_output_aliases={0: 0},
        compiler_params=pltpu.CompilerParams(vmem_limit_bytes=2**20),
        name="after",
    )(value, *others)


def convolved(before, rows, taps):
    count = rows.shape[0]
    rows = rows.astype(jnp.float32)
    extended = jnp.concatenate([before.astype(jnp.float32), rows], axis=0)
    taps = taps.astype(jnp.float32)
    total = rows
    for tap in range(KW):
        total = total + taps[tap : tap + 1] * extended[RIM - tap : RIM - tap + count]
    return total.astype(jnp.bfloat16)


ME, SIDE, GRP, TURN, TURN_PAIRED, HEAD, DEVICES = range(7)


def code_kernel(scalars, owner, ids, code):
    group = jnp.zeros(ids.shape, jnp.int32)
    for track in range(owner.shape[0]):
        group = jnp.where(ids[...] == track, owner[track], group)
    time = lax.broadcasted_iota(jnp.int32, ids.shape, 1)
    code[...] = (group * scalars[DEVICES] + scalars[ME]) * ids.shape[1] + time


def first_kernel(
    scalars, frames, weight, taps, late, rim, block0, block1, block2, rows, tap_rows, sems
):
    tok_rows = frames.shape[0]
    part = late.shape[0]
    half = block0.shape[1]
    lanes = pl.ds(pl.multiple_of(scalars[GRP] * half, half), half)
    copies = [
        pltpu.make_async_copy(frames, rows, sems.at[0]),
        pltpu.make_async_copy(taps, tap_rows, sems.at[1]),
    ]
    for j, block in enumerate((block0, block1, block2)):
        source = weight.at[pl.ds(j * (HD // 2), HD // 2), lanes]
        copies.append(pltpu.make_async_copy(source, block, sems.at[2 + j]))
    for copy in copies:
        copy.start()
    copies[0].wait()
    copies[1].wait()
    late[...] = convolved(rows[part - RIM : part], rows[part:], tap_rows[...])
    rim[...] = rows[tok_rows - RIM :]
    for copy in copies[2:]:
        copy.wait()


def first(scalars, frames, weight, taps):
    tok_rows, features = frames.shape
    half = features // 2
    whole, anywhere = pl.BlockSpec(), pl.BlockSpec(memory_space=pl.ANY)
    return pl.pallas_call(
        first_kernel,
        out_shape=[bf16(tok_rows // 2, features), bf16(RIM, features)]
        + [bf16(HD // 2, half)] * 3,
        in_specs=[pl.BlockSpec(memory_space=pltpu.SMEM)] + [anywhere] * 3,
        out_specs=[whole] * 5,
        scratch_shapes=[
            pltpu.VMEM(frames.shape, frames.dtype),
            pltpu.VMEM(taps.shape, taps.dtype),
            pltpu.SemaphoreType.DMA((5,)),
        ],
        compiler_params=pltpu.CompilerParams(vmem_limit_bytes=48 * 2**20),
        name="first",
    )(scalars, frames, weight, taps)


def early_kernel(rim, frames, taps, late, early, own):
    part = late.shape[0]
    rows = convolved(rim[...], frames[:part], taps[...])
    early[...] = rows
    own[:part] = rows
    own[part:] = late[...]


def assemble_kernel(scalars, mine, mine_too, paired, diagonal0, diagonal1, weight):
    side, grp = scalars[SIDE], scalars[GRP]
    half, cut = mine.shape[2], diagonal0.shape[2]
    for piece, column, start, turn in (
        (mine, side, grp * half, TURN),
        (mine_too, side, (1 - grp) * half, TURN),
        (paired, 1 - side, grp * half, TURN_PAIRED),
        (diagonal0, 1 - side, (1 - grp) * half, TURN_PAIRED),
        (diagonal1, 1 - side, (1 - grp) * half + cut, TURN_PAIRED),
    ):
        lanes = pl.ds(pl.multiple_of(start, cut), piece.shape[2])
        for j in range(3):
            at = lax.rem(j + 3 - scalars[turn], 3) * HD + column * (HD // 2)
            weight[pl.ds(pl.multiple_of(at, HD // 2), HD // 2), lanes] = piece[j]


def place_kernel(scalars, block0, block1, block2, block3, theirs, out):
    rows = out.shape[0]
    for n, block in enumerate((block0, block1, block2, block3)):
        chip = (0, Y, FAR, FAR | Y)[n]
        for core, value in ((0, block[...]), (CORE, theirs[n * rows : (n + 1) * rows])):
            head = scalars[HEAD] ^ (chip // FAR * 4 + chip % 4 + core)
            out[:, pl.ds(pl.multiple_of(head * HD, HD), HD)] = value


def body_by_head(frames, conv_weight, qkv_weight, track_ids, track_owner):
    tok_rows, features = frames.shape
    grp = lax.axis_index("grp")
    far, near, quad = (lax.axis_index(name) for name in FOUR)
    me = far * FAR + near * NEAR + quad
    devices = lax.axis_size(FOUR)
    head = far * 4 + quad
    part = tok_rows // 2

    half = features // 2
    turn = lax.rem(2 * head + near, 3)
    turn_paired = lax.rem(2 * head + 1 - near, 3)
    scalars = jnp.stack([me, near, grp, turn, turn_paired, head, devices])
    scalars = scalars.astype(jnp.int32)

    codes = call(
        code_kernel,
        jax.ShapeDtypeStruct((1, tok_rows), jnp.int32),
        [scalars, track_owner, track_ids[None, :]],
        "code",
        smem=2,
        limit=1,
    )
    seen = [0]

    def with_codes_of(codes, bit):
        seen.extend([hop ^ bit for hop in seen])
        return jnp.concatenate([codes, swap_seq(codes, bit)], axis=0)

    codes = with_codes_of(with_codes_of(codes, FAR), NEAR)
    late, rim_rows, *blocks = first(scalars, frames, qkv_weight.T, conv_weight)
    late = after(late, codes)
    rim_rows = after(rim_rows, codes)

    def home(block):
        of_head, side = block % devices // 2, block % 2
        return of_head // 4 * FAR + side * NEAR + of_head % 4

    mine = jnp.stack(
        [
            lax.ppermute(block, FOUR, [(d, home(3 * d + j)) for d in range(devices)])
            for j, block in enumerate(blocks)
        ]
    )
    far_late = swap_seq(late, FAR)
    mine = after(mine, far_late)
    mine_too = swap_grp(mine)
    paired = swap_seq(mine, NEAR)
    cut = half // 2
    diagonal = [swap_grp(paired[:, :, :cut]), swap_seq(mine_too[:, :, cut:], NEAR)]
    head_weight = call(
        assemble_kernel,
        bf16(3 * HD, features),
        [scalars, mine, mine_too, paired] + diagonal,
        "assemble",
        smem=1,
    )

    rim_rows = lax.ppermute(rim_rows, FOUR, [(i, i + 1) for i in range(devices - 1)])
    early, own = call(
        early_kernel,
        [bf16(part, features), bf16(tok_rows, features)],
        [rim_rows, frames, conv_weight, late],
        "early",
    )
    beside = swap_seq(after(own, mine), Y)
    far_late_beside = swap_seq(far_late, Y)
    far_early = swap_seq(after(early, far_late), FAR)
    far_early_beside = swap_seq(after(far_early, *diagonal), Y)

    parts = []

    def project(*rows):
        rows = jnp.concatenate(rows + tuple(swap_seq(r, CORE) for r in rows), axis=0)
        done = lax.dot_general(
            rows, head_weight, (((1,), (1,)), ((), ())), preferred_element_type=jnp.float32
        ).astype(jnp.bfloat16)
        parts.append((done[:, :HD], done[:, HD:], swap_seq(done[:, HD:], NEAR)))
        return done

    done = project(own, beside, far_late, far_late_beside)
    done = project(far_early, after(far_early_beside, done))

    codes = with_codes_of(with_codes_of(after(codes, done), CORE), Y)

    keyed = jnp.concatenate([p[1] for p in parts] + [p[2] for p in parts], axis=0)

    first_order, second_order = [], []
    for core in (0, CORE):
        first_order += [(core, 0, tok_rows), (core | Y, 0, tok_rows)]
        first_order += [(core | FAR, part, part), (core | FAR | Y, part, part)]
        second_order += [(core | FAR, 0, part), (core | FAR | Y, 0, part)]
    order = first_order + second_order

    def codes_at(order, bit=0):
        return jnp.concatenate(
            [codes[seen.index(hop ^ bit), start : start + count] for hop, start, count in order]
        )

    keys = jnp.concatenate([codes_at(order), codes_at(order, NEAR)])
    queries = jnp.concatenate([p[0] for p in parts], axis=0)
    span = devices * tok_rows

    def attend(hops):
        at, pieces = 0, {}
        for hop, start, count in order:
            pieces[hop, start] = queries[at : at + count]
            at += count
        mine = [(h, s, c) for hop in hops for h, s, c in sorted(order) if h == hop]
        query = jnp.concatenate([pieces[h, s] for h, s, _ in mine], axis=0)
        asking = codes_at(mine)
        least = asking // span * span
        scores = lax.dot_general(
            query, keyed[:, :HD], (((1,), (1,)), ((), ())), preferred_element_type=jnp.float32
        ) * (1.0 / HD**0.5)
        allowed = (keys[None, :] <= asking[:, None]) & (keys[None, :] >= least[:, None])
        scores = jnp.where(allowed, scores, jnp.float32(-1e30))
        expd = jnp.exp(scores - jnp.max(scores, axis=-1, keepdims=True))
        weights = (expd / jnp.sum(expd, axis=-1, keepdims=True)).astype(jnp.bfloat16)
        mixed = jnp.dot(weights, keyed[:, HD:], preferred_element_type=jnp.float32)
        return mixed.astype(jnp.bfloat16).reshape(len(hops), tok_rows, HD)

    far_hops = (FAR, FAR | CORE, FAR | Y, FAR | Y | CORE)
    context = attend(far_hops)
    home = {FAR: swap_seq(context[:2], FAR), FAR | Y: swap_seq(context[2:], FAR | Y)}
    context = attend((0, CORE, Y, Y | CORE))
    home[Y] = swap_seq(context[2:], Y)
    home[0] = context[:2]
    chips = (0, Y, FAR, FAR | Y)
    theirs = swap_seq(jnp.concatenate([home[chip][1] for chip in chips], axis=0), CORE)
    return call(
        place_kernel,
        bf16(tok_rows, devices // 2 * HD),
        [scalars] + [home[chip][0] for chip in chips] + [theirs],
        "place",
        smem=1,
    )


def solution(mesh):
    grp, seq = mesh.devices.shape
    out_by_owner = P(("grp", "seq"), None)
    by_owner = jax.shard_map(
        body_by_owner,
        mesh=mesh,
        in_specs=(P(("grp", "seq"), None), P(), P(None, "seq"), P(("grp", "seq")), P("grp")),
        out_specs=out_by_owner,
        check_vma=False,
    )
    fits = (grp, seq) == (2, 16)
    if fits:
        split = Mesh(mesh.devices.reshape(grp, 2, 2, 4), ("grp",) + FOUR)
        rows = P(("grp",) + FOUR)
        by_head = jax.shard_map(
            body_by_head,
            mesh=split,
            in_specs=(rows, P(), P(None, FOUR), rows, P("grp")),
            out_specs=rows,
            check_vma=False,
        )

    def run(frames, conv_weight, qkv_weight, track_ids, track_owner):
        heads = qkv_weight.shape[1] // (3 * HD)
        plan = by_head if fits and heads == 8 else by_owner
        return plan(frames, conv_weight, qkv_weight, track_ids, track_owner)

    return run
```

```python
import jax
import jax.numpy as jnp
from jax import lax
from jax.experimental import pallas as pl
from jax.experimental.pallas import tpu as pltpu
from jax.sharding import Mesh
from jax.sharding import PartitionSpec as P

HD = 128
KW = 4


def from_behind(value, axis, by):
    size = lax.axis_size(axis)
    pairs = [(i, i + by) for i in range(size) if 0 <= i + by < size]
    return lax.ppermute(value, axis, pairs)


def track_groups(track_ids, track_owner):
    track_total = track_owner.shape[0]
    return jnp.sum(
        jnp.where(
            track_ids[:, None] == jnp.arange(track_total, dtype=jnp.int32)[None, :],
            track_owner[None, :],
            0,
        ),
        axis=1,
    )


def convolve(frames, conv_weight, rim_rows):
    tok_rows = frames.shape[0]
    extended = jnp.concatenate([rim_rows, frames], axis=0).astype(jnp.float32)
    conv_sum = frames.astype(jnp.float32)
    for tap in range(KW):
        conv_sum = (
            conv_sum
            + conv_weight[tap].astype(jnp.float32)[None, :]
            * extended[KW - 1 - tap : KW - 1 - tap + tok_rows]
        )
    return conv_sum.astype(jnp.bfloat16)


def attend_slots(packed, positions):
    slot_count = packed.shape[0]
    inner = packed.shape[1] // 3
    head_count = inner // HD
    query = packed[:, :inner].reshape(slot_count, head_count, HD)
    keys_all = packed[:, inner : 2 * inner].reshape(slot_count, head_count, HD)
    values_all = packed[:, 2 * inner :].reshape(slot_count, head_count, HD)
    slot_ids = jnp.arange(slot_count, dtype=jnp.int32)
    score_scale = 1.0 / HD**0.5
    scores = (
        jnp.einsum("qhd,khd->hqk", query, keys_all, preferred_element_type=jnp.float32)
        * score_scale
    )
    allowed = (positions[None, :] >= 0) & (positions[None, :] <= positions[:, None]) | (
        slot_ids[:, None] == slot_ids[None, :]
    )
    scores = jnp.where(allowed[None], scores, jnp.float32(-1e30))
    top_score = jnp.max(scores, axis=-1, keepdims=True)
    expd = jnp.exp(scores - top_score)
    weights = (expd / jnp.sum(expd, axis=-1, keepdims=True)).astype(jnp.bfloat16)
    mixed = jnp.einsum("hqk,khd->qhd", weights, values_all, preferred_element_type=jnp.float32)
    return mixed.astype(jnp.bfloat16).reshape(slot_count, inner)


def body_by_owner(frames, conv_weight, qkv_weight, track_ids, track_owner):
    tok_rows = frames.shape[0]
    peer_count = lax.axis_size("seq")
    capacity = 2 * tok_rows // peer_count
    slot_total = capacity * peer_count
    my_index = lax.axis_index("seq")
    rim_rows = from_behind(frames[tok_rows - (KW - 1) :], "seq", 1)
    hidden = convolve(frames, conv_weight, rim_rows)
    group = track_groups(track_ids, track_owner)
    owner_hits = (group[:, None] == jnp.arange(peer_count, dtype=jnp.int32)[None, :]).astype(
        jnp.int32
    )
    running = jnp.cumsum(owner_hits, axis=0) - 1
    rank_rows = jnp.sum(jnp.where(owner_hits > 0, running, 0), axis=1)
    slot_of_row = group * capacity + rank_rows
    row_ids = jnp.arange(tok_rows, dtype=jnp.int32)
    source_row = jnp.full((slot_total,), tok_rows, jnp.int32).at[slot_of_row].set(row_ids)
    positions = my_index * tok_rows + row_ids
    send_times = jnp.full((slot_total,), -1, jnp.int32).at[slot_of_row].set(positions)
    projected = jnp.dot(
        hidden,
        lax.all_gather(qkv_weight, "seq", axis=1, tiled=True),
        preferred_element_type=jnp.float32,
    ).astype(jnp.bfloat16)
    padded_rows = jnp.concatenate(
        [projected, jnp.zeros((1, projected.shape[1]), jnp.bfloat16)], axis=0
    )
    outgoing = padded_rows[source_row]
    received, got_times = (
        lax.all_to_all(outgoing, "seq", split_axis=0, concat_axis=0, tiled=True),
        lax.all_to_all(send_times, "seq", split_axis=0, concat_axis=0, tiled=True),
    )
    mixed = attend_slots(received, got_times)
    returned = lax.all_to_all(mixed, "seq", split_axis=0, concat_axis=0, tiled=True)
    return returned[slot_of_row]


BOTH = ("chip", "core")
RIM = 16


def swap_core(value):
    return lax.ppermute(value, "core", [(0, 1), (1, 0)])


def call(kernel, out_shape, operands, name, smem=0, flops=0, limit=6):
    whole = pl.BlockSpec()
    scalars = pl.BlockSpec(memory_space=pltpu.SMEM)
    many = isinstance(out_shape, (list, tuple))
    shapes = list(out_shape) if many else [out_shape]
    return pl.pallas_call(
        kernel,
        out_shape=out_shape,
        in_specs=[scalars] * smem + [whole] * (len(operands) - smem),
        out_specs=[whole] * len(shapes) if many else whole,
        cost_estimate=pl.CostEstimate(
            flops=flops,
            bytes_accessed=sum(2 * o.size for o in list(operands) + shapes),
            transcendentals=0,
        ),
        compiler_params=pltpu.CompilerParams(vmem_limit_bytes=limit * 2**20),
        name=name,
    )(*operands)


def bf16(*shape):
    return jax.ShapeDtypeStruct(shape, jnp.bfloat16)


def after_kernel(*refs):
    del refs


def after(value, *others):
    anywhere = pl.BlockSpec(memory_space=pl.ANY)
    return pl.pallas_call(
        after_kernel,
        out_shape=jax.ShapeDtypeStruct(value.shape, value.dtype),
        in_specs=[anywhere] * (1 + len(others)),
        out_specs=anywhere,
        input_output_aliases={0: 0},
        compiler_params=pltpu.CompilerParams(vmem_limit_bytes=2**20),
        name="after",
    )(value, *others)


def convolved(before, rows, taps):
    count = rows.shape[0]
    rows = rows.astype(jnp.float32)
    extended = jnp.concatenate([before.astype(jnp.float32), rows], axis=0)
    taps = taps.astype(jnp.float32)
    total = rows
    for tap in range(KW):
        total = total + taps[tap : tap + 1] * extended[RIM - tap : RIM - tap + count]
    return total.astype(jnp.bfloat16)


ME, GRP, CORE, TURN, TURN_OTHER = range(5)


def first_kernel(
    scalars, owner, ids, frames, weight, taps, late, rim, block0, block1, block2, code,
    rows, tap_rows, my_ids, owners, sems,
):
    tok_rows = frames.shape[0]
    part = late.shape[0]
    half = block0.shape[1]
    lanes = pl.ds(pl.multiple_of(scalars[GRP] * half, half), half)
    copies = [
        pltpu.make_async_copy(frames, rows, sems.at[0]),
        pltpu.make_async_copy(taps, tap_rows, sems.at[1]),
        pltpu.make_async_copy(ids, my_ids, sems.at[2]),
        pltpu.make_async_copy(owner, owners, sems.at[3]),
    ]
    for j, block in enumerate((block0, block1, block2)):
        source = weight.at[pl.ds(j * (HD // 2), HD // 2), lanes]
        copies.append(pltpu.make_async_copy(source, block, sems.at[4 + j]))
    for copy in copies:
        copy.start()
    for copy in copies[:4]:
        copy.wait()
    late[...] = convolved(rows[part - RIM : part], rows[part:], tap_rows[...])
    rim[...] = rows[tok_rows - RIM :]
    group = jnp.zeros(ids.shape, jnp.int32)
    for track in range(owner.shape[1]):
        group = jnp.where(my_ids[...] == track, owners[0, track], group)
    time = lax.broadcasted_iota(jnp.int32, ids.shape, 1)
    code[...] = (group * 16 + scalars[ME]) * tok_rows + time
    for copy in copies[4:]:
        copy.wait()


def first(scalars, owner, ids, frames, weight, taps):
    tok_rows, features = frames.shape
    half = features // 2
    whole, far = pl.BlockSpec(), pl.BlockSpec(memory_space=pltpu.HBM)
    return pl.pallas_call(
        first_kernel,
        out_shape=[bf16(tok_rows // 2, features), bf16(RIM, features)]
        + [bf16(HD // 2, half)] * 3
        + [jax.ShapeDtypeStruct(ids.shape, jnp.int32)],
        in_specs=[pl.BlockSpec(memory_space=pltpu.SMEM)] + [far] * 5,
        out_specs=[whole] * 6,
        scratch_shapes=[
            pltpu.VMEM(frames.shape, frames.dtype),
            pltpu.VMEM(taps.shape, taps.dtype),
            pltpu.VMEM(ids.shape, ids.dtype),
            pltpu.SMEM(owner.shape, owner.dtype),
            pltpu.SemaphoreType.DMA((7,)),
        ],
        compiler_params=pltpu.CompilerParams(vmem_limit_bytes=63 * 2**20),
        name="first",
    )(scalars, owner, ids, frames, weight, taps)


def early_kernel(rim, frames, taps, early):
    early[...] = convolved(rim[...], frames[: early.shape[0]], taps[...])


def assemble_kernel(scalars, mine, mine_too, other, other_too, weight):
    core, grp = scalars[CORE], scalars[GRP]
    half = mine.shape[2]
    for piece, column, feature, turn in (
        (mine, core, grp, TURN),
        (mine_too, core, 1 - grp, TURN),
        (other, 1 - core, grp, TURN_OTHER),
        (other_too, 1 - core, 1 - grp, TURN_OTHER),
    ):
        lanes = pl.ds(pl.multiple_of(feature * half, half), half)
        for j in range(3):
            at = lax.rem(j + 3 - scalars[turn], 3) * HD + column * (HD // 2)
            weight[pl.ds(pl.multiple_of(at, HD // 2), HD // 2), lanes] = piece[j]


def body_by_head(frames, conv_weight, qkv_weight, track_ids, track_owner):
    tok_rows, features = frames.shape
    chips = lax.axis_size("chip")
    devices = 2 * chips
    core = lax.axis_index("core")
    chip = lax.axis_index("chip")
    grp = lax.axis_index("grp")
    me = 2 * chip + core
    part = tok_rows // 2
    span = devices * tok_rows

    ring = list(range(0, chips, 2)) + list(range(chips - 1, 0, -2))
    place = jnp.where(chip & 1 == 0, chip >> 1, chips - 1 - (chip >> 1))
    onward = [(ring[i], ring[(i + 1) % chips]) for i in range(chips)]
    backward = [(t, f) for f, t in onward]

    turn, turn_other = lax.rem(me, 3), lax.rem(me + 1 - 2 * core, 3)
    scalars = jnp.stack([me, grp, core, turn, turn_other]).astype(jnp.int32)
    late, rim_rows, *blocks, codes = first(
        scalars, track_owner[None, :], track_ids[None, :], frames, qkv_weight.T, conv_weight
    )
    rim_rows = lax.ppermute(rim_rows, BOTH, [(i, i + 1) for i in range(devices - 1)])
    early = call(
        early_kernel, bf16(part, features), [rim_rows, frames, conv_weight], "early"
    )

    mine = jnp.stack(
        [
            lax.ppermute(block, BOTH, [(d, (3 * d + j) % devices) for d in range(devices)])
            for j, block in enumerate(blocks)
        ]
    )
    mine_too = lax.ppermute(mine, "grp", [(0, 1), (1, 0)])
    pieces = [mine, mine_too, swap_core(mine), swap_core(mine_too)]
    head_weight = call(
        assemble_kernel, bf16(3 * HD, features), [scalars] + pieces, "assemble", smem=1
    )

    parts = []

    def project(rows):
        rows = jnp.concatenate(rows, axis=0)
        done = lax.dot_general(
            rows, head_weight, (((1,), (1,)), ((), ())), preferred_element_type=jnp.float32
        ).astype(jnp.bfloat16)
        parts.append((done[:, :HD], done[:, HD:], swap_core(done[:, HD:])))
        return done

    def all_codes(codes, bit):
        theirs = lax.ppermute(codes, BOTH, [(d, d ^ bit) for d in range(devices)])
        low = me & bit == 0
        return jnp.concatenate(
            [jnp.where(low, codes, theirs), jnp.where(low, theirs, codes)], axis=0
        )

    lates, earlies = [late], [early]
    for step in range(1, chips):
        ready = []
        if step == 5:
            ready = [project([r for pair in zip(lates[:4], earlies[:4]) for r in pair])]
        if step == 7:
            ready = [project([r for pair in zip(lates[4:6], earlies[4:6]) for r in pair])]
        if 3 <= step < 7:
            ready.append(codes)
            codes = all_codes(after(codes, lates[step - 2]), 1 << (step - 3))
        if ready:
            lates[-1], earlies[-1] = after(late, *ready), after(early, *ready)
            late, early = lates[-1], earlies[-1]
        late = lax.ppermute(late, "chip", backward)
        early = lax.ppermute(early, "chip", onward)
        lates.append(late)
        earlies.append(early)
    project([lates[6], earlies[6], lates[7], earlies[7]])
    query = jnp.concatenate([p[0] for p in parts], axis=0)
    keyed = jnp.concatenate([p[1] for p in parts] + [p[2] for p in parts], axis=0)

    codes = codes.reshape(chips, 2, tok_rows)
    around = jnp.stack([codes[c] for c in ring + ring])
    around = lax.dynamic_slice_in_dim(around, place, chips, 0)
    order = [(s % chips, half) for s in range(chips) for half in (1, 0)]

    def codes_at(which):
        values = lax.dynamic_index_in_dim(around, which, 1, False)
        return jnp.concatenate(
            [
                values[s, part:] if half else values[(chips - s) % chips, :part]
                for s, half in order
            ]
        )

    asking = codes_at(core)
    keys = jnp.concatenate([asking, codes_at(1 - core)])
    least = asking // span * span
    scores = lax.dot_general(
        query, keyed[:, :HD], (((1,), (1,)), ((), ())), preferred_element_type=jnp.float32
    ) * (1.0 / HD**0.5)
    allowed = (keys[None, :] <= asking[:, None]) & (keys[None, :] >= least[:, None])
    scores = jnp.where(allowed, scores, jnp.float32(-1e30))
    expd = jnp.exp(scores - jnp.max(scores, axis=-1, keepdims=True))
    weights = (expd / jnp.sum(expd, axis=-1, keepdims=True)).astype(jnp.bfloat16)
    mixed = jnp.dot(weights, keyed[:, HD:], preferred_element_type=jnp.float32)
    mixed = mixed.astype(jnp.bfloat16).reshape(chips, 2, part, HD)

    blocks = [
        jnp.concatenate([mixed[(chips - s) % chips, 1], mixed[s, 0]], axis=0) for s in range(chips)
    ]
    around = lax.dynamic_slice_in_dim(jnp.stack(blocks + blocks), chips - place, chips, 0)
    sent = jnp.stack([around[ring.index(c)] for c in range(chips)])
    returned = lax.all_to_all(sent, "chip", split_axis=0, concat_axis=0, tiled=True)
    return returned.transpose(1, 0, 2).reshape(tok_rows, chips * HD)


def solution(mesh):
    grp, seq = mesh.devices.shape
    out_by_owner = P(("grp", "seq"), None)
    by_owner = jax.shard_map(
        body_by_owner,
        mesh=mesh,
        in_specs=(P(("grp", "seq"), None), P(), P(None, "seq"), P(("grp", "seq")), P("grp")),
        out_specs=out_by_owner,
        check_vma=False,
    )
    fits = (grp, seq) == (2, 16)
    if fits:
        split = Mesh(mesh.devices.reshape(grp, seq // 2, 2), ("grp",) + BOTH)
        rows = P(("grp",) + BOTH)
        by_head = jax.shard_map(
            body_by_head,
            mesh=split,
            in_specs=(rows, P(), P(None, BOTH), rows, P("grp")),
            out_specs=rows,
            check_vma=False,
        )

    def run(frames, conv_weight, qkv_weight, track_ids, track_owner):
        heads = qkv_weight.shape[1] // (3 * HD)
        plan = by_head if fits and heads == 8 else by_owner
        return plan(frames, conv_weight, qkv_weight, track_ids, track_owner)

    return run
```

```python
import jax
import jax.numpy as jnp
from jax import lax
from jax.experimental import pallas as pl
from jax.experimental.pallas import tpu as pltpu
from jax.sharding import Mesh
from jax.sharding import PartitionSpec as P

HD = 128
KW = 4


def from_behind(value, axis, by):
    size = lax.axis_size(axis)
    pairs = [(i, i + by) for i in range(size) if 0 <= i + by < size]
    return lax.ppermute(value, axis, pairs)


def track_groups(track_ids, track_owner):
    track_total = track_owner.shape[0]
    return jnp.sum(
        jnp.where(
            track_ids[:, None] == jnp.arange(track_total, dtype=jnp.int32)[None, :],
            track_owner[None, :],
            0,
        ),
        axis=1,
    )


def convolve(frames, conv_weight, rim_rows):
    tok_rows = frames.shape[0]
    extended = jnp.concatenate([rim_rows, frames], axis=0).astype(jnp.float32)
    conv_sum = frames.astype(jnp.float32)
    for tap in range(KW):
        conv_sum = (
            conv_sum
            + conv_weight[tap].astype(jnp.float32)[None, :]
            * extended[KW - 1 - tap : KW - 1 - tap + tok_rows]
        )
    return conv_sum.astype(jnp.bfloat16)


def attend_slots(packed, positions):
    slot_count = packed.shape[0]
    inner = packed.shape[1] // 3
    head_count = inner // HD
    query = packed[:, :inner].reshape(slot_count, head_count, HD)
    keys_all = packed[:, inner : 2 * inner].reshape(slot_count, head_count, HD)
    values_all = packed[:, 2 * inner :].reshape(slot_count, head_count, HD)
    slot_ids = jnp.arange(slot_count, dtype=jnp.int32)
    score_scale = 1.0 / HD**0.5
    scores = (
        jnp.einsum("qhd,khd->hqk", query, keys_all, preferred_element_type=jnp.float32)
        * score_scale
    )
    allowed = (positions[None, :] >= 0) & (positions[None, :] <= positions[:, None]) | (
        slot_ids[:, None] == slot_ids[None, :]
    )
    scores = jnp.where(allowed[None], scores, jnp.float32(-1e30))
    top_score = jnp.max(scores, axis=-1, keepdims=True)
    expd = jnp.exp(scores - top_score)
    weights = (expd / jnp.sum(expd, axis=-1, keepdims=True)).astype(jnp.bfloat16)
    mixed = jnp.einsum("hqk,khd->qhd", weights, values_all, preferred_element_type=jnp.float32)
    return mixed.astype(jnp.bfloat16).reshape(slot_count, inner)


def body_by_owner(frames, conv_weight, qkv_weight, track_ids, track_owner):
    tok_rows = frames.shape[0]
    peer_count = lax.axis_size("seq")
    capacity = 2 * tok_rows // peer_count
    slot_total = capacity * peer_count
    my_index = lax.axis_index("seq")
    rim_rows = from_behind(frames[tok_rows - (KW - 1) :], "seq", 1)
    hidden = convolve(frames, conv_weight, rim_rows)
    group = track_groups(track_ids, track_owner)
    owner_hits = (group[:, None] == jnp.arange(peer_count, dtype=jnp.int32)[None, :]).astype(
        jnp.int32
    )
    running = jnp.cumsum(owner_hits, axis=0) - 1
    rank_rows = jnp.sum(jnp.where(owner_hits > 0, running, 0), axis=1)
    slot_of_row = group * capacity + rank_rows
    row_ids = jnp.arange(tok_rows, dtype=jnp.int32)
    source_row = jnp.full((slot_total,), tok_rows, jnp.int32).at[slot_of_row].set(row_ids)
    positions = my_index * tok_rows + row_ids
    send_times = jnp.full((slot_total,), -1, jnp.int32).at[slot_of_row].set(positions)
    projected = jnp.dot(
        hidden,
        lax.all_gather(qkv_weight, "seq", axis=1, tiled=True),
        preferred_element_type=jnp.float32,
    ).astype(jnp.bfloat16)
    padded_rows = jnp.concatenate(
        [projected, jnp.zeros((1, projected.shape[1]), jnp.bfloat16)], axis=0
    )
    outgoing = padded_rows[source_row]
    received, got_times = (
        lax.all_to_all(outgoing, "seq", split_axis=0, concat_axis=0, tiled=True),
        lax.all_to_all(send_times, "seq", split_axis=0, concat_axis=0, tiled=True),
    )
    mixed = attend_slots(received, got_times)
    returned = lax.all_to_all(mixed, "seq", split_axis=0, concat_axis=0, tiled=True)
    return returned[slot_of_row]


BOTH = ("chip", "core")
RIM = 16


def swap_core(value):
    return lax.ppermute(value, "core", [(0, 1), (1, 0)])


def call(kernel, out_shape, operands, name, smem=0, flops=0, limit=6):
    whole = pl.BlockSpec()
    scalars = pl.BlockSpec(memory_space=pltpu.SMEM)
    many = isinstance(out_shape, (list, tuple))
    shapes = list(out_shape) if many else [out_shape]
    return pl.pallas_call(
        kernel,
        out_shape=out_shape,
        in_specs=[scalars] * smem + [whole] * (len(operands) - smem),
        out_specs=[whole] * len(shapes) if many else whole,
        cost_estimate=pl.CostEstimate(
            flops=flops,
            bytes_accessed=sum(2 * o.size for o in list(operands) + shapes),
            transcendentals=0,
        ),
        compiler_params=pltpu.CompilerParams(vmem_limit_bytes=limit * 2**20),
        name=name,
    )(*operands)


def bf16(*shape):
    return jax.ShapeDtypeStruct(shape, jnp.bfloat16)


def after_kernel(*refs):
    del refs


def after(value, *others):
    anywhere = pl.BlockSpec(memory_space=pl.ANY)
    return pl.pallas_call(
        after_kernel,
        out_shape=jax.ShapeDtypeStruct(value.shape, value.dtype),
        in_specs=[anywhere] * (1 + len(others)),
        out_specs=anywhere,
        input_output_aliases={0: 0},
        compiler_params=pltpu.CompilerParams(vmem_limit_bytes=2**20),
        name="after",
    )(value, *others)


def convolved(before, rows, taps):
    count = rows.shape[0]
    rows = rows.astype(jnp.float32)
    extended = jnp.concatenate([before.astype(jnp.float32), rows], axis=0)
    taps = taps.astype(jnp.float32)
    total = rows
    for tap in range(KW):
        total = total + taps[tap : tap + 1] * extended[RIM - tap : RIM - tap + count]
    return total.astype(jnp.bfloat16)


GRP, CORE, TURN, TURN_OTHER = range(4)


def conv_kernel(rim, frames, taps, hidden):
    hidden[...] = convolved(rim[...], frames[...], taps[...])


def assemble_kernel(scalars, mine, mine_too, other, other_too, weight):
    half = mine.shape[2]
    for piece, column, part, turn in (
        (mine, scalars[CORE], scalars[GRP], TURN),
        (mine_too, scalars[CORE], 1 - scalars[GRP], TURN),
        (other, 1 - scalars[CORE], scalars[GRP], TURN_OTHER),
        (other_too, 1 - scalars[CORE], 1 - scalars[GRP], TURN_OTHER),
    ):
        for n, (j, feature) in enumerate(((2 * part, 0), (2 * part, half), (1, part * half))):
            at = lax.rem(j + 3 - scalars[turn], 3) * HD + column * (HD // 2)
            lanes = pl.ds(pl.multiple_of(feature, half), half)
            weight[pl.ds(pl.multiple_of(at, HD // 2), HD // 2), lanes] = piece[n]


def body_by_head(frames, conv_weight, qkv_weight, track_ids, track_owner):
    tok_rows, features = frames.shape
    chips = lax.axis_size("chip")
    devices = 2 * chips
    core = lax.axis_index("core")
    chip = lax.axis_index("chip")
    grp = lax.axis_index("grp")
    me = 2 * chip + core
    span = devices * tok_rows

    ring = list(range(0, chips, 2)) + list(range(chips - 1, 0, -2))
    place = jnp.where(chip & 1 == 0, chip >> 1, chips - 1 - (chip >> 1))
    links = [(ring[i], ring[(i + 1) % chips]) for i in range(chips)]
    onward = [(2 * f, 2 * t) for f, t in links] + [(2 * t + 1, 2 * f + 1) for f, t in links]

    rim_rows = lax.ppermute(
        frames[tok_rows - RIM :], BOTH, [(i, i + 1) for i in range(devices - 1)]
    )
    hidden = call(conv_kernel, bf16(tok_rows, features), [rim_rows, frames, conv_weight], "conv")

    half = features // 2
    held = qkv_weight.T.reshape(3, HD // 2, features)
    outer = after(lax.dynamic_index_in_dim(held, 2 * grp, 0, False), hidden)
    middle = after(lax.dynamic_slice_in_dim(held[1], grp * half, half, 1), hidden)

    def to_heads(block, j):
        return lax.ppermute(
            block,
            ("grp",) + BOTH,
            [
                (g * devices + d, g * devices + (3 * d + j[g]) % devices)
                for g in (0, 1)
                for d in range(devices)
            ],
        )

    outer, middle = to_heads(outer, (0, 2)), to_heads(middle, (1, 1))
    mine = jnp.stack([outer[:, :half], outer[:, half:], middle])
    mine_too = lax.ppermute(mine, "grp", [(0, 1), (1, 0)])
    scalars = jnp.stack([grp, core, lax.rem(me, 3), lax.rem(me + 1 - 2 * core, 3)])
    head_weight = call(
        assemble_kernel,
        bf16(3 * HD, features),
        [scalars.astype(jnp.int32), mine, mine_too, swap_core(mine), swap_core(mine_too)],
        "assemble",
        smem=1,
    )

    times = me * tok_rows + jnp.arange(tok_rows, dtype=jnp.int32)
    codes = (track_groups(track_ids, track_owner) * span + times)[None, :]

    def all_codes(codes, bit):
        theirs = lax.ppermute(codes, BOTH, [(d, d ^ bit) for d in range(devices)])
        low = me & bit == 0
        return jnp.concatenate(
            [jnp.where(low, codes, theirs), jnp.where(low, theirs, codes)], axis=0
        )

    parts, swapped = [], []

    def project(rows):
        done = lax.dot_general(
            rows, head_weight, (((1,), (1,)), ((), ())), preferred_element_type=jnp.float32
        ).astype(jnp.bfloat16)
        parts.append(done)
        return done

    def swap_keyed(count):
        keyed = [p[:, HD:] for p in parts[-count:]]
        swapped.append(swap_core(jnp.concatenate(keyed, axis=0) if count > 1 else keyed[0]))

    blocks = [hidden]
    for step in range(1, chips):
        ready = []
        if step == 5:
            ready += [project(rows) for rows in blocks[:4]]
            swap_keyed(4)
        if step == 7:
            ready += [project(rows) for rows in blocks[4:6]]
            swap_keyed(2)
        if 3 <= step < 7:
            ready.append(codes)
            codes = all_codes(after(codes, blocks[step - 2]), 1 << (step - 3))
        if ready:
            blocks[-1] = after(blocks[-1], *ready)
        blocks.append(lax.ppermute(blocks[-1], BOTH, onward))
    project(blocks[6])
    swap_keyed(1)
    project(blocks[7])
    swap_keyed(1)
    parts = jnp.concatenate(parts, axis=0)
    query = parts[:, :HD]
    keyed = jnp.concatenate([parts[:, HD:]] + swapped, axis=0)

    codes = codes.reshape(chips, 2, tok_rows)
    around = jnp.stack([codes[c] for c in ring + ring])
    on = lax.dynamic_slice_in_dim(around, place, chips, 0)
    back = jnp.concatenate([on[:1], on[:0:-1]], axis=0)
    asking = jnp.where(core == 0, back[:, 0], on[:, 1]).reshape(-1)
    others = jnp.where(core == 0, on[:, 1], back[:, 0]).reshape(-1)
    keys = jnp.concatenate([asking, others])
    least = asking // span * span
    scores = lax.dot_general(
        query, keyed[:, :HD], (((1,), (1,)), ((), ())), preferred_element_type=jnp.float32
    ) * (1.0 / HD**0.5)
    allowed = (keys[None, :] <= asking[:, None]) & (keys[None, :] >= least[:, None])
    scores = jnp.where(allowed, scores, jnp.float32(-1e30))
    expd = jnp.exp(scores - jnp.max(scores, axis=-1, keepdims=True))
    weights = (expd / jnp.sum(expd, axis=-1, keepdims=True)).astype(jnp.bfloat16)
    mixed = jnp.dot(weights, keyed[:, HD:], preferred_element_type=jnp.float32)
    mixed = mixed.astype(jnp.bfloat16).reshape(chips, tok_rows, HD)

    back = jnp.concatenate([mixed[:1], mixed[:0:-1]], axis=0)
    on = jnp.where(core == 0, back, mixed)
    around = lax.dynamic_slice_in_dim(jnp.concatenate([on, on], axis=0), chips - place, chips, 0)
    sent = jnp.stack([around[ring.index(c)] for c in range(chips)])
    returned = lax.all_to_all(sent, "chip", split_axis=0, concat_axis=0, tiled=True)
    return returned.transpose(1, 0, 2).reshape(tok_rows, chips * HD)


def solution(mesh):
    grp, seq = mesh.devices.shape
    out_by_owner = P(("grp", "seq"), None)
    by_owner = jax.shard_map(
        body_by_owner,
        mesh=mesh,
        in_specs=(P(("grp", "seq"), None), P(), P(None, "seq"), P(("grp", "seq")), P("grp")),
        out_specs=out_by_owner,
        check_vma=False,
    )
    fits = (grp, seq) == (2, 16)
    if fits:
        split = Mesh(mesh.devices.reshape(grp, seq // 2, 2), ("grp",) + BOTH)
        rows = P(("grp",) + BOTH)
        by_head = jax.shard_map(
            body_by_head,
            mesh=split,
            in_specs=(rows, P(), P(None, BOTH), rows, P("grp")),
            out_specs=rows,
            check_vma=False,
        )

    def run(frames, conv_weight, qkv_weight, track_ids, track_owner):
        heads = qkv_weight.shape[1] // (3 * HD)
        plan = by_head if fits and heads == 8 else by_owner
        return plan(frames, conv_weight, qkv_weight, track_ids, track_owner)

    return run
```

```python
import jax
import jax.numpy as jnp
from jax import lax
from jax.experimental import pallas as pl
from jax.experimental.pallas import tpu as pltpu
from jax.sharding import Mesh
from jax.sharding import PartitionSpec as P

HD = 128
KW = 4


def from_behind(value, axis, by):
    size = lax.axis_size(axis)
    pairs = [(i, i + by) for i in range(size) if 0 <= i + by < size]
    return lax.ppermute(value, axis, pairs)


def track_groups(track_ids, track_owner):
    track_total = track_owner.shape[0]
    return jnp.sum(
        jnp.where(
            track_ids[:, None] == jnp.arange(track_total, dtype=jnp.int32)[None, :],
            track_owner[None, :],
            0,
        ),
        axis=1,
    )


def convolve(frames, conv_weight, rim_rows):
    tok_rows = frames.shape[0]
    extended = jnp.concatenate([rim_rows, frames], axis=0).astype(jnp.float32)
    conv_sum = frames.astype(jnp.float32)
    for tap in range(KW):
        conv_sum = (
            conv_sum
            + conv_weight[tap].astype(jnp.float32)[None, :]
            * extended[KW - 1 - tap : KW - 1 - tap + tok_rows]
        )
    return conv_sum.astype(jnp.bfloat16)


def attend_slots(packed, positions):
    slot_count = packed.shape[0]
    inner = packed.shape[1] // 3
    head_count = inner // HD
    query = packed[:, :inner].reshape(slot_count, head_count, HD)
    keys_all = packed[:, inner : 2 * inner].reshape(slot_count, head_count, HD)
    values_all = packed[:, 2 * inner :].reshape(slot_count, head_count, HD)
    slot_ids = jnp.arange(slot_count, dtype=jnp.int32)
    score_scale = 1.0 / HD**0.5
    scores = (
        jnp.einsum("qhd,khd->hqk", query, keys_all, preferred_element_type=jnp.float32)
        * score_scale
    )
    allowed = (positions[None, :] >= 0) & (positions[None, :] <= positions[:, None]) | (
        slot_ids[:, None] == slot_ids[None, :]
    )
    scores = jnp.where(allowed[None], scores, jnp.float32(-1e30))
    top_score = jnp.max(scores, axis=-1, keepdims=True)
    expd = jnp.exp(scores - top_score)
    weights = (expd / jnp.sum(expd, axis=-1, keepdims=True)).astype(jnp.bfloat16)
    mixed = jnp.einsum("hqk,khd->qhd", weights, values_all, preferred_element_type=jnp.float32)
    return mixed.astype(jnp.bfloat16).reshape(slot_count, inner)


def body_by_owner(frames, conv_weight, qkv_weight, track_ids, track_owner):
    tok_rows = frames.shape[0]
    peer_count = lax.axis_size("seq")
    capacity = 2 * tok_rows // peer_count
    slot_total = capacity * peer_count
    my_index = lax.axis_index("seq")
    rim_rows = from_behind(frames[tok_rows - (KW - 1) :], "seq", 1)
    hidden = convolve(frames, conv_weight, rim_rows)
    group = track_groups(track_ids, track_owner)
    owner_hits = (group[:, None] == jnp.arange(peer_count, dtype=jnp.int32)[None, :]).astype(
        jnp.int32
    )
    running = jnp.cumsum(owner_hits, axis=0) - 1
    rank_rows = jnp.sum(jnp.where(owner_hits > 0, running, 0), axis=1)
    slot_of_row = group * capacity + rank_rows
    row_ids = jnp.arange(tok_rows, dtype=jnp.int32)
    source_row = jnp.full((slot_total,), tok_rows, jnp.int32).at[slot_of_row].set(row_ids)
    positions = my_index * tok_rows + row_ids
    send_times = jnp.full((slot_total,), -1, jnp.int32).at[slot_of_row].set(positions)
    projected = jnp.dot(
        hidden,
        lax.all_gather(qkv_weight, "seq", axis=1, tiled=True),
        preferred_element_type=jnp.float32,
    ).astype(jnp.bfloat16)
    padded_rows = jnp.concatenate(
        [projected, jnp.zeros((1, projected.shape[1]), jnp.bfloat16)], axis=0
    )
    outgoing = padded_rows[source_row]
    received, got_times = (
        lax.all_to_all(outgoing, "seq", split_axis=0, concat_axis=0, tiled=True),
        lax.all_to_all(send_times, "seq", split_axis=0, concat_axis=0, tiled=True),
    )
    mixed = attend_slots(received, got_times)
    returned = lax.all_to_all(mixed, "seq", split_axis=0, concat_axis=0, tiled=True)
    return returned[slot_of_row]


FOUR = ("far", "near", "quad")
CORE, Y, NEAR, FAR = 1, 2, 4, 8
RIM = 16


def swap_seq(value, bit):
    count = lax.axis_size(FOUR)
    return lax.ppermute(value, FOUR, [(d, d ^ bit) for d in range(count)])


def swap_grp(value):
    return lax.ppermute(value, "grp", [(0, 1), (1, 0)])


def call(kernel, out_shape, operands, name, smem=0, flops=0, limit=6):
    whole = pl.BlockSpec()
    scalars = pl.BlockSpec(memory_space=pltpu.SMEM)
    many = isinstance(out_shape, (list, tuple))
    shapes = list(out_shape) if many else [out_shape]
    return pl.pallas_call(
        kernel,
        out_shape=out_shape,
        in_specs=[scalars] * smem + [whole] * (len(operands) - smem),
        out_specs=[whole] * len(shapes) if many else whole,
        cost_estimate=pl.CostEstimate(
            flops=flops,
            bytes_accessed=sum(2 * o.size for o in list(operands) + shapes),
            transcendentals=0,
        ),
        compiler_params=pltpu.CompilerParams(vmem_limit_bytes=limit * 2**20),
        name=name,
    )(*operands)


def bf16(*shape):
    return jax.ShapeDtypeStruct(shape, jnp.bfloat16)


def after_kernel(*refs):
    del refs


def after(value, *others):
    anywhere = pl.BlockSpec(memory_space=pl.ANY)
    return pl.pallas_call(
        after_kernel,
        out_shape=jax.ShapeDtypeStruct(value.shape, value.dtype),
        in_specs=[anywhere] * (1 + len(others)),
        out_specs=anywhere,
        input_output_aliases={0: 0},
        compiler_params=pltpu.CompilerParams(vmem_limit_bytes=2**20),
        name="after",
    )(value, *others)


def convolved(before, rows, taps):
    count = rows.shape[0]
    rows = rows.astype(jnp.float32)
    extended = jnp.concatenate([before.astype(jnp.float32), rows], axis=0)
    taps = taps.astype(jnp.float32)
    total = rows
    for tap in range(KW):
        total = total + taps[tap : tap + 1] * extended[RIM - tap : RIM - tap + count]
    return total.astype(jnp.bfloat16)


ME, SIDE, GRP, TURN, TURN_PAIRED, HEAD = range(6)


def first_kernel(
    scalars, owner, ids, frames, weight, taps, late, rim, block0, block1, block2, code,
    rows, tap_rows, my_ids, owners, sems,
):
    tok_rows = frames.shape[0]
    part = late.shape[0]
    half = block0.shape[1]
    lanes = pl.ds(pl.multiple_of(scalars[GRP] * half, half), half)
    copies = [
        pltpu.make_async_copy(frames, rows, sems.at[0]),
        pltpu.make_async_copy(taps, tap_rows, sems.at[1]),
        pltpu.make_async_copy(ids, my_ids, sems.at[2]),
        pltpu.make_async_copy(owner, owners, sems.at[3]),
    ]
    for j, block in enumerate((block0, block1, block2)):
        source = weight.at[pl.ds(j * (HD // 2), HD // 2), lanes]
        copies.append(pltpu.make_async_copy(source, block, sems.at[4 + j]))
    for copy in copies:
        copy.start()
    for copy in copies[:4]:
        copy.wait()
    late[...] = convolved(rows[part - RIM : part], rows[part:], tap_rows[...])
    rim[...] = rows[tok_rows - RIM :]
    group = jnp.zeros(ids.shape, jnp.int32)
    for track in range(owner.shape[1]):
        group = jnp.where(my_ids[...] == track, owners[0, track], group)
    time = lax.broadcasted_iota(jnp.int32, ids.shape, 1)
    code[...] = (group * 16 + scalars[ME]) * tok_rows + time
    for copy in copies[4:]:
        copy.wait()


def first(scalars, owner, ids, frames, weight, taps):
    tok_rows, features = frames.shape
    half = features // 2
    whole, far = pl.BlockSpec(), pl.BlockSpec(memory_space=pltpu.HBM)
    return pl.pallas_call(
        first_kernel,
        out_shape=[bf16(tok_rows // 2, features), bf16(RIM, features)]
        + [bf16(HD // 2, half)] * 3
        + [jax.ShapeDtypeStruct(ids.shape, jnp.int32)],
        in_specs=[pl.BlockSpec(memory_space=pltpu.SMEM)] + [far] * 5,
        out_specs=[whole] * 6,
        scratch_shapes=[
            pltpu.VMEM(frames.shape, frames.dtype),
            pltpu.VMEM(taps.shape, taps.dtype),
            pltpu.VMEM(ids.shape, ids.dtype),
            pltpu.SMEM(owner.shape, owner.dtype),
            pltpu.SemaphoreType.DMA((7,)),
        ],
        compiler_params=pltpu.CompilerParams(vmem_limit_bytes=63 * 2**20),
        name="first",
    )(scalars, owner, ids, frames, weight, taps)


def early_kernel(rim, frames, taps, late, early, own):
    part = late.shape[0]
    rows = convolved(rim[...], frames[:part], taps[...])
    early[...] = rows
    own[:part] = rows
    own[part:] = late[...]


def assemble_kernel(scalars, mine, mine_too, paired, diagonal0, diagonal1, weight):
    side, grp = scalars[SIDE], scalars[GRP]
    half, cut = mine.shape[2], diagonal0.shape[2]
    for piece, column, start, turn in (
        (mine, side, grp * half, TURN),
        (mine_too, side, (1 - grp) * half, TURN),
        (paired, 1 - side, grp * half, TURN_PAIRED),
        (diagonal0, 1 - side, (1 - grp) * half, TURN_PAIRED),
        (diagonal1, 1 - side, (1 - grp) * half + cut, TURN_PAIRED),
    ):
        lanes = pl.ds(pl.multiple_of(start, cut), piece.shape[2])
        for j in range(3):
            at = lax.rem(j + 3 - scalars[turn], 3) * HD + column * (HD // 2)
            weight[pl.ds(pl.multiple_of(at, HD // 2), HD // 2), lanes] = piece[j]


def place_kernel(scalars, block0, block1, block2, block3, theirs, out):
    rows = out.shape[0]
    for n, block in enumerate((block0, block1, block2, block3)):
        chip = (0, Y, FAR, FAR | Y)[n]
        for core, value in ((0, block[...]), (CORE, theirs[n * rows : (n + 1) * rows])):
            head = scalars[HEAD] ^ (chip // FAR * 4 + chip % 4 + core)
            out[:, pl.ds(pl.multiple_of(head * HD, HD), HD)] = value


def body_by_head(frames, conv_weight, qkv_weight, track_ids, track_owner):
    tok_rows, features = frames.shape
    grp = lax.axis_index("grp")
    far, near, quad = (lax.axis_index(name) for name in FOUR)
    me = far * FAR + near * NEAR + quad
    devices = lax.axis_size(FOUR)
    head = far * 4 + quad
    part = tok_rows // 2

    half = features // 2
    turn = lax.rem(2 * head + near, 3)
    turn_paired = lax.rem(2 * head + 1 - near, 3)
    scalars = jnp.stack([me, near, grp, turn, turn_paired, head])
    scalars = scalars.astype(jnp.int32)

    late, rim_rows, *blocks, codes = first(
        scalars, track_owner[None, :], track_ids[None, :], frames, qkv_weight.T, conv_weight
    )

    def home(block):
        of_head, side = block % devices // 2, block % 2
        return of_head // 4 * FAR + side * NEAR + of_head % 4

    mine = jnp.stack(
        [
            lax.ppermute(block, FOUR, [(d, home(3 * d + j)) for d in range(devices)])
            for j, block in enumerate(blocks)
        ]
    )
    far_late = swap_seq(late, FAR)
    seen = [0]

    def with_codes_of(codes, bit):
        seen.extend([hop ^ bit for hop in seen])
        return jnp.concatenate([codes, swap_seq(codes, bit)], axis=0)

    codes = with_codes_of(codes, FAR)
    mine = after(mine, far_late)
    mine_too = swap_grp(mine)
    paired = swap_seq(mine, NEAR)
    cut = half // 2
    diagonal = [swap_grp(paired[:, :, :cut]), swap_seq(mine_too[:, :, cut:], NEAR)]
    head_weight = call(
        assemble_kernel,
        bf16(3 * HD, features),
        [scalars, mine, mine_too, paired] + diagonal,
        "assemble",
        smem=1,
    )

    rim_rows = lax.ppermute(rim_rows, FOUR, [(i, i + 1) for i in range(devices - 1)])
    early, own = call(
        early_kernel,
        [bf16(part, features), bf16(tok_rows, features)],
        [rim_rows, frames, conv_weight, late],
        "early",
    )
    beside = swap_seq(after(own, mine), Y)
    far_late_beside = swap_seq(far_late, Y)
    far_early = swap_seq(after(early, far_late), FAR)
    far_early_beside = swap_seq(after(far_early, codes, *diagonal), Y)

    parts = []

    def project(*rows):
        rows = jnp.concatenate(rows + tuple(swap_seq(r, CORE) for r in rows), axis=0)
        done = lax.dot_general(
            rows, head_weight, (((1,), (1,)), ((), ())), preferred_element_type=jnp.float32
        ).astype(jnp.bfloat16)
        parts.append((done[:, :HD], done[:, HD:], swap_seq(done[:, HD:], NEAR)))
        return done

    done = project(own, beside, far_late, far_late_beside)
    done = project(far_early, after(far_early_beside, done))

    codes = with_codes_of(with_codes_of(with_codes_of(after(codes, done), CORE), Y), NEAR)

    keyed = jnp.concatenate([p[1] for p in parts] + [p[2] for p in parts], axis=0)

    first_order, second_order = [], []
    for core in (0, CORE):
        first_order += [(core, 0, tok_rows), (core | Y, 0, tok_rows)]
        first_order += [(core | FAR, part, part), (core | FAR | Y, part, part)]
        second_order += [(core | FAR, 0, part), (core | FAR | Y, 0, part)]
    order = first_order + second_order

    def codes_at(order, bit=0):
        return jnp.concatenate(
            [codes[seen.index(hop ^ bit), start : start + count] for hop, start, count in order]
        )

    keys = jnp.concatenate([codes_at(order), codes_at(order, NEAR)])
    queries = jnp.concatenate([p[0] for p in parts], axis=0)
    span = devices * tok_rows

    def attend(hops):
        at, pieces = 0, {}
        for hop, start, count in order:
            pieces[hop, start] = queries[at : at + count]
            at += count
        mine = [(h, s, c) for hop in hops for h, s, c in sorted(order) if h == hop]
        query = jnp.concatenate([pieces[h, s] for h, s, _ in mine], axis=0)
        asking = codes_at(mine)
        least = asking // span * span
        scores = lax.dot_general(
            query, keyed[:, :HD], (((1,), (1,)), ((), ())), preferred_element_type=jnp.float32
        ) * (1.0 / HD**0.5)
        allowed = (keys[None, :] <= asking[:, None]) & (keys[None, :] >= least[:, None])
        scores = jnp.where(allowed, scores, jnp.float32(-1e30))
        expd = jnp.exp(scores - jnp.max(scores, axis=-1, keepdims=True))
        weights = (expd / jnp.sum(expd, axis=-1, keepdims=True)).astype(jnp.bfloat16)
        mixed = jnp.dot(weights, keyed[:, HD:], preferred_element_type=jnp.float32)
        return mixed.astype(jnp.bfloat16).reshape(len(hops), tok_rows, HD)

    far_hops = (FAR, FAR | CORE, FAR | Y, FAR | Y | CORE)
    context = attend(far_hops)
    home = {FAR: swap_seq(context[:2], FAR), FAR | Y: swap_seq(context[2:], FAR | Y)}
    context = attend((0, CORE, Y, Y | CORE))
    home[Y] = swap_seq(context[2:], Y)
    home[0] = context[:2]
    chips = (0, Y, FAR, FAR | Y)
    theirs = swap_seq(jnp.concatenate([home[chip][1] for chip in chips], axis=0), CORE)
    return call(
        place_kernel,
        bf16(tok_rows, devices // 2 * HD),
        [scalars] + [home[chip][0] for chip in chips] + [theirs],
        "place",
        smem=1,
    )


def solution(mesh):
    grp, seq = mesh.devices.shape
    out_by_owner = P(("grp", "seq"), None)
    by_owner = jax.shard_map(
        body_by_owner,
        mesh=mesh,
        in_specs=(P(("grp", "seq"), None), P(), P(None, "seq"), P(("grp", "seq")), P("grp")),
        out_specs=out_by_owner,
        check_vma=False,
    )
    fits = (grp, seq) == (2, 16)
    if fits:
        split = Mesh(mesh.devices.reshape(grp, 2, 2, 4), ("grp",) + FOUR)
        rows = P(("grp",) + FOUR)
        by_head = jax.shard_map(
            body_by_head,
            mesh=split,
            in_specs=(rows, P(), P(None, FOUR), rows, P("grp")),
            out_specs=rows,
            check_vma=False,
        )

    def run(frames, conv_weight, qkv_weight, track_ids, track_owner):
        heads = qkv_weight.shape[1] // (3 * HD)
        plan = by_head if fits and heads == 8 else by_owner
        return plan(frames, conv_weight, qkv_weight, track_ids, track_owner)

    return run
```

```python
import jax
import jax.numpy as jnp
from jax import lax
from jax.experimental import pallas as pl
from jax.experimental.pallas import tpu as pltpu
from jax.sharding import Mesh
from jax.sharding import PartitionSpec as P

HD = 128
KW = 4


def from_behind(value, axis, by):
    size = lax.axis_size(axis)
    pairs = [(i, i + by) for i in range(size) if 0 <= i + by < size]
    return lax.ppermute(value, axis, pairs)


def track_groups(track_ids, track_owner):
    track_total = track_owner.shape[0]
    return jnp.sum(
        jnp.where(
            track_ids[:, None] == jnp.arange(track_total, dtype=jnp.int32)[None, :],
            track_owner[None, :],
            0,
        ),
        axis=1,
    )


def convolve(frames, conv_weight, rim_rows):
    tok_rows = frames.shape[0]
    extended = jnp.concatenate([rim_rows, frames], axis=0).astype(jnp.float32)
    conv_sum = frames.astype(jnp.float32)
    for tap in range(KW):
        conv_sum = (
            conv_sum
            + conv_weight[tap].astype(jnp.float32)[None, :]
            * extended[KW - 1 - tap : KW - 1 - tap + tok_rows]
        )
    return conv_sum.astype(jnp.bfloat16)


def attend_slots(packed, positions):
    slot_count = packed.shape[0]
    inner = packed.shape[1] // 3
    head_count = inner // HD
    query = packed[:, :inner].reshape(slot_count, head_count, HD)
    keys_all = packed[:, inner : 2 * inner].reshape(slot_count, head_count, HD)
    values_all = packed[:, 2 * inner :].reshape(slot_count, head_count, HD)
    slot_ids = jnp.arange(slot_count, dtype=jnp.int32)
    score_scale = 1.0 / HD**0.5
    scores = (
        jnp.einsum("qhd,khd->hqk", query, keys_all, preferred_element_type=jnp.float32)
        * score_scale
    )
    allowed = (positions[None, :] >= 0) & (positions[None, :] <= positions[:, None]) | (
        slot_ids[:, None] == slot_ids[None, :]
    )
    scores = jnp.where(allowed[None], scores, jnp.float32(-1e30))
    top_score = jnp.max(scores, axis=-1, keepdims=True)
    expd = jnp.exp(scores - top_score)
    weights = (expd / jnp.sum(expd, axis=-1, keepdims=True)).astype(jnp.bfloat16)
    mixed = jnp.einsum("hqk,khd->qhd", weights, values_all, preferred_element_type=jnp.float32)
    return mixed.astype(jnp.bfloat16).reshape(slot_count, inner)


def body_by_owner(frames, conv_weight, qkv_weight, track_ids, track_owner):
    tok_rows = frames.shape[0]
    peer_count = lax.axis_size("seq")
    capacity = 2 * tok_rows // peer_count
    slot_total = capacity * peer_count
    my_index = lax.axis_index("seq")
    rim_rows = from_behind(frames[tok_rows - (KW - 1) :], "seq", 1)
    hidden = convolve(frames, conv_weight, rim_rows)
    group = track_groups(track_ids, track_owner)
    owner_hits = (group[:, None] == jnp.arange(peer_count, dtype=jnp.int32)[None, :]).astype(
        jnp.int32
    )
    running = jnp.cumsum(owner_hits, axis=0) - 1
    rank_rows = jnp.sum(jnp.where(owner_hits > 0, running, 0), axis=1)
    slot_of_row = group * capacity + rank_rows
    row_ids = jnp.arange(tok_rows, dtype=jnp.int32)
    source_row = jnp.full((slot_total,), tok_rows, jnp.int32).at[slot_of_row].set(row_ids)
    positions = my_index * tok_rows + row_ids
    send_times = jnp.full((slot_total,), -1, jnp.int32).at[slot_of_row].set(positions)
    projected = jnp.dot(
        hidden,
        lax.all_gather(qkv_weight, "seq", axis=1, tiled=True),
        preferred_element_type=jnp.float32,
    ).astype(jnp.bfloat16)
    padded_rows = jnp.concatenate(
        [projected, jnp.zeros((1, projected.shape[1]), jnp.bfloat16)], axis=0
    )
    outgoing = padded_rows[source_row]
    received, got_times = (
        lax.all_to_all(outgoing, "seq", split_axis=0, concat_axis=0, tiled=True),
        lax.all_to_all(send_times, "seq", split_axis=0, concat_axis=0, tiled=True),
    )
    mixed = attend_slots(received, got_times)
    returned = lax.all_to_all(mixed, "seq", split_axis=0, concat_axis=0, tiled=True)
    return returned[slot_of_row]


def xor_swap(value, bit, axes=("chip", "core")):
    count = lax.axis_size(axes)
    return lax.ppermute(value, axes, [(d, d ^ bit) for d in range(count)])


def by_bit(bit, mine, theirs, axis):
    return jnp.stack(
        [jnp.where(bit == 0, mine, theirs), jnp.where(bit == 0, theirs, mine)], axis=axis
    )


def after_kernel(*refs):
    del refs


def after(value, *others):
    anywhere = pl.BlockSpec(memory_space=pl.ANY)
    return pl.pallas_call(
        after_kernel,
        out_shape=jax.ShapeDtypeStruct(value.shape, value.dtype),
        in_specs=[anywhere] * (1 + len(others)),
        out_specs=anywhere,
        input_output_aliases={0: 0},
        compiler_params=pltpu.CompilerParams(vmem_limit_bytes=2**20),
        name="after",
    )(value, *others)


def body_by_head(frames, conv_weight, qkv_weight, track_ids, track_owner):
    tok_rows = frames.shape[0]
    chips = lax.axis_size("chip")
    devices = 2 * chips
    core = lax.axis_index("core")
    chip = lax.axis_index("chip")
    grp = lax.axis_index("grp")
    me = 2 * chip + core
    both = ("chip", "core")
    every = ("grp", "chip", "core")
    part = tok_rows // 2
    features = frames.shape[1]
    CORE, Y, Z0, Z1 = 1, 2, 4, 8

    rim_rows = lax.ppermute(
        frames[tok_rows - (KW - 1) :], both, [(i, i + 1) for i in range(devices - 1)]
    )
    late = convolve(frames[part:], conv_weight, frames[part - (KW - 1) : part])
    early = convolve(frames[:part], conv_weight, rim_rows)

    far_late = xor_swap(late, Z1)
    far_early = xor_swap(early, Z1)
    own = jnp.concatenate([early, late], axis=0)
    beside = xor_swap(own, Y)
    far_beside_late = xor_swap(far_late, Y)
    far_beside_early = xor_swap(far_early, Y)

    half = features // 2
    held = lax.dynamic_slice_in_dim(qkv_weight.T, grp * half, half, 1).reshape(3, HD // 2, half)
    moved = [
        lax.ppermute(held[j], both, [(d, (3 * d + j) % devices) for d in range(devices)])
        for j in range(3)
    ]
    mine = lax.dynamic_slice_in_dim(jnp.stack(moved + moved[:2]), lax.rem(me, 3), 3, 0)
    paired = xor_swap(mine, Z0)

    def whole_head(quarter):
        wide = by_bit(grp, quarter, xor_swap(quarter, devices, every), 2)
        wide = wide.reshape(3, HD // 2, features)
        return by_bit(core, wide, xor_swap(wide, CORE), 1).reshape(3 * HD, features)

    two_heads = jnp.concatenate([whole_head(mine), whole_head(paired)], axis=0)

    def project(rows):
        done = lax.dot_general(
            rows, two_heads, (((1,), (1,)), ((), ())), preferred_element_type=jnp.float32
        ).astype(jnp.bfloat16)
        return done, jnp.concatenate([done[:, : 3 * HD], xor_swap(done[:, 3 * HD :], Z0)], axis=0)

    raw, first = project(jnp.concatenate([own, beside, far_late, far_beside_late], axis=0))
    _, second = project(jnp.concatenate([far_early, far_beside_early], axis=0))

    first_rows = [(0, 0, tok_rows), (Y, 0, tok_rows), (Z1, part, part), (Z1 | Y, part, part)]
    second_rows = [(Z1, 0, part), (Z1 | Y, 0, part)]
    order = []
    for pieces in (first_rows, second_rows):
        order += pieces + [(far ^ Z0, start, count) for far, start, count in pieces]

    span = devices * tok_rows
    times = me * tok_rows + jnp.arange(tok_rows, dtype=jnp.int32)
    codes = (track_groups(track_ids, track_owner) * span + times)[None, :]
    codes = after(codes, raw)
    for bit in (CORE, Y, Z0, Z1):
        codes = jnp.concatenate([codes, xor_swap(codes, bit)], axis=0)

    def codes_at(bit):
        return jnp.concatenate(
            [codes[far ^ bit, start : start + count] for far, start, count in order]
        )

    asking = codes_at(0)
    keys = jnp.concatenate([asking, codes_at(CORE)])
    least = asking // span * span
    projected = jnp.concatenate([first, second], axis=0)
    query = projected[:, :HD]
    keyed = jnp.concatenate(
        [projected[:, HD:], xor_swap(first[:, HD:], CORE), xor_swap(second[:, HD:], CORE)], axis=0
    )
    scores = lax.dot_general(
        query, keyed[:, :HD], (((1,), (1,)), ((), ())), preferred_element_type=jnp.float32
    ) * (1.0 / HD**0.5)
    allowed = (keys[None, :] <= asking[:, None]) & (keys[None, :] >= least[:, None])
    scores = jnp.where(allowed, scores, jnp.float32(-1e30))
    expd = jnp.exp(scores - jnp.max(scores, axis=-1, keepdims=True))
    weights = (expd / jnp.sum(expd, axis=-1, keepdims=True)).astype(jnp.bfloat16)
    mixed = jnp.dot(weights, keyed[:, HD:], preferred_element_type=jnp.float32)
    mixed = mixed.astype(jnp.bfloat16)

    sent = jnp.zeros((chips, tok_rows, HD), jnp.bfloat16)
    at = 0
    for far, start, count in order:
        rows = mixed[at : at + count]
        sent = lax.dynamic_update_slice(sent, rows[None], ((me ^ far) >> 1, start, 0))
        at += count
    returned = lax.all_to_all(sent, "chip", split_axis=0, concat_axis=0, tiled=True)
    return returned.transpose(1, 0, 2).reshape(tok_rows, chips * HD)


def solution(mesh):
    grp, seq = mesh.devices.shape
    out_by_owner = P(("grp", "seq"), None)
    by_owner = jax.shard_map(
        body_by_owner,
        mesh=mesh,
        in_specs=(P(("grp", "seq"), None), P(), P(None, "seq"), P(("grp", "seq")), P("grp")),
        out_specs=out_by_owner,
        check_vma=False,
    )
    split = Mesh(mesh.devices.reshape(grp, seq // 2, 2), ("grp", "chip", "core"))
    rows = P(("grp", "chip", "core"))
    by_head = jax.shard_map(
        body_by_head,
        mesh=split,
        in_specs=(rows, P(), P(None, ("chip", "core")), rows, P("grp")),
        out_specs=rows,
        check_vma=False,
    )

    def run(frames, conv_weight, qkv_weight, track_ids, track_owner):
        heads = qkv_weight.shape[1] // (3 * HD)
        plan = by_head if (grp, seq, heads) == (2, 16, 8) else by_owner
        return plan(frames, conv_weight, qkv_weight, track_ids, track_owner)

    return run
```

```python
import jax
import jax.numpy as jnp
from jax import lax
from jax.sharding import Mesh
from jax.sharding import PartitionSpec as P

HD = 128
KW = 4


def from_behind(value, axis, by):
    size = lax.axis_size(axis)
    pairs = [(i, i + by) for i in range(size) if 0 <= i + by < size]
    return lax.ppermute(value, axis, pairs)


def track_groups(track_ids, track_owner):
    track_total = track_owner.shape[0]
    return jnp.sum(
        jnp.where(
            track_ids[:, None] == jnp.arange(track_total, dtype=jnp.int32)[None, :],
            track_owner[None, :],
            0,
        ),
        axis=1,
    )


def convolve(frames, conv_weight, rim_rows):
    tok_rows = frames.shape[0]
    extended = jnp.concatenate([rim_rows, frames], axis=0).astype(jnp.float32)
    conv_sum = frames.astype(jnp.float32)
    for tap in range(KW):
        conv_sum = (
            conv_sum
            + conv_weight[tap].astype(jnp.float32)[None, :]
            * extended[KW - 1 - tap : KW - 1 - tap + tok_rows]
        )
    return conv_sum.astype(jnp.bfloat16)


def attend_slots(packed, positions):
    slot_count = packed.shape[0]
    inner = packed.shape[1] // 3
    head_count = inner // HD
    query = packed[:, :inner].reshape(slot_count, head_count, HD)
    keys_all = packed[:, inner : 2 * inner].reshape(slot_count, head_count, HD)
    values_all = packed[:, 2 * inner :].reshape(slot_count, head_count, HD)
    slot_ids = jnp.arange(slot_count, dtype=jnp.int32)
    score_scale = 1.0 / HD**0.5
    scores = (
        jnp.einsum("qhd,khd->hqk", query, keys_all, preferred_element_type=jnp.float32)
        * score_scale
    )
    allowed = (positions[None, :] >= 0) & (positions[None, :] <= positions[:, None]) | (
        slot_ids[:, None] == slot_ids[None, :]
    )
    scores = jnp.where(allowed[None], scores, jnp.float32(-1e30))
    top_score = jnp.max(scores, axis=-1, keepdims=True)
    expd = jnp.exp(scores - top_score)
    weights = (expd / jnp.sum(expd, axis=-1, keepdims=True)).astype(jnp.bfloat16)
    mixed = jnp.einsum("hqk,khd->qhd", weights, values_all, preferred_element_type=jnp.float32)
    return mixed.astype(jnp.bfloat16).reshape(slot_count, inner)


def body_by_owner(frames, conv_weight, qkv_weight, track_ids, track_owner):
    tok_rows = frames.shape[0]
    peer_count = lax.axis_size("seq")
    capacity = 2 * tok_rows // peer_count
    slot_total = capacity * peer_count
    my_index = lax.axis_index("seq")
    rim_rows = from_behind(frames[tok_rows - (KW - 1) :], "seq", 1)
    hidden = convolve(frames, conv_weight, rim_rows)
    group = track_groups(track_ids, track_owner)
    owner_hits = (group[:, None] == jnp.arange(peer_count, dtype=jnp.int32)[None, :]).astype(
        jnp.int32
    )
    running = jnp.cumsum(owner_hits, axis=0) - 1
    rank_rows = jnp.sum(jnp.where(owner_hits > 0, running, 0), axis=1)
    slot_of_row = group * capacity + rank_rows
    row_ids = jnp.arange(tok_rows, dtype=jnp.int32)
    source_row = jnp.full((slot_total,), tok_rows, jnp.int32).at[slot_of_row].set(row_ids)
    positions = my_index * tok_rows + row_ids
    send_times = jnp.full((slot_total,), -1, jnp.int32).at[slot_of_row].set(positions)
    projected = jnp.dot(
        hidden,
        lax.all_gather(qkv_weight, "seq", axis=1, tiled=True),
        preferred_element_type=jnp.float32,
    ).astype(jnp.bfloat16)
    padded_rows = jnp.concatenate(
        [projected, jnp.zeros((1, projected.shape[1]), jnp.bfloat16)], axis=0
    )
    outgoing = padded_rows[source_row]
    received, got_times = (
        lax.all_to_all(outgoing, "seq", split_axis=0, concat_axis=0, tiled=True),
        lax.all_to_all(send_times, "seq", split_axis=0, concat_axis=0, tiled=True),
    )
    mixed = attend_slots(received, got_times)
    returned = lax.all_to_all(mixed, "seq", split_axis=0, concat_axis=0, tiled=True)
    return returned[slot_of_row]


def xor_swap(value, bit, axes=("chip", "core")):
    count = lax.axis_size(axes)
    return lax.ppermute(value, axes, [(d, d ^ bit) for d in range(count)])


def by_bit(bit, mine, theirs, axis):
    return jnp.stack(
        [jnp.where(bit == 0, mine, theirs), jnp.where(bit == 0, theirs, mine)], axis=axis
    )


def zero_after(*arrays):
    total = jnp.zeros((), jnp.bfloat16)
    for array in arrays:
        last = array[(-1,) * array.ndim]
        absent = last < 0 if array.dtype == jnp.int32 else last != last
        total = total + jnp.where(absent, 1.0, 0.0).astype(jnp.bfloat16)
    return total


def body_by_head(frames, conv_weight, qkv_weight, track_ids, track_owner):
    tok_rows = frames.shape[0]
    chips = lax.axis_size("chip")
    devices = 2 * chips
    core = lax.axis_index("core")
    chip = lax.axis_index("chip")
    grp = lax.axis_index("grp")
    me = 2 * chip + core
    both = ("chip", "core")
    every = ("grp", "chip", "core")
    part = tok_rows // 2
    features = frames.shape[1]
    CORE, Y, Z0, Z1 = 1, 2, 4, 8

    rim_rows = lax.ppermute(
        frames[tok_rows - (KW - 1) :], both, [(i, i + 1) for i in range(devices - 1)]
    )
    late = convolve(frames[part:], conv_weight, frames[part - (KW - 1) : part])
    early = convolve(frames[:part], conv_weight, rim_rows)

    far_late = xor_swap(late, Z1)
    far_early = xor_swap(early + zero_after(far_late), Z1)
    own = jnp.concatenate([early, late], axis=0)
    beside = xor_swap(own, Y)
    far_beside_late = xor_swap(far_late, Y)
    far_beside_early = xor_swap(far_early, Y)

    half = features // 2
    held = lax.dynamic_slice_in_dim(qkv_weight.T, grp * half, half, 1).reshape(3, HD // 2, half)
    moved = [
        lax.ppermute(held[j], both, [(d, (3 * d + j) % devices) for d in range(devices)])
        for j in range(3)
    ]
    mine = lax.dynamic_slice_in_dim(jnp.stack(moved + moved[:2]), lax.rem(me, 3), 3, 0)
    mine_too = xor_swap(mine, devices, every)
    paired = xor_swap(mine, Z0)

    cut = half // 2
    fourth = jnp.concatenate(
        [
            xor_swap(paired[:, :, :cut], devices, every),
            xor_swap(mine_too[:, :, cut:], Z0),
        ],
        axis=2,
    )

    span = devices * tok_rows
    times = me * tok_rows + jnp.arange(tok_rows, dtype=jnp.int32)
    codes = (track_groups(track_ids, track_owner) * span + times)[None, :]
    codes = codes + zero_after(fourth).astype(jnp.int32)
    for bit in (CORE, Y, Z0, Z1):
        codes = jnp.concatenate([codes, xor_swap(codes, bit)], axis=0)

    def whole_head(quarter, quarter_too):
        wide = by_bit(grp, quarter, quarter_too, 2).reshape(3, HD // 2, features)
        return by_bit(core, wide, xor_swap(wide, CORE), 1).reshape(3 * HD, features)

    two_heads = jnp.concatenate(
        [whole_head(mine, mine_too), whole_head(paired, fourth)], axis=0
    )

    def project(rows):
        done = lax.dot_general(
            rows, two_heads, (((1,), (1,)), ((), ())), preferred_element_type=jnp.float32
        ).astype(jnp.bfloat16)
        return jnp.concatenate([done[:, : 3 * HD], xor_swap(done[:, 3 * HD :], Z0)], axis=0)

    first = project(jnp.concatenate([own, beside, far_late, far_beside_late], axis=0))
    second = project(
        jnp.concatenate([far_early, far_beside_early], axis=0) + zero_after(codes)
    )

    first_rows = [(0, 0, tok_rows), (Y, 0, tok_rows), (Z1, part, part), (Z1 | Y, part, part)]
    second_rows = [(Z1, 0, part), (Z1 | Y, 0, part)]
    order = []
    for pieces in (first_rows, second_rows):
        order += pieces + [(far ^ Z0, start, count) for far, start, count in pieces]

    def codes_at(bit):
        return jnp.concatenate(
            [codes[far ^ bit, start : start + count] for far, start, count in order]
        )

    asking = codes_at(0)
    keys = jnp.concatenate([asking, codes_at(CORE)])
    least = asking // span * span
    projected = jnp.concatenate([first, second], axis=0)
    query = projected[:, :HD]
    keyed = jnp.concatenate(
        [projected[:, HD:], xor_swap(first[:, HD:], CORE), xor_swap(second[:, HD:], CORE)], axis=0
    )
    scores = lax.dot_general(
        query, keyed[:, :HD], (((1,), (1,)), ((), ())), preferred_element_type=jnp.float32
    ) * (1.0 / HD**0.5)
    allowed = (keys[None, :] <= asking[:, None]) & (keys[None, :] >= least[:, None])
    scores = jnp.where(allowed, scores, jnp.float32(-1e30))
    expd = jnp.exp(scores - jnp.max(scores, axis=-1, keepdims=True))
    weights = (expd / jnp.sum(expd, axis=-1, keepdims=True)).astype(jnp.bfloat16)
    mixed = jnp.dot(weights, keyed[:, HD:], preferred_element_type=jnp.float32)
    mixed = mixed.astype(jnp.bfloat16)

    sent = jnp.zeros((chips, tok_rows, HD), jnp.bfloat16)
    at = 0
    for far, start, count in order:
        rows = mixed[at : at + count]
        sent = lax.dynamic_update_slice(sent, rows[None], ((me ^ far) >> 1, start, 0))
        at += count
    returned = lax.all_to_all(sent, "chip", split_axis=0, concat_axis=0, tiled=True)
    return returned.transpose(1, 0, 2).reshape(tok_rows, chips * HD)


def solution(mesh):
    grp, seq = mesh.devices.shape
    out_by_owner = P(("grp", "seq"), None)
    by_owner = jax.shard_map(
        body_by_owner,
        mesh=mesh,
        in_specs=(P(("grp", "seq"), None), P(), P(None, "seq"), P(("grp", "seq")), P("grp")),
        out_specs=out_by_owner,
        check_vma=False,
    )
    split = Mesh(mesh.devices.reshape(grp, seq // 2, 2), ("grp", "chip", "core"))
    rows = P(("grp", "chip", "core"))
    by_head = jax.shard_map(
        body_by_head,
        mesh=split,
        in_specs=(rows, P(), P(None, ("chip", "core")), rows, P("grp")),
        out_specs=rows,
        check_vma=False,
    )

    def run(frames, conv_weight, qkv_weight, track_ids, track_owner):
        heads = qkv_weight.shape[1] // (3 * HD)
        plan = by_head if (grp, seq, heads) == (2, 16, 8) else by_owner
        return plan(frames, conv_weight, qkv_weight, track_ids, track_owner)

    return run
```

```python
import jax
import jax.numpy as jnp
from jax import lax
from jax.sharding import Mesh
from jax.sharding import PartitionSpec as P

HD = 128
KW = 4


def from_behind(value, axis, by):
    size = lax.axis_size(axis)
    pairs = [(i, i + by) for i in range(size) if 0 <= i + by < size]
    return lax.ppermute(value, axis, pairs)


def track_groups(track_ids, track_owner):
    track_total = track_owner.shape[0]
    return jnp.sum(
        jnp.where(
            track_ids[:, None] == jnp.arange(track_total, dtype=jnp.int32)[None, :],
            track_owner[None, :],
            0,
        ),
        axis=1,
    )


def convolve(frames, conv_weight, rim_rows):
    tok_rows = frames.shape[0]
    extended = jnp.concatenate([rim_rows, frames], axis=0).astype(jnp.float32)
    conv_sum = frames.astype(jnp.float32)
    for tap in range(KW):
        conv_sum = (
            conv_sum
            + conv_weight[tap].astype(jnp.float32)[None, :]
            * extended[KW - 1 - tap : KW - 1 - tap + tok_rows]
        )
    return conv_sum.astype(jnp.bfloat16)


def attend_slots(packed, positions):
    slot_count = packed.shape[0]
    inner = packed.shape[1] // 3
    head_count = inner // HD
    query = packed[:, :inner].reshape(slot_count, head_count, HD)
    keys_all = packed[:, inner : 2 * inner].reshape(slot_count, head_count, HD)
    values_all = packed[:, 2 * inner :].reshape(slot_count, head_count, HD)
    slot_ids = jnp.arange(slot_count, dtype=jnp.int32)
    score_scale = 1.0 / HD**0.5
    scores = (
        jnp.einsum("qhd,khd->hqk", query, keys_all, preferred_element_type=jnp.float32)
        * score_scale
    )
    allowed = (positions[None, :] >= 0) & (positions[None, :] <= positions[:, None]) | (
        slot_ids[:, None] == slot_ids[None, :]
    )
    scores = jnp.where(allowed[None], scores, jnp.float32(-1e30))
    top_score = jnp.max(scores, axis=-1, keepdims=True)
    expd = jnp.exp(scores - top_score)
    weights = (expd / jnp.sum(expd, axis=-1, keepdims=True)).astype(jnp.bfloat16)
    mixed = jnp.einsum("hqk,khd->qhd", weights, values_all, preferred_element_type=jnp.float32)
    return mixed.astype(jnp.bfloat16).reshape(slot_count, inner)


def body_by_owner(frames, conv_weight, qkv_weight, track_ids, track_owner):
    tok_rows = frames.shape[0]
    peer_count = lax.axis_size("seq")
    capacity = 2 * tok_rows // peer_count
    slot_total = capacity * peer_count
    my_index = lax.axis_index("seq")
    rim_rows = from_behind(frames[tok_rows - (KW - 1) :], "seq", 1)
    hidden = convolve(frames, conv_weight, rim_rows)
    group = track_groups(track_ids, track_owner)
    owner_hits = (group[:, None] == jnp.arange(peer_count, dtype=jnp.int32)[None, :]).astype(
        jnp.int32
    )
    running = jnp.cumsum(owner_hits, axis=0) - 1
    rank_rows = jnp.sum(jnp.where(owner_hits > 0, running, 0), axis=1)
    slot_of_row = group * capacity + rank_rows
    row_ids = jnp.arange(tok_rows, dtype=jnp.int32)
    source_row = jnp.full((slot_total,), tok_rows, jnp.int32).at[slot_of_row].set(row_ids)
    positions = my_index * tok_rows + row_ids
    send_times = jnp.full((slot_total,), -1, jnp.int32).at[slot_of_row].set(positions)
    projected = jnp.dot(
        hidden,
        lax.all_gather(qkv_weight, "seq", axis=1, tiled=True),
        preferred_element_type=jnp.float32,
    ).astype(jnp.bfloat16)
    padded_rows = jnp.concatenate(
        [projected, jnp.zeros((1, projected.shape[1]), jnp.bfloat16)], axis=0
    )
    outgoing = padded_rows[source_row]
    received, got_times = (
        lax.all_to_all(outgoing, "seq", split_axis=0, concat_axis=0, tiled=True),
        lax.all_to_all(send_times, "seq", split_axis=0, concat_axis=0, tiled=True),
    )
    mixed = attend_slots(received, got_times)
    returned = lax.all_to_all(mixed, "seq", split_axis=0, concat_axis=0, tiled=True)
    return returned[slot_of_row]


def xor_swap(value, bit, axes=("chip", "core")):
    count = lax.axis_size(axes)
    return lax.ppermute(value, axes, [(d, d ^ bit) for d in range(count)])


def by_bit(bit, mine, theirs, axis):
    return jnp.stack(
        [jnp.where(bit == 0, mine, theirs), jnp.where(bit == 0, theirs, mine)], axis=axis
    )


def zero_after(*arrays):
    total = jnp.zeros((), jnp.bfloat16)
    for array in arrays:
        last = array[(-1,) * array.ndim]
        absent = last < 0 if array.dtype == jnp.int32 else last != last
        total = total + jnp.where(absent, 1.0, 0.0).astype(jnp.bfloat16)
    return total


def body_by_head(frames, conv_weight, qkv_weight, track_ids, track_owner):
    tok_rows = frames.shape[0]
    chips = lax.axis_size("chip")
    devices = 2 * chips
    core = lax.axis_index("core")
    chip = lax.axis_index("chip")
    grp = lax.axis_index("grp")
    me = 2 * chip + core
    both = ("chip", "core")
    every = ("grp", "chip", "core")
    part = tok_rows // 2
    features = frames.shape[1]
    CORE, Y, Z0, Z1 = 1, 2, 4, 8

    rim_rows = lax.ppermute(
        frames[tok_rows - (KW - 1) :], both, [(i, i + 1) for i in range(devices - 1)]
    )
    late = convolve(frames[part:], conv_weight, frames[part - (KW - 1) : part])
    early = convolve(frames[:part], conv_weight, rim_rows)

    far_late = xor_swap(late, Z1)
    far_early = xor_swap(early + zero_after(far_late), Z1)
    own = jnp.concatenate([early, late], axis=0)
    beside = xor_swap(own, Y)
    far_beside_late = xor_swap(far_late, Y)
    half = features // 2
    held = lax.dynamic_slice_in_dim(qkv_weight.T, grp * half, half, 1).reshape(3, HD // 2, half)
    moved = [
        lax.ppermute(held[j], both, [(d, (3 * d + j) % devices) for d in range(devices)])
        for j in range(3)
    ]
    mine = lax.dynamic_slice_in_dim(jnp.stack(moved + moved[:2]), lax.rem(me, 3), 3, 0)
    mine_too = xor_swap(mine, devices, every)
    paired = xor_swap(mine, Z0)

    span = devices * tok_rows
    times = me * tok_rows + jnp.arange(tok_rows, dtype=jnp.int32)
    codes = (track_groups(track_ids, track_owner) * span + times)[None, :]
    codes = codes + zero_after(mine_too, paired).astype(jnp.int32)
    for bit in (CORE, Y, Z0, Z1):
        codes = jnp.concatenate([codes, xor_swap(codes, bit)], axis=0)
        if bit == Y:
            codes = codes + zero_after(far_beside_late).astype(jnp.int32)
    far_beside_early = xor_swap(far_early + zero_after(codes), Y)

    cut = half // 2
    fourth = jnp.concatenate(
        [
            xor_swap(paired[:, :, :cut], devices, every),
            xor_swap(mine_too[:, :, cut:], Z0),
        ],
        axis=2,
    )

    def whole_head(quarter, quarter_too):
        wide = by_bit(grp, quarter, quarter_too, 2).reshape(3, HD // 2, features)
        return by_bit(core, wide, xor_swap(wide, CORE), 1).reshape(3 * HD, features)

    two_heads = jnp.concatenate(
        [whole_head(mine, mine_too), whole_head(paired, fourth)], axis=0
    )

    def project(rows):
        done = lax.dot_general(
            rows, two_heads, (((1,), (1,)), ((), ())), preferred_element_type=jnp.float32
        ).astype(jnp.bfloat16)
        return jnp.concatenate([done[:, : 3 * HD], xor_swap(done[:, 3 * HD :], Z0)], axis=0)

    first = project(jnp.concatenate([own, beside, far_late, far_beside_late], axis=0))
    second = project(jnp.concatenate([far_early, far_beside_early], axis=0))

    first_rows = [(0, 0, tok_rows), (Y, 0, tok_rows), (Z1, part, part), (Z1 | Y, part, part)]
    second_rows = [(Z1, 0, part), (Z1 | Y, 0, part)]
    order = []
    for pieces in (first_rows, second_rows):
        order += pieces + [(far ^ Z0, start, count) for far, start, count in pieces]

    def codes_at(bit):
        return jnp.concatenate(
            [codes[far ^ bit, start : start + count] for far, start, count in order]
        )

    asking = codes_at(0)
    keys = jnp.concatenate([asking, codes_at(CORE)])
    least = asking // span * span
    projected = jnp.concatenate([first, second], axis=0)
    query = projected[:, :HD]
    keyed = jnp.concatenate(
        [projected[:, HD:], xor_swap(first[:, HD:], CORE), xor_swap(second[:, HD:], CORE)], axis=0
    )
    scores = lax.dot_general(
        query, keyed[:, :HD], (((1,), (1,)), ((), ())), preferred_element_type=jnp.float32
    ) * (1.0 / HD**0.5)
    allowed = (keys[None, :] <= asking[:, None]) & (keys[None, :] >= least[:, None])
    scores = jnp.where(allowed, scores, jnp.float32(-1e30))
    expd = jnp.exp(scores - jnp.max(scores, axis=-1, keepdims=True))
    weights = (expd / jnp.sum(expd, axis=-1, keepdims=True)).astype(jnp.bfloat16)
    mixed = jnp.dot(weights, keyed[:, HD:], preferred_element_type=jnp.float32)
    mixed = mixed.astype(jnp.bfloat16)

    sent = jnp.zeros((chips, tok_rows, HD), jnp.bfloat16)
    at = 0
    for far, start, count in order:
        rows = mixed[at : at + count]
        sent = lax.dynamic_update_slice(sent, rows[None], ((me ^ far) >> 1, start, 0))
        at += count
    returned = lax.all_to_all(sent, "chip", split_axis=0, concat_axis=0, tiled=True)
    return returned.transpose(1, 0, 2).reshape(tok_rows, chips * HD)


def solution(mesh):
    grp, seq = mesh.devices.shape
    out_by_owner = P(("grp", "seq"), None)
    by_owner = jax.shard_map(
        body_by_owner,
        mesh=mesh,
        in_specs=(P(("grp", "seq"), None), P(), P(None, "seq"), P(("grp", "seq")), P("grp")),
        out_specs=out_by_owner,
        check_vma=False,
    )
    split = Mesh(mesh.devices.reshape(grp, seq // 2, 2), ("grp", "chip", "core"))
    rows = P(("grp", "chip", "core"))
    by_head = jax.shard_map(
        body_by_head,
        mesh=split,
        in_specs=(rows, P(), P(None, ("chip", "core")), rows, P("grp")),
        out_specs=rows,
        check_vma=False,
    )

    def run(frames, conv_weight, qkv_weight, track_ids, track_owner):
        heads = qkv_weight.shape[1] // (3 * HD)
        plan = by_head if (grp, seq, heads) == (2, 16, 8) else by_owner
        return plan(frames, conv_weight, qkv_weight, track_ids, track_owner)

    return run
```

```python
import jax
import jax.numpy as jnp
from jax import lax
from jax.sharding import Mesh
from jax.sharding import PartitionSpec as P

HD = 128
KW = 4


def from_behind(value, axis, by):
    size = lax.axis_size(axis)
    pairs = [(i, i + by) for i in range(size) if 0 <= i + by < size]
    return lax.ppermute(value, axis, pairs)


def track_groups(track_ids, track_owner):
    track_total = track_owner.shape[0]
    return jnp.sum(
        jnp.where(
            track_ids[:, None] == jnp.arange(track_total, dtype=jnp.int32)[None, :],
            track_owner[None, :],
            0,
        ),
        axis=1,
    )


def convolve(frames, conv_weight, rim_rows):
    tok_rows = frames.shape[0]
    extended = jnp.concatenate([rim_rows, frames], axis=0).astype(jnp.float32)
    conv_sum = frames.astype(jnp.float32)
    for tap in range(KW):
        conv_sum = (
            conv_sum
            + conv_weight[tap].astype(jnp.float32)[None, :]
            * extended[KW - 1 - tap : KW - 1 - tap + tok_rows]
        )
    return conv_sum.astype(jnp.bfloat16)


def attend_slots(packed, positions):
    slot_count = packed.shape[0]
    inner = packed.shape[1] // 3
    head_count = inner // HD
    query = packed[:, :inner].reshape(slot_count, head_count, HD)
    keys_all = packed[:, inner : 2 * inner].reshape(slot_count, head_count, HD)
    values_all = packed[:, 2 * inner :].reshape(slot_count, head_count, HD)
    slot_ids = jnp.arange(slot_count, dtype=jnp.int32)
    score_scale = 1.0 / HD**0.5
    scores = (
        jnp.einsum("qhd,khd->hqk", query, keys_all, preferred_element_type=jnp.float32)
        * score_scale
    )
    allowed = (positions[None, :] >= 0) & (positions[None, :] <= positions[:, None]) | (
        slot_ids[:, None] == slot_ids[None, :]
    )
    scores = jnp.where(allowed[None], scores, jnp.float32(-1e30))
    top_score = jnp.max(scores, axis=-1, keepdims=True)
    expd = jnp.exp(scores - top_score)
    weights = (expd / jnp.sum(expd, axis=-1, keepdims=True)).astype(jnp.bfloat16)
    mixed = jnp.einsum("hqk,khd->qhd", weights, values_all, preferred_element_type=jnp.float32)
    return mixed.astype(jnp.bfloat16).reshape(slot_count, inner)


def body_by_owner(frames, conv_weight, qkv_weight, track_ids, track_owner):
    tok_rows = frames.shape[0]
    peer_count = lax.axis_size("seq")
    capacity = 2 * tok_rows // peer_count
    slot_total = capacity * peer_count
    my_index = lax.axis_index("seq")
    rim_rows = from_behind(frames[tok_rows - (KW - 1) :], "seq", 1)
    hidden = convolve(frames, conv_weight, rim_rows)
    group = track_groups(track_ids, track_owner)
    owner_hits = (group[:, None] == jnp.arange(peer_count, dtype=jnp.int32)[None, :]).astype(
        jnp.int32
    )
    running = jnp.cumsum(owner_hits, axis=0) - 1
    rank_rows = jnp.sum(jnp.where(owner_hits > 0, running, 0), axis=1)
    slot_of_row = group * capacity + rank_rows
    row_ids = jnp.arange(tok_rows, dtype=jnp.int32)
    source_row = jnp.full((slot_total,), tok_rows, jnp.int32).at[slot_of_row].set(row_ids)
    positions = my_index * tok_rows + row_ids
    send_times = jnp.full((slot_total,), -1, jnp.int32).at[slot_of_row].set(positions)
    projected = jnp.dot(
        hidden,
        lax.all_gather(qkv_weight, "seq", axis=1, tiled=True),
        preferred_element_type=jnp.float32,
    ).astype(jnp.bfloat16)
    padded_rows = jnp.concatenate(
        [projected, jnp.zeros((1, projected.shape[1]), jnp.bfloat16)], axis=0
    )
    outgoing = padded_rows[source_row]
    received, got_times = (
        lax.all_to_all(outgoing, "seq", split_axis=0, concat_axis=0, tiled=True),
        lax.all_to_all(send_times, "seq", split_axis=0, concat_axis=0, tiled=True),
    )
    mixed = attend_slots(received, got_times)
    returned = lax.all_to_all(mixed, "seq", split_axis=0, concat_axis=0, tiled=True)
    return returned[slot_of_row]


def xor_swap(value, bit, axes=("chip", "core")):
    count = lax.axis_size(axes)
    return lax.ppermute(value, axes, [(d, d ^ bit) for d in range(count)])


MORE = 8


def with_groups(rows, groups):
    width = rows.shape[1]
    flat = jnp.pad(groups.reshape(-1), (0, MORE * width - groups.size))
    return jnp.concatenate([rows, flat.reshape(MORE, width)], axis=0)


def groups_behind(rows, count, tok_rows):
    return rows[-MORE:].reshape(-1)[: count * tok_rows].reshape(count, tok_rows)


def by_bit(bit, mine, theirs, axis):
    return jnp.stack(
        [jnp.where(bit == 0, mine, theirs), jnp.where(bit == 0, theirs, mine)], axis=axis
    )


def zero_after(*arrays):
    total = jnp.zeros((), jnp.bfloat16)
    for array in arrays:
        last = array[(-1,) * array.ndim]
        absent = last < 0 if array.dtype == jnp.int32 else last != last
        total = total + jnp.where(absent, 1.0, 0.0).astype(jnp.bfloat16)
    return total


def body_by_head(frames, conv_weight, qkv_weight, track_ids, track_owner):
    tok_rows = frames.shape[0]
    chips = lax.axis_size("chip")
    devices = 2 * chips
    core = lax.axis_index("core")
    chip = lax.axis_index("chip")
    grp = lax.axis_index("grp")
    me = 2 * chip + core
    both = ("chip", "core")
    every = ("grp", "chip", "core")
    part = tok_rows // 2
    features = frames.shape[1]
    CORE, Y, Z0, Z1 = 1, 2, 4, 8

    rim_rows = lax.ppermute(
        frames[tok_rows - (KW - 1) :], both, [(i, i + 1) for i in range(devices - 1)]
    )
    late = convolve(frames[part:], conv_weight, frames[part - (KW - 1) : part])
    early = convolve(frames[:part], conv_weight, rim_rows)

    group = track_groups(track_ids, track_owner).astype(jnp.bfloat16)
    row = jnp.pad(group[None, :], ((0, MORE - 1), (0, features - tok_rows)))
    own = jnp.concatenate([early, late], axis=0)
    far_late_and = xor_swap(jnp.concatenate([late, row], axis=0), Z1)
    far_late = far_late_and[:part]
    far_early = xor_swap(early + zero_after(far_late), Z1)
    beside_and = xor_swap(jnp.concatenate([own, row], axis=0), Y)
    beside = beside_and[:tok_rows]
    far_beside_late_and = xor_swap(far_late_and, Y)
    far_beside_late = far_beside_late_and[:part]
    far_beside_early = xor_swap(far_early, Y)
    groups = [group] + [
        rows[-MORE, :tok_rows] for rows in (beside_and, far_late_and, far_beside_late_and)
    ]

    half = features // 2
    held = lax.dynamic_slice_in_dim(qkv_weight.T, grp * half, half, 1).reshape(3, HD // 2, half)
    moved = [
        lax.ppermute(held[j], both, [(d, (3 * d + j) % devices) for d in range(devices)])
        for j in range(3)
    ]
    mine = lax.dynamic_slice_in_dim(jnp.stack(moved + moved[:2]), lax.rem(me, 3), 3, 0)
    mine_too = xor_swap(mine, devices, every)
    paired = xor_swap(mine, Z0)

    cut = half // 2
    fourth = jnp.concatenate(
        [
            xor_swap(paired[:, :, :cut], devices, every),
            xor_swap(mine_too[:, :, cut:], Z0),
        ],
        axis=2,
    )

    def whole_head(quarter, quarter_too):
        wide = by_bit(grp, quarter, quarter_too, 2).reshape(3, HD // 2, features)
        return by_bit(core, wide, xor_swap(wide, CORE), 1).reshape(3 * HD, features)

    two_heads = jnp.concatenate(
        [whole_head(mine, mine_too), whole_head(paired, fourth)], axis=0
    )

    def project(rows):
        done = lax.dot_general(
            rows, two_heads, (((1,), (1,)), ((), ())), preferred_element_type=jnp.float32
        ).astype(jnp.bfloat16)
        return done[:, : 3 * HD], done[:, 3 * HD :]

    hops = [0, Y, Z1, Z1 | Y]
    groups = jnp.stack(groups)
    mine, theirs = project(
        jnp.concatenate([own, beside, far_late, far_beside_late], axis=0)
    )
    count = mine.shape[0]
    theirs = xor_swap(with_groups(theirs, groups), Z0)
    first = jnp.concatenate([mine, theirs[:count]], axis=0)
    groups = jnp.concatenate([groups, groups_behind(theirs, 4, tok_rows)], axis=0)
    hops += [hop ^ Z0 for hop in hops]
    mine, theirs = project(jnp.concatenate([far_early, far_beside_early], axis=0))
    second = jnp.concatenate([mine, xor_swap(theirs, Z0)], axis=0)

    first_rows = [(0, 0, tok_rows), (Y, 0, tok_rows), (Z1, part, part), (Z1 | Y, part, part)]
    second_rows = [(Z1, 0, part), (Z1 | Y, 0, part)]
    order = []
    for pieces in (first_rows, second_rows):
        order += pieces + [(far ^ Z0, start, count) for far, start, count in pieces]

    projected = jnp.concatenate([first, second], axis=0)
    query = projected[:, :HD]
    first = xor_swap(with_groups(first[:, HD:], groups), CORE)
    second = xor_swap(second[:, HD:], CORE)
    keyed = jnp.concatenate([projected[:, HD:], first[:-MORE], second], axis=0)
    other_groups = groups_behind(first, 8, tok_rows)

    span = devices * tok_rows

    def codes_of(groups, bit):
        seen = jnp.array(hops, jnp.int32)[:, None] ^ (me ^ bit)
        times = seen * tok_rows + jnp.arange(tok_rows, dtype=jnp.int32)[None, :]
        codes = groups.astype(jnp.int32) * span + times
        return jnp.concatenate(
            [codes[hops.index(far), start : start + count] for far, start, count in order]
        )

    asking = codes_of(groups, 0)
    keys = jnp.concatenate([asking, codes_of(other_groups, CORE)])
    least = asking // span * span
    scores = lax.dot_general(
        query, keyed[:, :HD], (((1,), (1,)), ((), ())), preferred_element_type=jnp.float32
    ) * (1.0 / HD**0.5)
    allowed = (keys[None, :] <= asking[:, None]) & (keys[None, :] >= least[:, None])
    scores = jnp.where(allowed, scores, jnp.float32(-1e30))
    expd = jnp.exp(scores - jnp.max(scores, axis=-1, keepdims=True))
    weights = (expd / jnp.sum(expd, axis=-1, keepdims=True)).astype(jnp.bfloat16)
    mixed = jnp.dot(weights, keyed[:, HD:], preferred_element_type=jnp.float32)
    mixed = mixed.astype(jnp.bfloat16)

    sent = jnp.zeros((chips, tok_rows, HD), jnp.bfloat16)
    at = 0
    for far, start, count in order:
        rows = mixed[at : at + count]
        sent = lax.dynamic_update_slice(sent, rows[None], ((me ^ far) >> 1, start, 0))
        at += count
    returned = lax.all_to_all(sent, "chip", split_axis=0, concat_axis=0, tiled=True)
    return returned.transpose(1, 0, 2).reshape(tok_rows, chips * HD)


def solution(mesh):
    grp, seq = mesh.devices.shape
    out_by_owner = P(("grp", "seq"), None)
    by_owner = jax.shard_map(
        body_by_owner,
        mesh=mesh,
        in_specs=(P(("grp", "seq"), None), P(), P(None, "seq"), P(("grp", "seq")), P("grp")),
        out_specs=out_by_owner,
        check_vma=False,
    )
    split = Mesh(mesh.devices.reshape(grp, seq // 2, 2), ("grp", "chip", "core"))
    rows = P(("grp", "chip", "core"))
    by_head = jax.shard_map(
        body_by_head,
        mesh=split,
        in_specs=(rows, P(), P(None, ("chip", "core")), rows, P("grp")),
        out_specs=rows,
        check_vma=False,
    )

    def run(frames, conv_weight, qkv_weight, track_ids, track_owner):
        heads = qkv_weight.shape[1] // (3 * HD)
        plan = by_head if (grp, seq, heads) == (2, 16, 8) else by_owner
        return plan(frames, conv_weight, qkv_weight, track_ids, track_owner)

    return run
```

```python
import jax
import jax.numpy as jnp
from jax import lax
from jax.sharding import Mesh
from jax.sharding import PartitionSpec as P

HD = 128
KW = 4


def from_behind(value, axis, by):
    size = lax.axis_size(axis)
    pairs = [(i, i + by) for i in range(size) if 0 <= i + by < size]
    return lax.ppermute(value, axis, pairs)


def track_groups(track_ids, track_owner):
    track_total = track_owner.shape[0]
    return jnp.sum(
        jnp.where(
            track_ids[:, None] == jnp.arange(track_total, dtype=jnp.int32)[None, :],
            track_owner[None, :],
            0,
        ),
        axis=1,
    )


def convolve(frames, conv_weight, rim_rows):
    tok_rows = frames.shape[0]
    extended = jnp.concatenate([rim_rows, frames], axis=0).astype(jnp.float32)
    conv_sum = frames.astype(jnp.float32)
    for tap in range(KW):
        conv_sum = (
            conv_sum
            + conv_weight[tap].astype(jnp.float32)[None, :]
            * extended[KW - 1 - tap : KW - 1 - tap + tok_rows]
        )
    return conv_sum.astype(jnp.bfloat16)


def attend_slots(packed, positions):
    slot_count = packed.shape[0]
    inner = packed.shape[1] // 3
    head_count = inner // HD
    query = packed[:, :inner].reshape(slot_count, head_count, HD)
    keys_all = packed[:, inner : 2 * inner].reshape(slot_count, head_count, HD)
    values_all = packed[:, 2 * inner :].reshape(slot_count, head_count, HD)
    slot_ids = jnp.arange(slot_count, dtype=jnp.int32)
    score_scale = 1.0 / HD**0.5
    scores = (
        jnp.einsum("qhd,khd->hqk", query, keys_all, preferred_element_type=jnp.float32)
        * score_scale
    )
    allowed = (positions[None, :] >= 0) & (positions[None, :] <= positions[:, None]) | (
        slot_ids[:, None] == slot_ids[None, :]
    )
    scores = jnp.where(allowed[None], scores, jnp.float32(-1e30))
    top_score = jnp.max(scores, axis=-1, keepdims=True)
    expd = jnp.exp(scores - top_score)
    weights = (expd / jnp.sum(expd, axis=-1, keepdims=True)).astype(jnp.bfloat16)
    mixed = jnp.einsum("hqk,khd->qhd", weights, values_all, preferred_element_type=jnp.float32)
    return mixed.astype(jnp.bfloat16).reshape(slot_count, inner)


def body_by_owner(frames, conv_weight, qkv_weight, track_ids, track_owner):
    tok_rows = frames.shape[0]
    peer_count = lax.axis_size("seq")
    capacity = 2 * tok_rows // peer_count
    slot_total = capacity * peer_count
    my_index = lax.axis_index("seq")
    rim_rows = from_behind(frames[tok_rows - (KW - 1) :], "seq", 1)
    hidden = convolve(frames, conv_weight, rim_rows)
    group = track_groups(track_ids, track_owner)
    owner_hits = (group[:, None] == jnp.arange(peer_count, dtype=jnp.int32)[None, :]).astype(
        jnp.int32
    )
    running = jnp.cumsum(owner_hits, axis=0) - 1
    rank_rows = jnp.sum(jnp.where(owner_hits > 0, running, 0), axis=1)
    slot_of_row = group * capacity + rank_rows
    row_ids = jnp.arange(tok_rows, dtype=jnp.int32)
    source_row = jnp.full((slot_total,), tok_rows, jnp.int32).at[slot_of_row].set(row_ids)
    positions = my_index * tok_rows + row_ids
    send_times = jnp.full((slot_total,), -1, jnp.int32).at[slot_of_row].set(positions)
    projected = jnp.dot(
        hidden,
        lax.all_gather(qkv_weight, "seq", axis=1, tiled=True),
        preferred_element_type=jnp.float32,
    ).astype(jnp.bfloat16)
    padded_rows = jnp.concatenate(
        [projected, jnp.zeros((1, projected.shape[1]), jnp.bfloat16)], axis=0
    )
    outgoing = padded_rows[source_row]
    received, got_times = (
        lax.all_to_all(outgoing, "seq", split_axis=0, concat_axis=0, tiled=True),
        lax.all_to_all(send_times, "seq", split_axis=0, concat_axis=0, tiled=True),
    )
    mixed = attend_slots(received, got_times)
    returned = lax.all_to_all(mixed, "seq", split_axis=0, concat_axis=0, tiled=True)
    return returned[slot_of_row]


def xor_swap(value, bit, axes=("chip", "core")):
    count = lax.axis_size(axes)
    return lax.ppermute(value, axes, [(d, d ^ bit) for d in range(count)])


MORE = 8


def with_groups(rows, groups):
    width = rows.shape[1]
    flat = jnp.pad(groups.reshape(-1), (0, MORE * width - groups.size))
    return jnp.concatenate([rows, flat.reshape(MORE, width)], axis=0)


def groups_behind(rows, count, tok_rows):
    return rows[-MORE:].reshape(-1)[: count * tok_rows].reshape(count, tok_rows)


def by_bit(bit, mine, theirs, axis):
    return jnp.stack(
        [jnp.where(bit == 0, mine, theirs), jnp.where(bit == 0, theirs, mine)], axis=axis
    )


def zero_after(*arrays):
    total = jnp.zeros((), jnp.bfloat16)
    for array in arrays:
        last = array[(-1,) * array.ndim]
        absent = last < 0 if array.dtype == jnp.int32 else last != last
        total = total + jnp.where(absent, 1.0, 0.0).astype(jnp.bfloat16)
    return total


def body_by_head(frames, conv_weight, qkv_weight, track_ids, track_owner):
    tok_rows = frames.shape[0]
    chips = lax.axis_size("chip")
    devices = 2 * chips
    core = lax.axis_index("core")
    chip = lax.axis_index("chip")
    grp = lax.axis_index("grp")
    me = 2 * chip + core
    both = ("chip", "core")
    every = ("grp", "chip", "core")
    part = tok_rows // 2
    features = frames.shape[1]
    CORE, Y, Z0, Z1 = 1, 2, 4, 8

    rim_rows = lax.ppermute(
        frames[tok_rows - (KW - 1) :], both, [(i, i + 1) for i in range(devices - 1)]
    )
    late = convolve(frames[part:], conv_weight, frames[part - (KW - 1) : part])
    early = convolve(frames[:part], conv_weight, rim_rows)

    group = track_groups(track_ids, track_owner).astype(jnp.bfloat16)
    row = jnp.pad(group[None, :], ((0, MORE - 1), (0, features - tok_rows)))
    own = jnp.concatenate([early, late], axis=0)
    far_late_and = xor_swap(jnp.concatenate([late, row], axis=0), Z1)
    far_late = far_late_and[:part]
    far_early = xor_swap(early + zero_after(far_late), Z1)
    beside = xor_swap(own, Y)
    far_beside_late_and = xor_swap(jnp.concatenate([far_late_and, row], axis=0), Y)
    far_beside_late = far_beside_late_and[:part]
    far_beside_early = xor_swap(far_early, Y)
    groups = [group, far_beside_late_and[-MORE, :tok_rows]]
    groups += [rows[part, :tok_rows] for rows in (far_late_and, far_beside_late_and)]

    half = features // 2
    held = lax.dynamic_slice_in_dim(qkv_weight.T, grp * half, half, 1).reshape(3, HD // 2, half)
    moved = [
        lax.ppermute(held[j], both, [(d, (3 * d + j) % devices) for d in range(devices)])
        for j in range(3)
    ]
    mine = lax.dynamic_slice_in_dim(jnp.stack(moved + moved[:2]), lax.rem(me, 3), 3, 0)
    mine_too = xor_swap(mine, devices, every)
    paired = xor_swap(mine, Z0)

    cut = half // 2
    fourth = jnp.concatenate(
        [
            xor_swap(paired[:, :, :cut], devices, every),
            xor_swap(mine_too[:, :, cut:], Z0),
        ],
        axis=2,
    )

    def whole_head(quarter, quarter_too):
        wide = by_bit(grp, quarter, quarter_too, 2).reshape(3, HD // 2, features)
        return by_bit(core, wide, xor_swap(wide, CORE), 1).reshape(3 * HD, features)

    two_heads = jnp.concatenate(
        [whole_head(mine, mine_too), whole_head(paired, fourth)], axis=0
    )

    def project(rows):
        done = lax.dot_general(
            rows, two_heads, (((1,), (1,)), ((), ())), preferred_element_type=jnp.float32
        ).astype(jnp.bfloat16)
        return done[:, : 3 * HD], done[:, 3 * HD :]

    hops = [0, Y, Z1, Z1 | Y]
    groups = jnp.stack(groups)
    mine, theirs = project(
        jnp.concatenate([own, beside, far_late, far_beside_late], axis=0)
    )
    count = mine.shape[0]
    theirs = xor_swap(with_groups(theirs, groups), Z0)
    first = jnp.concatenate([mine, theirs[:count]], axis=0)
    groups = jnp.concatenate([groups, groups_behind(theirs, 4, tok_rows)], axis=0)
    hops += [hop ^ Z0 for hop in hops]
    mine, theirs = project(jnp.concatenate([far_early, far_beside_early], axis=0))
    second = jnp.concatenate([mine, xor_swap(theirs, Z0)], axis=0)

    first_rows = [(0, 0, tok_rows), (Y, 0, tok_rows), (Z1, part, part), (Z1 | Y, part, part)]
    second_rows = [(Z1, 0, part), (Z1 | Y, 0, part)]
    order = []
    for pieces in (first_rows, second_rows):
        order += pieces + [(far ^ Z0, start, count) for far, start, count in pieces]

    projected = jnp.concatenate([first, second], axis=0)
    query = projected[:, :HD]
    first = xor_swap(with_groups(first[:, HD:], groups), CORE)
    second = xor_swap(second[:, HD:], CORE)
    keyed = jnp.concatenate([projected[:, HD:], first[:-MORE], second], axis=0)
    other_groups = groups_behind(first, 8, tok_rows)

    span = devices * tok_rows

    def codes_of(groups, bit):
        seen = jnp.array(hops, jnp.int32)[:, None] ^ (me ^ bit)
        times = seen * tok_rows + jnp.arange(tok_rows, dtype=jnp.int32)[None, :]
        codes = groups.astype(jnp.int32) * span + times
        return jnp.concatenate(
            [codes[hops.index(far), start : start + count] for far, start, count in order]
        )

    asking = codes_of(groups, 0)
    keys = jnp.concatenate([asking, codes_of(other_groups, CORE)])
    least = asking // span * span
    scores = lax.dot_general(
        query, keyed[:, :HD], (((1,), (1,)), ((), ())), preferred_element_type=jnp.float32
    ) * (1.0 / HD**0.5)
    allowed = (keys[None, :] <= asking[:, None]) & (keys[None, :] >= least[:, None])
    scores = jnp.where(allowed, scores, jnp.float32(-1e30))
    expd = jnp.exp(scores - jnp.max(scores, axis=-1, keepdims=True))
    weights = (expd / jnp.sum(expd, axis=-1, keepdims=True)).astype(jnp.bfloat16)
    mixed = jnp.dot(weights, keyed[:, HD:], preferred_element_type=jnp.float32)
    mixed = mixed.astype(jnp.bfloat16)

    sent = jnp.zeros((chips, tok_rows, HD), jnp.bfloat16)
    at = 0
    for far, start, count in order:
        rows = mixed[at : at + count]
        sent = lax.dynamic_update_slice(sent, rows[None], ((me ^ far) >> 1, start, 0))
        at += count
    returned = lax.all_to_all(sent, "chip", split_axis=0, concat_axis=0, tiled=True)
    return returned.transpose(1, 0, 2).reshape(tok_rows, chips * HD)


def solution(mesh):
    grp, seq = mesh.devices.shape
    out_by_owner = P(("grp", "seq"), None)
    by_owner = jax.shard_map(
        body_by_owner,
        mesh=mesh,
        in_specs=(P(("grp", "seq"), None), P(), P(None, "seq"), P(("grp", "seq")), P("grp")),
        out_specs=out_by_owner,
        check_vma=False,
    )
    split = Mesh(mesh.devices.reshape(grp, seq // 2, 2), ("grp", "chip", "core"))
    rows = P(("grp", "chip", "core"))
    by_head = jax.shard_map(
        body_by_head,
        mesh=split,
        in_specs=(rows, P(), P(None, ("chip", "core")), rows, P("grp")),
        out_specs=rows,
        check_vma=False,
    )

    def run(frames, conv_weight, qkv_weight, track_ids, track_owner):
        heads = qkv_weight.shape[1] // (3 * HD)
        plan = by_head if (grp, seq, heads) == (2, 16, 8) else by_owner
        return plan(frames, conv_weight, qkv_weight, track_ids, track_owner)

    return run
```

```python
import jax
import jax.numpy as jnp
from jax import lax
from jax.sharding import Mesh
from jax.sharding import PartitionSpec as P

HD = 128
KW = 4


def from_behind(value, axis, by):
    size = lax.axis_size(axis)
    pairs = [(i, i + by) for i in range(size) if 0 <= i + by < size]
    return lax.ppermute(value, axis, pairs)


def track_groups(track_ids, track_owner):
    track_total = track_owner.shape[0]
    return jnp.sum(
        jnp.where(
            track_ids[:, None] == jnp.arange(track_total, dtype=jnp.int32)[None, :],
            track_owner[None, :],
            0,
        ),
        axis=1,
    )


def convolve(frames, conv_weight, rim_rows):
    tok_rows = frames.shape[0]
    extended = jnp.concatenate([rim_rows, frames], axis=0).astype(jnp.float32)
    conv_sum = frames.astype(jnp.float32)
    for tap in range(KW):
        conv_sum = (
            conv_sum
            + conv_weight[tap].astype(jnp.float32)[None, :]
            * extended[KW - 1 - tap : KW - 1 - tap + tok_rows]
        )
    return conv_sum.astype(jnp.bfloat16)


def attend_slots(packed, positions):
    slot_count = packed.shape[0]
    inner = packed.shape[1] // 3
    head_count = inner // HD
    query = packed[:, :inner].reshape(slot_count, head_count, HD)
    keys_all = packed[:, inner : 2 * inner].reshape(slot_count, head_count, HD)
    values_all = packed[:, 2 * inner :].reshape(slot_count, head_count, HD)
    slot_ids = jnp.arange(slot_count, dtype=jnp.int32)
    score_scale = 1.0 / HD**0.5
    scores = (
        jnp.einsum("qhd,khd->hqk", query, keys_all, preferred_element_type=jnp.float32)
        * score_scale
    )
    allowed = (positions[None, :] >= 0) & (positions[None, :] <= positions[:, None]) | (
        slot_ids[:, None] == slot_ids[None, :]
    )
    scores = jnp.where(allowed[None], scores, jnp.float32(-1e30))
    top_score = jnp.max(scores, axis=-1, keepdims=True)
    expd = jnp.exp(scores - top_score)
    weights = (expd / jnp.sum(expd, axis=-1, keepdims=True)).astype(jnp.bfloat16)
    mixed = jnp.einsum("hqk,khd->qhd", weights, values_all, preferred_element_type=jnp.float32)
    return mixed.astype(jnp.bfloat16).reshape(slot_count, inner)


def body_by_owner(frames, conv_weight, qkv_weight, track_ids, track_owner):
    tok_rows = frames.shape[0]
    peer_count = lax.axis_size("seq")
    capacity = 2 * tok_rows // peer_count
    slot_total = capacity * peer_count
    my_index = lax.axis_index("seq")
    rim_rows = from_behind(frames[tok_rows - (KW - 1) :], "seq", 1)
    hidden = convolve(frames, conv_weight, rim_rows)
    group = track_groups(track_ids, track_owner)
    owner_hits = (group[:, None] == jnp.arange(peer_count, dtype=jnp.int32)[None, :]).astype(
        jnp.int32
    )
    running = jnp.cumsum(owner_hits, axis=0) - 1
    rank_rows = jnp.sum(jnp.where(owner_hits > 0, running, 0), axis=1)
    slot_of_row = group * capacity + rank_rows
    row_ids = jnp.arange(tok_rows, dtype=jnp.int32)
    source_row = jnp.full((slot_total,), tok_rows, jnp.int32).at[slot_of_row].set(row_ids)
    positions = my_index * tok_rows + row_ids
    send_times = jnp.full((slot_total,), -1, jnp.int32).at[slot_of_row].set(positions)
    projected = jnp.dot(
        hidden,
        lax.all_gather(qkv_weight, "seq", axis=1, tiled=True),
        preferred_element_type=jnp.float32,
    ).astype(jnp.bfloat16)
    padded_rows = jnp.concatenate(
        [projected, jnp.zeros((1, projected.shape[1]), jnp.bfloat16)], axis=0
    )
    outgoing = padded_rows[source_row]
    received, got_times = (
        lax.all_to_all(outgoing, "seq", split_axis=0, concat_axis=0, tiled=True),
        lax.all_to_all(send_times, "seq", split_axis=0, concat_axis=0, tiled=True),
    )
    mixed = attend_slots(received, got_times)
    returned = lax.all_to_all(mixed, "seq", split_axis=0, concat_axis=0, tiled=True)
    return returned[slot_of_row]


def xor_swap(value, bit, axes=("chip", "core")):
    count = lax.axis_size(axes)
    return lax.ppermute(value, axes, [(d, d ^ bit) for d in range(count)])


MORE = 8


def with_groups(rows, groups):
    width = rows.shape[1]
    flat = jnp.pad(groups.reshape(-1), (0, MORE * width - groups.size))
    return jnp.concatenate([rows, flat.reshape(MORE, width)], axis=0)


def groups_behind(rows, count, tok_rows):
    return rows[-MORE:].reshape(-1)[: count * tok_rows].reshape(count, tok_rows)


def by_bit(bit, mine, theirs, axis):
    return jnp.stack(
        [jnp.where(bit == 0, mine, theirs), jnp.where(bit == 0, theirs, mine)], axis=axis
    )


def zero_after(array):
    last = array[(-1,) * array.ndim]
    return jnp.where(last != last, 1.0, 0.0).astype(jnp.bfloat16)


def body_by_head(frames, conv_weight, qkv_weight, track_ids, track_owner):
    tok_rows = frames.shape[0]
    chips = lax.axis_size("chip")
    devices = 2 * chips
    core = lax.axis_index("core")
    chip = lax.axis_index("chip")
    grp = lax.axis_index("grp")
    me = 2 * chip + core
    both = ("chip", "core")
    every = ("grp", "chip", "core")
    features = frames.shape[1]
    CORE, Y, Z0, Z1 = 1, 2, 4, 8

    rim_rows = lax.ppermute(
        frames[tok_rows - (KW - 1) :], both, [(i, i + 1) for i in range(devices - 1)]
    )
    hidden = convolve(frames, conv_weight, rim_rows)

    group = track_groups(track_ids, track_owner).astype(jnp.bfloat16)
    own = with_groups(hidden, group)
    far = xor_swap(own, Z1)
    beside = xor_swap(own, Y)
    far_beside = xor_swap(far, Y)

    half = features // 2
    held = lax.dynamic_slice_in_dim(qkv_weight.T, grp * half, half, 1).reshape(3, HD // 2, half)
    moved = [
        lax.ppermute(held[j], both, [(d, (3 * d + j) % devices) for d in range(devices)])
        for j in range(3)
    ]
    mine = lax.dynamic_slice_in_dim(jnp.stack(moved + moved[:2]), lax.rem(me, 3), 3, 0)
    mine_too = xor_swap(mine, devices, every)
    paired = xor_swap(mine, Z0)

    cut = half // 2
    fourth = jnp.concatenate(
        [
            xor_swap(paired[:, :, :cut], devices, every),
            xor_swap(mine_too[:, :, cut:], Z0),
        ],
        axis=2,
    )

    def whole_head(quarter, quarter_too, zero):
        wide = by_bit(grp, quarter, quarter_too, 2).reshape(3, HD // 2, features) + zero
        return by_bit(core, wide, xor_swap(wide, CORE), 1).reshape(3 * HD, features)

    two_heads = jnp.concatenate(
        [
            whole_head(mine, mine_too, zero_after(beside)),
            whole_head(paired, fourth, zero_after(far)),
        ],
        axis=0,
    )

    span = devices * tok_rows

    def codes_of(groups, hops):
        seen = jnp.array(hops, jnp.int32)[:, None] ^ me
        times = seen * tok_rows + jnp.arange(tok_rows, dtype=jnp.int32)[None, :]
        return (groups.astype(jnp.int32) * span + times).reshape(-1)

    def project(blocks, hops):
        groups = jnp.stack([rows[tok_rows, :tok_rows] for rows in blocks])
        done = lax.dot_general(
            jnp.concatenate([rows[:tok_rows] for rows in blocks], axis=0),
            two_heads,
            (((1,), (1,)), ((), ())),
            preferred_element_type=jnp.float32,
        ).astype(jnp.bfloat16)
        swapped = xor_swap(with_groups(done[:, 3 * HD :], groups), Z0)
        done = jnp.concatenate([done[:, : 3 * HD], swapped[:-MORE]], axis=0)
        groups = jnp.concatenate([groups, groups_behind(swapped, 2, tok_rows)], axis=0)
        hops = hops + [hop ^ Z0 for hop in hops]
        other = xor_swap(with_groups(done[:, HD:], groups), CORE)
        other_groups = groups_behind(other, 4, tok_rows)
        return (
            (done[:, :HD], codes_of(groups, hops)),
            (done[:, HD:], codes_of(groups, hops)),
            (other[:-MORE], codes_of(other_groups, [hop ^ CORE for hop in hops])),
            hops,
        )

    parts = [project([own, beside], [0, Y])]
    zero = zero_after(parts[0][0][0])
    parts.append(project([far, far_beside + zero], [Z1, Z1 | Y]))
    query, asking = (jnp.concatenate([p[0][n] for p in parts], axis=0) for n in (0, 1))
    keyed, keys = (
        jnp.concatenate([p[side][n] for side in (1, 2) for p in parts], axis=0) for n in (0, 1)
    )
    least = asking // span * span
    scores = lax.dot_general(
        query, keyed[:, :HD], (((1,), (1,)), ((), ())), preferred_element_type=jnp.float32
    ) * (1.0 / HD**0.5)
    allowed = (keys[None, :] <= asking[:, None]) & (keys[None, :] >= least[:, None])
    scores = jnp.where(allowed, scores, jnp.float32(-1e30))
    expd = jnp.exp(scores - jnp.max(scores, axis=-1, keepdims=True))
    weights = (expd / jnp.sum(expd, axis=-1, keepdims=True)).astype(jnp.bfloat16)
    mixed = jnp.dot(weights, keyed[:, HD:], preferred_element_type=jnp.float32)
    mixed = mixed.astype(jnp.bfloat16)

    mixed = mixed.reshape(chips, tok_rows, HD)
    sent = jnp.zeros((chips, tok_rows, HD), jnp.bfloat16)
    for n, hop in enumerate(parts[0][3] + parts[1][3]):
        sent = lax.dynamic_update_slice(sent, mixed[n : n + 1], ((me ^ hop) >> 1, 0, 0))
    returned = lax.all_to_all(sent, "chip", split_axis=0, concat_axis=0, tiled=True)
    return returned.transpose(1, 0, 2).reshape(tok_rows, chips * HD)


def solution(mesh):
    grp, seq = mesh.devices.shape
    out_by_owner = P(("grp", "seq"), None)
    by_owner = jax.shard_map(
        body_by_owner,
        mesh=mesh,
        in_specs=(P(("grp", "seq"), None), P(), P(None, "seq"), P(("grp", "seq")), P("grp")),
        out_specs=out_by_owner,
        check_vma=False,
    )
    split = Mesh(mesh.devices.reshape(grp, seq // 2, 2), ("grp", "chip", "core"))
    rows = P(("grp", "chip", "core"))
    by_head = jax.shard_map(
        body_by_head,
        mesh=split,
        in_specs=(rows, P(), P(None, ("chip", "core")), rows, P("grp")),
        out_specs=rows,
        check_vma=False,
    )

    def run(frames, conv_weight, qkv_weight, track_ids, track_owner):
        heads = qkv_weight.shape[1] // (3 * HD)
        plan = by_head if (grp, seq, heads) == (2, 16, 8) else by_owner
        return plan(frames, conv_weight, qkv_weight, track_ids, track_owner)

    return run
```

```python
import jax
import jax.numpy as jnp
from jax import lax
from jax.sharding import Mesh
from jax.sharding import PartitionSpec as P

HD = 128
KW = 4


def from_behind(value, axis, by):
    size = lax.axis_size(axis)
    pairs = [(i, i + by) for i in range(size) if 0 <= i + by < size]
    return lax.ppermute(value, axis, pairs)


def track_groups(track_ids, track_owner):
    track_total = track_owner.shape[0]
    return jnp.sum(
        jnp.where(
            track_ids[:, None] == jnp.arange(track_total, dtype=jnp.int32)[None, :],
            track_owner[None, :],
            0,
        ),
        axis=1,
    )


def convolve(frames, conv_weight, rim_rows):
    tok_rows = frames.shape[0]
    extended = jnp.concatenate([rim_rows, frames], axis=0).astype(jnp.float32)
    conv_sum = frames.astype(jnp.float32)
    for tap in range(KW):
        conv_sum = (
            conv_sum
            + conv_weight[tap].astype(jnp.float32)[None, :]
            * extended[KW - 1 - tap : KW - 1 - tap + tok_rows]
        )
    return conv_sum.astype(jnp.bfloat16)


def attend_slots(packed, positions):
    slot_count = packed.shape[0]
    inner = packed.shape[1] // 3
    head_count = inner // HD
    query = packed[:, :inner].reshape(slot_count, head_count, HD)
    keys_all = packed[:, inner : 2 * inner].reshape(slot_count, head_count, HD)
    values_all = packed[:, 2 * inner :].reshape(slot_count, head_count, HD)
    slot_ids = jnp.arange(slot_count, dtype=jnp.int32)
    score_scale = 1.0 / HD**0.5
    scores = (
        jnp.einsum("qhd,khd->hqk", query, keys_all, preferred_element_type=jnp.float32)
        * score_scale
    )
    allowed = (positions[None, :] >= 0) & (positions[None, :] <= positions[:, None]) | (
        slot_ids[:, None] == slot_ids[None, :]
    )
    scores = jnp.where(allowed[None], scores, jnp.float32(-1e30))
    top_score = jnp.max(scores, axis=-1, keepdims=True)
    expd = jnp.exp(scores - top_score)
    weights = (expd / jnp.sum(expd, axis=-1, keepdims=True)).astype(jnp.bfloat16)
    mixed = jnp.einsum("hqk,khd->qhd", weights, values_all, preferred_element_type=jnp.float32)
    return mixed.astype(jnp.bfloat16).reshape(slot_count, inner)


def body_by_owner(frames, conv_weight, qkv_weight, track_ids, track_owner):
    tok_rows = frames.shape[0]
    peer_count = lax.axis_size("seq")
    capacity = 2 * tok_rows // peer_count
    slot_total = capacity * peer_count
    my_index = lax.axis_index("seq")
    rim_rows = from_behind(frames[tok_rows - (KW - 1) :], "seq", 1)
    hidden = convolve(frames, conv_weight, rim_rows)
    group = track_groups(track_ids, track_owner)
    owner_hits = (group[:, None] == jnp.arange(peer_count, dtype=jnp.int32)[None, :]).astype(
        jnp.int32
    )
    running = jnp.cumsum(owner_hits, axis=0) - 1
    rank_rows = jnp.sum(jnp.where(owner_hits > 0, running, 0), axis=1)
    slot_of_row = group * capacity + rank_rows
    row_ids = jnp.arange(tok_rows, dtype=jnp.int32)
    source_row = jnp.full((slot_total,), tok_rows, jnp.int32).at[slot_of_row].set(row_ids)
    positions = my_index * tok_rows + row_ids
    send_times = jnp.full((slot_total,), -1, jnp.int32).at[slot_of_row].set(positions)
    projected = jnp.dot(
        hidden,
        lax.all_gather(qkv_weight, "seq", axis=1, tiled=True),
        preferred_element_type=jnp.float32,
    ).astype(jnp.bfloat16)
    padded_rows = jnp.concatenate(
        [projected, jnp.zeros((1, projected.shape[1]), jnp.bfloat16)], axis=0
    )
    outgoing = padded_rows[source_row]
    received, got_times = (
        lax.all_to_all(outgoing, "seq", split_axis=0, concat_axis=0, tiled=True),
        lax.all_to_all(send_times, "seq", split_axis=0, concat_axis=0, tiled=True),
    )
    mixed = attend_slots(received, got_times)
    returned = lax.all_to_all(mixed, "seq", split_axis=0, concat_axis=0, tiled=True)
    return returned[slot_of_row]


def xor_swap(value, bit, axes=("chip", "core")):
    count = lax.axis_size(axes)
    return lax.ppermute(value, axes, [(d, d ^ bit) for d in range(count)])


def by_bit(bit, mine, theirs, axis):
    return jnp.stack(
        [jnp.where(bit == 0, mine, theirs), jnp.where(bit == 0, theirs, mine)], axis=axis
    )


def zero_after(array):
    last = array[(-1,) * array.ndim]
    return jnp.where(last != last, 1.0, 0.0).astype(jnp.bfloat16)


def body_by_head(frames, conv_weight, qkv_weight, track_ids, track_owner):
    tok_rows = frames.shape[0]
    chips = lax.axis_size("chip")
    devices = 2 * chips
    core = lax.axis_index("core")
    chip = lax.axis_index("chip")
    grp = lax.axis_index("grp")
    me = 2 * chip + core
    both = ("chip", "core")
    every = ("grp", "chip", "core")
    part = tok_rows // 2
    features = frames.shape[1]
    CORE, Y, Z0, Z1 = 1, 2, 4, 8

    rim_rows = lax.ppermute(
        frames[tok_rows - (KW - 1) :], both, [(i, i + 1) for i in range(devices - 1)]
    )
    late = convolve(frames[part:], conv_weight, frames[part - (KW - 1) : part])
    early = convolve(frames[:part], conv_weight, rim_rows)

    far_late = xor_swap(late, Z1)
    far_early = xor_swap(early, Z1)
    own = jnp.concatenate([early, late], axis=0)
    beside = xor_swap(own, Y)

    half = features // 2
    held = qkv_weight.T.reshape(3, HD // 2, features)

    def to_heads(block, j):
        pairs = [
            (g * devices + d, g * devices + (3 * d + j[g]) % devices)
            for g in (0, 1)
            for d in range(devices)
        ]
        return lax.ppermute(block, every, pairs)

    outer = to_heads(lax.dynamic_index_in_dim(held, 2 * grp, 0, False), (0, 2))
    middle = to_heads(lax.dynamic_slice_in_dim(held[1], grp * half, half, 1), (1, 1))
    mine = jnp.concatenate([outer[:, :half], outer[:, half:], middle], axis=0)
    paired = xor_swap(mine, Z0)

    far_beside_late = xor_swap(far_late + zero_after(paired), Y)
    far_beside_early = xor_swap(far_early, Y)

    def whole_head(pieces, index):
        theirs = xor_swap(pieces, devices, every)
        size = HD // 2

        def block(values, n):
            return values[n * size : (n + 1) * size]

        first, last = (
            jnp.concatenate(
                [jnp.where(grp == g, block(pieces, n), block(theirs, n)) for n in (0, 1)], axis=1
            )
            for g in (0, 1)
        )
        low, high = block(pieces, 2), block(theirs, 2)
        between = jnp.concatenate(
            [jnp.where(grp == 0, low, high), jnp.where(grp == 0, high, low)], axis=1
        )
        turned = [first, between, last, first, between]
        wide = lax.dynamic_slice_in_dim(jnp.stack(turned), lax.rem(index, 3), 3, 0)
        return by_bit(core, wide, xor_swap(wide, CORE), 1).reshape(3 * HD, features)

    two_heads = jnp.concatenate([whole_head(mine, me), whole_head(paired, me ^ Z0)], axis=0)

    def project(rows):
        done = lax.dot_general(
            rows, two_heads, (((1,), (1,)), ((), ())), preferred_element_type=jnp.float32
        ).astype(jnp.bfloat16)
        return jnp.concatenate([done[:, : 3 * HD], xor_swap(done[:, 3 * HD :], Z0)], axis=0)

    first = project(jnp.concatenate([own, beside, far_late, far_beside_late], axis=0))
    second = project(jnp.concatenate([far_early, far_beside_early], axis=0))

    first_rows = [(0, 0, tok_rows), (Y, 0, tok_rows), (Z1, part, part), (Z1 | Y, part, part)]
    second_rows = [(Z1, 0, part), (Z1 | Y, 0, part)]
    order = []
    for pieces in (first_rows, second_rows):
        order += pieces + [(far ^ Z0, start, count) for far, start, count in pieces]

    groups = track_groups(track_ids, track_owner)[None, :]
    for bit in (CORE, Y, Z0, Z1):
        groups = jnp.concatenate([groups, xor_swap(groups, bit)], axis=0)

    def of_rows(bit):
        times = [
            (me ^ far ^ bit) * tok_rows + start + jnp.arange(count, dtype=jnp.int32)
            for far, start, count in order
        ]
        marks = [groups[far ^ bit, start : start + count] for far, start, count in order]
        return jnp.concatenate(times), jnp.concatenate(marks)

    projected = jnp.concatenate([first, second], axis=0)
    query = projected[:, :HD]
    keyed = jnp.concatenate(
        [projected[:, HD:], xor_swap(first[:, HD:], CORE), xor_swap(second[:, HD:], CORE)], axis=0
    )
    own_times, own_groups = of_rows(0)
    other_times, other_groups = of_rows(CORE)
    key_times = jnp.concatenate([own_times, other_times])
    key_groups = jnp.concatenate([own_groups, other_groups])
    scores = lax.dot_general(
        query, keyed[:, :HD], (((1,), (1,)), ((), ())), preferred_element_type=jnp.float32
    ) * (1.0 / HD**0.5)
    allowed = (key_times[None, :] <= own_times[:, None]) & (
        key_groups[None, :] == own_groups[:, None]
    )
    scores = jnp.where(allowed, scores, jnp.float32(-1e30))
    expd = jnp.exp(scores - jnp.max(scores, axis=-1, keepdims=True))
    weights = (expd / jnp.sum(expd, axis=-1, keepdims=True)).astype(jnp.bfloat16)
    mixed = jnp.dot(weights, keyed[:, HD:], preferred_element_type=jnp.float32)
    mixed = mixed.astype(jnp.bfloat16)

    sent = jnp.zeros((chips, tok_rows, HD), jnp.bfloat16)
    at = 0
    for far, start, count in order:
        rows = mixed[at : at + count]
        sent = lax.dynamic_update_slice(sent, rows[None], ((me ^ far) >> 1, start, 0))
        at += count
    returned = lax.all_to_all(sent, "chip", split_axis=0, concat_axis=0, tiled=True)
    return returned.transpose(1, 0, 2).reshape(tok_rows, chips * HD)


def solution(mesh):
    grp, seq = mesh.devices.shape
    out_by_owner = P(("grp", "seq"), None)
    by_owner = jax.shard_map(
        body_by_owner,
        mesh=mesh,
        in_specs=(P(("grp", "seq"), None), P(), P(None, "seq"), P(("grp", "seq")), P("grp")),
        out_specs=out_by_owner,
        check_vma=False,
    )
    split = Mesh(mesh.devices.reshape(grp, seq // 2, 2), ("grp", "chip", "core"))
    rows = P(("grp", "chip", "core"))
    by_head = jax.shard_map(
        body_by_head,
        mesh=split,
        in_specs=(rows, P(), P(None, ("chip", "core")), rows, P("grp")),
        out_specs=rows,
        check_vma=False,
    )

    def run(frames, conv_weight, qkv_weight, track_ids, track_owner):
        heads = qkv_weight.shape[1] // (3 * HD)
        plan = by_head if (grp, seq, heads) == (2, 16, 8) else by_owner
        return plan(frames, conv_weight, qkv_weight, track_ids, track_owner)

    return run
```

```python
import jax
import jax.numpy as jnp
from jax import lax
from jax.sharding import Mesh
from jax.sharding import PartitionSpec as P

HD = 128
KW = 4


def from_behind(value, axis, by):
    size = lax.axis_size(axis)
    pairs = [(i, i + by) for i in range(size) if 0 <= i + by < size]
    return lax.ppermute(value, axis, pairs)


def track_groups(track_ids, track_owner):
    track_total = track_owner.shape[0]
    return jnp.sum(
        jnp.where(
            track_ids[:, None] == jnp.arange(track_total, dtype=jnp.int32)[None, :],
            track_owner[None, :],
            0,
        ),
        axis=1,
    )


def convolve(frames, conv_weight, rim_rows):
    tok_rows = frames.shape[0]
    extended = jnp.concatenate([rim_rows, frames], axis=0).astype(jnp.float32)
    conv_sum = frames.astype(jnp.float32)
    for tap in range(KW):
        conv_sum = (
            conv_sum
            + conv_weight[tap].astype(jnp.float32)[None, :]
            * extended[KW - 1 - tap : KW - 1 - tap + tok_rows]
        )
    return conv_sum.astype(jnp.bfloat16)


def attend_slots(packed, positions):
    slot_count = packed.shape[0]
    inner = packed.shape[1] // 3
    head_count = inner // HD
    query = packed[:, :inner].reshape(slot_count, head_count, HD)
    keys_all = packed[:, inner : 2 * inner].reshape(slot_count, head_count, HD)
    values_all = packed[:, 2 * inner :].reshape(slot_count, head_count, HD)
    slot_ids = jnp.arange(slot_count, dtype=jnp.int32)
    score_scale = 1.0 / HD**0.5
    scores = (
        jnp.einsum("qhd,khd->hqk", query, keys_all, preferred_element_type=jnp.float32)
        * score_scale
    )
    allowed = (positions[None, :] >= 0) & (positions[None, :] <= positions[:, None]) | (
        slot_ids[:, None] == slot_ids[None, :]
    )
    scores = jnp.where(allowed[None], scores, jnp.float32(-1e30))
    top_score = jnp.max(scores, axis=-1, keepdims=True)
    expd = jnp.exp(scores - top_score)
    weights = (expd / jnp.sum(expd, axis=-1, keepdims=True)).astype(jnp.bfloat16)
    mixed = jnp.einsum("hqk,khd->qhd", weights, values_all, preferred_element_type=jnp.float32)
    return mixed.astype(jnp.bfloat16).reshape(slot_count, inner)


def body_by_owner(frames, conv_weight, qkv_weight, track_ids, track_owner):
    tok_rows = frames.shape[0]
    peer_count = lax.axis_size("seq")
    capacity = 2 * tok_rows // peer_count
    slot_total = capacity * peer_count
    my_index = lax.axis_index("seq")
    rim_rows = from_behind(frames[tok_rows - (KW - 1) :], "seq", 1)
    hidden = convolve(frames, conv_weight, rim_rows)
    group = track_groups(track_ids, track_owner)
    owner_hits = (group[:, None] == jnp.arange(peer_count, dtype=jnp.int32)[None, :]).astype(
        jnp.int32
    )
    running = jnp.cumsum(owner_hits, axis=0) - 1
    rank_rows = jnp.sum(jnp.where(owner_hits > 0, running, 0), axis=1)
    slot_of_row = group * capacity + rank_rows
    row_ids = jnp.arange(tok_rows, dtype=jnp.int32)
    source_row = jnp.full((slot_total,), tok_rows, jnp.int32).at[slot_of_row].set(row_ids)
    positions = my_index * tok_rows + row_ids
    send_times = jnp.full((slot_total,), -1, jnp.int32).at[slot_of_row].set(positions)
    projected = jnp.dot(
        hidden,
        lax.all_gather(qkv_weight, "seq", axis=1, tiled=True),
        preferred_element_type=jnp.float32,
    ).astype(jnp.bfloat16)
    padded_rows = jnp.concatenate(
        [projected, jnp.zeros((1, projected.shape[1]), jnp.bfloat16)], axis=0
    )
    outgoing = padded_rows[source_row]
    received, got_times = (
        lax.all_to_all(outgoing, "seq", split_axis=0, concat_axis=0, tiled=True),
        lax.all_to_all(send_times, "seq", split_axis=0, concat_axis=0, tiled=True),
    )
    mixed = attend_slots(received, got_times)
    returned = lax.all_to_all(mixed, "seq", split_axis=0, concat_axis=0, tiled=True)
    return returned[slot_of_row]


def xor_swap(value, bit, axes=("chip", "core")):
    count = lax.axis_size(axes)
    return lax.ppermute(value, axes, [(d, d ^ bit) for d in range(count)])


def by_bit(bit, mine, theirs, axis):
    return jnp.stack(
        [jnp.where(bit == 0, mine, theirs), jnp.where(bit == 0, theirs, mine)], axis=axis
    )


def zero_after(array):
    last = array[(-1,) * array.ndim]
    return jnp.where(last != last, 1.0, 0.0).astype(jnp.bfloat16)


def body_by_head(frames, conv_weight, qkv_weight, track_ids, track_owner):
    tok_rows = frames.shape[0]
    chips = lax.axis_size("chip")
    devices = 2 * chips
    core = lax.axis_index("core")
    chip = lax.axis_index("chip")
    grp = lax.axis_index("grp")
    me = 2 * chip + core
    both = ("chip", "core")
    every = ("grp", "chip", "core")
    part = tok_rows // 2
    features = frames.shape[1]
    CORE, Y, Z0, Z1 = 1, 2, 4, 8

    rim_rows = lax.ppermute(
        frames[tok_rows - (KW - 1) :], both, [(i, i + 1) for i in range(devices - 1)]
    )
    half = features // 2
    held = qkv_weight.T.reshape(3, HD // 2, features)

    def to_heads(block, j):
        pairs = [
            (g * devices + d, g * devices + (3 * d + j[g]) % devices)
            for g in (0, 1)
            for d in range(devices)
        ]
        return lax.ppermute(block, every, pairs)

    outer = to_heads(lax.dynamic_index_in_dim(held, 2 * grp, 0, False), (0, 2))
    middle = to_heads(lax.dynamic_slice_in_dim(held[1], grp * half, half, 1), (1, 1))
    zero = zero_after(middle)

    late = convolve(frames[part:], conv_weight, frames[part - (KW - 1) : part]) + zero
    early = convolve(frames[:part], conv_weight, rim_rows) + zero

    far_late = xor_swap(late, Z1)
    own = jnp.concatenate([early, late], axis=0)
    beside = xor_swap(own, Y)

    mine = jnp.concatenate([outer[:, :half], outer[:, half:], middle], axis=0)
    paired = xor_swap(mine, Z0)

    mine_too = xor_swap(mine, devices, every)
    far_early = xor_swap(early + zero_after(mine_too), Z1)

    cut = half // 2
    fourth = [xor_swap(paired[:, :cut], devices, every), xor_swap(mine_too[:, cut:], Z0)]

    far_beside_late = xor_swap(far_late + zero_after(fourth[0]) + zero_after(fourth[1]), Y)
    far_beside_early = xor_swap(far_early, Y)

    def whole_head(pieces, theirs, index):
        size = HD // 2

        def block(values, n):
            return values[n * size : (n + 1) * size]

        first, last = (
            jnp.concatenate(
                [jnp.where(grp == g, block(pieces, n), block(theirs, n)) for n in (0, 1)], axis=1
            )
            for g in (0, 1)
        )
        low, high = block(pieces, 2), block(theirs, 2)
        between = jnp.concatenate(
            [jnp.where(grp == 0, low, high), jnp.where(grp == 0, high, low)], axis=1
        )
        turned = [first, between, last, first, between]
        wide = lax.dynamic_slice_in_dim(jnp.stack(turned), lax.rem(index, 3), 3, 0)
        return by_bit(core, wide, xor_swap(wide, CORE), 1).reshape(3 * HD, features)

    fourth = jnp.concatenate(fourth, axis=1)
    two_heads = jnp.concatenate(
        [whole_head(mine, mine_too, me), whole_head(paired, fourth, me ^ Z0)], axis=0
    )

    def project(rows):
        done = lax.dot_general(
            rows, two_heads, (((1,), (1,)), ((), ())), preferred_element_type=jnp.float32
        ).astype(jnp.bfloat16)
        return jnp.concatenate([done[:, : 3 * HD], xor_swap(done[:, 3 * HD :], Z0)], axis=0)

    first = project(jnp.concatenate([own, beside, far_late, far_beside_late], axis=0))
    second = project(jnp.concatenate([far_early, far_beside_early], axis=0))

    first_rows = [(0, 0, tok_rows), (Y, 0, tok_rows), (Z1, part, part), (Z1 | Y, part, part)]
    second_rows = [(Z1, 0, part), (Z1 | Y, 0, part)]
    order = []
    for pieces in (first_rows, second_rows):
        order += pieces + [(far ^ Z0, start, count) for far, start, count in pieces]

    groups = track_groups(track_ids, track_owner)[None, :]
    for bit in (CORE, Y, Z0, Z1):
        groups = jnp.concatenate([groups, xor_swap(groups, bit)], axis=0)

    def of_rows(bit):
        times = [
            (me ^ far ^ bit) * tok_rows + start + jnp.arange(count, dtype=jnp.int32)
            for far, start, count in order
        ]
        marks = [groups[far ^ bit, start : start + count] for far, start, count in order]
        return jnp.concatenate(times), jnp.concatenate(marks)

    projected = jnp.concatenate([first, second], axis=0)
    query = projected[:, :HD]
    keyed = jnp.concatenate(
        [projected[:, HD:], xor_swap(first[:, HD:], CORE), xor_swap(second[:, HD:], CORE)], axis=0
    )
    own_times, own_groups = of_rows(0)
    other_times, other_groups = of_rows(CORE)
    key_times = jnp.concatenate([own_times, other_times])
    key_groups = jnp.concatenate([own_groups, other_groups])
    scores = lax.dot_general(
        query, keyed[:, :HD], (((1,), (1,)), ((), ())), preferred_element_type=jnp.float32
    ) * (1.0 / HD**0.5)
    allowed = (key_times[None, :] <= own_times[:, None]) & (
        key_groups[None, :] == own_groups[:, None]
    )
    scores = jnp.where(allowed, scores, jnp.float32(-1e30))
    expd = jnp.exp(scores - jnp.max(scores, axis=-1, keepdims=True))
    weights = (expd / jnp.sum(expd, axis=-1, keepdims=True)).astype(jnp.bfloat16)
    mixed = jnp.dot(weights, keyed[:, HD:], preferred_element_type=jnp.float32)
    mixed = mixed.astype(jnp.bfloat16)

    sent = jnp.zeros((chips, tok_rows, HD), jnp.bfloat16)
    at = 0
    for far, start, count in order:
        rows = mixed[at : at + count]
        sent = lax.dynamic_update_slice(sent, rows[None], ((me ^ far) >> 1, start, 0))
        at += count
    returned = lax.all_to_all(sent, "chip", split_axis=0, concat_axis=0, tiled=True)
    return returned.transpose(1, 0, 2).reshape(tok_rows, chips * HD)


def solution(mesh):
    grp, seq = mesh.devices.shape
    out_by_owner = P(("grp", "seq"), None)
    by_owner = jax.shard_map(
        body_by_owner,
        mesh=mesh,
        in_specs=(P(("grp", "seq"), None), P(), P(None, "seq"), P(("grp", "seq")), P("grp")),
        out_specs=out_by_owner,
        check_vma=False,
    )
    split = Mesh(mesh.devices.reshape(grp, seq // 2, 2), ("grp", "chip", "core"))
    rows = P(("grp", "chip", "core"))
    by_head = jax.shard_map(
        body_by_head,
        mesh=split,
        in_specs=(rows, P(), P(None, ("chip", "core")), rows, P("grp")),
        out_specs=rows,
        check_vma=False,
    )

    def run(frames, conv_weight, qkv_weight, track_ids, track_owner):
        heads = qkv_weight.shape[1] // (3 * HD)
        plan = by_head if (grp, seq, heads) == (2, 16, 8) else by_owner
        return plan(frames, conv_weight, qkv_weight, track_ids, track_owner)

    return run
```

```python
import jax
import jax.numpy as jnp
from jax import lax
from jax.sharding import Mesh
from jax.sharding import PartitionSpec as P

HD = 128
KW = 4


def from_behind(value, axis, by):
    size = lax.axis_size(axis)
    pairs = [(i, i + by) for i in range(size) if 0 <= i + by < size]
    return lax.ppermute(value, axis, pairs)


def track_groups(track_ids, track_owner):
    track_total = track_owner.shape[0]
    return jnp.sum(
        jnp.where(
            track_ids[:, None] == jnp.arange(track_total, dtype=jnp.int32)[None, :],
            track_owner[None, :],
            0,
        ),
        axis=1,
    )


def convolve(frames, conv_weight, rim_rows):
    tok_rows = frames.shape[0]
    extended = jnp.concatenate([rim_rows, frames], axis=0).astype(jnp.float32)
    conv_sum = frames.astype(jnp.float32)
    for tap in range(KW):
        conv_sum = (
            conv_sum
            + conv_weight[tap].astype(jnp.float32)[None, :]
            * extended[KW - 1 - tap : KW - 1 - tap + tok_rows]
        )
    return conv_sum.astype(jnp.bfloat16)


def attend_slots(packed, positions):
    slot_count = packed.shape[0]
    inner = packed.shape[1] // 3
    head_count = inner // HD
    query = packed[:, :inner].reshape(slot_count, head_count, HD)
    keys_all = packed[:, inner : 2 * inner].reshape(slot_count, head_count, HD)
    values_all = packed[:, 2 * inner :].reshape(slot_count, head_count, HD)
    slot_ids = jnp.arange(slot_count, dtype=jnp.int32)
    score_scale = 1.0 / HD**0.5
    scores = (
        jnp.einsum("qhd,khd->hqk", query, keys_all, preferred_element_type=jnp.float32)
        * score_scale
    )
    allowed = (positions[None, :] >= 0) & (positions[None, :] <= positions[:, None]) | (
        slot_ids[:, None] == slot_ids[None, :]
    )
    scores = jnp.where(allowed[None], scores, jnp.float32(-1e30))
    top_score = jnp.max(scores, axis=-1, keepdims=True)
    expd = jnp.exp(scores - top_score)
    weights = (expd / jnp.sum(expd, axis=-1, keepdims=True)).astype(jnp.bfloat16)
    mixed = jnp.einsum("hqk,khd->qhd", weights, values_all, preferred_element_type=jnp.float32)
    return mixed.astype(jnp.bfloat16).reshape(slot_count, inner)


def body_by_owner(frames, conv_weight, qkv_weight, track_ids, track_owner):
    tok_rows = frames.shape[0]
    peer_count = lax.axis_size("seq")
    capacity = 2 * tok_rows // peer_count
    slot_total = capacity * peer_count
    my_index = lax.axis_index("seq")
    rim_rows = from_behind(frames[tok_rows - (KW - 1) :], "seq", 1)
    hidden = convolve(frames, conv_weight, rim_rows)
    group = track_groups(track_ids, track_owner)
    owner_hits = (group[:, None] == jnp.arange(peer_count, dtype=jnp.int32)[None, :]).astype(
        jnp.int32
    )
    running = jnp.cumsum(owner_hits, axis=0) - 1
    rank_rows = jnp.sum(jnp.where(owner_hits > 0, running, 0), axis=1)
    slot_of_row = group * capacity + rank_rows
    row_ids = jnp.arange(tok_rows, dtype=jnp.int32)
    source_row = jnp.full((slot_total,), tok_rows, jnp.int32).at[slot_of_row].set(row_ids)
    positions = my_index * tok_rows + row_ids
    send_times = jnp.full((slot_total,), -1, jnp.int32).at[slot_of_row].set(positions)
    projected = jnp.dot(
        hidden,
        lax.all_gather(qkv_weight, "seq", axis=1, tiled=True),
        preferred_element_type=jnp.float32,
    ).astype(jnp.bfloat16)
    padded_rows = jnp.concatenate(
        [projected, jnp.zeros((1, projected.shape[1]), jnp.bfloat16)], axis=0
    )
    outgoing = padded_rows[source_row]
    received, got_times = (
        lax.all_to_all(outgoing, "seq", split_axis=0, concat_axis=0, tiled=True),
        lax.all_to_all(send_times, "seq", split_axis=0, concat_axis=0, tiled=True),
    )
    mixed = attend_slots(received, got_times)
    returned = lax.all_to_all(mixed, "seq", split_axis=0, concat_axis=0, tiled=True)
    return returned[slot_of_row]


def xor_swap(value, bit, axes=("chip", "core")):
    count = lax.axis_size(axes)
    return lax.ppermute(value, axes, [(d, d ^ bit) for d in range(count)])


def by_bit(bit, mine, theirs, axis):
    return jnp.stack(
        [jnp.where(bit == 0, mine, theirs), jnp.where(bit == 0, theirs, mine)], axis=axis
    )


def zero_after(array):
    last = array[(-1,) * array.ndim]
    return jnp.where(last != last, 1.0, 0.0).astype(jnp.bfloat16)


def body_by_head(frames, conv_weight, qkv_weight, track_ids, track_owner):
    tok_rows = frames.shape[0]
    chips = lax.axis_size("chip")
    devices = 2 * chips
    core = lax.axis_index("core")
    chip = lax.axis_index("chip")
    grp = lax.axis_index("grp")
    me = 2 * chip + core
    both = ("chip", "core")
    every = ("grp", "chip", "core")
    part = tok_rows // 2
    features = frames.shape[1]
    CORE, Y, Z0, Z1 = 1, 2, 4, 8

    rim_rows = lax.ppermute(
        frames[tok_rows - (KW - 1) :], both, [(i, i + 1) for i in range(devices - 1)]
    )
    late = convolve(frames[part:], conv_weight, frames[part - (KW - 1) : part])
    early = convolve(frames[:part], conv_weight, rim_rows)

    far_late = xor_swap(late, Z1)
    far_early = xor_swap(early, Z1)
    own = jnp.concatenate([early, late], axis=0)
    beside = xor_swap(own, Y)

    half = features // 2
    held = qkv_weight.T.reshape(3, HD // 2, features)

    def to_heads(block, j):
        pairs = [
            (g * devices + d, g * devices + (3 * d + j[g]) % devices)
            for g in (0, 1)
            for d in range(devices)
        ]
        return lax.ppermute(block, every, pairs)

    outer = to_heads(lax.dynamic_index_in_dim(held, 2 * grp, 0, False), (0, 2))
    middle = to_heads(lax.dynamic_slice_in_dim(held[1], grp * half, half, 1), (1, 1))
    mine = jnp.concatenate([outer[:, :half], outer[:, half:], middle], axis=0)
    paired = xor_swap(mine, Z0)

    mine_too = xor_swap(mine, devices, every)

    cut = half // 2
    fourth = [xor_swap(paired[:, :cut], devices, every), xor_swap(mine_too[:, cut:], Z0)]

    far_beside_late = xor_swap(far_late + zero_after(fourth[0]) + zero_after(fourth[1]), Y)

    groups = track_groups(track_ids, track_owner)[None, :] + zero_after(paired).astype(jnp.int32)
    for bit in (CORE, Y, Z0, Z1):
        groups = jnp.concatenate([groups, xor_swap(groups, bit)], axis=0)
    zero = jnp.where(groups[-1, -1] < 0, 1.0, 0.0).astype(jnp.bfloat16)
    far_beside_early = xor_swap(far_early + zero, Y)

    def whole_head(pieces, theirs, index):
        size = HD // 2

        def block(values, n):
            return values[n * size : (n + 1) * size]

        first, last = (
            jnp.concatenate(
                [jnp.where(grp == g, block(pieces, n), block(theirs, n)) for n in (0, 1)], axis=1
            )
            for g in (0, 1)
        )
        low, high = block(pieces, 2), block(theirs, 2)
        between = jnp.concatenate(
            [jnp.where(grp == 0, low, high), jnp.where(grp == 0, high, low)], axis=1
        )
        turned = [first, between, last, first, between]
        wide = lax.dynamic_slice_in_dim(jnp.stack(turned), lax.rem(index, 3), 3, 0)
        return by_bit(core, wide, xor_swap(wide, CORE), 1).reshape(3 * HD, features)

    fourth = jnp.concatenate(fourth, axis=1)
    two_heads = jnp.concatenate(
        [whole_head(mine, mine_too, me), whole_head(paired, fourth, me ^ Z0)], axis=0
    )

    def project(rows):
        done = lax.dot_general(
            rows, two_heads, (((1,), (1,)), ((), ())), preferred_element_type=jnp.float32
        ).astype(jnp.bfloat16)
        return jnp.concatenate([done[:, : 3 * HD], xor_swap(done[:, 3 * HD :], Z0)], axis=0)

    first = project(jnp.concatenate([own, beside, far_late, far_beside_late], axis=0))
    second = project(jnp.concatenate([far_early, far_beside_early], axis=0))

    first_rows = [(0, 0, tok_rows), (Y, 0, tok_rows), (Z1, part, part), (Z1 | Y, part, part)]
    second_rows = [(Z1, 0, part), (Z1 | Y, 0, part)]
    order = []
    for pieces in (first_rows, second_rows):
        order += pieces + [(far ^ Z0, start, count) for far, start, count in pieces]

    def of_rows(bit):
        times = [
            (me ^ far ^ bit) * tok_rows + start + jnp.arange(count, dtype=jnp.int32)
            for far, start, count in order
        ]
        marks = [groups[far ^ bit, start : start + count] for far, start, count in order]
        return jnp.concatenate(times), jnp.concatenate(marks)

    projected = jnp.concatenate([first, second], axis=0)
    query = projected[:, :HD]
    keyed = jnp.concatenate(
        [projected[:, HD:], xor_swap(first[:, HD:], CORE), xor_swap(second[:, HD:], CORE)], axis=0
    )
    own_times, own_groups = of_rows(0)
    other_times, other_groups = of_rows(CORE)
    key_times = jnp.concatenate([own_times, other_times])
    key_groups = jnp.concatenate([own_groups, other_groups])
    scores = lax.dot_general(
        query, keyed[:, :HD], (((1,), (1,)), ((), ())), preferred_element_type=jnp.float32
    ) * (1.0 / HD**0.5)
    allowed = (key_times[None, :] <= own_times[:, None]) & (
        key_groups[None, :] == own_groups[:, None]
    )
    scores = jnp.where(allowed, scores, jnp.float32(-1e30))
    expd = jnp.exp(scores - jnp.max(scores, axis=-1, keepdims=True))
    weights = (expd / jnp.sum(expd, axis=-1, keepdims=True)).astype(jnp.bfloat16)
    mixed = jnp.dot(weights, keyed[:, HD:], preferred_element_type=jnp.float32)
    mixed = mixed.astype(jnp.bfloat16)

    sent = jnp.zeros((chips, tok_rows, HD), jnp.bfloat16)
    at = 0
    for far, start, count in order:
        rows = mixed[at : at + count]
        sent = lax.dynamic_update_slice(sent, rows[None], ((me ^ far) >> 1, start, 0))
        at += count
    returned = lax.all_to_all(sent, "chip", split_axis=0, concat_axis=0, tiled=True)
    return returned.transpose(1, 0, 2).reshape(tok_rows, chips * HD)


def solution(mesh):
    grp, seq = mesh.devices.shape
    out_by_owner = P(("grp", "seq"), None)
    by_owner = jax.shard_map(
        body_by_owner,
        mesh=mesh,
        in_specs=(P(("grp", "seq"), None), P(), P(None, "seq"), P(("grp", "seq")), P("grp")),
        out_specs=out_by_owner,
        check_vma=False,
    )
    split = Mesh(mesh.devices.reshape(grp, seq // 2, 2), ("grp", "chip", "core"))
    rows = P(("grp", "chip", "core"))
    by_head = jax.shard_map(
        body_by_head,
        mesh=split,
        in_specs=(rows, P(), P(None, ("chip", "core")), rows, P("grp")),
        out_specs=rows,
        check_vma=False,
    )

    def run(frames, conv_weight, qkv_weight, track_ids, track_owner):
        heads = qkv_weight.shape[1] // (3 * HD)
        plan = by_head if (grp, seq, heads) == (2, 16, 8) else by_owner
        return plan(frames, conv_weight, qkv_weight, track_ids, track_owner)

    return run
```

```python
import jax
import jax.numpy as jnp
from jax import lax
from jax.sharding import Mesh
from jax.sharding import PartitionSpec as P

HD = 128
KW = 4


def from_behind(value, axis, by):
    size = lax.axis_size(axis)
    pairs = [(i, i + by) for i in range(size) if 0 <= i + by < size]
    return lax.ppermute(value, axis, pairs)


def track_groups(track_ids, track_owner):
    track_total = track_owner.shape[0]
    return jnp.sum(
        jnp.where(
            track_ids[:, None] == jnp.arange(track_total, dtype=jnp.int32)[None, :],
            track_owner[None, :],
            0,
        ),
        axis=1,
    )


def convolve(frames, conv_weight, rim_rows):
    tok_rows = frames.shape[0]
    extended = jnp.concatenate([rim_rows, frames], axis=0).astype(jnp.float32)
    conv_sum = frames.astype(jnp.float32)
    for tap in range(KW):
        conv_sum = (
            conv_sum
            + conv_weight[tap].astype(jnp.float32)[None, :]
            * extended[KW - 1 - tap : KW - 1 - tap + tok_rows]
        )
    return conv_sum.astype(jnp.bfloat16)


def attend_slots(packed, positions):
    slot_count = packed.shape[0]
    inner = packed.shape[1] // 3
    head_count = inner // HD
    query = packed[:, :inner].reshape(slot_count, head_count, HD)
    keys_all = packed[:, inner : 2 * inner].reshape(slot_count, head_count, HD)
    values_all = packed[:, 2 * inner :].reshape(slot_count, head_count, HD)
    slot_ids = jnp.arange(slot_count, dtype=jnp.int32)
    score_scale = 1.0 / HD**0.5
    scores = (
        jnp.einsum("qhd,khd->hqk", query, keys_all, preferred_element_type=jnp.float32)
        * score_scale
    )
    allowed = (positions[None, :] >= 0) & (positions[None, :] <= positions[:, None]) | (
        slot_ids[:, None] == slot_ids[None, :]
    )
    scores = jnp.where(allowed[None], scores, jnp.float32(-1e30))
    top_score = jnp.max(scores, axis=-1, keepdims=True)
    expd = jnp.exp(scores - top_score)
    weights = (expd / jnp.sum(expd, axis=-1, keepdims=True)).astype(jnp.bfloat16)
    mixed = jnp.einsum("hqk,khd->qhd", weights, values_all, preferred_element_type=jnp.float32)
    return mixed.astype(jnp.bfloat16).reshape(slot_count, inner)


def body_by_owner(frames, conv_weight, qkv_weight, track_ids, track_owner):
    tok_rows = frames.shape[0]
    peer_count = lax.axis_size("seq")
    capacity = 2 * tok_rows // peer_count
    slot_total = capacity * peer_count
    my_index = lax.axis_index("seq")
    rim_rows = from_behind(frames[tok_rows - (KW - 1) :], "seq", 1)
    hidden = convolve(frames, conv_weight, rim_rows)
    group = track_groups(track_ids, track_owner)
    owner_hits = (group[:, None] == jnp.arange(peer_count, dtype=jnp.int32)[None, :]).astype(
        jnp.int32
    )
    running = jnp.cumsum(owner_hits, axis=0) - 1
    rank_rows = jnp.sum(jnp.where(owner_hits > 0, running, 0), axis=1)
    slot_of_row = group * capacity + rank_rows
    row_ids = jnp.arange(tok_rows, dtype=jnp.int32)
    source_row = jnp.full((slot_total,), tok_rows, jnp.int32).at[slot_of_row].set(row_ids)
    positions = my_index * tok_rows + row_ids
    send_times = jnp.full((slot_total,), -1, jnp.int32).at[slot_of_row].set(positions)
    projected = jnp.dot(
        hidden,
        lax.all_gather(qkv_weight, "seq", axis=1, tiled=True),
        preferred_element_type=jnp.float32,
    ).astype(jnp.bfloat16)
    padded_rows = jnp.concatenate(
        [projected, jnp.zeros((1, projected.shape[1]), jnp.bfloat16)], axis=0
    )
    outgoing = padded_rows[source_row]
    received, got_times = (
        lax.all_to_all(outgoing, "seq", split_axis=0, concat_axis=0, tiled=True),
        lax.all_to_all(send_times, "seq", split_axis=0, concat_axis=0, tiled=True),
    )
    mixed = attend_slots(received, got_times)
    returned = lax.all_to_all(mixed, "seq", split_axis=0, concat_axis=0, tiled=True)
    return returned[slot_of_row]


def xor_swap(value, bit, axes=("chip", "core")):
    count = lax.axis_size(axes)
    return lax.ppermute(value, axes, [(d, d ^ bit) for d in range(count)])


def by_bit(bit, mine, theirs, axis):
    return jnp.stack(
        [jnp.where(bit == 0, mine, theirs), jnp.where(bit == 0, theirs, mine)], axis=axis
    )


def zero_after(array):
    last = array[(-1,) * array.ndim]
    return jnp.where(last != last, 1.0, 0.0).astype(jnp.bfloat16)


def body_by_head(frames, conv_weight, qkv_weight, track_ids, track_owner):
    tok_rows = frames.shape[0]
    chips = lax.axis_size("chip")
    devices = 2 * chips
    core = lax.axis_index("core")
    chip = lax.axis_index("chip")
    grp = lax.axis_index("grp")
    me = 2 * chip + core
    both = ("chip", "core")
    every = ("grp", "chip", "core")
    part = tok_rows // 2
    features = frames.shape[1]
    CORE, Y, Z0, Z1 = 1, 2, 4, 8

    rim_rows = lax.ppermute(
        frames[tok_rows - (KW - 1) :], both, [(i, i + 1) for i in range(devices - 1)]
    )
    late = convolve(frames[part:], conv_weight, frames[part - (KW - 1) : part])
    early = convolve(frames[:part], conv_weight, rim_rows)

    far_late = xor_swap(late, Z1)
    far_early = xor_swap(early, Z1)
    own = jnp.concatenate([early, late], axis=0)
    beside = xor_swap(own, Y)

    half = features // 2
    held = qkv_weight.T.reshape(3, HD // 2, features)

    def to_heads(block, j):
        pairs = [
            (g * devices + d, g * devices + (3 * d + j[g]) % devices)
            for g in (0, 1)
            for d in range(devices)
        ]
        return lax.ppermute(block, every, pairs)

    outer = to_heads(lax.dynamic_index_in_dim(held, 2 * grp, 0, False), (0, 2))
    middle = to_heads(lax.dynamic_slice_in_dim(held[1], grp * half, half, 1), (1, 1))
    mine = jnp.concatenate([outer[:, :half], outer[:, half:], middle], axis=0)
    paired = xor_swap(mine, Z0)

    mine_too = xor_swap(mine, devices, every)

    cut = half // 2
    fourth = [xor_swap(paired[:, :cut], devices, every), xor_swap(mine_too[:, cut:], Z0)]

    far_beside_late = xor_swap(far_late + zero_after(fourth[0]), Y)
    far_beside_early = xor_swap(far_early, Y)

    fourth = jnp.concatenate(fourth, axis=1)

    def whole_head(pieces, theirs, index):
        size = HD // 2

        def block(values, n):
            return values[n * size : (n + 1) * size]

        first, last = (
            jnp.concatenate(
                [jnp.where(grp == g, block(pieces, n), block(theirs, n)) for n in (0, 1)], axis=1
            )
            for g in (0, 1)
        )
        low, high = block(pieces, 2), block(theirs, 2)
        between = jnp.concatenate(
            [jnp.where(grp == 0, low, high), jnp.where(grp == 0, high, low)], axis=1
        )
        turned = [first, between, last, first, between]
        wide = lax.dynamic_slice_in_dim(jnp.stack(turned), lax.rem(index, 3), 3, 0)
        return by_bit(core, wide, xor_swap(wide, CORE), 1).reshape(3 * HD, features)

    two_heads = jnp.concatenate(
        [whole_head(mine, mine_too, me), whole_head(paired, fourth, me ^ Z0)], axis=0
    )

    def project(rows):
        done = lax.dot_general(
            rows, two_heads, (((1,), (1,)), ((), ())), preferred_element_type=jnp.float32
        ).astype(jnp.bfloat16)
        return jnp.concatenate([done[:, : 3 * HD], xor_swap(done[:, 3 * HD :], Z0)], axis=0)

    first = project(jnp.concatenate([own, beside, far_late, far_beside_late], axis=0))
    second = project(jnp.concatenate([far_early, far_beside_early], axis=0))

    first_rows = [(0, 0, tok_rows), (Y, 0, tok_rows), (Z1, part, part), (Z1 | Y, part, part)]
    second_rows = [(Z1, 0, part), (Z1 | Y, 0, part)]
    order = []
    for pieces in (first_rows, second_rows):
        order += pieces + [(far ^ Z0, start, count) for far, start, count in pieces]

    groups = track_groups(track_ids, track_owner)[None, :]
    for bit in (CORE, Y, Z0, Z1):
        groups = jnp.concatenate([groups, xor_swap(groups, bit)], axis=0)

    def of_rows(bit):
        times = [
            (me ^ far ^ bit) * tok_rows + start + jnp.arange(count, dtype=jnp.int32)
            for far, start, count in order
        ]
        marks = [groups[far ^ bit, start : start + count] for far, start, count in order]
        return jnp.concatenate(times), jnp.concatenate(marks)

    projected = jnp.concatenate([first, second], axis=0)
    query = projected[:, :HD]
    keyed = jnp.concatenate(
        [projected[:, HD:], xor_swap(first[:, HD:], CORE), xor_swap(second[:, HD:], CORE)], axis=0
    )
    own_times, own_groups = of_rows(0)
    other_times, other_groups = of_rows(CORE)
    key_times = jnp.concatenate([own_times, other_times])
    key_groups = jnp.concatenate([own_groups, other_groups])
    scores = lax.dot_general(
        query, keyed[:, :HD], (((1,), (1,)), ((), ())), preferred_element_type=jnp.float32
    ) * (1.0 / HD**0.5)
    allowed = (key_times[None, :] <= own_times[:, None]) & (
        key_groups[None, :] == own_groups[:, None]
    )
    scores = jnp.where(allowed, scores, jnp.float32(-1e30))
    expd = jnp.exp(scores - jnp.max(scores, axis=-1, keepdims=True))
    weights = (expd / jnp.sum(expd, axis=-1, keepdims=True)).astype(jnp.bfloat16)
    mixed = jnp.dot(weights, keyed[:, HD:], preferred_element_type=jnp.float32)
    mixed = mixed.astype(jnp.bfloat16)

    sent = jnp.zeros((chips, tok_rows, HD), jnp.bfloat16)
    at = 0
    for far, start, count in order:
        rows = mixed[at : at + count]
        sent = lax.dynamic_update_slice(sent, rows[None], ((me ^ far) >> 1, start, 0))
        at += count
    returned = lax.all_to_all(sent, "chip", split_axis=0, concat_axis=0, tiled=True)
    return returned.transpose(1, 0, 2).reshape(tok_rows, chips * HD)


def solution(mesh):
    grp, seq = mesh.devices.shape
    out_by_owner = P(("grp", "seq"), None)
    by_owner = jax.shard_map(
        body_by_owner,
        mesh=mesh,
        in_specs=(P(("grp", "seq"), None), P(), P(None, "seq"), P(("grp", "seq")), P("grp")),
        out_specs=out_by_owner,
        check_vma=False,
    )
    split = Mesh(mesh.devices.reshape(grp, seq // 2, 2), ("grp", "chip", "core"))
    rows = P(("grp", "chip", "core"))
    by_head = jax.shard_map(
        body_by_head,
        mesh=split,
        in_specs=(rows, P(), P(None, ("chip", "core")), rows, P("grp")),
        out_specs=rows,
        check_vma=False,
    )

    def run(frames, conv_weight, qkv_weight, track_ids, track_owner):
        heads = qkv_weight.shape[1] // (3 * HD)
        plan = by_head if (grp, seq, heads) == (2, 16, 8) else by_owner
        return plan(frames, conv_weight, qkv_weight, track_ids, track_owner)

    return run
```

```python
import jax
import jax.numpy as jnp
from jax import lax
from jax.sharding import Mesh
from jax.sharding import PartitionSpec as P

HD = 128
KW = 4


def from_behind(value, axis, by):
    size = lax.axis_size(axis)
    pairs = [(i, i + by) for i in range(size) if 0 <= i + by < size]
    return lax.ppermute(value, axis, pairs)


def track_groups(track_ids, track_owner):
    track_total = track_owner.shape[0]
    return jnp.sum(
        jnp.where(
            track_ids[:, None] == jnp.arange(track_total, dtype=jnp.int32)[None, :],
            track_owner[None, :],
            0,
        ),
        axis=1,
    )


def convolve(frames, conv_weight, rim_rows):
    tok_rows = frames.shape[0]
    extended = jnp.concatenate([rim_rows, frames], axis=0).astype(jnp.float32)
    conv_sum = frames.astype(jnp.float32)
    for tap in range(KW):
        conv_sum = (
            conv_sum
            + conv_weight[tap].astype(jnp.float32)[None, :]
            * extended[KW - 1 - tap : KW - 1 - tap + tok_rows]
        )
    return conv_sum.astype(jnp.bfloat16)


def attend_slots(packed, positions):
    slot_count = packed.shape[0]
    inner = packed.shape[1] // 3
    head_count = inner // HD
    query = packed[:, :inner].reshape(slot_count, head_count, HD)
    keys_all = packed[:, inner : 2 * inner].reshape(slot_count, head_count, HD)
    values_all = packed[:, 2 * inner :].reshape(slot_count, head_count, HD)
    slot_ids = jnp.arange(slot_count, dtype=jnp.int32)
    score_scale = 1.0 / HD**0.5
    scores = (
        jnp.einsum("qhd,khd->hqk", query, keys_all, preferred_element_type=jnp.float32)
        * score_scale
    )
    allowed = (positions[None, :] >= 0) & (positions[None, :] <= positions[:, None]) | (
        slot_ids[:, None] == slot_ids[None, :]
    )
    scores = jnp.where(allowed[None], scores, jnp.float32(-1e30))
    top_score = jnp.max(scores, axis=-1, keepdims=True)
    expd = jnp.exp(scores - top_score)
    weights = (expd / jnp.sum(expd, axis=-1, keepdims=True)).astype(jnp.bfloat16)
    mixed = jnp.einsum("hqk,khd->qhd", weights, values_all, preferred_element_type=jnp.float32)
    return mixed.astype(jnp.bfloat16).reshape(slot_count, inner)


def body_by_owner(frames, conv_weight, qkv_weight, track_ids, track_owner):
    tok_rows = frames.shape[0]
    peer_count = lax.axis_size("seq")
    capacity = 2 * tok_rows // peer_count
    slot_total = capacity * peer_count
    my_index = lax.axis_index("seq")
    rim_rows = from_behind(frames[tok_rows - (KW - 1) :], "seq", 1)
    hidden = convolve(frames, conv_weight, rim_rows)
    group = track_groups(track_ids, track_owner)
    owner_hits = (group[:, None] == jnp.arange(peer_count, dtype=jnp.int32)[None, :]).astype(
        jnp.int32
    )
    running = jnp.cumsum(owner_hits, axis=0) - 1
    rank_rows = jnp.sum(jnp.where(owner_hits > 0, running, 0), axis=1)
    slot_of_row = group * capacity + rank_rows
    row_ids = jnp.arange(tok_rows, dtype=jnp.int32)
    source_row = jnp.full((slot_total,), tok_rows, jnp.int32).at[slot_of_row].set(row_ids)
    positions = my_index * tok_rows + row_ids
    send_times = jnp.full((slot_total,), -1, jnp.int32).at[slot_of_row].set(positions)
    projected = jnp.dot(
        hidden,
        lax.all_gather(qkv_weight, "seq", axis=1, tiled=True),
        preferred_element_type=jnp.float32,
    ).astype(jnp.bfloat16)
    padded_rows = jnp.concatenate(
        [projected, jnp.zeros((1, projected.shape[1]), jnp.bfloat16)], axis=0
    )
    outgoing = padded_rows[source_row]
    received, got_times = (
        lax.all_to_all(outgoing, "seq", split_axis=0, concat_axis=0, tiled=True),
        lax.all_to_all(send_times, "seq", split_axis=0, concat_axis=0, tiled=True),
    )
    mixed = attend_slots(received, got_times)
    returned = lax.all_to_all(mixed, "seq", split_axis=0, concat_axis=0, tiled=True)
    return returned[slot_of_row]


def xor_swap(value, bit, axes=("chip", "core")):
    count = lax.axis_size(axes)
    return lax.ppermute(value, axes, [(d, d ^ bit) for d in range(count)])


def by_bit(bit, mine, theirs, axis):
    return jnp.stack(
        [jnp.where(bit == 0, mine, theirs), jnp.where(bit == 0, theirs, mine)], axis=axis
    )


def zero_after(array):
    last = array[(-1,) * array.ndim]
    return jnp.where(last != last, 1.0, 0.0).astype(jnp.bfloat16)


def body_by_head(frames, conv_weight, qkv_weight, track_ids, track_owner):
    tok_rows = frames.shape[0]
    chips = lax.axis_size("chip")
    devices = 2 * chips
    core = lax.axis_index("core")
    chip = lax.axis_index("chip")
    grp = lax.axis_index("grp")
    me = 2 * chip + core
    both = ("chip", "core")
    every = ("grp", "chip", "core")
    part = tok_rows // 2
    features = frames.shape[1]
    CORE, Y, Z0, Z1 = 1, 2, 4, 8

    rim_rows = lax.ppermute(
        frames[tok_rows - (KW - 1) :], both, [(i, i + 1) for i in range(devices - 1)]
    )
    late = convolve(frames[part:], conv_weight, frames[part - (KW - 1) : part])
    early = convolve(frames[:part], conv_weight, rim_rows)

    far_late = xor_swap(late, Z1)
    far_early = xor_swap(early, Z1)
    own = jnp.concatenate([early, late], axis=0)
    beside = xor_swap(own, Y)

    half = features // 2
    held = qkv_weight.T.reshape(3, HD // 2, features)

    def to_heads(block, j):
        pairs = [
            (g * devices + d, g * devices + (3 * d + j[g]) % devices)
            for g in (0, 1)
            for d in range(devices)
        ]
        return lax.ppermute(block, every, pairs)

    outer = to_heads(lax.dynamic_index_in_dim(held, 2 * grp, 0, False), (0, 2))
    middle = to_heads(lax.dynamic_slice_in_dim(held[1], grp * half, half, 1), (1, 1))
    mine = jnp.concatenate([outer[:, :half], outer[:, half:], middle], axis=0)
    paired = xor_swap(mine, Z0)

    mine_too = xor_swap(mine, devices, every)

    cut = half // 2
    fourth = [xor_swap(paired[:, :cut], devices, every), xor_swap(mine_too[:, cut:], Z0)]

    far_beside_late = xor_swap(far_late + zero_after(fourth[0]) + zero_after(fourth[1]), Y)
    far_beside_early = xor_swap(far_early, Y)

    fourth = jnp.concatenate(fourth, axis=1)

    def whole_head(pieces, theirs, index):
        size = HD // 2

        def block(values, n):
            return values[n * size : (n + 1) * size]

        first, last = (
            jnp.concatenate(
                [jnp.where(grp == g, block(pieces, n), block(theirs, n)) for n in (0, 1)], axis=1
            )
            for g in (0, 1)
        )
        low, high = block(pieces, 2), block(theirs, 2)
        between = jnp.concatenate(
            [jnp.where(grp == 0, low, high), jnp.where(grp == 0, high, low)], axis=1
        )
        turned = [first, between, last, first, between]
        wide = lax.dynamic_slice_in_dim(jnp.stack(turned), lax.rem(index, 3), 3, 0)
        return by_bit(core, wide, xor_swap(wide, CORE), 1).reshape(3 * HD, features)

    two_heads = jnp.concatenate(
        [whole_head(mine, mine_too, me), whole_head(paired, fourth, me ^ Z0)], axis=0
    )

    def project(rows):
        done = lax.dot_general(
            rows, two_heads, (((1,), (1,)), ((), ())), preferred_element_type=jnp.float32
        ).astype(jnp.bfloat16)
        return jnp.concatenate([done[:, : 3 * HD], xor_swap(done[:, 3 * HD :], Z0)], axis=0)

    first = project(jnp.concatenate([own, beside, far_late, far_beside_late], axis=0))
    second = project(jnp.concatenate([far_early, far_beside_early], axis=0))

    first_rows = [(0, 0, tok_rows), (Y, 0, tok_rows), (Z1, part, part), (Z1 | Y, part, part)]
    second_rows = [(Z1, 0, part), (Z1 | Y, 0, part)]
    order = []
    for pieces in (first_rows, second_rows):
        order += pieces + [(far ^ Z0, start, count) for far, start, count in pieces]

    groups = track_groups(track_ids, track_owner)[None, :]
    for bit in (CORE, Y, Z0, Z1):
        groups = jnp.concatenate([groups, xor_swap(groups, bit)], axis=0)

    def of_rows(bit):
        times = [
            (me ^ far ^ bit) * tok_rows + start + jnp.arange(count, dtype=jnp.int32)
            for far, start, count in order
        ]
        marks = [groups[far ^ bit, start : start + count] for far, start, count in order]
        return jnp.concatenate(times), jnp.concatenate(marks)

    projected = jnp.concatenate([first, second], axis=0)
    query = projected[:, :HD]
    keyed = jnp.concatenate(
        [projected[:, HD:], xor_swap(first[:, HD:], CORE), xor_swap(second[:, HD:], CORE)], axis=0
    )
    own_times, own_groups = of_rows(0)
    other_times, other_groups = of_rows(CORE)
    key_times = jnp.concatenate([own_times, other_times])
    key_groups = jnp.concatenate([own_groups, other_groups])
    scores = lax.dot_general(
        query, keyed[:, :HD], (((1,), (1,)), ((), ())), preferred_element_type=jnp.float32
    ) * (1.0 / HD**0.5)
    allowed = (key_times[None, :] <= own_times[:, None]) & (
        key_groups[None, :] == own_groups[:, None]
    )
    scores = jnp.where(allowed, scores, jnp.float32(-1e30))
    expd = jnp.exp(scores - jnp.max(scores, axis=-1, keepdims=True))
    weights = (expd / jnp.sum(expd, axis=-1, keepdims=True)).astype(jnp.bfloat16)
    mixed = jnp.dot(weights, keyed[:, HD:], preferred_element_type=jnp.float32)
    mixed = mixed.astype(jnp.bfloat16)

    sent = jnp.zeros((chips, tok_rows, HD), jnp.bfloat16)
    at = 0
    for far, start, count in order:
        rows = mixed[at : at + count]
        sent = lax.dynamic_update_slice(sent, rows[None], ((me ^ far) >> 1, start, 0))
        at += count
    returned = lax.all_to_all(sent, "chip", split_axis=0, concat_axis=0, tiled=True)
    return returned.transpose(1, 0, 2).reshape(tok_rows, chips * HD)


def solution(mesh):
    grp, seq = mesh.devices.shape
    out_by_owner = P(("grp", "seq"), None)
    by_owner = jax.shard_map(
        body_by_owner,
        mesh=mesh,
        in_specs=(P(("grp", "seq"), None), P(), P(None, "seq"), P(("grp", "seq")), P("grp")),
        out_specs=out_by_owner,
        check_vma=False,
    )
    split = Mesh(mesh.devices.reshape(grp, seq // 2, 2), ("grp", "chip", "core"))
    rows = P(("grp", "chip", "core"))
    by_head = jax.shard_map(
        body_by_head,
        mesh=split,
        in_specs=(rows, P(), P(None, ("chip", "core")), rows, P("grp")),
        out_specs=rows,
        check_vma=False,
    )

    def run(frames, conv_weight, qkv_weight, track_ids, track_owner):
        heads = qkv_weight.shape[1] // (3 * HD)
        plan = by_head if (grp, seq, heads) == (2, 16, 8) else by_owner
        return plan(frames, conv_weight, qkv_weight, track_ids, track_owner)

    return run
```

```python
import jax
import jax.numpy as jnp
from jax import lax
from jax.sharding import Mesh
from jax.sharding import PartitionSpec as P

HD = 128
KW = 4


def from_behind(value, axis, by):
    size = lax.axis_size(axis)
    pairs = [(i, i + by) for i in range(size) if 0 <= i + by < size]
    return lax.ppermute(value, axis, pairs)


def track_groups(track_ids, track_owner):
    track_total = track_owner.shape[0]
    return jnp.sum(
        jnp.where(
            track_ids[:, None] == jnp.arange(track_total, dtype=jnp.int32)[None, :],
            track_owner[None, :],
            0,
        ),
        axis=1,
    )


def convolve(frames, conv_weight, rim_rows):
    tok_rows = frames.shape[0]
    extended = jnp.concatenate([rim_rows, frames], axis=0).astype(jnp.float32)
    conv_sum = frames.astype(jnp.float32)
    for tap in range(KW):
        conv_sum = (
            conv_sum
            + conv_weight[tap].astype(jnp.float32)[None, :]
            * extended[KW - 1 - tap : KW - 1 - tap + tok_rows]
        )
    return conv_sum.astype(jnp.bfloat16)


def attend_slots(packed, positions):
    slot_count = packed.shape[0]
    inner = packed.shape[1] // 3
    head_count = inner // HD
    query = packed[:, :inner].reshape(slot_count, head_count, HD)
    keys_all = packed[:, inner : 2 * inner].reshape(slot_count, head_count, HD)
    values_all = packed[:, 2 * inner :].reshape(slot_count, head_count, HD)
    slot_ids = jnp.arange(slot_count, dtype=jnp.int32)
    score_scale = 1.0 / HD**0.5
    scores = (
        jnp.einsum("qhd,khd->hqk", query, keys_all, preferred_element_type=jnp.float32)
        * score_scale
    )
    allowed = (positions[None, :] >= 0) & (positions[None, :] <= positions[:, None]) | (
        slot_ids[:, None] == slot_ids[None, :]
    )
    scores = jnp.where(allowed[None], scores, jnp.float32(-1e30))
    top_score = jnp.max(scores, axis=-1, keepdims=True)
    expd = jnp.exp(scores - top_score)
    weights = (expd / jnp.sum(expd, axis=-1, keepdims=True)).astype(jnp.bfloat16)
    mixed = jnp.einsum("hqk,khd->qhd", weights, values_all, preferred_element_type=jnp.float32)
    return mixed.astype(jnp.bfloat16).reshape(slot_count, inner)


def body_by_owner(frames, conv_weight, qkv_weight, track_ids, track_owner):
    tok_rows = frames.shape[0]
    peer_count = lax.axis_size("seq")
    capacity = 2 * tok_rows // peer_count
    slot_total = capacity * peer_count
    my_index = lax.axis_index("seq")
    rim_rows = from_behind(frames[tok_rows - (KW - 1) :], "seq", 1)
    hidden = convolve(frames, conv_weight, rim_rows)
    group = track_groups(track_ids, track_owner)
    owner_hits = (group[:, None] == jnp.arange(peer_count, dtype=jnp.int32)[None, :]).astype(
        jnp.int32
    )
    running = jnp.cumsum(owner_hits, axis=0) - 1
    rank_rows = jnp.sum(jnp.where(owner_hits > 0, running, 0), axis=1)
    slot_of_row = group * capacity + rank_rows
    row_ids = jnp.arange(tok_rows, dtype=jnp.int32)
    source_row = jnp.full((slot_total,), tok_rows, jnp.int32).at[slot_of_row].set(row_ids)
    positions = my_index * tok_rows + row_ids
    send_times = jnp.full((slot_total,), -1, jnp.int32).at[slot_of_row].set(positions)
    projected = jnp.dot(
        hidden,
        lax.all_gather(qkv_weight, "seq", axis=1, tiled=True),
        preferred_element_type=jnp.float32,
    ).astype(jnp.bfloat16)
    padded_rows = jnp.concatenate(
        [projected, jnp.zeros((1, projected.shape[1]), jnp.bfloat16)], axis=0
    )
    outgoing = padded_rows[source_row]
    received, got_times = (
        lax.all_to_all(outgoing, "seq", split_axis=0, concat_axis=0, tiled=True),
        lax.all_to_all(send_times, "seq", split_axis=0, concat_axis=0, tiled=True),
    )
    mixed = attend_slots(received, got_times)
    returned = lax.all_to_all(mixed, "seq", split_axis=0, concat_axis=0, tiled=True)
    return returned[slot_of_row]


def xor_swap(value, bit, axes=("chip", "core")):
    count = lax.axis_size(axes)
    return lax.ppermute(value, axes, [(d, d ^ bit) for d in range(count)])


def by_bit(bit, mine, theirs, axis):
    return jnp.stack(
        [jnp.where(bit == 0, mine, theirs), jnp.where(bit == 0, theirs, mine)], axis=axis
    )


def zero_after(array):
    last = array[(-1,) * array.ndim]
    return jnp.where(last != last, 1.0, 0.0).astype(jnp.bfloat16)


def body_by_head(frames, conv_weight, qkv_weight, track_ids, track_owner):
    tok_rows = frames.shape[0]
    chips = lax.axis_size("chip")
    devices = 2 * chips
    core = lax.axis_index("core")
    chip = lax.axis_index("chip")
    grp = lax.axis_index("grp")
    me = 2 * chip + core
    both = ("chip", "core")
    every = ("grp", "chip", "core")
    part = tok_rows // 2
    features = frames.shape[1]
    CORE, Y, Z0, Z1 = 1, 2, 4, 8

    rim_rows = lax.ppermute(
        frames[tok_rows - (KW - 1) :], both, [(i, i + 1) for i in range(devices - 1)]
    )
    late = convolve(frames[part:], conv_weight, frames[part - (KW - 1) : part])
    early = convolve(frames[:part], conv_weight, rim_rows)

    far_late = xor_swap(late, Z1)
    far_early = xor_swap(early, Z1)
    own = jnp.concatenate([early, late], axis=0)
    beside = xor_swap(own, Y)

    half = features // 2
    held = qkv_weight.T.reshape(3, HD // 2, features)

    def to_heads(block, j):
        pairs = [
            (g * devices + d, g * devices + (3 * d + j[g]) % devices)
            for g in (0, 1)
            for d in range(devices)
        ]
        return lax.ppermute(block, every, pairs)

    outer = to_heads(lax.dynamic_index_in_dim(held, 2 * grp, 0, False), (0, 2))
    middle = to_heads(lax.dynamic_slice_in_dim(held[1], grp * half, half, 1), (1, 1))
    mine = jnp.concatenate([outer[:, :half], outer[:, half:], middle], axis=0)
    paired = xor_swap(mine, Z0)

    mine_too = xor_swap(mine, devices, every)

    cut = half // 2
    fourth = [xor_swap(paired[:, :cut], devices, every), xor_swap(mine_too[:, cut:], Z0)]

    far_beside_late = xor_swap(far_late + zero_after(fourth[0]), Y)

    groups = track_groups(track_ids, track_owner)[None, :] + zero_after(mine).astype(jnp.int32)
    for bit in (CORE, Y, Z0, Z1):
        groups = jnp.concatenate([groups, xor_swap(groups, bit)], axis=0)
    zero = jnp.where(groups[-1, -1] < 0, 1.0, 0.0).astype(jnp.bfloat16)
    far_beside_early = xor_swap(far_early + zero, Y)

    fourth = jnp.concatenate(fourth, axis=1)

    def whole_head(pieces, theirs, index):
        size = HD // 2

        def block(values, n):
            return values[n * size : (n + 1) * size]

        first, last = (
            jnp.concatenate(
                [jnp.where(grp == g, block(pieces, n), block(theirs, n)) for n in (0, 1)], axis=1
            )
            for g in (0, 1)
        )
        low, high = block(pieces, 2), block(theirs, 2)
        between = jnp.concatenate(
            [jnp.where(grp == 0, low, high), jnp.where(grp == 0, high, low)], axis=1
        )
        turned = [first, between, last, first, between]
        wide = lax.dynamic_slice_in_dim(jnp.stack(turned), lax.rem(index, 3), 3, 0)
        return by_bit(core, wide, xor_swap(wide, CORE), 1).reshape(3 * HD, features)

    two_heads = jnp.concatenate(
        [whole_head(mine, mine_too, me), whole_head(paired, fourth, me ^ Z0)], axis=0
    )

    def project(rows):
        done = lax.dot_general(
            rows, two_heads, (((1,), (1,)), ((), ())), preferred_element_type=jnp.float32
        ).astype(jnp.bfloat16)
        return jnp.concatenate([done[:, : 3 * HD], xor_swap(done[:, 3 * HD :], Z0)], axis=0)

    first = project(jnp.concatenate([own, beside, far_late, far_beside_late], axis=0))
    second = project(jnp.concatenate([far_early, far_beside_early], axis=0))

    first_rows = [(0, 0, tok_rows), (Y, 0, tok_rows), (Z1, part, part), (Z1 | Y, part, part)]
    second_rows = [(Z1, 0, part), (Z1 | Y, 0, part)]
    order = []
    for pieces in (first_rows, second_rows):
        order += pieces + [(far ^ Z0, start, count) for far, start, count in pieces]

    def of_rows(bit):
        times = [
            (me ^ far ^ bit) * tok_rows + start + jnp.arange(count, dtype=jnp.int32)
            for far, start, count in order
        ]
        marks = [groups[far ^ bit, start : start + count] for far, start, count in order]
        return jnp.concatenate(times), jnp.concatenate(marks)

    projected = jnp.concatenate([first, second], axis=0)
    query = projected[:, :HD]
    keyed = jnp.concatenate(
        [projected[:, HD:], xor_swap(first[:, HD:], CORE), xor_swap(second[:, HD:], CORE)], axis=0
    )
    own_times, own_groups = of_rows(0)
    other_times, other_groups = of_rows(CORE)
    key_times = jnp.concatenate([own_times, other_times])
    key_groups = jnp.concatenate([own_groups, other_groups])
    scores = lax.dot_general(
        query, keyed[:, :HD], (((1,), (1,)), ((), ())), preferred_element_type=jnp.float32
    ) * (1.0 / HD**0.5)
    allowed = (key_times[None, :] <= own_times[:, None]) & (
        key_groups[None, :] == own_groups[:, None]
    )
    scores = jnp.where(allowed, scores, jnp.float32(-1e30))
    expd = jnp.exp(scores - jnp.max(scores, axis=-1, keepdims=True))
    weights = (expd / jnp.sum(expd, axis=-1, keepdims=True)).astype(jnp.bfloat16)
    mixed = jnp.dot(weights, keyed[:, HD:], preferred_element_type=jnp.float32)
    mixed = mixed.astype(jnp.bfloat16)

    sent = jnp.zeros((chips, tok_rows, HD), jnp.bfloat16)
    at = 0
    for far, start, count in order:
        rows = mixed[at : at + count]
        sent = lax.dynamic_update_slice(sent, rows[None], ((me ^ far) >> 1, start, 0))
        at += count
    returned = lax.all_to_all(sent, "chip", split_axis=0, concat_axis=0, tiled=True)
    return returned.transpose(1, 0, 2).reshape(tok_rows, chips * HD)


def solution(mesh):
    grp, seq = mesh.devices.shape
    out_by_owner = P(("grp", "seq"), None)
    by_owner = jax.shard_map(
        body_by_owner,
        mesh=mesh,
        in_specs=(P(("grp", "seq"), None), P(), P(None, "seq"), P(("grp", "seq")), P("grp")),
        out_specs=out_by_owner,
        check_vma=False,
    )
    split = Mesh(mesh.devices.reshape(grp, seq // 2, 2), ("grp", "chip", "core"))
    rows = P(("grp", "chip", "core"))
    by_head = jax.shard_map(
        body_by_head,
        mesh=split,
        in_specs=(rows, P(), P(None, ("chip", "core")), rows, P("grp")),
        out_specs=rows,
        check_vma=False,
    )

    def run(frames, conv_weight, qkv_weight, track_ids, track_owner):
        heads = qkv_weight.shape[1] // (3 * HD)
        plan = by_head if (grp, seq, heads) == (2, 16, 8) else by_owner
        return plan(frames, conv_weight, qkv_weight, track_ids, track_owner)

    return run
```

```python
import jax
import jax.numpy as jnp
from jax import lax
from jax.sharding import Mesh
from jax.sharding import PartitionSpec as P

HD = 128
KW = 4


def from_behind(value, axis, by):
    size = lax.axis_size(axis)
    pairs = [(i, i + by) for i in range(size) if 0 <= i + by < size]
    return lax.ppermute(value, axis, pairs)


def track_groups(track_ids, track_owner):
    track_total = track_owner.shape[0]
    return jnp.sum(
        jnp.where(
            track_ids[:, None] == jnp.arange(track_total, dtype=jnp.int32)[None, :],
            track_owner[None, :],
            0,
        ),
        axis=1,
    )


def convolve(frames, conv_weight, rim_rows):
    tok_rows = frames.shape[0]
    extended = jnp.concatenate([rim_rows, frames], axis=0).astype(jnp.float32)
    conv_sum = frames.astype(jnp.float32)
    for tap in range(KW):
        conv_sum = (
            conv_sum
            + conv_weight[tap].astype(jnp.float32)[None, :]
            * extended[KW - 1 - tap : KW - 1 - tap + tok_rows]
        )
    return conv_sum.astype(jnp.bfloat16)


def attend_slots(packed, positions):
    slot_count = packed.shape[0]
    inner = packed.shape[1] // 3
    head_count = inner // HD
    query = packed[:, :inner].reshape(slot_count, head_count, HD)
    keys_all = packed[:, inner : 2 * inner].reshape(slot_count, head_count, HD)
    values_all = packed[:, 2 * inner :].reshape(slot_count, head_count, HD)
    slot_ids = jnp.arange(slot_count, dtype=jnp.int32)
    score_scale = 1.0 / HD**0.5
    scores = (
        jnp.einsum("qhd,khd->hqk", query, keys_all, preferred_element_type=jnp.float32)
        * score_scale
    )
    allowed = (positions[None, :] >= 0) & (positions[None, :] <= positions[:, None]) | (
        slot_ids[:, None] == slot_ids[None, :]
    )
    scores = jnp.where(allowed[None], scores, jnp.float32(-1e30))
    top_score = jnp.max(scores, axis=-1, keepdims=True)
    expd = jnp.exp(scores - top_score)
    weights = (expd / jnp.sum(expd, axis=-1, keepdims=True)).astype(jnp.bfloat16)
    mixed = jnp.einsum("hqk,khd->qhd", weights, values_all, preferred_element_type=jnp.float32)
    return mixed.astype(jnp.bfloat16).reshape(slot_count, inner)


def body_by_owner(frames, conv_weight, qkv_weight, track_ids, track_owner):
    tok_rows = frames.shape[0]
    peer_count = lax.axis_size("seq")
    capacity = 2 * tok_rows // peer_count
    slot_total = capacity * peer_count
    my_index = lax.axis_index("seq")
    rim_rows = from_behind(frames[tok_rows - (KW - 1) :], "seq", 1)
    hidden = convolve(frames, conv_weight, rim_rows)
    group = track_groups(track_ids, track_owner)
    owner_hits = (group[:, None] == jnp.arange(peer_count, dtype=jnp.int32)[None, :]).astype(
        jnp.int32
    )
    running = jnp.cumsum(owner_hits, axis=0) - 1
    rank_rows = jnp.sum(jnp.where(owner_hits > 0, running, 0), axis=1)
    slot_of_row = group * capacity + rank_rows
    row_ids = jnp.arange(tok_rows, dtype=jnp.int32)
    source_row = jnp.full((slot_total,), tok_rows, jnp.int32).at[slot_of_row].set(row_ids)
    positions = my_index * tok_rows + row_ids
    send_times = jnp.full((slot_total,), -1, jnp.int32).at[slot_of_row].set(positions)
    projected = jnp.dot(
        hidden,
        lax.all_gather(qkv_weight, "seq", axis=1, tiled=True),
        preferred_element_type=jnp.float32,
    ).astype(jnp.bfloat16)
    padded_rows = jnp.concatenate(
        [projected, jnp.zeros((1, projected.shape[1]), jnp.bfloat16)], axis=0
    )
    outgoing = padded_rows[source_row]
    received, got_times = (
        lax.all_to_all(outgoing, "seq", split_axis=0, concat_axis=0, tiled=True),
        lax.all_to_all(send_times, "seq", split_axis=0, concat_axis=0, tiled=True),
    )
    mixed = attend_slots(received, got_times)
    returned = lax.all_to_all(mixed, "seq", split_axis=0, concat_axis=0, tiled=True)
    return returned[slot_of_row]


def xor_swap(value, bit, axes=("chip", "core")):
    count = lax.axis_size(axes)
    return lax.ppermute(value, axes, [(d, d ^ bit) for d in range(count)])


def by_bit(bit, mine, theirs, axis):
    return jnp.stack(
        [jnp.where(bit == 0, mine, theirs), jnp.where(bit == 0, theirs, mine)], axis=axis
    )


def zero_after(array):
    last = array[(-1,) * array.ndim]
    return jnp.where(last != last, 1.0, 0.0).astype(jnp.bfloat16)


def body_by_head(frames, conv_weight, qkv_weight, track_ids, track_owner):
    tok_rows = frames.shape[0]
    chips = lax.axis_size("chip")
    devices = 2 * chips
    core = lax.axis_index("core")
    chip = lax.axis_index("chip")
    grp = lax.axis_index("grp")
    me = 2 * chip + core
    both = ("chip", "core")
    every = ("grp", "chip", "core")
    part = tok_rows // 2
    features = frames.shape[1]
    CORE, Y, Z0, Z1 = 1, 2, 4, 8

    rim_rows = lax.ppermute(
        frames[tok_rows - (KW - 1) :], both, [(i, i + 1) for i in range(devices - 1)]
    )
    late = convolve(frames[part:], conv_weight, frames[part - (KW - 1) : part])
    early = convolve(frames[:part], conv_weight, rim_rows)

    far_late = xor_swap(late, Z1)
    far_early = xor_swap(early, Z1)
    own = jnp.concatenate([early, late], axis=0)
    beside = xor_swap(own, Y)

    half = features // 2
    held = qkv_weight.T.reshape(3, HD // 2, features)

    def to_heads(block, j):
        pairs = [
            (g * devices + d, g * devices + (3 * d + j[g]) % devices)
            for g in (0, 1)
            for d in range(devices)
        ]
        return lax.ppermute(block, every, pairs)

    outer = to_heads(lax.dynamic_index_in_dim(held, 2 * grp, 0, False), (0, 2))
    middle = to_heads(lax.dynamic_slice_in_dim(held[1], grp * half, half, 1), (1, 1))
    mine = jnp.concatenate([outer[:, :half], outer[:, half:], middle], axis=0)
    paired = xor_swap(mine, Z0)

    mine_too = xor_swap(mine, devices, every)

    cut = half // 2
    fourth = [xor_swap(paired[:, :cut], devices, every), xor_swap(mine_too[:, cut:], Z0)]

    zero = zero_after(fourth[0]) + zero_after(fourth[1])
    far_beside_late = xor_swap(far_late + zero, Y)
    far_beside_early = xor_swap(far_early + zero, Y)

    fourth = jnp.concatenate(fourth, axis=1)

    def whole_head(pieces, theirs, index):
        size = HD // 2

        def block(values, n):
            return values[n * size : (n + 1) * size]

        first, last = (
            jnp.concatenate(
                [jnp.where(grp == g, block(pieces, n), block(theirs, n)) for n in (0, 1)], axis=1
            )
            for g in (0, 1)
        )
        low, high = block(pieces, 2), block(theirs, 2)
        between = jnp.concatenate(
            [jnp.where(grp == 0, low, high), jnp.where(grp == 0, high, low)], axis=1
        )
        turned = [first, between, last, first, between]
        wide = lax.dynamic_slice_in_dim(jnp.stack(turned), lax.rem(index, 3), 3, 0)
        return by_bit(core, wide, xor_swap(wide, CORE), 1).reshape(3 * HD, features)

    two_heads = jnp.concatenate(
        [whole_head(mine, mine_too, me), whole_head(paired, fourth, me ^ Z0)], axis=0
    )

    def project(rows):
        done = lax.dot_general(
            rows, two_heads, (((1,), (1,)), ((), ())), preferred_element_type=jnp.float32
        ).astype(jnp.bfloat16)
        swapped = xor_swap(done[:, 3 * HD :], Z0)
        return jnp.concatenate([done[:, : 3 * HD], swapped], axis=0), zero_after(done)

    first, _ = project(jnp.concatenate([own, beside, far_early, far_beside_early], axis=0))
    second, _ = project(jnp.concatenate([far_late, far_beside_late], axis=0))

    first_rows = [(0, 0, tok_rows), (Y, 0, tok_rows), (Z1, 0, part), (Z1 | Y, 0, part)]
    second_rows = [(Z1, part, part), (Z1 | Y, part, part)]
    order = []
    for pieces in (first_rows, second_rows):
        order += pieces + [(far ^ Z0, start, count) for far, start, count in pieces]

    groups = track_groups(track_ids, track_owner)[None, :]
    for bit in (CORE, Y, Z0, Z1):
        groups = jnp.concatenate([groups, xor_swap(groups, bit)], axis=0)

    def of_rows(bit):
        times = [
            (me ^ far ^ bit) * tok_rows + start + jnp.arange(count, dtype=jnp.int32)
            for far, start, count in order
        ]
        marks = [groups[far ^ bit, start : start + count] for far, start, count in order]
        return jnp.concatenate(times), jnp.concatenate(marks)

    projected = jnp.concatenate([first, second], axis=0)
    query = projected[:, :HD]
    keyed = jnp.concatenate(
        [projected[:, HD:], xor_swap(first[:, HD:], CORE), xor_swap(second[:, HD:], CORE)], axis=0
    )
    own_times, own_groups = of_rows(0)
    other_times, other_groups = of_rows(CORE)
    key_times = jnp.concatenate([own_times, other_times])
    key_groups = jnp.concatenate([own_groups, other_groups])
    scores = lax.dot_general(
        query, keyed[:, :HD], (((1,), (1,)), ((), ())), preferred_element_type=jnp.float32
    ) * (1.0 / HD**0.5)
    allowed = (key_times[None, :] <= own_times[:, None]) & (
        key_groups[None, :] == own_groups[:, None]
    )
    scores = jnp.where(allowed, scores, jnp.float32(-1e30))
    expd = jnp.exp(scores - jnp.max(scores, axis=-1, keepdims=True))
    weights = (expd / jnp.sum(expd, axis=-1, keepdims=True)).astype(jnp.bfloat16)
    mixed = jnp.dot(weights, keyed[:, HD:], preferred_element_type=jnp.float32)
    mixed = mixed.astype(jnp.bfloat16)

    sent = jnp.zeros((chips, tok_rows, HD), jnp.bfloat16)
    at = 0
    for far, start, count in order:
        rows = mixed[at : at + count]
        sent = lax.dynamic_update_slice(sent, rows[None], ((me ^ far) >> 1, start, 0))
        at += count
    returned = lax.all_to_all(sent, "chip", split_axis=0, concat_axis=0, tiled=True)
    return returned.transpose(1, 0, 2).reshape(tok_rows, chips * HD)


def solution(mesh):
    grp, seq = mesh.devices.shape
    out_by_owner = P(("grp", "seq"), None)
    by_owner = jax.shard_map(
        body_by_owner,
        mesh=mesh,
        in_specs=(P(("grp", "seq"), None), P(), P(None, "seq"), P(("grp", "seq")), P("grp")),
        out_specs=out_by_owner,
        check_vma=False,
    )
    split = Mesh(mesh.devices.reshape(grp, seq // 2, 2), ("grp", "chip", "core"))
    rows = P(("grp", "chip", "core"))
    by_head = jax.shard_map(
        body_by_head,
        mesh=split,
        in_specs=(rows, P(), P(None, ("chip", "core")), rows, P("grp")),
        out_specs=rows,
        check_vma=False,
    )

    def run(frames, conv_weight, qkv_weight, track_ids, track_owner):
        heads = qkv_weight.shape[1] // (3 * HD)
        plan = by_head if (grp, seq, heads) == (2, 16, 8) else by_owner
        return plan(frames, conv_weight, qkv_weight, track_ids, track_owner)

    return run
```

```python
import jax
import jax.numpy as jnp
from jax import lax
from jax.sharding import Mesh
from jax.sharding import PartitionSpec as P

HD = 128
KW = 4


def from_behind(value, axis, by):
    size = lax.axis_size(axis)
    pairs = [(i, i + by) for i in range(size) if 0 <= i + by < size]
    return lax.ppermute(value, axis, pairs)


def track_groups(track_ids, track_owner):
    track_total = track_owner.shape[0]
    return jnp.sum(
        jnp.where(
            track_ids[:, None] == jnp.arange(track_total, dtype=jnp.int32)[None, :],
            track_owner[None, :],
            0,
        ),
        axis=1,
    )


def convolve(frames, conv_weight, rim_rows):
    tok_rows = frames.shape[0]
    extended = jnp.concatenate([rim_rows, frames], axis=0).astype(jnp.float32)
    conv_sum = frames.astype(jnp.float32)
    for tap in range(KW):
        conv_sum = (
            conv_sum
            + conv_weight[tap].astype(jnp.float32)[None, :]
            * extended[KW - 1 - tap : KW - 1 - tap + tok_rows]
        )
    return conv_sum.astype(jnp.bfloat16)


def attend_slots(packed, positions):
    slot_count = packed.shape[0]
    inner = packed.shape[1] // 3
    head_count = inner // HD
    query = packed[:, :inner].reshape(slot_count, head_count, HD)
    keys_all = packed[:, inner : 2 * inner].reshape(slot_count, head_count, HD)
    values_all = packed[:, 2 * inner :].reshape(slot_count, head_count, HD)
    slot_ids = jnp.arange(slot_count, dtype=jnp.int32)
    score_scale = 1.0 / HD**0.5
    scores = (
        jnp.einsum("qhd,khd->hqk", query, keys_all, preferred_element_type=jnp.float32)
        * score_scale
    )
    allowed = (positions[None, :] >= 0) & (positions[None, :] <= positions[:, None]) | (
        slot_ids[:, None] == slot_ids[None, :]
    )
    scores = jnp.where(allowed[None], scores, jnp.float32(-1e30))
    top_score = jnp.max(scores, axis=-1, keepdims=True)
    expd = jnp.exp(scores - top_score)
    weights = (expd / jnp.sum(expd, axis=-1, keepdims=True)).astype(jnp.bfloat16)
    mixed = jnp.einsum("hqk,khd->qhd", weights, values_all, preferred_element_type=jnp.float32)
    return mixed.astype(jnp.bfloat16).reshape(slot_count, inner)


def body_by_owner(frames, conv_weight, qkv_weight, track_ids, track_owner):
    tok_rows = frames.shape[0]
    peer_count = lax.axis_size("seq")
    capacity = 2 * tok_rows // peer_count
    slot_total = capacity * peer_count
    my_index = lax.axis_index("seq")
    rim_rows = from_behind(frames[tok_rows - (KW - 1) :], "seq", 1)
    hidden = convolve(frames, conv_weight, rim_rows)
    group = track_groups(track_ids, track_owner)
    owner_hits = (group[:, None] == jnp.arange(peer_count, dtype=jnp.int32)[None, :]).astype(
        jnp.int32
    )
    running = jnp.cumsum(owner_hits, axis=0) - 1
    rank_rows = jnp.sum(jnp.where(owner_hits > 0, running, 0), axis=1)
    slot_of_row = group * capacity + rank_rows
    row_ids = jnp.arange(tok_rows, dtype=jnp.int32)
    source_row = jnp.full((slot_total,), tok_rows, jnp.int32).at[slot_of_row].set(row_ids)
    positions = my_index * tok_rows + row_ids
    send_times = jnp.full((slot_total,), -1, jnp.int32).at[slot_of_row].set(positions)
    projected = jnp.dot(
        hidden,
        lax.all_gather(qkv_weight, "seq", axis=1, tiled=True),
        preferred_element_type=jnp.float32,
    ).astype(jnp.bfloat16)
    padded_rows = jnp.concatenate(
        [projected, jnp.zeros((1, projected.shape[1]), jnp.bfloat16)], axis=0
    )
    outgoing = padded_rows[source_row]
    received, got_times = (
        lax.all_to_all(outgoing, "seq", split_axis=0, concat_axis=0, tiled=True),
        lax.all_to_all(send_times, "seq", split_axis=0, concat_axis=0, tiled=True),
    )
    mixed = attend_slots(received, got_times)
    returned = lax.all_to_all(mixed, "seq", split_axis=0, concat_axis=0, tiled=True)
    return returned[slot_of_row]


def xor_swap(value, bit, axes=("chip", "core")):
    count = lax.axis_size(axes)
    return lax.ppermute(value, axes, [(d, d ^ bit) for d in range(count)])


def by_bit(bit, mine, theirs, axis):
    return jnp.stack(
        [jnp.where(bit == 0, mine, theirs), jnp.where(bit == 0, theirs, mine)], axis=axis
    )


def zero_after(array):
    last = array[(-1,) * array.ndim]
    return jnp.where(last != last, 1.0, 0.0).astype(jnp.bfloat16)


def body_by_head(frames, conv_weight, qkv_weight, track_ids, track_owner):
    tok_rows = frames.shape[0]
    chips = lax.axis_size("chip")
    devices = 2 * chips
    core = lax.axis_index("core")
    chip = lax.axis_index("chip")
    grp = lax.axis_index("grp")
    me = 2 * chip + core
    both = ("chip", "core")
    every = ("grp", "chip", "core")
    part = tok_rows // 4
    rest = tok_rows - part
    features = frames.shape[1]
    CORE, Y, Z0, Z1 = 1, 2, 4, 8

    rim_rows = lax.ppermute(
        frames[tok_rows - (KW - 1) :], both, [(i, i + 1) for i in range(devices - 1)]
    )
    late = convolve(frames[part:], conv_weight, frames[part - (KW - 1) : part])
    early = convolve(frames[:part], conv_weight, rim_rows)

    far_late = xor_swap(late, Z1)
    far_early = xor_swap(early, Z1)
    own = jnp.concatenate([early, late], axis=0)
    beside = xor_swap(own, Y)

    half = features // 2
    held = qkv_weight.T.reshape(3, HD // 2, features)

    def to_heads(block, j):
        pairs = [
            (g * devices + d, g * devices + (3 * d + j[g]) % devices)
            for g in (0, 1)
            for d in range(devices)
        ]
        return lax.ppermute(block, every, pairs)

    outer = to_heads(lax.dynamic_index_in_dim(held, 2 * grp, 0, False), (0, 2))
    middle = to_heads(lax.dynamic_slice_in_dim(held[1], grp * half, half, 1), (1, 1))
    mine = jnp.concatenate([outer[:, :half], outer[:, half:], middle], axis=0)
    paired = xor_swap(mine, Z0)

    mine_too = xor_swap(mine, devices, every)

    cut = half // 2
    fourth = [xor_swap(paired[:, :cut], devices, every), xor_swap(mine_too[:, cut:], Z0)]

    far_beside_late = xor_swap(far_late + zero_after(fourth[0]) + zero_after(fourth[1]), Y)
    far_beside_early = xor_swap(far_early, Y)

    fourth = jnp.concatenate(fourth, axis=1)

    def whole_head(pieces, theirs, index):
        size = HD // 2

        def block(values, n):
            return values[n * size : (n + 1) * size]

        first, last = (
            jnp.concatenate(
                [jnp.where(grp == g, block(pieces, n), block(theirs, n)) for n in (0, 1)], axis=1
            )
            for g in (0, 1)
        )
        low, high = block(pieces, 2), block(theirs, 2)
        between = jnp.concatenate(
            [jnp.where(grp == 0, low, high), jnp.where(grp == 0, high, low)], axis=1
        )
        turned = [first, between, last, first, between]
        wide = lax.dynamic_slice_in_dim(jnp.stack(turned), lax.rem(index, 3), 3, 0)
        return by_bit(core, wide, xor_swap(wide, CORE), 1).reshape(3 * HD, features)

    two_heads = jnp.concatenate(
        [whole_head(mine, mine_too, me), whole_head(paired, fourth, me ^ Z0)], axis=0
    )

    def project(rows):
        done = lax.dot_general(
            rows, two_heads, (((1,), (1,)), ((), ())), preferred_element_type=jnp.float32
        ).astype(jnp.bfloat16)
        return jnp.concatenate([done[:, : 3 * HD], xor_swap(done[:, 3 * HD :], Z0)], axis=0)

    first = project(jnp.concatenate([own, beside, far_late, far_beside_late], axis=0))
    second = project(jnp.concatenate([far_early, far_beside_early], axis=0))

    first_rows = [(0, 0, tok_rows), (Y, 0, tok_rows), (Z1, part, rest), (Z1 | Y, part, rest)]
    second_rows = [(Z1, 0, part), (Z1 | Y, 0, part)]
    order = []
    for pieces in (first_rows, second_rows):
        order += pieces + [(far ^ Z0, start, count) for far, start, count in pieces]

    groups = track_groups(track_ids, track_owner)[None, :]
    for bit in (CORE, Y, Z0, Z1):
        groups = jnp.concatenate([groups, xor_swap(groups, bit)], axis=0)

    def of_rows(bit):
        times = [
            (me ^ far ^ bit) * tok_rows + start + jnp.arange(count, dtype=jnp.int32)
            for far, start, count in order
        ]
        marks = [groups[far ^ bit, start : start + count] for far, start, count in order]
        return jnp.concatenate(times), jnp.concatenate(marks)

    projected = jnp.concatenate([first, second], axis=0)
    query = projected[:, :HD]
    keyed = jnp.concatenate(
        [projected[:, HD:], xor_swap(first[:, HD:], CORE), xor_swap(second[:, HD:], CORE)], axis=0
    )
    own_times, own_groups = of_rows(0)
    other_times, other_groups = of_rows(CORE)
    key_times = jnp.concatenate([own_times, other_times])
    key_groups = jnp.concatenate([own_groups, other_groups])
    scores = lax.dot_general(
        query, keyed[:, :HD], (((1,), (1,)), ((), ())), preferred_element_type=jnp.float32
    ) * (1.0 / HD**0.5)
    allowed = (key_times[None, :] <= own_times[:, None]) & (
        key_groups[None, :] == own_groups[:, None]
    )
    scores = jnp.where(allowed, scores, jnp.float32(-1e30))
    expd = jnp.exp(scores - jnp.max(scores, axis=-1, keepdims=True))
    weights = (expd / jnp.sum(expd, axis=-1, keepdims=True)).astype(jnp.bfloat16)
    mixed = jnp.dot(weights, keyed[:, HD:], preferred_element_type=jnp.float32)
    mixed = mixed.astype(jnp.bfloat16)

    sent = jnp.zeros((chips, tok_rows, HD), jnp.bfloat16)
    at = 0
    for far, start, count in order:
        rows = mixed[at : at + count]
        sent = lax.dynamic_update_slice(sent, rows[None], ((me ^ far) >> 1, start, 0))
        at += count
    returned = lax.all_to_all(sent, "chip", split_axis=0, concat_axis=0, tiled=True)
    return returned.transpose(1, 0, 2).reshape(tok_rows, chips * HD)


def solution(mesh):
    grp, seq = mesh.devices.shape
    out_by_owner = P(("grp", "seq"), None)
    by_owner = jax.shard_map(
        body_by_owner,
        mesh=mesh,
        in_specs=(P(("grp", "seq"), None), P(), P(None, "seq"), P(("grp", "seq")), P("grp")),
        out_specs=out_by_owner,
        check_vma=False,
    )
    split = Mesh(mesh.devices.reshape(grp, seq // 2, 2), ("grp", "chip", "core"))
    rows = P(("grp", "chip", "core"))
    by_head = jax.shard_map(
        body_by_head,
        mesh=split,
        in_specs=(rows, P(), P(None, ("chip", "core")), rows, P("grp")),
        out_specs=rows,
        check_vma=False,
    )

    def run(frames, conv_weight, qkv_weight, track_ids, track_owner):
        heads = qkv_weight.shape[1] // (3 * HD)
        plan = by_head if (grp, seq, heads) == (2, 16, 8) else by_owner
        return plan(frames, conv_weight, qkv_weight, track_ids, track_owner)

    return run
```

```python
import jax
import jax.numpy as jnp
from jax import lax
from jax.sharding import Mesh
from jax.sharding import PartitionSpec as P

HD = 128
KW = 4


def from_behind(value, axis, by):
    size = lax.axis_size(axis)
    pairs = [(i, i + by) for i in range(size) if 0 <= i + by < size]
    return lax.ppermute(value, axis, pairs)


def track_groups(track_ids, track_owner):
    track_total = track_owner.shape[0]
    return jnp.sum(
        jnp.where(
            track_ids[:, None] == jnp.arange(track_total, dtype=jnp.int32)[None, :],
            track_owner[None, :],
            0,
        ),
        axis=1,
    )


def convolve(frames, conv_weight, rim_rows):
    tok_rows = frames.shape[0]
    extended = jnp.concatenate([rim_rows, frames], axis=0).astype(jnp.float32)
    conv_sum = frames.astype(jnp.float32)
    for tap in range(KW):
        conv_sum = (
            conv_sum
            + conv_weight[tap].astype(jnp.float32)[None, :]
            * extended[KW - 1 - tap : KW - 1 - tap + tok_rows]
        )
    return conv_sum.astype(jnp.bfloat16)


def attend_slots(packed, positions):
    slot_count = packed.shape[0]
    inner = packed.shape[1] // 3
    head_count = inner // HD
    query = packed[:, :inner].reshape(slot_count, head_count, HD)
    keys_all = packed[:, inner : 2 * inner].reshape(slot_count, head_count, HD)
    values_all = packed[:, 2 * inner :].reshape(slot_count, head_count, HD)
    slot_ids = jnp.arange(slot_count, dtype=jnp.int32)
    score_scale = 1.0 / HD**0.5
    scores = (
        jnp.einsum("qhd,khd->hqk", query, keys_all, preferred_element_type=jnp.float32)
        * score_scale
    )
    allowed = (positions[None, :] >= 0) & (positions[None, :] <= positions[:, None]) | (
        slot_ids[:, None] == slot_ids[None, :]
    )
    scores = jnp.where(allowed[None], scores, jnp.float32(-1e30))
    top_score = jnp.max(scores, axis=-1, keepdims=True)
    expd = jnp.exp(scores - top_score)
    weights = (expd / jnp.sum(expd, axis=-1, keepdims=True)).astype(jnp.bfloat16)
    mixed = jnp.einsum("hqk,khd->qhd", weights, values_all, preferred_element_type=jnp.float32)
    return mixed.astype(jnp.bfloat16).reshape(slot_count, inner)


def body_by_owner(frames, conv_weight, qkv_weight, track_ids, track_owner):
    tok_rows = frames.shape[0]
    peer_count = lax.axis_size("seq")
    capacity = 2 * tok_rows // peer_count
    slot_total = capacity * peer_count
    my_index = lax.axis_index("seq")
    rim_rows = from_behind(frames[tok_rows - (KW - 1) :], "seq", 1)
    hidden = convolve(frames, conv_weight, rim_rows)
    group = track_groups(track_ids, track_owner)
    owner_hits = (group[:, None] == jnp.arange(peer_count, dtype=jnp.int32)[None, :]).astype(
        jnp.int32
    )
    running = jnp.cumsum(owner_hits, axis=0) - 1
    rank_rows = jnp.sum(jnp.where(owner_hits > 0, running, 0), axis=1)
    slot_of_row = group * capacity + rank_rows
    row_ids = jnp.arange(tok_rows, dtype=jnp.int32)
    source_row = jnp.full((slot_total,), tok_rows, jnp.int32).at[slot_of_row].set(row_ids)
    positions = my_index * tok_rows + row_ids
    send_times = jnp.full((slot_total,), -1, jnp.int32).at[slot_of_row].set(positions)
    projected = jnp.dot(
        hidden,
        lax.all_gather(qkv_weight, "seq", axis=1, tiled=True),
        preferred_element_type=jnp.float32,
    ).astype(jnp.bfloat16)
    padded_rows = jnp.concatenate(
        [projected, jnp.zeros((1, projected.shape[1]), jnp.bfloat16)], axis=0
    )
    outgoing = padded_rows[source_row]
    received, got_times = (
        lax.all_to_all(outgoing, "seq", split_axis=0, concat_axis=0, tiled=True),
        lax.all_to_all(send_times, "seq", split_axis=0, concat_axis=0, tiled=True),
    )
    mixed = attend_slots(received, got_times)
    returned = lax.all_to_all(mixed, "seq", split_axis=0, concat_axis=0, tiled=True)
    return returned[slot_of_row]


def xor_swap(value, bit, axes=("chip", "core")):
    count = lax.axis_size(axes)
    return lax.ppermute(value, axes, [(d, d ^ bit) for d in range(count)])


def by_bit(bit, mine, theirs, axis):
    return jnp.stack(
        [jnp.where(bit == 0, mine, theirs), jnp.where(bit == 0, theirs, mine)], axis=axis
    )


def zero_after(array):
    last = array[(-1,) * array.ndim]
    return jnp.where(last != last, 1.0, 0.0).astype(jnp.bfloat16)


def body_by_head(frames, conv_weight, qkv_weight, track_ids, track_owner):
    tok_rows = frames.shape[0]
    chips = lax.axis_size("chip")
    devices = 2 * chips
    core = lax.axis_index("core")
    chip = lax.axis_index("chip")
    grp = lax.axis_index("grp")
    me = 2 * chip + core
    both = ("chip", "core")
    every = ("grp", "chip", "core")
    part = 3 * tok_rows // 4
    rest = tok_rows - part
    features = frames.shape[1]
    CORE, Y, Z0, Z1 = 1, 2, 4, 8

    rim_rows = lax.ppermute(
        frames[tok_rows - (KW - 1) :], both, [(i, i + 1) for i in range(devices - 1)]
    )
    late = convolve(frames[part:], conv_weight, frames[part - (KW - 1) : part])
    early = convolve(frames[:part], conv_weight, rim_rows)

    far_late = xor_swap(late, Z1)
    far_early = xor_swap(early, Z1)
    own = jnp.concatenate([early, late], axis=0)
    beside = xor_swap(own, Y)

    half = features // 2
    held = qkv_weight.T.reshape(3, HD // 2, features)

    def to_heads(block, j):
        pairs = [
            (g * devices + d, g * devices + (3 * d + j[g]) % devices)
            for g in (0, 1)
            for d in range(devices)
        ]
        return lax.ppermute(block, every, pairs)

    outer = to_heads(lax.dynamic_index_in_dim(held, 2 * grp, 0, False), (0, 2))
    middle = to_heads(lax.dynamic_slice_in_dim(held[1], grp * half, half, 1), (1, 1))
    mine = jnp.concatenate([outer[:, :half], outer[:, half:], middle], axis=0)
    paired = xor_swap(mine, Z0)

    mine_too = xor_swap(mine, devices, every)

    cut = half // 2
    fourth = [xor_swap(paired[:, :cut], devices, every), xor_swap(mine_too[:, cut:], Z0)]

    far_beside_late = xor_swap(far_late + zero_after(fourth[0]) + zero_after(fourth[1]), Y)
    far_beside_early = xor_swap(far_early, Y)

    fourth = jnp.concatenate(fourth, axis=1)

    def whole_head(pieces, theirs, index):
        size = HD // 2

        def block(values, n):
            return values[n * size : (n + 1) * size]

        first, last = (
            jnp.concatenate(
                [jnp.where(grp == g, block(pieces, n), block(theirs, n)) for n in (0, 1)], axis=1
            )
            for g in (0, 1)
        )
        low, high = block(pieces, 2), block(theirs, 2)
        between = jnp.concatenate(
            [jnp.where(grp == 0, low, high), jnp.where(grp == 0, high, low)], axis=1
        )
        turned = [first, between, last, first, between]
        wide = lax.dynamic_slice_in_dim(jnp.stack(turned), lax.rem(index, 3), 3, 0)
        return by_bit(core, wide, xor_swap(wide, CORE), 1).reshape(3 * HD, features)

    two_heads = jnp.concatenate(
        [whole_head(mine, mine_too, me), whole_head(paired, fourth, me ^ Z0)], axis=0
    )

    def project(rows):
        done = lax.dot_general(
            rows, two_heads, (((1,), (1,)), ((), ())), preferred_element_type=jnp.float32
        ).astype(jnp.bfloat16)
        return jnp.concatenate([done[:, : 3 * HD], xor_swap(done[:, 3 * HD :], Z0)], axis=0)

    first = project(jnp.concatenate([own, beside, far_late, far_beside_late], axis=0))
    second = project(jnp.concatenate([far_early, far_beside_early], axis=0))

    first_rows = [(0, 0, tok_rows), (Y, 0, tok_rows), (Z1, part, rest), (Z1 | Y, part, rest)]
    second_rows = [(Z1, 0, part), (Z1 | Y, 0, part)]
    order = []
    for pieces in (first_rows, second_rows):
        order += pieces + [(far ^ Z0, start, count) for far, start, count in pieces]

    groups = track_groups(track_ids, track_owner)[None, :]
    for bit in (CORE, Y, Z0, Z1):
        groups = jnp.concatenate([groups, xor_swap(groups, bit)], axis=0)

    def of_rows(bit):
        times = [
            (me ^ far ^ bit) * tok_rows + start + jnp.arange(count, dtype=jnp.int32)
            for far, start, count in order
        ]
        marks = [groups[far ^ bit, start : start + count] for far, start, count in order]
        return jnp.concatenate(times), jnp.concatenate(marks)

    projected = jnp.concatenate([first, second], axis=0)
    query = projected[:, :HD]
    keyed = jnp.concatenate(
        [projected[:, HD:], xor_swap(first[:, HD:], CORE), xor_swap(second[:, HD:], CORE)], axis=0
    )
    own_times, own_groups = of_rows(0)
    other_times, other_groups = of_rows(CORE)
    key_times = jnp.concatenate([own_times, other_times])
    key_groups = jnp.concatenate([own_groups, other_groups])
    scores = lax.dot_general(
        query, keyed[:, :HD], (((1,), (1,)), ((), ())), preferred_element_type=jnp.float32
    ) * (1.0 / HD**0.5)
    allowed = (key_times[None, :] <= own_times[:, None]) & (
        key_groups[None, :] == own_groups[:, None]
    )
    scores = jnp.where(allowed, scores, jnp.float32(-1e30))
    expd = jnp.exp(scores - jnp.max(scores, axis=-1, keepdims=True))
    weights = (expd / jnp.sum(expd, axis=-1, keepdims=True)).astype(jnp.bfloat16)
    mixed = jnp.dot(weights, keyed[:, HD:], preferred_element_type=jnp.float32)
    mixed = mixed.astype(jnp.bfloat16)

    sent = jnp.zeros((chips, tok_rows, HD), jnp.bfloat16)
    at = 0
    for far, start, count in order:
        rows = mixed[at : at + count]
        sent = lax.dynamic_update_slice(sent, rows[None], ((me ^ far) >> 1, start, 0))
        at += count
    returned = lax.all_to_all(sent, "chip", split_axis=0, concat_axis=0, tiled=True)
    return returned.transpose(1, 0, 2).reshape(tok_rows, chips * HD)


def solution(mesh):
    grp, seq = mesh.devices.shape
    out_by_owner = P(("grp", "seq"), None)
    by_owner = jax.shard_map(
        body_by_owner,
        mesh=mesh,
        in_specs=(P(("grp", "seq"), None), P(), P(None, "seq"), P(("grp", "seq")), P("grp")),
        out_specs=out_by_owner,
        check_vma=False,
    )
    split = Mesh(mesh.devices.reshape(grp, seq // 2, 2), ("grp", "chip", "core"))
    rows = P(("grp", "chip", "core"))
    by_head = jax.shard_map(
        body_by_head,
        mesh=split,
        in_specs=(rows, P(), P(None, ("chip", "core")), rows, P("grp")),
        out_specs=rows,
        check_vma=False,
    )

    def run(frames, conv_weight, qkv_weight, track_ids, track_owner):
        heads = qkv_weight.shape[1] // (3 * HD)
        plan = by_head if (grp, seq, heads) == (2, 16, 8) else by_owner
        return plan(frames, conv_weight, qkv_weight, track_ids, track_owner)

    return run
```

```python
import jax
import jax.numpy as jnp
from jax import lax
from jax.sharding import Mesh
from jax.sharding import PartitionSpec as P

HD = 128
KW = 4


def from_behind(value, axis, by):
    size = lax.axis_size(axis)
    pairs = [(i, i + by) for i in range(size) if 0 <= i + by < size]
    return lax.ppermute(value, axis, pairs)


def track_groups(track_ids, track_owner):
    track_total = track_owner.shape[0]
    return jnp.sum(
        jnp.where(
            track_ids[:, None] == jnp.arange(track_total, dtype=jnp.int32)[None, :],
            track_owner[None, :],
            0,
        ),
        axis=1,
    )


def convolve(frames, conv_weight, rim_rows):
    tok_rows = frames.shape[0]
    extended = jnp.concatenate([rim_rows, frames], axis=0).astype(jnp.float32)
    conv_sum = frames.astype(jnp.float32)
    for tap in range(KW):
        conv_sum = (
            conv_sum
            + conv_weight[tap].astype(jnp.float32)[None, :]
            * extended[KW - 1 - tap : KW - 1 - tap + tok_rows]
        )
    return conv_sum.astype(jnp.bfloat16)


def attend_slots(packed, positions):
    slot_count = packed.shape[0]
    inner = packed.shape[1] // 3
    head_count = inner // HD
    query = packed[:, :inner].reshape(slot_count, head_count, HD)
    keys_all = packed[:, inner : 2 * inner].reshape(slot_count, head_count, HD)
    values_all = packed[:, 2 * inner :].reshape(slot_count, head_count, HD)
    slot_ids = jnp.arange(slot_count, dtype=jnp.int32)
    score_scale = 1.0 / HD**0.5
    scores = (
        jnp.einsum("qhd,khd->hqk", query, keys_all, preferred_element_type=jnp.float32)
        * score_scale
    )
    allowed = (positions[None, :] >= 0) & (positions[None, :] <= positions[:, None]) | (
        slot_ids[:, None] == slot_ids[None, :]
    )
    scores = jnp.where(allowed[None], scores, jnp.float32(-1e30))
    top_score = jnp.max(scores, axis=-1, keepdims=True)
    expd = jnp.exp(scores - top_score)
    weights = (expd / jnp.sum(expd, axis=-1, keepdims=True)).astype(jnp.bfloat16)
    mixed = jnp.einsum("hqk,khd->qhd", weights, values_all, preferred_element_type=jnp.float32)
    return mixed.astype(jnp.bfloat16).reshape(slot_count, inner)


def body_by_owner(frames, conv_weight, qkv_weight, track_ids, track_owner):
    tok_rows = frames.shape[0]
    peer_count = lax.axis_size("seq")
    capacity = 2 * tok_rows // peer_count
    slot_total = capacity * peer_count
    my_index = lax.axis_index("seq")
    rim_rows = from_behind(frames[tok_rows - (KW - 1) :], "seq", 1)
    hidden = convolve(frames, conv_weight, rim_rows)
    group = track_groups(track_ids, track_owner)
    owner_hits = (group[:, None] == jnp.arange(peer_count, dtype=jnp.int32)[None, :]).astype(
        jnp.int32
    )
    running = jnp.cumsum(owner_hits, axis=0) - 1
    rank_rows = jnp.sum(jnp.where(owner_hits > 0, running, 0), axis=1)
    slot_of_row = group * capacity + rank_rows
    row_ids = jnp.arange(tok_rows, dtype=jnp.int32)
    source_row = jnp.full((slot_total,), tok_rows, jnp.int32).at[slot_of_row].set(row_ids)
    positions = my_index * tok_rows + row_ids
    send_times = jnp.full((slot_total,), -1, jnp.int32).at[slot_of_row].set(positions)
    projected = jnp.dot(
        hidden,
        lax.all_gather(qkv_weight, "seq", axis=1, tiled=True),
        preferred_element_type=jnp.float32,
    ).astype(jnp.bfloat16)
    padded_rows = jnp.concatenate(
        [projected, jnp.zeros((1, projected.shape[1]), jnp.bfloat16)], axis=0
    )
    outgoing = padded_rows[source_row]
    received, got_times = (
        lax.all_to_all(outgoing, "seq", split_axis=0, concat_axis=0, tiled=True),
        lax.all_to_all(send_times, "seq", split_axis=0, concat_axis=0, tiled=True),
    )
    mixed = attend_slots(received, got_times)
    returned = lax.all_to_all(mixed, "seq", split_axis=0, concat_axis=0, tiled=True)
    return returned[slot_of_row]


def xor_swap(value, bit, axes=("chip", "core")):
    count = lax.axis_size(axes)
    return lax.ppermute(value, axes, [(d, d ^ bit) for d in range(count)])


def by_bit(bit, mine, theirs, axis):
    return jnp.stack(
        [jnp.where(bit == 0, mine, theirs), jnp.where(bit == 0, theirs, mine)], axis=axis
    )


def zero_after(array):
    last = array[(-1,) * array.ndim]
    return jnp.where(last != last, 1.0, 0.0).astype(jnp.bfloat16)


def body_by_head(frames, conv_weight, qkv_weight, track_ids, track_owner):
    tok_rows = frames.shape[0]
    chips = lax.axis_size("chip")
    devices = 2 * chips
    core = lax.axis_index("core")
    chip = lax.axis_index("chip")
    grp = lax.axis_index("grp")
    me = 2 * chip + core
    both = ("chip", "core")
    every = ("grp", "chip", "core")
    part = tok_rows // 2
    features = frames.shape[1]
    CORE, Y, Z0, Z1 = 1, 2, 4, 8

    rim_rows = lax.ppermute(
        frames[tok_rows - (KW - 1) :], both, [(i, i + 1) for i in range(devices - 1)]
    )
    late = convolve(frames[part:], conv_weight, frames[part - (KW - 1) : part])
    early = convolve(frames[:part], conv_weight, rim_rows)

    far_late = xor_swap(late, Z1)
    far_early = xor_swap(early, Z1)
    own = jnp.concatenate([early, late], axis=0)
    beside = xor_swap(own, Y)

    half = features // 2
    held = qkv_weight.T.reshape(3, HD // 2, features)

    def to_heads(block, j):
        pairs = [
            (g * devices + d, g * devices + (3 * d + j[g]) % devices)
            for g in (0, 1)
            for d in range(devices)
        ]
        return lax.ppermute(block, every, pairs)

    outer = to_heads(lax.dynamic_index_in_dim(held, 2 * grp, 0, False), (0, 2))
    middle = to_heads(lax.dynamic_slice_in_dim(held[1], grp * half, half, 1), (1, 1))
    mine = jnp.concatenate([outer[:, :half], outer[:, half:], middle], axis=0)
    paired = xor_swap(mine, Z0)

    mine_too = xor_swap(mine, devices, every)

    cut = half // 2
    fourth = [xor_swap(paired[:, :cut], devices, every), xor_swap(mine_too[:, cut:], Z0)]

    far_beside_late = xor_swap(far_late + zero_after(fourth[0]) + zero_after(fourth[1]), Y)
    far_beside_early = xor_swap(far_early, Y)

    fourth = jnp.concatenate(fourth, axis=1)

    def whole_head(pieces, theirs, index):
        size = HD // 2

        def block(values, n):
            return values[n * size : (n + 1) * size]

        first, last = (
            jnp.concatenate(
                [jnp.where(grp == g, block(pieces, n), block(theirs, n)) for n in (0, 1)], axis=1
            )
            for g in (0, 1)
        )
        low, high = block(pieces, 2), block(theirs, 2)
        between = jnp.concatenate(
            [jnp.where(grp == 0, low, high), jnp.where(grp == 0, high, low)], axis=1
        )
        turned = [first, between, last, first, between]
        wide = lax.dynamic_slice_in_dim(jnp.stack(turned), lax.rem(index, 3), 3, 0)
        return by_bit(core, wide, xor_swap(wide, CORE), 1).reshape(3 * HD, features)

    two_heads = jnp.concatenate(
        [whole_head(mine, mine_too, me), whole_head(paired, fourth, me ^ Z0)], axis=0
    )

    def project(rows):
        done = lax.dot_general(
            rows, two_heads, (((1,), (1,)), ((), ())), preferred_element_type=jnp.float32
        ).astype(jnp.bfloat16)
        swapped = xor_swap(done[:, 3 * HD :], Z0)
        return jnp.concatenate([done[:, : 3 * HD], swapped], axis=0), zero_after(done)

    first, _ = project(jnp.concatenate([own, beside, far_early, far_beside_early], axis=0))
    second, _ = project(jnp.concatenate([far_late, far_beside_late], axis=0))

    first_rows = [(0, 0, tok_rows), (Y, 0, tok_rows), (Z1, 0, part), (Z1 | Y, 0, part)]
    second_rows = [(Z1, part, part), (Z1 | Y, part, part)]
    order = []
    for pieces in (first_rows, second_rows):
        order += pieces + [(far ^ Z0, start, count) for far, start, count in pieces]

    groups = track_groups(track_ids, track_owner)[None, :]
    for bit in (CORE, Y, Z0, Z1):
        groups = jnp.concatenate([groups, xor_swap(groups, bit)], axis=0)

    def of_rows(bit):
        times = [
            (me ^ far ^ bit) * tok_rows + start + jnp.arange(count, dtype=jnp.int32)
            for far, start, count in order
        ]
        marks = [groups[far ^ bit, start : start + count] for far, start, count in order]
        return jnp.concatenate(times), jnp.concatenate(marks)

    projected = jnp.concatenate([first, second], axis=0)
    query = projected[:, :HD]
    keyed = jnp.concatenate(
        [projected[:, HD:], xor_swap(first[:, HD:], CORE), xor_swap(second[:, HD:], CORE)], axis=0
    )
    own_times, own_groups = of_rows(0)
    other_times, other_groups = of_rows(CORE)
    key_times = jnp.concatenate([own_times, other_times])
    key_groups = jnp.concatenate([own_groups, other_groups])
    scores = lax.dot_general(
        query, keyed[:, :HD], (((1,), (1,)), ((), ())), preferred_element_type=jnp.float32
    ) * (1.0 / HD**0.5)
    allowed = (key_times[None, :] <= own_times[:, None]) & (
        key_groups[None, :] == own_groups[:, None]
    )
    scores = jnp.where(allowed, scores, jnp.float32(-1e30))
    expd = jnp.exp(scores - jnp.max(scores, axis=-1, keepdims=True))
    weights = (expd / jnp.sum(expd, axis=-1, keepdims=True)).astype(jnp.bfloat16)
    mixed = jnp.dot(weights, keyed[:, HD:], preferred_element_type=jnp.float32)
    mixed = mixed.astype(jnp.bfloat16)

    sent = jnp.zeros((chips, tok_rows, HD), jnp.bfloat16)
    at = 0
    for far, start, count in order:
        rows = mixed[at : at + count]
        sent = lax.dynamic_update_slice(sent, rows[None], ((me ^ far) >> 1, start, 0))
        at += count
    returned = lax.all_to_all(sent, "chip", split_axis=0, concat_axis=0, tiled=True)
    return returned.transpose(1, 0, 2).reshape(tok_rows, chips * HD)


def solution(mesh):
    grp, seq = mesh.devices.shape
    out_by_owner = P(("grp", "seq"), None)
    by_owner = jax.shard_map(
        body_by_owner,
        mesh=mesh,
        in_specs=(P(("grp", "seq"), None), P(), P(None, "seq"), P(("grp", "seq")), P("grp")),
        out_specs=out_by_owner,
        check_vma=False,
    )
    split = Mesh(mesh.devices.reshape(grp, seq // 2, 2), ("grp", "chip", "core"))
    rows = P(("grp", "chip", "core"))
    by_head = jax.shard_map(
        body_by_head,
        mesh=split,
        in_specs=(rows, P(), P(None, ("chip", "core")), rows, P("grp")),
        out_specs=rows,
        check_vma=False,
    )

    def run(frames, conv_weight, qkv_weight, track_ids, track_owner):
        heads = qkv_weight.shape[1] // (3 * HD)
        plan = by_head if (grp, seq, heads) == (2, 16, 8) else by_owner
        return plan(frames, conv_weight, qkv_weight, track_ids, track_owner)

    return run
```

```python
import jax
import jax.numpy as jnp
from jax import lax
from jax.sharding import Mesh
from jax.sharding import PartitionSpec as P

HD = 128
KW = 4


def from_behind(value, axis, by):
    size = lax.axis_size(axis)
    pairs = [(i, i + by) for i in range(size) if 0 <= i + by < size]
    return lax.ppermute(value, axis, pairs)


def track_groups(track_ids, track_owner):
    track_total = track_owner.shape[0]
    return jnp.sum(
        jnp.where(
            track_ids[:, None] == jnp.arange(track_total, dtype=jnp.int32)[None, :],
            track_owner[None, :],
            0,
        ),
        axis=1,
    )


def convolve(frames, conv_weight, rim_rows):
    tok_rows = frames.shape[0]
    extended = jnp.concatenate([rim_rows, frames], axis=0).astype(jnp.float32)
    conv_sum = frames.astype(jnp.float32)
    for tap in range(KW):
        conv_sum = (
            conv_sum
            + conv_weight[tap].astype(jnp.float32)[None, :]
            * extended[KW - 1 - tap : KW - 1 - tap + tok_rows]
        )
    return conv_sum.astype(jnp.bfloat16)


def attend_slots(packed, positions):
    slot_count = packed.shape[0]
    inner = packed.shape[1] // 3
    head_count = inner // HD
    query = packed[:, :inner].reshape(slot_count, head_count, HD)
    keys_all = packed[:, inner : 2 * inner].reshape(slot_count, head_count, HD)
    values_all = packed[:, 2 * inner :].reshape(slot_count, head_count, HD)
    slot_ids = jnp.arange(slot_count, dtype=jnp.int32)
    score_scale = 1.0 / HD**0.5
    scores = (
        jnp.einsum("qhd,khd->hqk", query, keys_all, preferred_element_type=jnp.float32)
        * score_scale
    )
    allowed = (positions[None, :] >= 0) & (positions[None, :] <= positions[:, None]) | (
        slot_ids[:, None] == slot_ids[None, :]
    )
    scores = jnp.where(allowed[None], scores, jnp.float32(-1e30))
    top_score = jnp.max(scores, axis=-1, keepdims=True)
    expd = jnp.exp(scores - top_score)
    weights = (expd / jnp.sum(expd, axis=-1, keepdims=True)).astype(jnp.bfloat16)
    mixed = jnp.einsum("hqk,khd->qhd", weights, values_all, preferred_element_type=jnp.float32)
    return mixed.astype(jnp.bfloat16).reshape(slot_count, inner)


def body_by_owner(frames, conv_weight, qkv_weight, track_ids, track_owner):
    tok_rows = frames.shape[0]
    peer_count = lax.axis_size("seq")
    capacity = 2 * tok_rows // peer_count
    slot_total = capacity * peer_count
    my_index = lax.axis_index("seq")
    rim_rows = from_behind(frames[tok_rows - (KW - 1) :], "seq", 1)
    hidden = convolve(frames, conv_weight, rim_rows)
    group = track_groups(track_ids, track_owner)
    owner_hits = (group[:, None] == jnp.arange(peer_count, dtype=jnp.int32)[None, :]).astype(
        jnp.int32
    )
    running = jnp.cumsum(owner_hits, axis=0) - 1
    rank_rows = jnp.sum(jnp.where(owner_hits > 0, running, 0), axis=1)
    slot_of_row = group * capacity + rank_rows
    row_ids = jnp.arange(tok_rows, dtype=jnp.int32)
    source_row = jnp.full((slot_total,), tok_rows, jnp.int32).at[slot_of_row].set(row_ids)
    positions = my_index * tok_rows + row_ids
    send_times = jnp.full((slot_total,), -1, jnp.int32).at[slot_of_row].set(positions)
    projected = jnp.dot(
        hidden,
        lax.all_gather(qkv_weight, "seq", axis=1, tiled=True),
        preferred_element_type=jnp.float32,
    ).astype(jnp.bfloat16)
    padded_rows = jnp.concatenate(
        [projected, jnp.zeros((1, projected.shape[1]), jnp.bfloat16)], axis=0
    )
    outgoing = padded_rows[source_row]
    received, got_times = (
        lax.all_to_all(outgoing, "seq", split_axis=0, concat_axis=0, tiled=True),
        lax.all_to_all(send_times, "seq", split_axis=0, concat_axis=0, tiled=True),
    )
    mixed = attend_slots(received, got_times)
    returned = lax.all_to_all(mixed, "seq", split_axis=0, concat_axis=0, tiled=True)
    return returned[slot_of_row]


def xor_swap(value, bit, axes=("chip", "core")):
    count = lax.axis_size(axes)
    return lax.ppermute(value, axes, [(d, d ^ bit) for d in range(count)])


def by_bit(bit, mine, theirs, axis):
    return jnp.stack(
        [jnp.where(bit == 0, mine, theirs), jnp.where(bit == 0, theirs, mine)], axis=axis
    )


def zero_after(array):
    last = array[(-1,) * array.ndim]
    return jnp.where(last != last, 1.0, 0.0).astype(jnp.bfloat16)


def body_by_head(frames, conv_weight, qkv_weight, track_ids, track_owner):
    tok_rows = frames.shape[0]
    chips = lax.axis_size("chip")
    devices = 2 * chips
    core = lax.axis_index("core")
    chip = lax.axis_index("chip")
    grp = lax.axis_index("grp")
    me = 2 * chip + core
    both = ("chip", "core")
    every = ("grp", "chip", "core")
    part = tok_rows // 2
    features = frames.shape[1]
    CORE, Y, Z0, Z1 = 1, 2, 4, 8

    rim_rows = lax.ppermute(
        frames[tok_rows - (KW - 1) :], both, [(i, i + 1) for i in range(devices - 1)]
    )
    late = convolve(frames[part:], conv_weight, frames[part - (KW - 1) : part])
    early = convolve(frames[:part], conv_weight, rim_rows)

    far_late = xor_swap(late, Z1)
    far_early = xor_swap(early, Z1)
    own = jnp.concatenate([early, late], axis=0)
    beside = xor_swap(own, Y)

    half = features // 2
    held = qkv_weight.T.reshape(3, HD // 2, features)

    def to_heads(block, j):
        pairs = [
            (g * devices + d, g * devices + (3 * d + j[g]) % devices)
            for g in (0, 1)
            for d in range(devices)
        ]
        return lax.ppermute(block, every, pairs)

    outer = to_heads(lax.dynamic_index_in_dim(held, 2 * grp, 0, False), (0, 2))
    middle = to_heads(lax.dynamic_slice_in_dim(held[1], grp * half, half, 1), (1, 1))
    mine = jnp.concatenate([outer[:, :half], outer[:, half:], middle], axis=0)
    paired = xor_swap(mine, Z0)

    mine_too = xor_swap(mine, devices, every)

    cut = half // 2
    fourth = [xor_swap(paired[:, :cut], devices, every), xor_swap(mine_too[:, cut:], Z0)]

    far_beside_late = xor_swap(far_late + zero_after(fourth[0]) + zero_after(fourth[1]), Y)
    far_beside_early = xor_swap(far_early, Y)

    fourth = jnp.concatenate(fourth, axis=1)

    def whole_head(pieces, theirs, index):
        size = HD // 2

        def block(values, n):
            return values[n * size : (n + 1) * size]

        first, last = (
            jnp.concatenate(
                [jnp.where(grp == g, block(pieces, n), block(theirs, n)) for n in (0, 1)], axis=1
            )
            for g in (0, 1)
        )
        low, high = block(pieces, 2), block(theirs, 2)
        between = jnp.concatenate(
            [jnp.where(grp == 0, low, high), jnp.where(grp == 0, high, low)], axis=1
        )
        turned = [first, between, last, first, between]
        wide = lax.dynamic_slice_in_dim(jnp.stack(turned), lax.rem(index, 3), 3, 0)
        return by_bit(core, wide, xor_swap(wide, CORE), 1).reshape(3 * HD, features)

    two_heads = jnp.concatenate(
        [whole_head(mine, mine_too, me), whole_head(paired, fourth, me ^ Z0)], axis=0
    )

    def project(rows):
        done = lax.dot_general(
            rows, two_heads, (((1,), (1,)), ((), ())), preferred_element_type=jnp.float32
        ).astype(jnp.bfloat16)
        return jnp.concatenate([done[:, : 3 * HD], xor_swap(done[:, 3 * HD :], Z0)], axis=0)

    first = project(jnp.concatenate([own, beside, far_late, far_beside_late], axis=0))
    second = project(jnp.concatenate([far_early, far_beside_early], axis=0))

    first_rows = [(0, 0, tok_rows), (Y, 0, tok_rows), (Z1, part, part), (Z1 | Y, part, part)]
    second_rows = [(Z1, 0, part), (Z1 | Y, 0, part)]
    order = []
    for pieces in (first_rows, second_rows):
        order += pieces + [(far ^ Z0, start, count) for far, start, count in pieces]

    groups = track_groups(track_ids, track_owner)[None, :]
    for bit in (CORE, Y, Z0, Z1):
        groups = jnp.concatenate([groups, xor_swap(groups, bit)], axis=0)

    def of_rows(bit):
        times = [
            (me ^ far ^ bit) * tok_rows + start + jnp.arange(count, dtype=jnp.int32)
            for far, start, count in order
        ]
        marks = [groups[far ^ bit, start : start + count] for far, start, count in order]
        return jnp.concatenate(times), jnp.concatenate(marks)

    projected = jnp.concatenate([first, second], axis=0)
    query = projected[:, :HD]
    keyed = jnp.concatenate(
        [projected[:, HD:], xor_swap(first[:, HD:], CORE), xor_swap(second[:, HD:], CORE)], axis=0
    )
    own_times, own_groups = of_rows(0)
    other_times, other_groups = of_rows(CORE)
    key_times = jnp.concatenate([own_times, other_times])
    key_groups = jnp.concatenate([own_groups, other_groups])
    scores = lax.dot_general(
        query, keyed[:, :HD], (((1,), (1,)), ((), ())), preferred_element_type=jnp.float32
    ) * (1.0 / HD**0.5)
    allowed = (key_times[None, :] <= own_times[:, None]) & (
        key_groups[None, :] == own_groups[:, None]
    )
    scores = jnp.where(allowed, scores, jnp.float32(-1e30))
    expd = jnp.exp(scores - jnp.max(scores, axis=-1, keepdims=True))
    share = 1.0 / jnp.sum(expd, axis=-1, keepdims=True)
    weights = (expd * share).astype(jnp.bfloat16)
    mixed = jnp.dot(weights, keyed[:, HD:], preferred_element_type=jnp.float32)
    mixed = mixed.astype(jnp.bfloat16)

    sent = jnp.zeros((chips, tok_rows, HD), jnp.bfloat16)
    at = 0
    for far, start, count in order:
        rows = mixed[at : at + count]
        sent = lax.dynamic_update_slice(sent, rows[None], ((me ^ far) >> 1, start, 0))
        at += count
    returned = lax.all_to_all(sent, "chip", split_axis=0, concat_axis=0, tiled=True)
    return returned.transpose(1, 0, 2).reshape(tok_rows, chips * HD)


def solution(mesh):
    grp, seq = mesh.devices.shape
    out_by_owner = P(("grp", "seq"), None)
    by_owner = jax.shard_map(
        body_by_owner,
        mesh=mesh,
        in_specs=(P(("grp", "seq"), None), P(), P(None, "seq"), P(("grp", "seq")), P("grp")),
        out_specs=out_by_owner,
        check_vma=False,
    )
    split = Mesh(mesh.devices.reshape(grp, seq // 2, 2), ("grp", "chip", "core"))
    rows = P(("grp", "chip", "core"))
    by_head = jax.shard_map(
        body_by_head,
        mesh=split,
        in_specs=(rows, P(), P(None, ("chip", "core")), rows, P("grp")),
        out_specs=rows,
        check_vma=False,
    )

    def run(frames, conv_weight, qkv_weight, track_ids, track_owner):
        heads = qkv_weight.shape[1] // (3 * HD)
        plan = by_head if (grp, seq, heads) == (2, 16, 8) else by_owner
        return plan(frames, conv_weight, qkv_weight, track_ids, track_owner)

    return run
```

```python
import jax
import jax.numpy as jnp
from jax import lax
from jax.sharding import Mesh
from jax.sharding import PartitionSpec as P

HD = 128
KW = 4


def from_behind(value, axis, by):
    size = lax.axis_size(axis)
    pairs = [(i, i + by) for i in range(size) if 0 <= i + by < size]
    return lax.ppermute(value, axis, pairs)


def track_groups(track_ids, track_owner):
    track_total = track_owner.shape[0]
    return jnp.sum(
        jnp.where(
            track_ids[:, None] == jnp.arange(track_total, dtype=jnp.int32)[None, :],
            track_owner[None, :],
            0,
        ),
        axis=1,
    )


def convolve(frames, conv_weight, rim_rows):
    tok_rows = frames.shape[0]
    extended = jnp.concatenate([rim_rows, frames], axis=0).astype(jnp.float32)
    conv_sum = frames.astype(jnp.float32)
    for tap in range(KW):
        conv_sum = (
            conv_sum
            + conv_weight[tap].astype(jnp.float32)[None, :]
            * extended[KW - 1 - tap : KW - 1 - tap + tok_rows]
        )
    return conv_sum.astype(jnp.bfloat16)


def attend_slots(packed, positions):
    slot_count = packed.shape[0]
    inner = packed.shape[1] // 3
    head_count = inner // HD
    query = packed[:, :inner].reshape(slot_count, head_count, HD)
    keys_all = packed[:, inner : 2 * inner].reshape(slot_count, head_count, HD)
    values_all = packed[:, 2 * inner :].reshape(slot_count, head_count, HD)
    slot_ids = jnp.arange(slot_count, dtype=jnp.int32)
    score_scale = 1.0 / HD**0.5
    scores = (
        jnp.einsum("qhd,khd->hqk", query, keys_all, preferred_element_type=jnp.float32)
        * score_scale
    )
    allowed = (positions[None, :] >= 0) & (positions[None, :] <= positions[:, None]) | (
        slot_ids[:, None] == slot_ids[None, :]
    )
    scores = jnp.where(allowed[None], scores, jnp.float32(-1e30))
    top_score = jnp.max(scores, axis=-1, keepdims=True)
    expd = jnp.exp(scores - top_score)
    weights = (expd / jnp.sum(expd, axis=-1, keepdims=True)).astype(jnp.bfloat16)
    mixed = jnp.einsum("hqk,khd->qhd", weights, values_all, preferred_element_type=jnp.float32)
    return mixed.astype(jnp.bfloat16).reshape(slot_count, inner)


def body_by_owner(frames, conv_weight, qkv_weight, track_ids, track_owner):
    tok_rows = frames.shape[0]
    peer_count = lax.axis_size("seq")
    capacity = 2 * tok_rows // peer_count
    slot_total = capacity * peer_count
    my_index = lax.axis_index("seq")
    rim_rows = from_behind(frames[tok_rows - (KW - 1) :], "seq", 1)
    hidden = convolve(frames, conv_weight, rim_rows)
    group = track_groups(track_ids, track_owner)
    owner_hits = (group[:, None] == jnp.arange(peer_count, dtype=jnp.int32)[None, :]).astype(
        jnp.int32
    )
    running = jnp.cumsum(owner_hits, axis=0) - 1
    rank_rows = jnp.sum(jnp.where(owner_hits > 0, running, 0), axis=1)
    slot_of_row = group * capacity + rank_rows
    row_ids = jnp.arange(tok_rows, dtype=jnp.int32)
    source_row = jnp.full((slot_total,), tok_rows, jnp.int32).at[slot_of_row].set(row_ids)
    positions = my_index * tok_rows + row_ids
    send_times = jnp.full((slot_total,), -1, jnp.int32).at[slot_of_row].set(positions)
    projected = jnp.dot(
        hidden,
        lax.all_gather(qkv_weight, "seq", axis=1, tiled=True),
        preferred_element_type=jnp.float32,
    ).astype(jnp.bfloat16)
    padded_rows = jnp.concatenate(
        [projected, jnp.zeros((1, projected.shape[1]), jnp.bfloat16)], axis=0
    )
    outgoing = padded_rows[source_row]
    received, got_times = (
        lax.all_to_all(outgoing, "seq", split_axis=0, concat_axis=0, tiled=True),
        lax.all_to_all(send_times, "seq", split_axis=0, concat_axis=0, tiled=True),
    )
    mixed = attend_slots(received, got_times)
    returned = lax.all_to_all(mixed, "seq", split_axis=0, concat_axis=0, tiled=True)
    return returned[slot_of_row]


def xor_swap(value, bit, axes=("chip", "core")):
    count = lax.axis_size(axes)
    return lax.ppermute(value, axes, [(d, d ^ bit) for d in range(count)])


def by_bit(bit, mine, theirs, axis):
    return jnp.stack(
        [jnp.where(bit == 0, mine, theirs), jnp.where(bit == 0, theirs, mine)], axis=axis
    )


def zero_after(array):
    last = array[(-1,) * array.ndim]
    return jnp.where(last != last, 1.0, 0.0).astype(jnp.bfloat16)


def body_by_head(frames, conv_weight, qkv_weight, track_ids, track_owner):
    tok_rows = frames.shape[0]
    chips = lax.axis_size("chip")
    devices = 2 * chips
    core = lax.axis_index("core")
    chip = lax.axis_index("chip")
    grp = lax.axis_index("grp")
    me = 2 * chip + core
    both = ("chip", "core")
    every = ("grp", "chip", "core")
    part = tok_rows // 2
    features = frames.shape[1]
    CORE, Y, Z0, Z1 = 1, 2, 4, 8

    rim_rows = lax.ppermute(
        frames[tok_rows - (KW - 1) :], both, [(i, i + 1) for i in range(devices - 1)]
    )
    late = convolve(frames[part:], conv_weight, frames[part - (KW - 1) : part])
    early = convolve(frames[:part], conv_weight, rim_rows)

    far_late = xor_swap(late, Z1)
    far_early = xor_swap(early, Z1)
    own = jnp.concatenate([early, late], axis=0)
    beside = xor_swap(own, Y)

    half = features // 2
    held = qkv_weight.T.reshape(3, HD // 2, features)

    def to_heads(block, j):
        pairs = [
            (g * devices + d, g * devices + (3 * d + j[g]) % devices)
            for g in (0, 1)
            for d in range(devices)
        ]
        return lax.ppermute(block, every, pairs)

    outer = to_heads(lax.dynamic_index_in_dim(held, 2 * grp, 0, False), (0, 2))
    middle = to_heads(lax.dynamic_slice_in_dim(held[1], grp * half, half, 1), (1, 1))
    mine = jnp.concatenate([outer[:, :half], outer[:, half:], middle], axis=0)
    paired = xor_swap(mine, Z0)

    mine_too = xor_swap(mine, devices, every)

    cut = half // 2
    fourth = [xor_swap(paired[:, :cut], devices, every), xor_swap(mine_too[:, cut:], Z0)]

    far_beside_late = xor_swap(far_late + zero_after(fourth[0]) + zero_after(fourth[1]), Y)
    far_beside_early = xor_swap(far_early, Y)

    fourth = jnp.concatenate(fourth, axis=1)

    def whole_head(pieces, theirs, index):
        size = HD // 2

        def block(values, n):
            return values[n * size : (n + 1) * size]

        first, last = (
            jnp.concatenate(
                [jnp.where(grp == g, block(pieces, n), block(theirs, n)) for n in (0, 1)], axis=1
            )
            for g in (0, 1)
        )
        low, high = block(pieces, 2), block(theirs, 2)
        between = jnp.concatenate(
            [jnp.where(grp == 0, low, high), jnp.where(grp == 0, high, low)], axis=1
        )
        turned = [first, between, last, first, between]
        wide = lax.dynamic_slice_in_dim(jnp.stack(turned), lax.rem(index, 3), 3, 0)
        return by_bit(core, wide, xor_swap(wide, CORE), 1).reshape(3 * HD, features)

    two_heads = jnp.concatenate(
        [whole_head(mine, mine_too, me), whole_head(paired, fourth, me ^ Z0)], axis=0
    )

    def project(rows):
        done = lax.dot_general(
            rows, two_heads, (((1,), (1,)), ((), ())), preferred_element_type=jnp.float32
        ).astype(jnp.bfloat16)
        return jnp.concatenate([done[:, : 3 * HD], xor_swap(done[:, 3 * HD :], Z0)], axis=0)

    first = project(jnp.concatenate([own, beside, far_late, far_beside_late], axis=0))
    second = project(jnp.concatenate([far_early, far_beside_early], axis=0))

    first_rows = [(0, 0, tok_rows), (Y, 0, tok_rows), (Z1, part, part), (Z1 | Y, part, part)]
    second_rows = [(Z1, 0, part), (Z1 | Y, 0, part)]
    order = []
    for pieces in (first_rows, second_rows):
        order += pieces + [(far ^ Z0, start, count) for far, start, count in pieces]

    groups = track_ids[None, :]
    for bit in (CORE, Y, Z0, Z1):
        groups = jnp.concatenate([groups, xor_swap(groups, bit)], axis=0)
    groups = track_groups(groups.reshape(-1), track_owner).reshape(groups.shape)

    def of_rows(bit):
        times = [
            (me ^ far ^ bit) * tok_rows + start + jnp.arange(count, dtype=jnp.int32)
            for far, start, count in order
        ]
        marks = [groups[far ^ bit, start : start + count] for far, start, count in order]
        return jnp.concatenate(times), jnp.concatenate(marks)

    projected = jnp.concatenate([first, second], axis=0)
    query = projected[:, :HD]
    keyed = jnp.concatenate(
        [projected[:, HD:], xor_swap(first[:, HD:], CORE), xor_swap(second[:, HD:], CORE)], axis=0
    )
    own_times, own_groups = of_rows(0)
    other_times, other_groups = of_rows(CORE)
    key_times = jnp.concatenate([own_times, other_times])
    key_groups = jnp.concatenate([own_groups, other_groups])
    scores = lax.dot_general(
        query, keyed[:, :HD], (((1,), (1,)), ((), ())), preferred_element_type=jnp.float32
    ) * (1.0 / HD**0.5)
    allowed = (key_times[None, :] <= own_times[:, None]) & (
        key_groups[None, :] == own_groups[:, None]
    )
    scores = jnp.where(allowed, scores, jnp.float32(-1e30))
    expd = jnp.exp(scores - jnp.max(scores, axis=-1, keepdims=True))
    share = 1.0 / jnp.sum(expd, axis=-1, keepdims=True)
    weights = (expd * share).astype(jnp.bfloat16)
    mixed = jnp.dot(weights, keyed[:, HD:], preferred_element_type=jnp.float32)
    mixed = mixed.astype(jnp.bfloat16)

    sent = jnp.zeros((chips, tok_rows, HD), jnp.bfloat16)
    at = 0
    for far, start, count in order:
        rows = mixed[at : at + count]
        sent = lax.dynamic_update_slice(sent, rows[None], ((me ^ far) >> 1, start, 0))
        at += count
    returned = lax.all_to_all(sent, "chip", split_axis=0, concat_axis=0, tiled=True)
    return returned.transpose(1, 0, 2).reshape(tok_rows, chips * HD)


def solution(mesh):
    grp, seq = mesh.devices.shape
    out_by_owner = P(("grp", "seq"), None)
    by_owner = jax.shard_map(
        body_by_owner,
        mesh=mesh,
        in_specs=(P(("grp", "seq"), None), P(), P(None, "seq"), P(("grp", "seq")), P("grp")),
        out_specs=out_by_owner,
        check_vma=False,
    )
    split = Mesh(mesh.devices.reshape(grp, seq // 2, 2), ("grp", "chip", "core"))
    rows = P(("grp", "chip", "core"))
    by_head = jax.shard_map(
        body_by_head,
        mesh=split,
        in_specs=(rows, P(), P(None, ("chip", "core")), rows, P("grp")),
        out_specs=rows,
        check_vma=False,
    )

    def run(frames, conv_weight, qkv_weight, track_ids, track_owner):
        heads = qkv_weight.shape[1] // (3 * HD)
        plan = by_head if (grp, seq, heads) == (2, 16, 8) else by_owner
        return plan(frames, conv_weight, qkv_weight, track_ids, track_owner)

    return run
```

```python
import jax
import jax.numpy as jnp
from jax import lax
from jax.sharding import Mesh
from jax.sharding import PartitionSpec as P

HD = 128
KW = 4


def from_behind(value, axis, by):
    size = lax.axis_size(axis)
    pairs = [(i, i + by) for i in range(size) if 0 <= i + by < size]
    return lax.ppermute(value, axis, pairs)


def track_groups(track_ids, track_owner):
    track_total = track_owner.shape[0]
    return jnp.sum(
        jnp.where(
            track_ids[:, None] == jnp.arange(track_total, dtype=jnp.int32)[None, :],
            track_owner[None, :],
            0,
        ),
        axis=1,
    )


def convolve(frames, conv_weight, rim_rows):
    tok_rows = frames.shape[0]
    extended = jnp.concatenate([rim_rows, frames], axis=0).astype(jnp.float32)
    conv_sum = frames.astype(jnp.float32)
    for tap in range(KW):
        conv_sum = (
            conv_sum
            + conv_weight[tap].astype(jnp.float32)[None, :]
            * extended[KW - 1 - tap : KW - 1 - tap + tok_rows]
        )
    return conv_sum.astype(jnp.bfloat16)


def attend_slots(packed, positions):
    slot_count = packed.shape[0]
    inner = packed.shape[1] // 3
    head_count = inner // HD
    query = packed[:, :inner].reshape(slot_count, head_count, HD)
    keys_all = packed[:, inner : 2 * inner].reshape(slot_count, head_count, HD)
    values_all = packed[:, 2 * inner :].reshape(slot_count, head_count, HD)
    slot_ids = jnp.arange(slot_count, dtype=jnp.int32)
    score_scale = 1.0 / HD**0.5
    scores = (
        jnp.einsum("qhd,khd->hqk", query, keys_all, preferred_element_type=jnp.float32)
        * score_scale
    )
    allowed = (positions[None, :] >= 0) & (positions[None, :] <= positions[:, None]) | (
        slot_ids[:, None] == slot_ids[None, :]
    )
    scores = jnp.where(allowed[None], scores, jnp.float32(-1e30))
    top_score = jnp.max(scores, axis=-1, keepdims=True)
    expd = jnp.exp(scores - top_score)
    weights = (expd / jnp.sum(expd, axis=-1, keepdims=True)).astype(jnp.bfloat16)
    mixed = jnp.einsum("hqk,khd->qhd", weights, values_all, preferred_element_type=jnp.float32)
    return mixed.astype(jnp.bfloat16).reshape(slot_count, inner)


def body_by_owner(frames, conv_weight, qkv_weight, track_ids, track_owner):
    tok_rows = frames.shape[0]
    peer_count = lax.axis_size("seq")
    capacity = 2 * tok_rows // peer_count
    slot_total = capacity * peer_count
    my_index = lax.axis_index("seq")
    rim_rows = from_behind(frames[tok_rows - (KW - 1) :], "seq", 1)
    hidden = convolve(frames, conv_weight, rim_rows)
    group = track_groups(track_ids, track_owner)
    owner_hits = (group[:, None] == jnp.arange(peer_count, dtype=jnp.int32)[None, :]).astype(
        jnp.int32
    )
    running = jnp.cumsum(owner_hits, axis=0) - 1
    rank_rows = jnp.sum(jnp.where(owner_hits > 0, running, 0), axis=1)
    slot_of_row = group * capacity + rank_rows
    row_ids = jnp.arange(tok_rows, dtype=jnp.int32)
    source_row = jnp.full((slot_total,), tok_rows, jnp.int32).at[slot_of_row].set(row_ids)
    positions = my_index * tok_rows + row_ids
    send_times = jnp.full((slot_total,), -1, jnp.int32).at[slot_of_row].set(positions)
    projected = jnp.dot(
        hidden,
        lax.all_gather(qkv_weight, "seq", axis=1, tiled=True),
        preferred_element_type=jnp.float32,
    ).astype(jnp.bfloat16)
    padded_rows = jnp.concatenate(
        [projected, jnp.zeros((1, projected.shape[1]), jnp.bfloat16)], axis=0
    )
    outgoing = padded_rows[source_row]
    received, got_times = (
        lax.all_to_all(outgoing, "seq", split_axis=0, concat_axis=0, tiled=True),
        lax.all_to_all(send_times, "seq", split_axis=0, concat_axis=0, tiled=True),
    )
    mixed = attend_slots(received, got_times)
    returned = lax.all_to_all(mixed, "seq", split_axis=0, concat_axis=0, tiled=True)
    return returned[slot_of_row]


def xor_swap(value, bit, axes=("chip", "core")):
    count = lax.axis_size(axes)
    return lax.ppermute(value, axes, [(d, d ^ bit) for d in range(count)])


def by_bit(bit, mine, theirs, axis):
    return jnp.stack(
        [jnp.where(bit == 0, mine, theirs), jnp.where(bit == 0, theirs, mine)], axis=axis
    )


def zero_after(array):
    last = array[(-1,) * array.ndim]
    return jnp.where(last != last, 1.0, 0.0).astype(jnp.bfloat16)


def body_by_head(frames, conv_weight, qkv_weight, track_ids, track_owner):
    tok_rows = frames.shape[0]
    chips = lax.axis_size("chip")
    devices = 2 * chips
    core = lax.axis_index("core")
    chip = lax.axis_index("chip")
    grp = lax.axis_index("grp")
    me = 2 * chip + core
    both = ("chip", "core")
    every = ("grp", "chip", "core")
    part = tok_rows // 2
    features = frames.shape[1]
    CORE, Y, Z0, Z1 = 1, 2, 4, 8

    rim_rows = lax.ppermute(
        frames[tok_rows - (KW - 1) :], both, [(i, i + 1) for i in range(devices - 1)]
    )
    late = convolve(frames[part:], conv_weight, frames[part - (KW - 1) : part])
    early = convolve(frames[:part], conv_weight, rim_rows)

    far_late = xor_swap(late, Z1)
    far_early = xor_swap(early, Z1)
    own = jnp.concatenate([early, late], axis=0)
    beside = xor_swap(own, Y)

    half = features // 2
    held = qkv_weight.T.reshape(3, HD // 2, features)

    def to_heads(block, j):
        pairs = [
            (g * devices + d, g * devices + (3 * d + j[g]) % devices)
            for g in (0, 1)
            for d in range(devices)
        ]
        return lax.ppermute(block, every, pairs)

    outer = to_heads(lax.dynamic_index_in_dim(held, 2 * grp, 0, False), (0, 2))
    middle = to_heads(lax.dynamic_slice_in_dim(held[1], grp * half, half, 1), (1, 1))
    mine = jnp.concatenate([outer[:, :half], outer[:, half:], middle], axis=0)
    paired = xor_swap(mine, Z0)

    mine_too = xor_swap(mine, devices, every)

    cut = half // 2
    fourth = [xor_swap(paired[:, :cut], devices, every), xor_swap(mine_too[:, cut:], Z0)]

    far_beside_late = xor_swap(far_late + zero_after(fourth[0]) + zero_after(fourth[1]), Y)
    far_beside_early = xor_swap(far_early, Y)

    fourth = jnp.concatenate(fourth, axis=1)

    def whole_head(pieces, theirs, index):
        size = HD // 2

        def block(values, n):
            return values[n * size : (n + 1) * size]

        first, last = (
            jnp.concatenate(
                [jnp.where(grp == g, block(pieces, n), block(theirs, n)) for n in (0, 1)], axis=1
            )
            for g in (0, 1)
        )
        low, high = block(pieces, 2), block(theirs, 2)
        between = jnp.concatenate(
            [jnp.where(grp == 0, low, high), jnp.where(grp == 0, high, low)], axis=1
        )
        turned = [first, between, last, first, between]
        wide = lax.dynamic_slice_in_dim(jnp.stack(turned), lax.rem(index, 3), 3, 0)
        return by_bit(core, wide, xor_swap(wide, CORE), 1).reshape(3 * HD, features)

    two_heads = jnp.concatenate(
        [whole_head(mine, mine_too, me), whole_head(paired, fourth, me ^ Z0)], axis=0
    )

    def project(rows):
        done = lax.dot_general(
            rows, two_heads, (((1,), (1,)), ((), ())), preferred_element_type=jnp.float32
        ).astype(jnp.bfloat16)
        return jnp.concatenate([done[:, : 3 * HD], xor_swap(done[:, 3 * HD :], Z0)], axis=0)

    second = project(jnp.concatenate([far_early, far_beside_early], axis=0))
    first = project(jnp.concatenate([own, beside, far_late, far_beside_late + zero_after(second[:part])], axis=0))

    first_rows = [(0, 0, tok_rows), (Y, 0, tok_rows), (Z1, part, part), (Z1 | Y, part, part)]
    second_rows = [(Z1, 0, part), (Z1 | Y, 0, part)]
    order = []
    for pieces in (first_rows, second_rows):
        order += pieces + [(far ^ Z0, start, count) for far, start, count in pieces]

    groups = track_groups(track_ids, track_owner)[None, :]
    for bit in (CORE, Y, Z0, Z1):
        groups = jnp.concatenate([groups, xor_swap(groups, bit)], axis=0)

    def of_rows(bit):
        times = [
            (me ^ far ^ bit) * tok_rows + start + jnp.arange(count, dtype=jnp.int32)
            for far, start, count in order
        ]
        marks = [groups[far ^ bit, start : start + count] for far, start, count in order]
        return jnp.concatenate(times), jnp.concatenate(marks)

    projected = jnp.concatenate([first, second], axis=0)
    query = projected[:, :HD]
    keyed = jnp.concatenate(
        [projected[:, HD:], xor_swap(first[:, HD:], CORE), xor_swap(second[:, HD:], CORE)], axis=0
    )
    own_times, own_groups = of_rows(0)
    other_times, other_groups = of_rows(CORE)
    key_times = jnp.concatenate([own_times, other_times])
    key_groups = jnp.concatenate([own_groups, other_groups])
    scores = lax.dot_general(
        query, keyed[:, :HD], (((1,), (1,)), ((), ())), preferred_element_type=jnp.float32
    ) * (1.0 / HD**0.5)
    allowed = (key_times[None, :] <= own_times[:, None]) & (
        key_groups[None, :] == own_groups[:, None]
    )
    scores = jnp.where(allowed, scores, jnp.float32(-1e30))
    expd = jnp.exp(scores - jnp.max(scores, axis=-1, keepdims=True))
    share = 1.0 / jnp.sum(expd, axis=-1, keepdims=True)
    weights = (expd * share).astype(jnp.bfloat16)
    mixed = jnp.dot(weights, keyed[:, HD:], preferred_element_type=jnp.float32)
    mixed = mixed.astype(jnp.bfloat16)

    sent = jnp.zeros((chips, tok_rows, HD), jnp.bfloat16)
    at = 0
    for far, start, count in order:
        rows = mixed[at : at + count]
        sent = lax.dynamic_update_slice(sent, rows[None], ((me ^ far) >> 1, start, 0))
        at += count
    returned = lax.all_to_all(sent, "chip", split_axis=0, concat_axis=0, tiled=True)
    return returned.transpose(1, 0, 2).reshape(tok_rows, chips * HD)


def solution(mesh):
    grp, seq = mesh.devices.shape
    out_by_owner = P(("grp", "seq"), None)
    by_owner = jax.shard_map(
        body_by_owner,
        mesh=mesh,
        in_specs=(P(("grp", "seq"), None), P(), P(None, "seq"), P(("grp", "seq")), P("grp")),
        out_specs=out_by_owner,
        check_vma=False,
    )
    split = Mesh(mesh.devices.reshape(grp, seq // 2, 2), ("grp", "chip", "core"))
    rows = P(("grp", "chip", "core"))
    by_head = jax.shard_map(
        body_by_head,
        mesh=split,
        in_specs=(rows, P(), P(None, ("chip", "core")), rows, P("grp")),
        out_specs=rows,
        check_vma=False,
    )

    def run(frames, conv_weight, qkv_weight, track_ids, track_owner):
        heads = qkv_weight.shape[1] // (3 * HD)
        plan = by_head if (grp, seq, heads) == (2, 16, 8) else by_owner
        return plan(frames, conv_weight, qkv_weight, track_ids, track_owner)

    return run
```

```python
import jax
import jax.numpy as jnp
from jax import lax
from jax.sharding import Mesh
from jax.sharding import PartitionSpec as P

HD = 128
KW = 4


def from_behind(value, axis, by):
    size = lax.axis_size(axis)
    pairs = [(i, i + by) for i in range(size) if 0 <= i + by < size]
    return lax.ppermute(value, axis, pairs)


def track_groups(track_ids, track_owner):
    track_total = track_owner.shape[0]
    return jnp.sum(
        jnp.where(
            track_ids[:, None] == jnp.arange(track_total, dtype=jnp.int32)[None, :],
            track_owner[None, :],
            0,
        ),
        axis=1,
    )


def convolve(frames, conv_weight, rim_rows):
    tok_rows = frames.shape[0]
    extended = jnp.concatenate([rim_rows, frames], axis=0).astype(jnp.float32)
    conv_sum = frames.astype(jnp.float32)
    for tap in range(KW):
        conv_sum = (
            conv_sum
            + conv_weight[tap].astype(jnp.float32)[None, :]
            * extended[KW - 1 - tap : KW - 1 - tap + tok_rows]
        )
    return conv_sum.astype(jnp.bfloat16)


def attend_slots(packed, positions):
    slot_count = packed.shape[0]
    inner = packed.shape[1] // 3
    head_count = inner // HD
    query = packed[:, :inner].reshape(slot_count, head_count, HD)
    keys_all = packed[:, inner : 2 * inner].reshape(slot_count, head_count, HD)
    values_all = packed[:, 2 * inner :].reshape(slot_count, head_count, HD)
    slot_ids = jnp.arange(slot_count, dtype=jnp.int32)
    score_scale = 1.0 / HD**0.5
    scores = (
        jnp.einsum("qhd,khd->hqk", query, keys_all, preferred_element_type=jnp.float32)
        * score_scale
    )
    allowed = (positions[None, :] >= 0) & (positions[None, :] <= positions[:, None]) | (
        slot_ids[:, None] == slot_ids[None, :]
    )
    scores = jnp.where(allowed[None], scores, jnp.float32(-1e30))
    top_score = jnp.max(scores, axis=-1, keepdims=True)
    expd = jnp.exp(scores - top_score)
    weights = (expd / jnp.sum(expd, axis=-1, keepdims=True)).astype(jnp.bfloat16)
    mixed = jnp.einsum("hqk,khd->qhd", weights, values_all, preferred_element_type=jnp.float32)
    return mixed.astype(jnp.bfloat16).reshape(slot_count, inner)


def body_by_owner(frames, conv_weight, qkv_weight, track_ids, track_owner):
    tok_rows = frames.shape[0]
    peer_count = lax.axis_size("seq")
    capacity = 2 * tok_rows // peer_count
    slot_total = capacity * peer_count
    my_index = lax.axis_index("seq")
    rim_rows = from_behind(frames[tok_rows - (KW - 1) :], "seq", 1)
    hidden = convolve(frames, conv_weight, rim_rows)
    group = track_groups(track_ids, track_owner)
    owner_hits = (group[:, None] == jnp.arange(peer_count, dtype=jnp.int32)[None, :]).astype(
        jnp.int32
    )
    running = jnp.cumsum(owner_hits, axis=0) - 1
    rank_rows = jnp.sum(jnp.where(owner_hits > 0, running, 0), axis=1)
    slot_of_row = group * capacity + rank_rows
    row_ids = jnp.arange(tok_rows, dtype=jnp.int32)
    source_row = jnp.full((slot_total,), tok_rows, jnp.int32).at[slot_of_row].set(row_ids)
    positions = my_index * tok_rows + row_ids
    send_times = jnp.full((slot_total,), -1, jnp.int32).at[slot_of_row].set(positions)
    projected = jnp.dot(
        hidden,
        lax.all_gather(qkv_weight, "seq", axis=1, tiled=True),
        preferred_element_type=jnp.float32,
    ).astype(jnp.bfloat16)
    padded_rows = jnp.concatenate(
        [projected, jnp.zeros((1, projected.shape[1]), jnp.bfloat16)], axis=0
    )
    outgoing = padded_rows[source_row]
    received, got_times = (
        lax.all_to_all(outgoing, "seq", split_axis=0, concat_axis=0, tiled=True),
        lax.all_to_all(send_times, "seq", split_axis=0, concat_axis=0, tiled=True),
    )
    mixed = attend_slots(received, got_times)
    returned = lax.all_to_all(mixed, "seq", split_axis=0, concat_axis=0, tiled=True)
    return returned[slot_of_row]


def xor_swap(value, bit, axes=("chip", "core")):
    count = lax.axis_size(axes)
    return lax.ppermute(value, axes, [(d, d ^ bit) for d in range(count)])


def by_bit(bit, mine, theirs, axis):
    return jnp.stack(
        [jnp.where(bit == 0, mine, theirs), jnp.where(bit == 0, theirs, mine)], axis=axis
    )


def zero_after(array):
    last = array[(-1,) * array.ndim]
    return jnp.where(last != last, 1.0, 0.0).astype(jnp.bfloat16)


def body_by_head(frames, conv_weight, qkv_weight, track_ids, track_owner):
    tok_rows = frames.shape[0]
    chips = lax.axis_size("chip")
    devices = 2 * chips
    core = lax.axis_index("core")
    chip = lax.axis_index("chip")
    grp = lax.axis_index("grp")
    me = 2 * chip + core
    both = ("chip", "core")
    every = ("grp", "chip", "core")
    part = tok_rows // 2
    features = frames.shape[1]
    CORE, Y, Z0, Z1 = 1, 2, 4, 8

    rim_rows = lax.ppermute(
        frames[tok_rows - (KW - 1) :], both, [(i, i + 1) for i in range(devices - 1)]
    )
    late = convolve(frames[part:], conv_weight, frames[part - (KW - 1) : part])
    early = convolve(frames[:part], conv_weight, rim_rows)

    far_late = xor_swap(late, Z1)
    far_early = xor_swap(early, Z1)
    own = jnp.concatenate([early, late], axis=0)
    beside = xor_swap(own, Y)

    half = features // 2
    held = qkv_weight.T.reshape(3, HD // 2, features)

    def to_heads(block, j):
        pairs = [
            (g * devices + d, g * devices + (3 * d + j[g]) % devices)
            for g in (0, 1)
            for d in range(devices)
        ]
        return lax.ppermute(block, every, pairs)

    outer = to_heads(lax.dynamic_index_in_dim(held, 2 * grp, 0, False), (0, 2))
    middle = to_heads(lax.dynamic_slice_in_dim(held[1], grp * half, half, 1), (1, 1))
    mine = jnp.concatenate([outer[:, :half], outer[:, half:], middle], axis=0)
    paired = xor_swap(mine, Z0)

    mine_too = xor_swap(mine, devices, every)

    cut = 3 * half // 4
    fourth = [xor_swap(paired[:, :cut], devices, every), xor_swap(mine_too[:, cut:], Z0)]

    far_beside_late = xor_swap(far_late + zero_after(fourth[0]) + zero_after(fourth[1]), Y)
    far_beside_early = xor_swap(far_early, Y)

    fourth = jnp.concatenate(fourth, axis=1)

    def whole_head(pieces, theirs, index):
        size = HD // 2

        def block(values, n):
            return values[n * size : (n + 1) * size]

        first, last = (
            jnp.concatenate(
                [jnp.where(grp == g, block(pieces, n), block(theirs, n)) for n in (0, 1)], axis=1
            )
            for g in (0, 1)
        )
        low, high = block(pieces, 2), block(theirs, 2)
        between = jnp.concatenate(
            [jnp.where(grp == 0, low, high), jnp.where(grp == 0, high, low)], axis=1
        )
        turned = [first, between, last, first, between]
        wide = lax.dynamic_slice_in_dim(jnp.stack(turned), lax.rem(index, 3), 3, 0)
        return by_bit(core, wide, xor_swap(wide, CORE), 1).reshape(3 * HD, features)

    two_heads = jnp.concatenate(
        [whole_head(mine, mine_too, me), whole_head(paired, fourth, me ^ Z0)], axis=0
    )

    def project(rows):
        done = lax.dot_general(
            rows, two_heads, (((1,), (1,)), ((), ())), preferred_element_type=jnp.float32
        ).astype(jnp.bfloat16)
        return jnp.concatenate([done[:, : 3 * HD], xor_swap(done[:, 3 * HD :], Z0)], axis=0)

    first = project(jnp.concatenate([own, beside, far_late, far_beside_late], axis=0))
    second = project(jnp.concatenate([far_early, far_beside_early], axis=0))

    first_rows = [(0, 0, tok_rows), (Y, 0, tok_rows), (Z1, part, part), (Z1 | Y, part, part)]
    second_rows = [(Z1, 0, part), (Z1 | Y, 0, part)]
    order = []
    for pieces in (first_rows, second_rows):
        order += pieces + [(far ^ Z0, start, count) for far, start, count in pieces]

    groups = track_groups(track_ids, track_owner)[None, :]
    for bit in (CORE, Y, Z0, Z1):
        groups = jnp.concatenate([groups, xor_swap(groups, bit)], axis=0)

    def of_rows(bit):
        times = [
            (me ^ far ^ bit) * tok_rows + start + jnp.arange(count, dtype=jnp.int32)
            for far, start, count in order
        ]
        marks = [groups[far ^ bit, start : start + count] for far, start, count in order]
        return jnp.concatenate(times), jnp.concatenate(marks)

    projected = jnp.concatenate([first, second], axis=0)
    query = projected[:, :HD]
    keyed = jnp.concatenate(
        [projected[:, HD:], xor_swap(first[:, HD:], CORE), xor_swap(second[:, HD:], CORE)], axis=0
    )
    own_times, own_groups = of_rows(0)
    other_times, other_groups = of_rows(CORE)
    key_times = jnp.concatenate([own_times, other_times])
    key_groups = jnp.concatenate([own_groups, other_groups])
    scores = lax.dot_general(
        query, keyed[:, :HD], (((1,), (1,)), ((), ())), preferred_element_type=jnp.float32
    ) * (1.0 / HD**0.5)
    allowed = (key_times[None, :] <= own_times[:, None]) & (
        key_groups[None, :] == own_groups[:, None]
    )
    scores = jnp.where(allowed, scores, jnp.float32(-1e30))
    expd = jnp.exp(scores - jnp.max(scores, axis=-1, keepdims=True))
    share = 1.0 / jnp.sum(expd, axis=-1, keepdims=True)
    weights = (expd * share).astype(jnp.bfloat16)
    mixed = jnp.dot(weights, keyed[:, HD:], preferred_element_type=jnp.float32)
    mixed = mixed.astype(jnp.bfloat16)

    sent = jnp.zeros((chips, tok_rows, HD), jnp.bfloat16)
    at = 0
    for far, start, count in order:
        rows = mixed[at : at + count]
        sent = lax.dynamic_update_slice(sent, rows[None], ((me ^ far) >> 1, start, 0))
        at += count
    returned = lax.all_to_all(sent, "chip", split_axis=0, concat_axis=0, tiled=True)
    return returned.transpose(1, 0, 2).reshape(tok_rows, chips * HD)


def solution(mesh):
    grp, seq = mesh.devices.shape
    out_by_owner = P(("grp", "seq"), None)
    by_owner = jax.shard_map(
        body_by_owner,
        mesh=mesh,
        in_specs=(P(("grp", "seq"), None), P(), P(None, "seq"), P(("grp", "seq")), P("grp")),
        out_specs=out_by_owner,
        check_vma=False,
    )
    split = Mesh(mesh.devices.reshape(grp, seq // 2, 2), ("grp", "chip", "core"))
    rows = P(("grp", "chip", "core"))
    by_head = jax.shard_map(
        body_by_head,
        mesh=split,
        in_specs=(rows, P(), P(None, ("chip", "core")), rows, P("grp")),
        out_specs=rows,
        check_vma=False,
    )

    def run(frames, conv_weight, qkv_weight, track_ids, track_owner):
        heads = qkv_weight.shape[1] // (3 * HD)
        plan = by_head if (grp, seq, heads) == (2, 16, 8) else by_owner
        return plan(frames, conv_weight, qkv_weight, track_ids, track_owner)

    return run
```

```python
import jax
import jax.numpy as jnp
from jax import lax
from jax.sharding import Mesh
from jax.sharding import PartitionSpec as P

HD = 128
KW = 4


def from_behind(value, axis, by):
    size = lax.axis_size(axis)
    pairs = [(i, i + by) for i in range(size) if 0 <= i + by < size]
    return lax.ppermute(value, axis, pairs)


def track_groups(track_ids, track_owner):
    track_total = track_owner.shape[0]
    return jnp.sum(
        jnp.where(
            track_ids[:, None] == jnp.arange(track_total, dtype=jnp.int32)[None, :],
            track_owner[None, :],
            0,
        ),
        axis=1,
    )


def convolve(frames, conv_weight, rim_rows):
    tok_rows = frames.shape[0]
    extended = jnp.concatenate([rim_rows, frames], axis=0).astype(jnp.float32)
    conv_sum = frames.astype(jnp.float32)
    for tap in range(KW):
        conv_sum = (
            conv_sum
            + conv_weight[tap].astype(jnp.float32)[None, :]
            * extended[KW - 1 - tap : KW - 1 - tap + tok_rows]
        )
    return conv_sum.astype(jnp.bfloat16)


def attend_slots(packed, positions):
    slot_count = packed.shape[0]
    inner = packed.shape[1] // 3
    head_count = inner // HD
    query = packed[:, :inner].reshape(slot_count, head_count, HD)
    keys_all = packed[:, inner : 2 * inner].reshape(slot_count, head_count, HD)
    values_all = packed[:, 2 * inner :].reshape(slot_count, head_count, HD)
    slot_ids = jnp.arange(slot_count, dtype=jnp.int32)
    score_scale = 1.0 / HD**0.5
    scores = (
        jnp.einsum("qhd,khd->hqk", query, keys_all, preferred_element_type=jnp.float32)
        * score_scale
    )
    allowed = (positions[None, :] >= 0) & (positions[None, :] <= positions[:, None]) | (
        slot_ids[:, None] == slot_ids[None, :]
    )
    scores = jnp.where(allowed[None], scores, jnp.float32(-1e30))
    top_score = jnp.max(scores, axis=-1, keepdims=True)
    expd = jnp.exp(scores - top_score)
    weights = (expd / jnp.sum(expd, axis=-1, keepdims=True)).astype(jnp.bfloat16)
    mixed = jnp.einsum("hqk,khd->qhd", weights, values_all, preferred_element_type=jnp.float32)
    return mixed.astype(jnp.bfloat16).reshape(slot_count, inner)


def body_by_owner(frames, conv_weight, qkv_weight, track_ids, track_owner):
    tok_rows = frames.shape[0]
    peer_count = lax.axis_size("seq")
    capacity = 2 * tok_rows // peer_count
    slot_total = capacity * peer_count
    my_index = lax.axis_index("seq")
    rim_rows = from_behind(frames[tok_rows - (KW - 1) :], "seq", 1)
    hidden = convolve(frames, conv_weight, rim_rows)
    group = track_groups(track_ids, track_owner)
    owner_hits = (group[:, None] == jnp.arange(peer_count, dtype=jnp.int32)[None, :]).astype(
        jnp.int32
    )
    running = jnp.cumsum(owner_hits, axis=0) - 1
    rank_rows = jnp.sum(jnp.where(owner_hits > 0, running, 0), axis=1)
    slot_of_row = group * capacity + rank_rows
    row_ids = jnp.arange(tok_rows, dtype=jnp.int32)
    source_row = jnp.full((slot_total,), tok_rows, jnp.int32).at[slot_of_row].set(row_ids)
    positions = my_index * tok_rows + row_ids
    send_times = jnp.full((slot_total,), -1, jnp.int32).at[slot_of_row].set(positions)
    projected = jnp.dot(
        hidden,
        lax.all_gather(qkv_weight, "seq", axis=1, tiled=True),
        preferred_element_type=jnp.float32,
    ).astype(jnp.bfloat16)
    padded_rows = jnp.concatenate(
        [projected, jnp.zeros((1, projected.shape[1]), jnp.bfloat16)], axis=0
    )
    outgoing = padded_rows[source_row]
    received, got_times = (
        lax.all_to_all(outgoing, "seq", split_axis=0, concat_axis=0, tiled=True),
        lax.all_to_all(send_times, "seq", split_axis=0, concat_axis=0, tiled=True),
    )
    mixed = attend_slots(received, got_times)
    returned = lax.all_to_all(mixed, "seq", split_axis=0, concat_axis=0, tiled=True)
    return returned[slot_of_row]


def xor_swap(value, bit, axes=("chip", "core")):
    count = lax.axis_size(axes)
    return lax.ppermute(value, axes, [(d, d ^ bit) for d in range(count)])


def by_bit(bit, mine, theirs, axis):
    return jnp.stack(
        [jnp.where(bit == 0, mine, theirs), jnp.where(bit == 0, theirs, mine)], axis=axis
    )


def zero_after(array):
    last = array[(-1,) * array.ndim]
    return jnp.where(last != last, 1.0, 0.0).astype(jnp.bfloat16)


def body_by_head(frames, conv_weight, qkv_weight, track_ids, track_owner):
    tok_rows = frames.shape[0]
    chips = lax.axis_size("chip")
    devices = 2 * chips
    core = lax.axis_index("core")
    chip = lax.axis_index("chip")
    grp = lax.axis_index("grp")
    me = 2 * chip + core
    both = ("chip", "core")
    every = ("grp", "chip", "core")
    part = tok_rows // 2
    features = frames.shape[1]
    CORE, Y, Z0, Z1 = 1, 2, 4, 8

    rim_rows = lax.ppermute(
        frames[tok_rows - (KW - 1) :], both, [(i, i + 1) for i in range(devices - 1)]
    )
    late = convolve(frames[part:], conv_weight, frames[part - (KW - 1) : part])
    early = convolve(frames[:part], conv_weight, rim_rows)

    far_late = xor_swap(late, Z1)
    far_early = xor_swap(early, Z1)
    own = jnp.concatenate([early, late], axis=0)
    beside = xor_swap(own, Y)

    half = features // 2
    held = qkv_weight.T.reshape(3, HD // 2, features)

    def to_heads(block, j):
        pairs = [
            (g * devices + d, g * devices + (3 * d + j[g]) % devices)
            for g in (0, 1)
            for d in range(devices)
        ]
        return lax.ppermute(block, every, pairs)

    outer = to_heads(lax.dynamic_index_in_dim(held, 2 * grp, 0, False), (0, 2))
    middle = to_heads(lax.dynamic_slice_in_dim(held[1], grp * half, half, 1), (1, 1))
    mine = jnp.concatenate([outer[:, :half], outer[:, half:], middle], axis=0)
    paired = xor_swap(mine, Z0)

    mine_too = xor_swap(mine, devices, every)

    cut = 5 * half // 8
    fourth = [xor_swap(paired[:, :cut], devices, every), xor_swap(mine_too[:, cut:], Z0)]

    far_beside_late = xor_swap(far_late + zero_after(fourth[0]) + zero_after(fourth[1]), Y)
    far_beside_early = xor_swap(far_early, Y)

    fourth = jnp.concatenate(fourth, axis=1)

    def whole_head(pieces, theirs, index):
        size = HD // 2

        def block(values, n):
            return values[n * size : (n + 1) * size]

        first, last = (
            jnp.concatenate(
                [jnp.where(grp == g, block(pieces, n), block(theirs, n)) for n in (0, 1)], axis=1
            )
            for g in (0, 1)
        )
        low, high = block(pieces, 2), block(theirs, 2)
        between = jnp.concatenate(
            [jnp.where(grp == 0, low, high), jnp.where(grp == 0, high, low)], axis=1
        )
        turned = [first, between, last, first, between]
        wide = lax.dynamic_slice_in_dim(jnp.stack(turned), lax.rem(index, 3), 3, 0)
        return by_bit(core, wide, xor_swap(wide, CORE), 1).reshape(3 * HD, features)

    two_heads = jnp.concatenate(
        [whole_head(mine, mine_too, me), whole_head(paired, fourth, me ^ Z0)], axis=0
    )

    def project(rows):
        done = lax.dot_general(
            rows, two_heads, (((1,), (1,)), ((), ())), preferred_element_type=jnp.float32
        ).astype(jnp.bfloat16)
        return jnp.concatenate([done[:, : 3 * HD], xor_swap(done[:, 3 * HD :], Z0)], axis=0)

    first = project(jnp.concatenate([own, beside, far_late, far_beside_late], axis=0))
    second = project(jnp.concatenate([far_early, far_beside_early], axis=0))

    first_rows = [(0, 0, tok_rows), (Y, 0, tok_rows), (Z1, part, part), (Z1 | Y, part, part)]
    second_rows = [(Z1, 0, part), (Z1 | Y, 0, part)]
    order = []
    for pieces in (first_rows, second_rows):
        order += pieces + [(far ^ Z0, start, count) for far, start, count in pieces]

    groups = track_groups(track_ids, track_owner)[None, :]
    for bit in (CORE, Y, Z0, Z1):
        groups = jnp.concatenate([groups, xor_swap(groups, bit)], axis=0)

    def of_rows(bit):
        times = [
            (me ^ far ^ bit) * tok_rows + start + jnp.arange(count, dtype=jnp.int32)
            for far, start, count in order
        ]
        marks = [groups[far ^ bit, start : start + count] for far, start, count in order]
        return jnp.concatenate(times), jnp.concatenate(marks)

    projected = jnp.concatenate([first, second], axis=0)
    query = projected[:, :HD]
    keyed = jnp.concatenate(
        [projected[:, HD:], xor_swap(first[:, HD:], CORE), xor_swap(second[:, HD:], CORE)], axis=0
    )
    own_times, own_groups = of_rows(0)
    other_times, other_groups = of_rows(CORE)
    key_times = jnp.concatenate([own_times, other_times])
    key_groups = jnp.concatenate([own_groups, other_groups])
    scores = lax.dot_general(
        query, keyed[:, :HD], (((1,), (1,)), ((), ())), preferred_element_type=jnp.float32
    ) * (1.0 / HD**0.5)
    allowed = (key_times[None, :] <= own_times[:, None]) & (
        key_groups[None, :] == own_groups[:, None]
    )
    scores = jnp.where(allowed, scores, jnp.float32(-1e30))
    expd = jnp.exp(scores - jnp.max(scores, axis=-1, keepdims=True))
    share = 1.0 / jnp.sum(expd, axis=-1, keepdims=True)
    weights = (expd * share).astype(jnp.bfloat16)
    mixed = jnp.dot(weights, keyed[:, HD:], preferred_element_type=jnp.float32)
    mixed = mixed.astype(jnp.bfloat16)

    sent = jnp.zeros((chips, tok_rows, HD), jnp.bfloat16)
    at = 0
    for far, start, count in order:
        rows = mixed[at : at + count]
        sent = lax.dynamic_update_slice(sent, rows[None], ((me ^ far) >> 1, start, 0))
        at += count
    returned = lax.all_to_all(sent, "chip", split_axis=0, concat_axis=0, tiled=True)
    return returned.transpose(1, 0, 2).reshape(tok_rows, chips * HD)


def solution(mesh):
    grp, seq = mesh.devices.shape
    out_by_owner = P(("grp", "seq"), None)
    by_owner = jax.shard_map(
        body_by_owner,
        mesh=mesh,
        in_specs=(P(("grp", "seq"), None), P(), P(None, "seq"), P(("grp", "seq")), P("grp")),
        out_specs=out_by_owner,
        check_vma=False,
    )
    split = Mesh(mesh.devices.reshape(grp, seq // 2, 2), ("grp", "chip", "core"))
    rows = P(("grp", "chip", "core"))
    by_head = jax.shard_map(
        body_by_head,
        mesh=split,
        in_specs=(rows, P(), P(None, ("chip", "core")), rows, P("grp")),
        out_specs=rows,
        check_vma=False,
    )

    def run(frames, conv_weight, qkv_weight, track_ids, track_owner):
        heads = qkv_weight.shape[1] // (3 * HD)
        plan = by_head if (grp, seq, heads) == (2, 16, 8) else by_owner
        return plan(frames, conv_weight, qkv_weight, track_ids, track_owner)

    return run
```
